128 devices in a mesh: dp: 4 (over y_hi, core), tensor: 32 (over x, y_lo, z).
Axes of the slice: x: 4, y: 4 (y_hi: 2, y_lo: 2; y = y_hi * 2 + y_lo), z: 4, core: 2. Of those that a mesh axis runs over, the one named last changes fastest.
Arguments:
- tokens: bfloat16 [512, 6144], P('dp', 'tensor'), may hold values from -6 to 6
- out_grad: bfloat16 [512, 6144], P('dp', 'tensor'), may hold values from -6 to 6
- gate_codes: int32 [2048, 16384], P(None, 'tensor'), may hold values from 0 to 4095
- gate_zeros: int32 [48, 16384], P(None, 'tensor'), may hold values from 0 to 15
- gate_log_scale: float32 [48, 16384], P(None, 'tensor'), may hold values from -6.9 to -5.5
- up_codes: int32 [2048, 16384], P(None, 'tensor'), may hold values from 0 to 4095
- up_zeros: int32 [48, 16384], P(None, 'tensor'), may hold values from 0 to 15
- up_log_scale: float32 [48, 16384], P(None, 'tensor'), may hold values from -6.9 to -5.5
- down_codes: int32 [16384, 2048], P('tensor'), may hold values from 0 to 4095
- down_zeros: int32 [128, 6144], P('tensor'), may hold values from 0 to 15
- down_log_scale: float32 [128, 6144], P('tensor'), may hold values from -7.66 to -6.27
Outputs:
- tokens_grad: float32 [512, 6144], P('dp', 'tensor')
- gate_scale_grad: float32 [48, 16384], P(None, 'tensor')
- gate_zero_grad: float32 [48, 16384], P(None, 'tensor')
- up_scale_grad: float32 [48, 16384], P(None, 'tensor')
- up_zero_grad: float32 [48, 16384], P(None, 'tensor')
- down_scale_grad: float32 [128, 6144], P('tensor')
- down_zero_grad: float32 [128, 6144], P('tensor')
The draws below stay inside these ranges and needn't reach their ends.
Inputs may be any that keep to these rules, and one draw needn't show every extreme that they name: `gate_codes`: each word holds three 4-bit codes in bits 0-3, 4-7 and 8-11. `up_codes`: each word holds three 4-bit codes in bits 0-3, 4-7 and 8-11. `down_codes`: each word holds three 4-bit codes in bits 0-3, 4-7 and 8-11.
All inputs are finite; a program needn't handle non-finite values.
Results may differ from the reference program's by a relative error of at most 0.0059.
Values may be sent and summed in bfloat16 or wider, within the bound.
No kernel may reach another device: no remote copies, remote signals or barrier semaphores. Data moves between devices by JAX's collectives and lax.ppermute only.
A program may use at most 256 MiB of HBM per device.

```python
import jax
import jax.numpy as jnp
from jax import lax

D = 6144
FF = 16384
GROUP = 128
TOKENS = 512
N_TENSOR = 32


def plant(drawn, own_key, low, largest):
    longest = drawn.shape.index(max(drawn.shape))
    spots = []
    for shift in (0, 1):
        where = [jax.random.randint(jax.random.fold_in(own_key, axis), (), 0, length) for axis, length in enumerate(drawn.shape)]
        where[longest] = (where[longest] + shift) % drawn.shape[longest]
        spots.append(tuple(where))
    return drawn.at[spots[0]].set(low).at[spots[1]].set(largest)


def steps_of(rng, extent, split, smallest, top_value):
    loudness, own = 1.0, jax.random.fold_in(rng, 6)
    for dim, blocks in split:
        steps = jnp.exp(jax.random.uniform(jax.random.fold_in(own, dim), (blocks,), jnp.float32, smallest / len(split), top_value / len(split)))
        loudness = loudness * jnp.repeat(steps, extent[dim] // blocks).reshape([-1 if axis == dim else 1 for axis in range(len(extent))])
    return loudness


def normal_values(key, shape, width, most, cuts=(), kind=jnp.bfloat16):
    drawn = width * jax.random.normal(key, shape, jnp.float32)
    if cuts:
        drawn = drawn * steps_of(key, shape, cuts, -0.22, 0.18)
    return jnp.clip(drawn, -most, most).astype(kind)


def setup_inputs(seed: int = 0) -> dict:
    seeds = jax.random.split(jax.random.key(seed), 12)
    return {
        "tokens": normal_values(seeds[0], (TOKENS, D), 1.0, 6.0, ((0, 4), (1, 32))),
        "out_grad": normal_values(seeds[1], (TOKENS, D), 1.0, 6.0, ((0, 4), (1, 32))),
        "gate_codes": plant(jax.random.randint(seeds[2], (D // 3, FF), 0, 4096), jax.random.fold_in(seeds[2], 1), 0, 4095).astype(jnp.int32),
        "gate_zeros": plant(jax.random.randint(seeds[3], (D // GROUP, FF), 0, 16), jax.random.fold_in(seeds[3], 1), 0, 15).astype(jnp.int32),
        "gate_log_scale": jnp.clip(-6.9 + 1.4000001 * jax.random.uniform(seeds[4], (D // GROUP, FF), jnp.float32) ** steps_of(seeds[4], (D // GROUP, FF), ((1, 32),), -0.2, 0.2), -6.9, -5.5),
        "up_codes": plant(jax.random.randint(seeds[5], (D // 3, FF), 0, 4096), jax.random.fold_in(seeds[5], 1), 0, 4095).astype(jnp.int32),
        "up_zeros": plant(jax.random.randint(seeds[6], (D // GROUP, FF), 0, 16), jax.random.fold_in(seeds[6], 1), 0, 15).astype(jnp.int32),
        "up_log_scale": jnp.clip(-6.9 + 1.4000001 * jax.random.uniform(seeds[7], (D // GROUP, FF), jnp.float32) ** steps_of(seeds[7], (D // GROUP, FF), ((1, 32),), -0.2, 0.2), -6.9, -5.5),
        "down_codes": plant(jax.random.randint(seeds[8], (FF, D // 3), 0, 4096), jax.random.fold_in(seeds[8], 1), 0, 4095).astype(jnp.int32),
        "down_zeros": plant(jax.random.randint(seeds[9], (FF // GROUP, D), 0, 16), jax.random.fold_in(seeds[9], 1), 0, 15).astype(jnp.int32),
        "down_log_scale": jnp.clip(-7.66 + 1.3899999 * jax.random.uniform(seeds[10], (FF // GROUP, D), jnp.float32) ** steps_of(seeds[10], (FF // GROUP, D), ((0, 32),), -0.2, 0.2), -7.66, -6.27),
    }


CONTRACT_LAST = (((1,), (1,)), ((), ()))
CONTRACT_FIRST = (((0,), (0,)), ((), ()))


def unpack_rows(packed):
    fields = [jnp.bitwise_and(jnp.right_shift(packed, 4 * nibble), 15) for nibble in range(3)]
    return jnp.stack(fields, axis=1).reshape(packed.shape[0] * 3, packed.shape[1])


def unpack_columns(packed):
    fields = [jnp.bitwise_and(jnp.right_shift(packed, 4 * nibble), 15) for nibble in range(3)]
    return jnp.stack(fields, axis=2).reshape(packed.shape[0], packed.shape[1] * 3)


def centre(code_values, zero_points):
    row_count, column_count = code_values.shape
    grouped = code_values.reshape(row_count // GROUP, GROUP, column_count).astype(jnp.float32)
    return grouped - zero_points.astype(jnp.float32)[:, None, :]


def dequantize(code_values, zero_points, log_scale):
    row_count, column_count = code_values.shape
    centred = centre(code_values, zero_points)
    weight = (jnp.exp(log_scale)[:, None, :] * centred).astype(jnp.bfloat16)
    return weight.reshape(row_count, column_count)


def group_grads(code_values, zero_points, log_scale, weight_grad):
    row_count, column_count = weight_grad.shape
    scales = jnp.exp(log_scale)
    grouped = weight_grad.reshape(row_count // GROUP, GROUP, column_count)
    weighted = (centre(code_values, zero_points) * grouped).sum(axis=1)
    totals = grouped.sum(axis=1)
    return scales * weighted, -scales * totals


def swiglu_backward(full_tokens, full_grad, gate_weight, up_weight, down_weight):
    gate_pre = jnp.dot(full_tokens, gate_weight, preferred_element_type=jnp.float32)
    up_pre = jnp.dot(full_tokens, up_weight, preferred_element_type=jnp.float32)
    sigmoid_gate = jax.nn.sigmoid(gate_pre)
    silu_gate = gate_pre * sigmoid_gate
    hidden = (silu_gate * up_pre).astype(jnp.bfloat16)
    hidden_grad = lax.dot_general(full_grad, down_weight, CONTRACT_LAST, preferred_element_type=jnp.float32)
    down_weight_grad = lax.dot_general(hidden, full_grad, CONTRACT_FIRST, preferred_element_type=jnp.float32)
    gate_grad_pre = (hidden_grad * up_pre * sigmoid_gate * (1.0 + gate_pre * (1.0 - sigmoid_gate))).astype(jnp.bfloat16)
    up_grad_pre = (hidden_grad * silu_gate).astype(jnp.bfloat16)
    return gate_grad_pre, up_grad_pre, down_weight_grad


def reference(tokens, out_grad, gate_codes, gate_zeros, gate_log_scale, up_codes, up_zeros, up_log_scale, down_codes, down_zeros, down_log_scale):
    block_width = FF // N_TENSOR

    def block(running, block_index):
        first_col = (block_index * block_width).astype(jnp.int32)
        group_first = (block_index * (block_width // GROUP)).astype(jnp.int32)

        def columns(source_array):
            return lax.dynamic_slice_in_dim(source_array, first_col, block_width, 1)

        gate_code = unpack_rows(columns(gate_codes))
        up_code = unpack_rows(columns(up_codes))
        gate_weight = dequantize(gate_code, columns(gate_zeros), columns(gate_log_scale))
        up_weight = dequantize(up_code, columns(up_zeros), columns(up_log_scale))
        down_rows = lax.dynamic_slice_in_dim(down_codes, first_col, block_width, 0)
        down_zero_rows = lax.dynamic_slice_in_dim(down_zeros, group_first, block_width // GROUP, 0)
        down_log_rows = lax.dynamic_slice_in_dim(down_log_scale, group_first, block_width // GROUP, 0)
        down_code = unpack_columns(down_rows)
        down_weight = dequantize(down_code, down_zero_rows, down_log_rows)
        gate_grad_pre, up_grad_pre, down_weight_grad = swiglu_backward(tokens, out_grad, gate_weight, up_weight, down_weight)
        down_scale, down_zero = group_grads(down_code, down_zero_rows, down_log_rows, down_weight_grad)
        gate_weight_grad = lax.dot_general(tokens, gate_grad_pre, CONTRACT_FIRST, preferred_element_type=jnp.float32)
        gate_scale, gate_zero = group_grads(gate_code, columns(gate_zeros), columns(gate_log_scale), gate_weight_grad)
        up_weight_grad = lax.dot_general(tokens, up_grad_pre, CONTRACT_FIRST, preferred_element_type=jnp.float32)
        up_scale, up_zero = group_grads(up_code, columns(up_zeros), columns(up_log_scale), up_weight_grad)
        tokens_part = lax.dot_general(gate_grad_pre, gate_weight, CONTRACT_LAST, preferred_element_type=jnp.float32)
        tokens_part = tokens_part + lax.dot_general(up_grad_pre, up_weight, CONTRACT_LAST, preferred_element_type=jnp.float32)
        return running + tokens_part, (gate_scale, gate_zero, up_scale, up_zero, down_scale, down_zero)

    tokens_grad, block_grads = lax.scan(block, jnp.zeros((TOKENS, D), jnp.float32), jnp.arange(N_TENSOR, dtype=jnp.int32))

    def across(stacked):
        return jnp.transpose(stacked, (1, 0, 2)).reshape(D // GROUP, FF)

    def down_rows_of(stacked):
        return stacked.reshape(FF // GROUP, D)

    return (tokens_grad, across(block_grads[0]), across(block_grads[1]), across(block_grads[2]), across(block_grads[3]), down_rows_of(block_grads[4]), down_rows_of(block_grads[5]))
```

```python
import jax
import jax.numpy as jnp
from jax import lax
from jax.experimental import pallas as pl
from jax.experimental.pallas import tpu as pltpu
from jax.sharding import PartitionSpec as P

N_X, N_Y, N_Z = 4, 2, 4
SHARDS = 32
OWN = 192
THIRD = 64
BLOCKS = 16
WORDS = 128
FEATURES = 384
HIDDEN = 512
LOCAL = 128
MIB = 1 << 20

CONTRACT_LAST = (((1,), (1,)), ((), ()))
CONTRACT_FIRST = (((0,), (0,)), ((), ()))


SPAN = 4


def shard_row(k, word):
    return (word // THIRD) * OWN + k * THIRD + word % THIRD


def first_word(k, group):
    return -((k - 128 * group) // 3)


def spread_over_groups(k, start, rows, values):
    first, last = (3 * start + k) // 128, (3 * (start + rows - 1) + k) // 128
    if first == last:
        return values[first]
    row = start + lax.broadcasted_iota(jnp.int32, (rows, 1), 0)
    return jnp.where(row < first_word(k, last), values[first], values[last])


def call(body, out_shape, in_specs, out_specs, scratch=(), grid=(), flops=0, traffic=0, vmem=24):
    return pl.pallas_call(
        body,
        out_shape=out_shape,
        grid=grid,
        in_specs=in_specs,
        out_specs=out_specs,
        scratch_shapes=list(scratch),
        compiler_params=pltpu.CompilerParams(vmem_limit_bytes=vmem * MIB),
        cost_estimate=pl.CostEstimate(flops=flops, bytes_accessed=traffic, transcendentals=0),
    )


def struct(shape, dtype):
    return jax.ShapeDtypeStruct(shape, dtype)


def from_hbm(*arrays):
    return [pltpu.with_memory_space_constraint(array, pltpu.HBM) for array in arrays]


def from_vmem(*arrays):
    return [pltpu.with_memory_space_constraint(array, pltpu.VMEM) for array in arrays]


VMEM = pl.BlockSpec(memory_space=pltpu.VMEM)
SMEM = pl.BlockSpec(memory_space=pltpu.SMEM)
ANY = pl.BlockSpec(memory_space=pl.ANY)


def by_field_body(tokens_ref, grad_ref, out_ref, wide):
    for index, ref in enumerate((tokens_ref, grad_ref)):
        wide[...] = ref[...].astype(jnp.float32)
        for k in range(3):
            out_ref[index, k * THIRD : (k + 1) * THIRD, :] = wide[pl.ds(k, THIRD, stride=3), :].astype(jnp.bfloat16)


def by_field(tokens, out_grad):
    return call(
        by_field_body,
        struct((2, OWN, LOCAL), jnp.bfloat16),
        [VMEM, VMEM],
        VMEM,
        [pltpu.VMEM((OWN, LOCAL), jnp.float32)],
        traffic=200000,
    )(*from_hbm(tokens.T, out_grad.T))


def field(words, k):
    if k:
        words = jnp.right_shift(words, 4 * k)
    if k < 2:
        words = jnp.bitwise_and(words, 15)
    return words.astype(jnp.float32)


CHUNKS = 4


def row_copy(chunk, source, to, sems):
    rows = pl.ds(chunk * SPAN * WORDS, SPAN * WORDS)
    return pltpu.make_async_copy(source.at[rows], to.at[rows], sems.at[chunk])


def column_copy(chunk, source, to, sems):
    columns = pl.ds(chunk * SPAN * WORDS, SPAN * WORDS)
    return pltpu.make_async_copy(source.at[:, columns], to.at[:, columns], sems.at[chunk])


def unpack_rows_body(codes_hbm, zeros_ref, log_ref, out_ref, codes, sems):
    for chunk in range(CHUNKS):
        row_copy(chunk, codes_hbm, codes, sems).start()

    def unpack_pair(pair, carry):
        @pl.when(pair % 2 == 0)
        def _():
            row_copy(pair // 2, codes_hbm, codes, sems).wait()

        for part in range(2):
            block = pair * 2 + part
            zeros = [zeros_ref[pl.ds(3 * block + g, 1), :].astype(jnp.float32) for g in range(3)]
            scales = [jnp.exp(log_ref[pl.ds(3 * block + g, 1), :]) for g in range(3)]
            for start in range(0, WORDS, 16):
                words = codes[pl.ds(pl.multiple_of(block * WORDS + start, 16), 16), :]
                for k in range(3):
                    zero = spread_over_groups(k, start, 16, zeros)
                    scale = spread_over_groups(k, start, 16, scales)
                    weight = (scale * (field(words, k) - zero)).astype(jnp.bfloat16)
                    row = k * THIRD + start % THIRD
                    out_ref[part * 2 + start // THIRD, pair, row : row + 16, :] = weight
        return carry

    lax.fori_loop(0, BLOCKS // 2, unpack_pair, 0)


def unpack_rows(codes, zeros, log_scale):
    return call(
        unpack_rows_body,
        pltpu.VMEM((N_Z, N_X * N_Y, OWN, HIDDEN), jnp.bfloat16),
        [ANY, VMEM, VMEM],
        VMEM,
        [pltpu.VMEM((BLOCKS * WORDS, HIDDEN), jnp.int32), pltpu.SemaphoreType.DMA((CHUNKS,))],
        flops=20000000,
        traffic=10500000,
    )(*from_hbm(codes, zeros, log_scale))


def field_order(transposed):
    feature = lax.broadcasted_iota(jnp.int32, (FEATURES, FEATURES), 1 if transposed else 0)
    column = lax.broadcasted_iota(jnp.int32, (FEATURES, FEATURES), 0 if transposed else 1)
    wanted = 3 * jnp.bitwise_and(column, 127) + jnp.right_shift(column, 7)
    return (feature == wanted).astype(jnp.float32)


def reorder(rows, transposed):
    return jnp.dot(
        rows, field_order(transposed), precision=lax.Precision.HIGHEST, preferred_element_type=jnp.float32
    )


def unpack_columns_body(codes_hbm, zeros_ref, log_ref, out_ref, table_ref, natural, codes, sems):
    for chunk in range(CHUNKS):
        column_copy(chunk, codes_hbm, codes, sems).start()
    for b in range(BLOCKS):
        columns = slice(b * FEATURES, (b + 1) * FEATURES)
        natural[8 * b : 8 * b + 4, :] = zeros_ref[:, columns].astype(jnp.float32)
        natural[8 * b + 4 : 8 * b + 8, :] = jnp.exp(log_ref[:, columns])
    table_ref[...] = reorder(natural[...], False)

    def unpack_pair(pair, carry):
        @pl.when(pair % 2 == 0)
        def _():
            column_copy(pair // 2, codes_hbm, codes, sems).wait()

        for part in range(2):
            block = pair * 2 + part
            table = table_ref[pl.ds(pl.multiple_of(8 * block, 8), 8), :]
            for g in range(4):
                words = codes[g * 128 : (g + 1) * 128, pl.ds(pl.multiple_of(block * WORDS, WORDS), WORDS)]
                for k in range(3):
                    columns = slice(k * WORDS, (k + 1) * WORDS)
                    zero, scale = table[g : g + 1, columns], table[4 + g : 5 + g, columns]
                    weight = (scale * (field(words, k) - zero)).astype(jnp.bfloat16)
                    to = slice(part * FEATURES + k * WORDS, part * FEATURES + (k + 1) * WORDS)
                    out_ref[pair, g * 128 : (g + 1) * 128, to] = weight
        return carry

    lax.fori_loop(0, BLOCKS // 2, unpack_pair, 0)


def unpack_columns(codes, zeros, log_scale):
    return call(
        unpack_columns_body,
        (
            pltpu.VMEM((N_X * N_Y, HIDDEN, 2 * FEATURES), jnp.bfloat16),
            pltpu.HBM((8 * BLOCKS, FEATURES), jnp.float32),
        ),
        [ANY, VMEM, VMEM],
        (VMEM, VMEM),
        [
            pltpu.VMEM((8 * BLOCKS, FEATURES), jnp.float32),
            pltpu.VMEM((HIDDEN, BLOCKS * WORDS), jnp.int32),
            pltpu.SemaphoreType.DMA((CHUNKS,)),
        ],
        flops=20000000,
        traffic=10700000,
    )(*from_hbm(codes, zeros, log_scale))


SLAB = 8 * OWN


def place_of(place_ref):
    return place_ref[0], place_ref[1], place_ref[2]


def lay_tokens(place, sources, far, to):
    x, y, z = place
    slab = (z + 4 - far) % 4
    for near in range(4):
        source, first = (sources[0], 0) if near < 2 else (sources[-1], 4 if len(sources) == 2 else 0)
        for dy in range(2):
            to[slab, ((x + 4 - near) % 4) * 2 + (y + dy) % 2, :, :] = source[near * 2 + dy - first]
    return slab


def lay_grad(place, sources, far, to):
    x, y, z = place
    slab = (x + 4 - far) % 4
    for near in range(4):
        source, first = (sources[0], 0) if near < 2 else (sources[-1], 4 if len(sources) == 2 else 0)
        z_from = (z + 4 - near) % 4
        for dy in range(2):
            for k in range(3):
                row = pl.multiple_of((z_from // 2) * FEATURES + k * WORDS + (z_from % 2) * THIRD, THIRD)
                to[slab * 2 + (y + dy) % 2, pl.ds(row, THIRD), :] = source[
                    near * 2 + dy - first, k * THIRD : (k + 1) * THIRD, :
                ]
    return slab


def slab_products(place, fars, tokens_refs, grad_refs, gate_ref, up_ref, down_ref, tokens_to, grad_to, totals):
    gate_pre, up_pre, hidden_grad = totals
    for far, tokens_ref, grad_ref in zip(fars, tokens_refs, grad_refs):
        slab = lay_tokens(place, tokens_ref, far, tokens_to)
        features = tokens_to[slab].reshape(SLAB, LOCAL).T
        gate_pre += jnp.dot(features, gate_ref[slab].reshape(SLAB, HIDDEN), preferred_element_type=jnp.float32)
        up_pre += jnp.dot(features, up_ref[slab].reshape(SLAB, HIDDEN), preferred_element_type=jnp.float32)
        slab = lay_grad(place, grad_ref, far, grad_to)
        for dy in range(2):
            piece = grad_to[slab * 2 + dy]
            hidden_grad += jnp.dot(down_ref[slab * 2 + dy], piece, preferred_element_type=jnp.float32)
    return gate_pre, up_pre, hidden_grad


def forward_body(
    place_ref, t0, t1, t3, o0, o1, o3, gate_ref, up_ref, down_ref,
    gate_pre_ref, up_pre_ref, hidden_grad_ref,
    tokens_to, grad_to,
):
    zero = jnp.zeros((LOCAL, HIDDEN), jnp.float32)
    gate_pre_ref[...], up_pre_ref[...], hidden_grad_ref[...] = slab_products(
        place_of(place_ref), (0, 1, 3), ((t0,), (t1,), (t3,)), ((o0,), (o1,), (o3,)), gate_ref, up_ref, down_ref, tokens_to, grad_to,
        (zero, zero, jnp.zeros((HIDDEN, LOCAL), jnp.float32)),
    )


TOKENS_SHAPE = (N_Z, N_X * N_Y, OWN, LOCAL)
GRAD_SHAPE = (N_X * N_Y, 2 * FEATURES, LOCAL)


def forward(place, tokens_parts, grad_parts, gate, up, down):
    f32, bf16 = jnp.float32, jnp.bfloat16
    near = (0, 1, 3)
    return call(
        forward_body,
        (pltpu.VMEM((LOCAL, HIDDEN), f32), pltpu.VMEM((LOCAL, HIDDEN), f32), pltpu.VMEM((HIDDEN, LOCAL), f32)),
        [SMEM] + [VMEM] * 9,
        (VMEM,) * 3,
        [pltpu.VMEM(TOKENS_SHAPE, bf16), pltpu.VMEM(GRAD_SHAPE, bf16)],
        flops=3 * 3 * 2 * 128 * 1536 * 512,
        traffic=18000000,
    )(
        place,
        *from_vmem(*[tokens_parts[far] for far in near], *[grad_parts[far] for far in near]),
        *from_vmem(gate, up, down),
    )


def backward_body(
    place_ref, t0, t1, t2, t2_more, t3, o0, o1, o2, o2_more, o3, gate_ref, up_ref, down_ref, gate_pre_ref, up_pre_ref, hidden_grad_ref,
    partial_ref, tokens_ref, grad_ref, gate_grad_ref, up_grad_ref, hidden_ref,
):
    place = place_of(place_ref)
    gate_pre, up_pre, hidden_grad = slab_products(
        place, (2,), ((t2, t2_more),), ((o2, o2_more),), gate_ref, up_ref, down_ref, tokens_ref, grad_ref,
        (gate_pre_ref[...], up_pre_ref[...], hidden_grad_ref[...]),
    )
    hidden_grad = hidden_grad.T
    sigmoid_gate = jax.nn.sigmoid(gate_pre)
    silu_gate = gate_pre * sigmoid_gate
    hidden = silu_gate * up_pre
    gate_grad = hidden_grad * up_pre * sigmoid_gate * (1.0 + gate_pre * (1.0 - sigmoid_gate))
    up_grad = hidden_grad * silu_gate
    gate_grad_ref[...] = gate_grad.astype(jnp.bfloat16)
    up_grad_ref[...] = up_grad.astype(jnp.bfloat16)
    hidden_ref[...] = hidden.T.astype(jnp.bfloat16)
    gate_turned = gate_grad.T.astype(jnp.bfloat16)
    up_turned = up_grad.T.astype(jnp.bfloat16)
    for slab in range(N_Z):
        total = jnp.dot(gate_ref[slab].reshape(SLAB, HIDDEN), gate_turned, preferred_element_type=jnp.float32)
        total += jnp.dot(up_ref[slab].reshape(SLAB, HIDDEN), up_turned, preferred_element_type=jnp.float32)
        total = total.astype(jnp.bfloat16)
        for shard in range(8):
            partial_ref[shard * 4 + slab] = total[shard * OWN : (shard + 1) * OWN, :]
    for far, source in ((0, t0), (1, t1), (3, t3)):
        lay_tokens(place, (source,), far, tokens_ref)
    for far, source in ((0, o0), (1, o1), (3, o3)):
        lay_grad(place, (source,), far, grad_ref)


def backward(place, tokens_parts, grad_parts, gate, up, down, sums):
    bf16 = jnp.bfloat16
    return call(
        backward_body,
        (
            pltpu.HBM((SHARDS, OWN, LOCAL), bf16),
            pltpu.HBM(TOKENS_SHAPE, bf16),
            pltpu.HBM(GRAD_SHAPE, bf16),
            pltpu.HBM((LOCAL, HIDDEN), bf16),
            pltpu.HBM((LOCAL, HIDDEN), bf16),
            pltpu.HBM((HIDDEN, LOCAL), bf16),
        ),
        [SMEM] + [VMEM] * 16,
        (VMEM,) * 6,
        flops=3 * 2 * 128 * 6144 * 512,
        traffic=24000000,
    )(
        place,
        *from_vmem(*tokens_parts[:2], *tokens_parts[2], tokens_parts[3]),
        *from_vmem(*grad_parts[:2], *grad_parts[2], grad_parts[3]),
        *from_vmem(gate, up, down, *sums),
    )


def row_groups(block, codes, weight_grad, zeros_ref, log_ref, out_ref):
    weighted = [jnp.zeros((8, HIDDEN), jnp.float32)] * 3
    totals = [jnp.zeros((8, HIDDEN), jnp.float32)] * 3
    for start in range(0, WORDS, 8):
        words = codes[pl.ds(pl.multiple_of(block * WORDS + start, 8), 8), :]
        for k in range(3):
            value = weight_grad[shard_row(k, start) : shard_row(k, start) + 8, :]
            product = field(words, k) * value
            first, last = (3 * start + k) // 128, (3 * (start + 7) + k) // 128
            if first == last:
                weighted[first] = weighted[first] + product
                totals[first] = totals[first] + value
            else:
                row = start + lax.broadcasted_iota(jnp.int32, (8, 1), 0)
                low = row < first_word(k, last)
                low_product, low_value = jnp.where(low, product, 0.0), jnp.where(low, value, 0.0)
                weighted[first] = weighted[first] + low_product
                totals[first] = totals[first] + low_value
                weighted[last] = weighted[last] + (product - low_product)
                totals[last] = totals[last] + (value - low_value)
    for g in range(3):
        row = 3 * block + g
        scale = jnp.exp(log_ref[pl.ds(row, 1), :])
        zero = zeros_ref[pl.ds(row, 1), :].astype(jnp.float32)
        total = jnp.sum(totals[g], axis=0, keepdims=True)
        inner = jnp.sum(weighted[g], axis=0, keepdims=True) - zero * total
        out_ref[pl.ds(row, 1), :] = scale * inner
        out_ref[pl.ds(48 + row, 1), :] = -scale * total


def column_groups(block, codes, weight_grad, table_ref, down_rows):
    here = pl.ds(pl.multiple_of(8 * block, 8), 8)
    table = table_ref[here, :]
    for k in range(3):
        columns = slice(k * WORDS, (k + 1) * WORDS)
        scale_rows, zero_rows = [], []
        for g in range(4):
            weighted = jnp.zeros((8, WORDS), jnp.float32)
            total = jnp.zeros((8, WORDS), jnp.float32)
            for start in range(g * 128, g * 128 + 128, 8):
                value = weight_grad[start : start + 8, columns]
                words = codes[start : start + 8, pl.ds(pl.multiple_of(block * WORDS, WORDS), WORDS)]
                weighted = weighted + field(words, k) * value
                total = total + value
            zero, scale = table[g : g + 1, columns], table[4 + g : 5 + g, columns]
            total = jnp.sum(total, axis=0, keepdims=True)
            inner = jnp.sum(weighted, axis=0, keepdims=True) - zero * total
            scale_rows.append(scale * inner)
            zero_rows.append(-scale * total)
        down_rows[here, columns] = jnp.concatenate(scale_rows + zero_rows, axis=0)


def group_body(
    gate_hbm, up_hbm, down_hbm,
    tokens_ref, grad_ref, gate_grad_ref, up_grad_ref, hidden_ref,
    gate_zeros, gate_log, up_zeros, up_log, table_ref,
    first_ref, second_ref,
    gate_codes, up_codes, down_codes, gate_sems, up_sems, down_sems,
    gate_even, up_even, down_even, gate_odd, up_odd, down_odd, down_rows,
):
    def copies(chunk):
        return (
            row_copy(chunk, gate_hbm, gate_codes, gate_sems),
            row_copy(chunk, up_hbm, up_codes, up_sems),
            column_copy(chunk, down_hbm, down_codes, down_sems),
        )

    for chunk in range(CHUNKS):
        for copy in copies(chunk):
            copy.start()

    def products(pair, part, gate_to, up_to, down_to):
        features = jnp.concatenate([tokens_ref[part * 2 + half, pair] for half in range(2)], axis=0)
        gate_to[...] = jnp.dot(features, gate_grad_ref[...], preferred_element_type=jnp.float32)
        up_to[...] = jnp.dot(features, up_grad_ref[...], preferred_element_type=jnp.float32)
        down_to[...] = lax.dot_general(
            hidden_ref[...],
            grad_ref[pair, part * FEATURES : (part + 1) * FEATURES, :],
            CONTRACT_LAST,
            preferred_element_type=jnp.float32,
        )

    def groups(block, gate_from, up_from, down_from):
        row_groups(block, gate_codes, gate_from, gate_zeros, gate_log, first_ref)
        row_groups(block, up_codes, up_from, up_zeros, up_log, second_ref)
        column_groups(block, down_codes, down_from, table_ref, down_rows)

    products(0, 0, gate_even, up_even, down_even)

    def pair_step(pair, carry):
        @pl.when(pair % 2 == 0)
        def _():
            for copy in copies(pair // 2):
                copy.wait()

        products(pair, 1, gate_odd, up_odd, down_odd)
        groups(pair * 2, gate_even, up_even, down_even)
        products(jnp.minimum(pair + 1, BLOCKS // 2 - 1), 0, gate_even, up_even, down_even)
        groups(pair * 2 + 1, gate_odd, up_odd, down_odd)
        return carry

    lax.fori_loop(0, BLOCKS // 2, pair_step, 0)

    for out_ref, begin in ((first_ref, 0), (second_ref, 48)):
        for j in range(3):
            out_ref[96:144, j * 128 : (j + 1) * 128] = down_rows[begin : begin + 48, j * 128 : (j + 1) * 128]
    first_ref[96:128, 384:] = down_rows[96:128, 0:128]
    first_ref[128:144, 384:] = down_rows[96:112, 128:256]
    second_ref[96:112, 384:] = down_rows[112:128, 128:256]
    second_ref[112:144, 384:] = down_rows[96:128, 256:384]


def group_grads(tokens, grad, gate_grad, up_grad, hidden, gate_tables, up_tables, down_codes, table):
    half = struct((144, HIDDEN), jnp.float32)
    gate_codes, *gate_tables = gate_tables
    up_codes, *up_tables = up_tables
    rows, columns = (FEATURES, HIDDEN), (HIDDEN, FEATURES)
    return call(
        group_body,
        (half, half),
        [ANY] * 3 + [VMEM] * 10,
        (VMEM, VMEM),
        [
            pltpu.VMEM((BLOCKS * WORDS, HIDDEN), jnp.int32),
            pltpu.VMEM((BLOCKS * WORDS, HIDDEN), jnp.int32),
            pltpu.VMEM((HIDDEN, BLOCKS * WORDS), jnp.int32),
        ]
        + [pltpu.SemaphoreType.DMA((CHUNKS,))] * 3
        + [pltpu.VMEM(shape, jnp.float32) for shape in (rows, rows, columns) * 2]
        + [pltpu.VMEM((8 * BLOCKS, FEATURES), jnp.float32)],
        flops=3 * 2 * 128 * 6144 * 512,
        traffic=17000000,
        vmem=40,
    )(
        *from_hbm(gate_codes, up_codes, down_codes),
        *from_hbm(tokens, grad, gate_grad, up_grad, hidden, *gate_tables, *up_tables, table),
    )


def split_body(core_ref, mine_ref, other_ref, gs_ref, gz_ref, us_ref, uz_ref, ds_ref, dz_ref, halves, rows):
    core = core_ref[0]

    @pl.when(core == 0)
    def _():
        halves[0] = mine_ref[...]
        halves[1] = other_ref[...]

    @pl.when(core != 0)
    def _():
        halves[1] = mine_ref[...]
        halves[0] = other_ref[...]

    for half, scale_ref, zero_ref in ((0, gs_ref, gz_ref), (1, us_ref, uz_ref)):
        scale_ref[...] = halves[half, 0:48, :]
        zero_ref[...] = halves[half, 48:96, :]
        for j in range(3):
            rows[48 * half : 48 * half + 48, j * 128 : (j + 1) * 128] = halves[half, 96:144, j * 128 : (j + 1) * 128]
    rows[96:128, 0:128] = halves[0, 96:128, 384:]
    rows[96:112, 128:256] = halves[0, 128:144, 384:]
    rows[112:128, 128:256] = halves[1, 96:112, 384:]
    rows[96:128, 256:384] = halves[1, 112:144, 384:]
    natural = reorder(rows[...], True)
    for b in range(BLOCKS):
        columns = slice(b * FEATURES, (b + 1) * FEATURES)
        ds_ref[:, columns] = natural[8 * b : 8 * b + 4, :]
        dz_ref[:, columns] = natural[8 * b + 4 : 8 * b + 8, :]


def split(core, mine, other):
    f32 = jnp.float32
    return call(
        split_body,
        (struct((48, HIDDEN), f32),) * 4 + (struct((4, BLOCKS * FEATURES), f32),) * 2,
        [SMEM, VMEM, VMEM],
        (VMEM,) * 6,
        [pltpu.VMEM((2, 144, HIDDEN), f32), pltpu.VMEM((8 * BLOCKS, FEATURES), f32)],
        traffic=1200000,
    )(core, mine, other)


def sum_body(parts_ref, out_ref):
    total = parts_ref[0].astype(jnp.float32)
    for part in range(1, SHARDS):
        total = total + parts_ref[part].astype(jnp.float32)
    for k in range(3):
        out_ref[pl.ds(k, THIRD, stride=3), :] = total[k * THIRD : (k + 1) * THIRD, :]


def sum_parts(parts):
    return call(sum_body, struct((OWN, LOCAL), jnp.float32), [VMEM], VMEM, traffic=1700000)(parts)


def shifted(block, axis, step):
    return lax.ppermute(block, axis, [(place, (place + step) % 4) for place in range(4)])


def gather_over(block, axis):
    return [block] + [shifted(block, axis, step) for step in range(1, 4)]


def gather_by_passing(block, axis):
    below, above = shifted(block, axis, 1), shifted(block, axis, 3)
    return [block, below, (shifted(below[:4], axis, 1), shifted(above[4:], axis, 3)), above]


def swap(value, axis):
    return lax.ppermute(value, axis, [(0, 1), (1, 0)])


def shards(
    tokens,
    out_grad,
    gate_codes,
    gate_zeros,
    gate_log_scale,
    up_codes,
    up_zeros,
    up_log_scale,
    down_codes,
    down_zeros,
    down_log_scale,
):
    core = lax.axis_index("core")
    place = jnp.stack([lax.axis_index(axis) for axis in ("x", "y_lo", "z")])
    both = by_field(tokens, out_grad)
    other = swap(both, "y_lo")
    gate = unpack_rows(gate_codes, gate_zeros, gate_log_scale)
    both, other, gate = lax.optimization_barrier((both, other, gate))
    tokens_near = jnp.concatenate(gather_over(jnp.stack([both[0], other[0]]), "x"))
    grad_near = jnp.concatenate(gather_over(jnp.stack([both[1], other[1]]), "z"))
    tokens_near, grad_near, up_log_scale, down_log_scale = lax.optimization_barrier(
        (tokens_near, grad_near, up_log_scale, down_log_scale)
    )
    tokens_parts = gather_by_passing(tokens_near, "z")
    grad_parts = gather_by_passing(grad_near, "x")
    up = unpack_rows(up_codes, up_zeros, up_log_scale)
    down, table = unpack_columns(down_codes, down_zeros, down_log_scale)
    sums = forward(place, tokens_parts, grad_parts, gate, up, down)
    partial, all_tokens, all_grad, gate_grad, up_grad, hidden = backward(
        place, tokens_parts, grad_parts, gate, up, down, sums
    )
    parts = lax.all_to_all(partial, ("x", "y_lo", "z"), 0, 0, tiled=True)
    first, second = group_grads(
        all_tokens,
        all_grad,
        gate_grad,
        up_grad,
        hidden,
        (gate_codes, gate_zeros, gate_log_scale),
        (up_codes, up_zeros, up_log_scale),
        down_codes,
        table,
    )
    own = jnp.where(core == 0, first, second)
    given = jnp.where(core == 0, second, first)
    own = own + swap(given, "core")
    own = own.astype(jnp.bfloat16)
    mine = own.astype(jnp.float32) + swap(own, "y_hi").astype(jnp.float32)
    theirs = swap(mine, "core")
    tokens_grad = sum_parts(parts).T
    return (tokens_grad, *split(core.reshape(1), mine, theirs))


def solution(mesh):
    axes = jax.sharding.Mesh(mesh.devices.reshape(2, 2, N_X, N_Y, N_Z), ("y_hi", "core", "x", "y_lo", "z"))
    dp, tensor = ("y_hi", "core"), ("x", "y_lo", "z")
    columns, rows = P(None, tensor), P(tensor, None)
    return jax.shard_map(
        shards,
        mesh=axes,
        in_specs=(P(dp, tensor),) * 2 + (columns,) * 6 + (rows,) * 3,
        out_specs=(P(dp, tensor),) + (columns,) * 4 + (rows,) * 2,
        check_vma=False,
    )
```

```python
import jax
import jax.numpy as jnp
from jax import lax
from jax.experimental import pallas as pl
from jax.experimental.pallas import tpu as pltpu
from jax.sharding import PartitionSpec as P

N_X, N_Y, N_Z = 4, 2, 4
SHARDS = 32
OWN = 192
THIRD = 64
BLOCKS = 16
WORDS = 128
FEATURES = 384
HIDDEN = 512
LOCAL = 128
MIB = 1 << 20

CONTRACT_LAST = (((1,), (1,)), ((), ()))
CONTRACT_FIRST = (((0,), (0,)), ((), ()))


def shard_row(k, word):
    return (word // THIRD) * OWN + k * THIRD + word % THIRD


def first_word(k, group):
    return -((k - 128 * group) // 3)


def spread_over_groups(k, start, rows, values):
    first, last = (3 * start + k) // 128, (3 * (start + rows - 1) + k) // 128
    if first == last:
        return values[first]
    row = start + lax.broadcasted_iota(jnp.int32, (rows, 1), 0)
    return jnp.where(row < first_word(k, last), values[first], values[last])


def call(body, out_shape, in_specs, out_specs, scratch=(), flops=0, traffic=0, vmem=16, aliases=None):
    return pl.pallas_call(
        body,
        out_shape=out_shape,
        in_specs=in_specs,
        out_specs=out_specs,
        scratch_shapes=list(scratch),
        input_output_aliases=aliases or {},
        compiler_params=pltpu.CompilerParams(vmem_limit_bytes=vmem * MIB),
        cost_estimate=pl.CostEstimate(flops=flops, bytes_accessed=traffic, transcendentals=0),
    )


def struct(shape, dtype):
    return jax.ShapeDtypeStruct(shape, dtype)


def from_hbm(*arrays):
    return [pltpu.with_memory_space_constraint(array, pltpu.HBM) for array in arrays]


def from_vmem(*arrays):
    return [pltpu.with_memory_space_constraint(array, pltpu.VMEM) for array in arrays]


VMEM = pl.BlockSpec(memory_space=pltpu.VMEM)
ANY = pl.BlockSpec(memory_space=pl.ANY)


def by_field_body(tokens_ref, grad_ref, tokens_out, grad_out, wide):
    for ref, out_ref in ((tokens_ref, tokens_out), (grad_ref, grad_out)):
        wide[...] = ref[...].astype(jnp.float32)
        for k in range(3):
            out_ref[0, k * THIRD : (k + 1) * THIRD, :] = wide[pl.ds(k, THIRD, stride=3), :].astype(jnp.bfloat16)


def by_field(tokens, out_grad):
    return call(
        by_field_body,
        (struct((1, OWN, LOCAL), jnp.bfloat16),) * 2,
        [VMEM, VMEM],
        (VMEM, VMEM),
        [pltpu.VMEM((OWN, LOCAL), jnp.float32)],
        traffic=200000,
    )(*from_hbm(tokens.T, out_grad.T))


def field(words, k):
    if k:
        words = jnp.right_shift(words, 4 * k)
    if k < 2:
        words = jnp.bitwise_and(words, 15)
    return words.astype(jnp.float32)


CHUNKS = 8
AHEAD = 3


def row_copy(chunk, source, to, sems):
    rows = pl.ds(pl.multiple_of(chunk * 2 * WORDS, 2 * WORDS), 2 * WORDS)
    return pltpu.make_async_copy(source.at[rows], to.at[rows], sems.at[chunk])


def column_copy(chunk, source, to, sems):
    columns = pl.ds(pl.multiple_of(chunk * 2 * WORDS, 2 * WORDS), 2 * WORDS)
    return pltpu.make_async_copy(source.at[:, columns], to.at[:, columns], sems.at[chunk])


def tables_in(sources, targets, sems):
    copies = [pltpu.make_async_copy(a, b, sems.at[i]) for i, (a, b) in enumerate(zip(sources, targets))]
    for copy in copies:
        copy.start()
    return copies


def unpack_rows_pair(pair, codes, zeros_ref, log_ref, out_ref):
    for part in range(2):
        block = pair * 2 + part
        zeros = [zeros_ref[pl.ds(3 * block + g, 1), :].astype(jnp.float32) for g in range(3)]
        scales = [jnp.exp(log_ref[pl.ds(3 * block + g, 1), :]) for g in range(3)]
        for start in range(0, WORDS, 16):
            words = codes[pl.ds(pl.multiple_of(block * WORDS + start, 16), 16), :]
            for k in range(3):
                zero = spread_over_groups(k, start, 16, zeros)
                scale = spread_over_groups(k, start, 16, scales)
                weight = (scale * (field(words, k) - zero)).astype(jnp.bfloat16)
                row = k * THIRD + start % THIRD
                out_ref[part * 2 + start // THIRD, pair, row : row + 16, :] = weight


def streamed(copy_of, source, to, sems, work, at_last=None):
    def step(chunk, carry):
        copy_of(chunk, source, to, sems).wait()

        @pl.when(chunk + AHEAD < CHUNKS)
        def _():
            copy_of(chunk + AHEAD, source, to, sems).start()

        if at_last is not None:
            pl.when(chunk == CHUNKS - AHEAD)(at_last)
        work(chunk)
        return carry

    lax.fori_loop(0, CHUNKS, step, 0)


def start_first(copy_of, source, to, sems):
    for chunk in range(AHEAD):
        copy_of(chunk, source, to, sems).start()


def unpack_rows_body(codes_hbm, zeros_hbm, log_hbm, out_ref, zeros_ref, log_ref, table_sems, codes, sems):
    tables = tables_in((zeros_hbm, log_hbm), (zeros_ref, log_ref), table_sems)
    start_first(row_copy, codes_hbm, codes, sems)
    for table in tables:
        table.wait()
    streamed(
        row_copy, codes_hbm, codes, sems, lambda pair: unpack_rows_pair(pair, codes, zeros_ref, log_ref, out_ref)
    )


def unpack_rows(codes, zeros, log_scale):
    return call(
        unpack_rows_body,
        pltpu.VMEM((N_Z, N_X * N_Y, OWN, HIDDEN), jnp.bfloat16),
        [ANY] * 3,
        VMEM,
        [
            pltpu.VMEM((48, HIDDEN), jnp.int32),
            pltpu.VMEM((48, HIDDEN), jnp.float32),
            pltpu.SemaphoreType.DMA((2,)),
            pltpu.VMEM((BLOCKS * WORDS, HIDDEN), jnp.int32),
            pltpu.SemaphoreType.DMA((CHUNKS,)),
        ],
        flops=20000000,
        traffic=10500000,
    )(*from_hbm(codes, zeros, log_scale))


def field_order(transposed):
    feature = lax.broadcasted_iota(jnp.int32, (FEATURES, FEATURES), 1 if transposed else 0)
    column = lax.broadcasted_iota(jnp.int32, (FEATURES, FEATURES), 0 if transposed else 1)
    wanted = 3 * jnp.bitwise_and(column, 127) + jnp.right_shift(column, 7)
    return (feature == wanted).astype(jnp.float32)


def reorder(rows, transposed):
    return jnp.dot(
        rows, field_order(transposed), precision=lax.Precision.HIGHEST, preferred_element_type=jnp.float32
    )


def unpack_columns_pair(pair, codes, table_ref, out_ref):
    for part in range(2):
        block = pair * 2 + part
        table = table_ref[pl.ds(pl.multiple_of(8 * block, 8), 8), :]
        for g in range(4):
            words = codes[g * 128 : (g + 1) * 128, pl.ds(pl.multiple_of(block * WORDS, WORDS), WORDS)]
            for k in range(3):
                columns = slice(k * WORDS, (k + 1) * WORDS)
                zero, scale = table[g : g + 1, columns], table[4 + g : 5 + g, columns]
                weight = (scale * (field(words, k) - zero)).astype(jnp.bfloat16)
                to = slice(part * FEATURES + k * WORDS, part * FEATURES + (k + 1) * WORDS)
                out_ref[pair, g * 128 : (g + 1) * 128, to] = weight


def unpack_both_body(
    rows_hbm, row_zeros_hbm, row_log_hbm, columns_hbm, zeros_hbm, log_hbm,
    rows_out, columns_out, table_ref,
    row_zeros, row_log, zeros_ref, log_ref, table_sems, natural, row_codes, row_sems, column_codes, column_sems,
):
    tables = tables_in(
        (row_zeros_hbm, row_log_hbm, zeros_hbm, log_hbm), (row_zeros, row_log, zeros_ref, log_ref), table_sems
    )
    start_first(row_copy, rows_hbm, row_codes, row_sems)
    for table in tables:
        table.wait()
    for b in range(BLOCKS):
        columns = slice(b * FEATURES, (b + 1) * FEATURES)
        natural[8 * b : 8 * b + 4, :] = zeros_ref[:, columns].astype(jnp.float32)
        natural[8 * b + 4 : 8 * b + 8, :] = jnp.exp(log_ref[:, columns])
    table_ref[...] = reorder(natural[...], False)
    streamed(
        row_copy, rows_hbm, row_codes, row_sems,
        lambda pair: unpack_rows_pair(pair, row_codes, row_zeros, row_log, rows_out),
        lambda: start_first(column_copy, columns_hbm, column_codes, column_sems),
    )
    streamed(
        column_copy, columns_hbm, column_codes, column_sems,
        lambda pair: unpack_columns_pair(pair, column_codes, table_ref, columns_out),
    )


def unpack_both(row_codes, row_zeros, row_log, codes, zeros, log_scale):
    wide = (4, BLOCKS * FEATURES)
    return call(
        unpack_both_body,
        (
            pltpu.VMEM((N_Z, N_X * N_Y, OWN, HIDDEN), jnp.bfloat16),
            pltpu.VMEM((N_X * N_Y, HIDDEN, 2 * FEATURES), jnp.bfloat16),
            pltpu.HBM((8 * BLOCKS, FEATURES), jnp.float32),
        ),
        [ANY] * 6,
        (VMEM,) * 3,
        [
            pltpu.VMEM((48, HIDDEN), jnp.int32),
            pltpu.VMEM((48, HIDDEN), jnp.float32),
            pltpu.VMEM(wide, jnp.int32),
            pltpu.VMEM(wide, jnp.float32),
            pltpu.SemaphoreType.DMA((4,)),
            pltpu.VMEM((8 * BLOCKS, FEATURES), jnp.float32),
            pltpu.VMEM((BLOCKS * WORDS, HIDDEN), jnp.int32),
            pltpu.SemaphoreType.DMA((CHUNKS,)),
            pltpu.VMEM((HIDDEN, BLOCKS * WORDS), jnp.int32),
            pltpu.SemaphoreType.DMA((CHUNKS,)),
        ],
        flops=40000000,
        traffic=21000000,
    )(*from_hbm(row_codes, row_zeros, row_log, codes, zeros, log_scale))


SLAB = 8 * OWN


def position():
    return tuple(lax.axis_index(axis) for axis in ("x", "y_lo", "z"))


def swapped_with(here, near):
    place = 3 - here if near // 2 else here
    return place + 1 - 2 * (place % 2) if near % 2 else place


def lay_tokens(place, sources, far, to):
    x, y, z = place
    slab = (z + 4 - far) % 4
    for near in range(4):
        source, first = (sources[0], 0) if near < 2 else (sources[-1], 4 if len(sources) == 2 else 0)
        for dy in range(2):
            to[slab, swapped_with(x, near) * 2 + (y + dy) % 2, :, :] = source[near * 2 + dy - first]
    return slab


def lay_grad(place, sources, far, to):
    x, y, z = place
    slab = (x + 4 - far) % 4
    for near in range(4):
        source, first = (sources[0], 0) if near < 2 else (sources[-1], 4 if len(sources) == 2 else 0)
        z_from = swapped_with(z, near)
        for dy in range(2):
            for k in range(3):
                row = pl.multiple_of((z_from // 2) * FEATURES + k * WORDS + (z_from % 2) * THIRD, THIRD)
                to[slab * 2 + (y + dy) % 2, pl.ds(row, THIRD), :] = source[
                    near * 2 + dy - first, k * THIRD : (k + 1) * THIRD, :
                ]
    return slab


def slab_out(slab, tokens_from, tokens_hbm, sems):
    return pltpu.make_async_copy(tokens_from.at[slab], tokens_hbm.at[slab], sems)


def pair_out(slab, grad_from, grad_hbm, sems):
    pairs = pl.ds(slab * 2, 2)
    return pltpu.make_async_copy(grad_from.at[pairs], grad_hbm.at[pairs], sems)


def slab_products(fars, tokens_refs, grad_refs, weights, scratch, hbm, totals):
    gate_ref, up_ref, down_ref = weights
    tokens_to, grad_to, tokens_sems, grad_sems = scratch
    tokens_hbm, grad_hbm = hbm
    place = position()
    gate_pre, up_pre, hidden_grad = totals
    copies, laid = [], []
    for i, far in enumerate(fars):
        slabs = lay_tokens(place, tokens_refs[i], far, tokens_to), lay_grad(place, grad_refs[i], far, grad_to)
        copies.append(slab_out(slabs[0], tokens_to, tokens_hbm, tokens_sems.at[i]))
        copies.append(pair_out(slabs[1], grad_to, grad_hbm, grad_sems.at[i]))
        laid.append(slabs)
    for copy in copies:
        copy.start()
    for slab, grad_slab in laid:
        features = tokens_to[slab].reshape(SLAB, LOCAL).T
        gate_pre += jnp.dot(features, gate_ref[slab].reshape(SLAB, HIDDEN), preferred_element_type=jnp.float32)
        up_pre += jnp.dot(features, up_ref[slab].reshape(SLAB, HIDDEN), preferred_element_type=jnp.float32)
        for dy in range(2):
            piece = grad_to[grad_slab * 2 + dy]
            hidden_grad += jnp.dot(down_ref[grad_slab * 2 + dy], piece, preferred_element_type=jnp.float32)
    return (gate_pre, up_pre, hidden_grad), copies


def forward_body(
    t0, t1, t3, o0, o1, o3, gate_ref, up_ref, down_ref,
    gate_pre_ref, up_pre_ref, hidden_grad_ref, tokens_hbm, grad_hbm,
    tokens_to, grad_to, tokens_sems, grad_sems,
):
    zero = jnp.zeros((LOCAL, HIDDEN), jnp.float32)
    (gate_pre_ref[...], up_pre_ref[...], hidden_grad_ref[...]), copies = slab_products(
        (0, 1, 3), ((t0,), (t1,), (t3,)), ((o0,), (o1,), (o3,)), (gate_ref, up_ref, down_ref),
        (tokens_to, grad_to, tokens_sems, grad_sems), (tokens_hbm, grad_hbm),
        (zero, zero, jnp.zeros((HIDDEN, LOCAL), jnp.float32)),
    )
    for copy in copies:
        copy.wait()


TOKENS_SHAPE = (N_Z, N_X * N_Y, OWN, LOCAL)
GRAD_SHAPE = (N_X * N_Y, 2 * FEATURES, LOCAL)


def slab_scratch(slabs):
    return [
        pltpu.VMEM(TOKENS_SHAPE, jnp.bfloat16),
        pltpu.VMEM(GRAD_SHAPE, jnp.bfloat16),
        pltpu.SemaphoreType.DMA((slabs,)),
        pltpu.SemaphoreType.DMA((slabs,)),
    ]


def forward(tokens_parts, grad_parts, gate, up, down):
    f32, bf16 = jnp.float32, jnp.bfloat16
    near = (0, 1, 3)
    return call(
        forward_body,
        (
            pltpu.VMEM((LOCAL, HIDDEN), f32),
            pltpu.VMEM((LOCAL, HIDDEN), f32),
            pltpu.VMEM((HIDDEN, LOCAL), f32),
            pltpu.HBM(TOKENS_SHAPE, bf16),
            pltpu.HBM(GRAD_SHAPE, bf16),
        ),
        [VMEM] * 9,
        (VMEM,) * 3 + (ANY,) * 2,
        slab_scratch(3),
        flops=3 * 3 * 2 * 128 * 1536 * 512,
        traffic=18000000,
    )(
        *from_vmem(*[tokens_parts[far] for far in near], *[grad_parts[far] for far in near]),
        *from_vmem(gate, up, down),
    )


def backward_body(
    t2, t2_more, o2, o2_more, gate_ref, up_ref, down_ref, gate_pre_ref, up_pre_ref, hidden_grad_ref, tokens_in, grad_in,
    partial_hbm, tokens_hbm, grad_hbm, gate_grad_ref, up_grad_ref, hidden_ref,
    tokens_to, grad_to, tokens_sems, grad_sems, partial, partial_sems,
):
    (gate_pre, up_pre, hidden_grad), copies = slab_products(
        (2,), ((t2, t2_more),), ((o2, o2_more),), (gate_ref, up_ref, down_ref),
        (tokens_to, grad_to, tokens_sems, grad_sems), (tokens_hbm, grad_hbm),
        (gate_pre_ref[...], up_pre_ref[...], hidden_grad_ref[...]),
    )
    hidden_grad = hidden_grad.T
    sigmoid_gate = jax.nn.sigmoid(gate_pre)
    silu_gate = gate_pre * sigmoid_gate
    hidden = silu_gate * up_pre
    gate_grad = hidden_grad * up_pre * sigmoid_gate * (1.0 + gate_pre * (1.0 - sigmoid_gate))
    up_grad = hidden_grad * silu_gate
    gate_grad_ref[...] = gate_grad.astype(jnp.bfloat16)
    up_grad_ref[...] = up_grad.astype(jnp.bfloat16)
    hidden_ref[...] = hidden.T.astype(jnp.bfloat16)
    gate_turned = gate_grad.T.astype(jnp.bfloat16)
    up_turned = up_grad.T.astype(jnp.bfloat16)
    for slab in range(N_Z):
        total = jnp.dot(gate_ref[slab].reshape(SLAB, HIDDEN), gate_turned, preferred_element_type=jnp.float32)
        total += jnp.dot(up_ref[slab].reshape(SLAB, HIDDEN), up_turned, preferred_element_type=jnp.float32)
        partial[slab] = total.astype(jnp.bfloat16).reshape(N_X * N_Y, OWN, LOCAL)
        copy = pltpu.make_async_copy(partial.at[slab], partial_hbm.at[:, slab], partial_sems.at[slab])
        copy.start()
        copies.append(copy)
    for copy in copies:
        copy.wait()


def backward(tokens_parts, grad_parts, gate, up, down, sums, all_tokens, all_grad):
    bf16 = jnp.bfloat16
    return call(
        backward_body,
        (
            pltpu.HBM((N_X * N_Y, N_Z, OWN, LOCAL), bf16),
            pltpu.HBM(TOKENS_SHAPE, bf16),
            pltpu.HBM(GRAD_SHAPE, bf16),
            pltpu.HBM((LOCAL, HIDDEN), bf16),
            pltpu.HBM((LOCAL, HIDDEN), bf16),
            pltpu.HBM((HIDDEN, LOCAL), bf16),
        ),
        [VMEM] * 10 + [ANY] * 2,
        (ANY,) * 3 + (VMEM,) * 3,
        slab_scratch(1) + [pltpu.VMEM(TOKENS_SHAPE, bf16), pltpu.SemaphoreType.DMA((N_Z,))],
        flops=3 * 2 * 128 * 6144 * 512,
        traffic=24000000,
        aliases={10: 1, 11: 2},
    )(
        *from_vmem(*tokens_parts[2], *grad_parts[2], gate, up, down, *sums),
        *from_hbm(all_tokens, all_grad),
    )


EXTRA = 16


def with_sums(rows, members):
    sums = jnp.dot(members, rows, preferred_element_type=jnp.float32)
    head = sums.astype(jnp.bfloat16)
    rest = (sums - head.astype(jnp.float32)).astype(jnp.bfloat16)
    return jnp.concatenate([rows, jnp.concatenate([head, rest], axis=0)], axis=0)


def block_members():
    group = lax.broadcasted_iota(jnp.int32, (8, FEATURES), 0)
    place = lax.broadcasted_iota(jnp.int32, (8, FEATURES), 1)
    half = (place >= OWN).astype(jnp.int32)
    place = place - OWN * half
    k = jnp.right_shift(place, 6)
    feature = 3 * (half * THIRD + place - THIRD * k) + k
    scale = jnp.where(k == 0, 1.0, jnp.where(k == 1, 16.0, 256.0))
    return jnp.where(jnp.right_shift(feature, 7) == group, scale, 0.0).astype(jnp.bfloat16)


def hidden_members():
    group = lax.broadcasted_iota(jnp.int32, (8, HIDDEN), 0)
    unit = lax.broadcasted_iota(jnp.int32, (8, HIDDEN), 1)
    return (jnp.right_shift(unit, 7) == group).astype(jnp.float32).astype(jnp.bfloat16)


MASKS = (15, 240, 3840)
SHRINK = (1.0, 1.0 / 16.0, 1.0 / 256.0)


def in_place(words, k):
    return jnp.bitwise_and(words, MASKS[k]).astype(jnp.float32)


def row_groups(block, codes, weight_grad, zeros_ref, log_ref, out_ref):
    weighted = [jnp.zeros((8, HIDDEN), jnp.float32)] * 3
    for start in range(0, WORDS, 8):
        words = codes[pl.ds(pl.multiple_of(block * WORDS + start, 8), 8), :]
        for k in range(3):
            product = in_place(words, k) * weight_grad[shard_row(k, start) : shard_row(k, start) + 8, :]
            first, last = (3 * start + k) // 128, (3 * (start + 7) + k) // 128
            if first == last:
                weighted[first] = weighted[first] + product
            else:
                low = start + lax.broadcasted_iota(jnp.int32, (8, 1), 0) < first_word(k, last)
                low_product = jnp.where(low, product, 0.0)
                weighted[first] = weighted[first] + low_product
                weighted[last] = weighted[last] + (product - low_product)
    for g in range(3):
        row = 3 * block + g
        scale = jnp.exp(log_ref[pl.ds(row, 1), :])
        zero = zeros_ref[pl.ds(row, 1), :].astype(jnp.float32)
        total = weight_grad[FEATURES + g : FEATURES + g + 1, :] + weight_grad[FEATURES + 8 + g : FEATURES + 9 + g, :]
        out_ref[pl.ds(row, 1), :] = scale * (jnp.sum(weighted[g], axis=0, keepdims=True) - zero * total)
        out_ref[pl.ds(48 + row, 1), :] = -scale * total


def column_groups(block, codes, weight_grad, table_ref, down_rows):
    here = pl.ds(pl.multiple_of(8 * block, 8), 8)
    table = table_ref[here, :]
    totals = weight_grad[HIDDEN : HIDDEN + 4, :] + weight_grad[HIDDEN + 8 : HIDDEN + 12, :]
    for k in range(3):
        columns = slice(k * WORDS, (k + 1) * WORDS)
        sums = []
        for g in range(4):
            weighted = jnp.zeros((8, WORDS), jnp.float32)
            for start in range(g * 128, g * 128 + 128, 8):
                words = codes[start : start + 8, pl.ds(pl.multiple_of(block * WORDS, WORDS), WORDS)]
                weighted = weighted + in_place(words, k) * weight_grad[start : start + 8, columns]
            sums.append(jnp.sum(weighted, axis=0, keepdims=True))
        zero, scale, total = table[0:4, columns], table[4:8, columns], totals[:, columns]
        scale_rows = scale * (jnp.concatenate(sums, axis=0) * SHRINK[k] - zero * total)
        down_rows[here, columns] = jnp.concatenate([scale_rows, -scale * total], axis=0)


def group_body(
    gate_hbm, up_hbm, down_hbm, tokens_hbm, grad_hbm, *small_hbm_and_rest
):
    small_hbm, rest = small_hbm_and_rest[:8], small_hbm_and_rest[8:]
    small, rest = rest[-8:], rest[:-8]
    group_work(gate_hbm, up_hbm, down_hbm, tokens_hbm, grad_hbm, small_hbm, small, *rest)


def group_work(
    gate_hbm, up_hbm, down_hbm, tokens_hbm, grad_hbm, small_hbm, small,
    own_ref, given_ref,
    gate_codes, up_codes, down_codes, gate_sems, up_sems, down_sems, tokens_ref, grad_ref, tokens_sems, grad_sems, small_sems,
    hidden_rows, gate_even, up_even, down_even, gate_odd, up_odd, down_odd, down_rows, halves,
):
    def copies(chunk):
        return (
            row_copy(chunk, gate_hbm, gate_codes, gate_sems),
            row_copy(chunk, up_hbm, up_codes, up_sems),
            column_copy(chunk, down_hbm, down_codes, down_sems),
        )

    def start(chunk):
        for copy in copies(chunk):
            copy.start()

    def rows_in(pair):
        return (
            pltpu.make_async_copy(tokens_hbm.at[:, pair], tokens_ref.at[:, pair], tokens_sems.at[pair]),
            pltpu.make_async_copy(grad_hbm.at[pair], grad_ref.at[pair], grad_sems.at[pair]),
        )

    gate_grad_ref, up_grad_ref, hidden_ref, gate_zeros, gate_log, up_zeros, up_log, table_ref = small
    arrivals = tables_in(small_hbm, small, small_sems)
    for copy in rows_in(0):
        copy.start()
    start(0)
    for pair in range(1, BLOCKS // 2):
        for copy in rows_in(pair):
            copy.start()
    start(1)
    for arrival in arrivals:
        arrival.wait()
    hidden_rows[...] = with_sums(hidden_ref[...], hidden_members())
    members = block_members()
    field_of_row = jnp.right_shift(lax.broadcasted_iota(jnp.int32, (OWN, 1), 0), 6)
    shrink = jnp.where(field_of_row == 0, SHRINK[0], jnp.where(field_of_row == 1, SHRINK[1], SHRINK[2]))
    shrink = jnp.broadcast_to(shrink, (OWN, LOCAL)).astype(jnp.bfloat16)

    def products(pair, part, gate_to, up_to, down_to):
        features = jnp.concatenate([tokens_ref[part * 2 + half, pair] * shrink for half in range(2)], axis=0)
        features = with_sums(features, members)
        gate_to[...] = jnp.dot(features, gate_grad_ref[...], preferred_element_type=jnp.float32)
        up_to[...] = jnp.dot(features, up_grad_ref[...], preferred_element_type=jnp.float32)
        down_to[...] = lax.dot_general(
            hidden_rows[...],
            grad_ref[pair, part * FEATURES : (part + 1) * FEATURES, :],
            CONTRACT_LAST,
            preferred_element_type=jnp.float32,
        )

    def groups(block, gate_from, up_from, down_from):
        row_groups(block, gate_codes, gate_from, gate_zeros, gate_log, halves.at[0])
        row_groups(block, up_codes, up_from, up_zeros, up_log, halves.at[1])
        column_groups(block, down_codes, down_from, table_ref, down_rows)

    for copy in rows_in(0):
        copy.wait()
    products(0, 0, gate_even, up_even, down_even)

    def pair_step(pair, carry):
        for copy in copies(pair):
            copy.wait()

        @pl.when(pair + 2 < CHUNKS)
        def _():
            start(pair + 2)

        products(pair, 1, gate_odd, up_odd, down_odd)
        groups(pair * 2, gate_even, up_even, down_even)
        following = jnp.minimum(pair + 1, BLOCKS // 2 - 1)

        @pl.when(pair < BLOCKS // 2 - 1)
        def _():
            for copy in rows_in(following):
                copy.wait()

        products(following, 0, gate_even, up_even, down_even)
        groups(pair * 2 + 1, gate_odd, up_odd, down_odd)
        return carry

    lax.fori_loop(0, BLOCKS // 2, pair_step, 0)

    for half, begin in ((0, 0), (1, 48)):
        for j in range(3):
            halves[half, 96:144, j * 128 : (j + 1) * 128] = down_rows[begin : begin + 48, j * 128 : (j + 1) * 128]
    halves[0, 96:128, 384:] = down_rows[96:128, 0:128]
    halves[0, 128:144, 384:] = down_rows[96:112, 128:256]
    halves[1, 96:112, 384:] = down_rows[112:128, 128:256]
    halves[1, 112:144, 384:] = down_rows[96:128, 256:384]
    core = lax.axis_index("core")
    own_ref[...] = halves[core]
    given_ref[...] = halves[1 - core]


def group_grads(tokens, grad, gate_grad, up_grad, hidden, gate_tables, up_tables, down_codes, table):
    half = struct((144, HIDDEN), jnp.float32)
    gate_codes, *gate_tables = gate_tables
    up_codes, *up_tables = up_tables
    small = (gate_grad, up_grad, hidden, *gate_tables, *up_tables, table)
    rows, columns = (FEATURES + EXTRA, HIDDEN), (HIDDEN + EXTRA, FEATURES)
    return call(
        group_body,
        (half, half),
        [ANY] * 13,
        (VMEM, VMEM),
        [
            pltpu.VMEM((BLOCKS * WORDS, HIDDEN), jnp.int32),
            pltpu.VMEM((BLOCKS * WORDS, HIDDEN), jnp.int32),
            pltpu.VMEM((HIDDEN, BLOCKS * WORDS), jnp.int32),
        ]
        + [pltpu.SemaphoreType.DMA((CHUNKS,))] * 3
        + [
            pltpu.VMEM(TOKENS_SHAPE, jnp.bfloat16),
            pltpu.VMEM(GRAD_SHAPE, jnp.bfloat16),
            pltpu.SemaphoreType.DMA((BLOCKS // 2,)),
            pltpu.SemaphoreType.DMA((BLOCKS // 2,)),
            pltpu.SemaphoreType.DMA((8,)),
            pltpu.VMEM((HIDDEN + EXTRA, LOCAL), jnp.bfloat16),
        ]
        + [pltpu.VMEM(shape, jnp.float32) for shape in (rows, rows, columns) * 2]
        + [pltpu.VMEM((8 * BLOCKS, FEATURES), jnp.float32), pltpu.VMEM((2, 144, HIDDEN), jnp.float32)]
        + [pltpu.VMEM(array.shape, array.dtype) for array in small],
        flops=3 * 2 * 128 * 6144 * 512,
        traffic=17000000,
        vmem=40,
    )(
        *from_hbm(gate_codes, up_codes, down_codes, tokens, grad, *small),
    )


def split_body(mine_ref, other_ref, gs_ref, gz_ref, us_ref, uz_ref, ds_ref, dz_ref, halves, rows):
    core = lax.axis_index("core")
    halves[core] = mine_ref[...]
    halves[1 - core] = other_ref[...]
    for half, scale_ref, zero_ref in ((0, gs_ref, gz_ref), (1, us_ref, uz_ref)):
        scale_ref[...] = halves[half, 0:48, :]
        zero_ref[...] = halves[half, 48:96, :]
        for j in range(3):
            rows[48 * half : 48 * half + 48, j * 128 : (j + 1) * 128] = halves[half, 96:144, j * 128 : (j + 1) * 128]
    rows[96:128, 0:128] = halves[0, 96:128, 384:]
    rows[96:112, 128:256] = halves[0, 128:144, 384:]
    rows[112:128, 128:256] = halves[1, 96:112, 384:]
    rows[96:128, 256:384] = halves[1, 112:144, 384:]
    natural = reorder(rows[...], True)
    for b in range(BLOCKS):
        columns = slice(b * FEATURES, (b + 1) * FEATURES)
        ds_ref[:, columns] = natural[8 * b : 8 * b + 4, :]
        dz_ref[:, columns] = natural[8 * b + 4 : 8 * b + 8, :]


def split(mine, other):
    f32 = jnp.float32
    return call(
        split_body,
        (struct((48, HIDDEN), f32),) * 4 + (struct((4, BLOCKS * FEATURES), f32),) * 2,
        [VMEM, VMEM],
        (VMEM,) * 6,
        [pltpu.VMEM((2, 144, HIDDEN), f32), pltpu.VMEM((8 * BLOCKS, FEATURES), f32)],
        traffic=1200000,
    )(mine, other)


def sum_body(parts_ref, out_ref):
    total = parts_ref[0].astype(jnp.float32)
    for part in range(1, SHARDS):
        total = total + parts_ref[part].astype(jnp.float32)
    for k in range(3):
        out_ref[pl.ds(k, THIRD, stride=3), :] = total[k * THIRD : (k + 1) * THIRD, :]


def sum_parts(parts):
    return call(sum_body, struct((OWN, LOCAL), jnp.float32), [VMEM], VMEM, traffic=1700000)(parts)


def shifted(block, axis, step):
    return lax.ppermute(block, axis, [(place, (place + step) % 4) for place in range(4)])


NEAR, ACROSS = ((0, 1), (2, 3)), ((0, 3), (1, 2))


def paired(block, axis, pairs):
    other = lax.ppermute(block, axis, [pair for a, b in pairs for pair in ((a, b), (b, a))])
    return jnp.concatenate([block, other])


def passed_on(block, below, above, axis):
    return [block, below, (shifted(below[:4], axis, 1), shifted(above[4:], axis, 3)), above]


def swap(value, axis):
    return lax.ppermute(value, axis, [(0, 1), (1, 0)])


def shards(
    tokens,
    out_grad,
    gate_codes,
    gate_zeros,
    gate_log_scale,
    up_codes,
    up_zeros,
    up_log_scale,
    down_codes,
    down_zeros,
    down_log_scale,
):
    tokens_near, grad_near = by_field(tokens, out_grad)
    tokens_near, grad_near = paired(tokens_near, "y_lo", ((0, 1),)), paired(grad_near, "y_lo", ((0, 1),))
    tokens_near, grad_near = paired(tokens_near, "x", NEAR), paired(grad_near, "z", NEAR)
    tokens_near, gate_zeros = lax.optimization_barrier((tokens_near, gate_zeros))
    tokens_near, grad_near = paired(tokens_near, "x", ACROSS), paired(grad_near, "z", ACROSS)
    gate = unpack_rows(gate_codes, gate_zeros, gate_log_scale)
    tokens_near, gate, up_zeros = lax.optimization_barrier((tokens_near, gate, up_zeros))
    sides = [shifted(tokens_near, "z", 1), shifted(tokens_near, "z", 3), shifted(grad_near, "x", 1), shifted(grad_near, "x", 3)]
    grad_near, up_zeros = lax.optimization_barrier((grad_near, up_zeros))
    up, down, table = unpack_both(up_codes, up_zeros, up_log_scale, down_codes, down_zeros, down_log_scale)
    *sides, up, down = lax.optimization_barrier((*sides, up, down))
    tokens_parts = passed_on(tokens_near, *sides[:2], "z")
    grad_parts = passed_on(grad_near, *sides[2:], "x")
    *sums, all_tokens, all_grad = forward(tokens_parts, grad_parts, gate, up, down)
    partial, all_tokens, all_grad, gate_grad, up_grad, hidden = backward(
        tokens_parts, grad_parts, gate, up, down, sums, all_tokens, all_grad
    )
    parts = lax.all_to_all(partial.reshape(SHARDS, OWN, LOCAL), ("x", "y_lo", "z"), 0, 0, tiled=True)
    own, given = group_grads(
        all_tokens,
        all_grad,
        gate_grad,
        up_grad,
        hidden,
        (gate_codes, gate_zeros, gate_log_scale),
        (up_codes, up_zeros, up_log_scale),
        down_codes,
        table,
    )
    own = own + swap(given, "core")
    own = own.astype(jnp.bfloat16)
    tokens_grad = sum_parts(parts).T
    far, tokens_grad = lax.optimization_barrier((swap(own, "y_hi"), tokens_grad))
    mine = own.astype(jnp.float32) + far.astype(jnp.float32)
    theirs = swap(mine, "core")
    return (tokens_grad, *split(mine, theirs))


def solution(mesh):
    axes = jax.sharding.Mesh(mesh.devices.reshape(2, 2, N_X, N_Y, N_Z), ("y_hi", "core", "x", "y_lo", "z"))
    dp, tensor = ("y_hi", "core"), ("x", "y_lo", "z")
    columns, rows = P(None, tensor), P(tensor, None)
    return jax.shard_map(
        shards,
        mesh=axes,
        in_specs=(P(dp, tensor),) * 2 + (columns,) * 6 + (rows,) * 3,
        out_specs=(P(dp, tensor),) + (columns,) * 4 + (rows,) * 2,
        check_vma=False,
    )
```

```python
import jax
import jax.numpy as jnp
from jax import lax
from jax.experimental import pallas as pl
from jax.experimental.pallas import tpu as pltpu
from jax.sharding import PartitionSpec as P

N_X, N_Y, N_Z = 4, 2, 4
SHARDS = 32
OWN = 192
THIRD = 64
BLOCKS = 16
WORDS = 128
FEATURES = 384
HIDDEN = 512
LOCAL = 128
MIB = 1 << 20

CONTRACT_LAST = (((1,), (1,)), ((), ()))
CONTRACT_FIRST = (((0,), (0,)), ((), ()))


def shard_row(k, word):
    return (word // THIRD) * OWN + k * THIRD + word % THIRD


def first_word(k, group):
    return -((k - 128 * group) // 3)


def spread_over_groups(k, start, rows, values):
    first, last = (3 * start + k) // 128, (3 * (start + rows - 1) + k) // 128
    if first == last:
        return values[first]
    row = start + lax.broadcasted_iota(jnp.int32, (rows, 1), 0)
    return jnp.where(row < first_word(k, last), values[first], values[last])


def call(body, out_shape, in_specs, out_specs, scratch=(), flops=0, traffic=0, vmem=16, aliases=None):
    return pl.pallas_call(
        body,
        out_shape=out_shape,
        in_specs=in_specs,
        out_specs=out_specs,
        scratch_shapes=list(scratch),
        input_output_aliases=aliases or {},
        compiler_params=pltpu.CompilerParams(vmem_limit_bytes=vmem * MIB),
        cost_estimate=pl.CostEstimate(flops=flops, bytes_accessed=traffic, transcendentals=0),
    )


def struct(shape, dtype):
    return jax.ShapeDtypeStruct(shape, dtype)


def from_hbm(*arrays):
    return [pltpu.with_memory_space_constraint(array, pltpu.HBM) for array in arrays]


def from_vmem(*arrays):
    return [pltpu.with_memory_space_constraint(array, pltpu.VMEM) for array in arrays]


VMEM = pl.BlockSpec(memory_space=pltpu.VMEM)
ANY = pl.BlockSpec(memory_space=pl.ANY)


def by_field_body(tokens_ref, grad_ref, tokens_out, grad_out, wide):
    for ref, out_ref in ((tokens_ref, tokens_out), (grad_ref, grad_out)):
        wide[...] = ref[...].astype(jnp.float32)
        for k in range(3):
            out_ref[0, k * THIRD : (k + 1) * THIRD, :] = wide[pl.ds(k, THIRD, stride=3), :].astype(jnp.bfloat16)


def by_field(tokens, out_grad):
    return call(
        by_field_body,
        (struct((1, OWN, LOCAL), jnp.bfloat16),) * 2,
        [VMEM, VMEM],
        (VMEM, VMEM),
        [pltpu.VMEM((OWN, LOCAL), jnp.float32)],
        traffic=200000,
    )(*from_hbm(tokens.T, out_grad.T))


def field(words, k):
    if k:
        words = jnp.right_shift(words, 4 * k)
    if k < 2:
        words = jnp.bitwise_and(words, 15)
    return words.astype(jnp.float32)


CHUNKS = 8
AHEAD = 3


def row_copy(chunk, source, to, sems):
    rows = pl.ds(pl.multiple_of(chunk * 2 * WORDS, 2 * WORDS), 2 * WORDS)
    return pltpu.make_async_copy(source.at[rows], to.at[rows], sems.at[chunk])


def column_copy(chunk, source, to, sems):
    columns = pl.ds(pl.multiple_of(chunk * 2 * WORDS, 2 * WORDS), 2 * WORDS)
    return pltpu.make_async_copy(source.at[:, columns], to.at[:, columns], sems.at[chunk])


def tables_in(sources, targets, sems):
    copies = [pltpu.make_async_copy(a, b, sems.at[i]) for i, (a, b) in enumerate(zip(sources, targets))]
    for copy in copies:
        copy.start()
    return copies


def unpack_rows_pair(pair, codes, zeros_ref, log_ref, out_ref):
    for part in range(2):
        block = pair * 2 + part
        zeros = [zeros_ref[pl.ds(3 * block + g, 1), :].astype(jnp.float32) for g in range(3)]
        scales = [jnp.exp(log_ref[pl.ds(3 * block + g, 1), :]) for g in range(3)]
        for start in range(0, WORDS, 16):
            words = codes[pl.ds(pl.multiple_of(block * WORDS + start, 16), 16), :]
            for k in range(3):
                zero = spread_over_groups(k, start, 16, zeros)
                scale = spread_over_groups(k, start, 16, scales)
                weight = (scale * (field(words, k) - zero)).astype(jnp.bfloat16)
                row = k * THIRD + start % THIRD
                out_ref[part * 2 + start // THIRD, pair, row : row + 16, :] = weight


def streamed(copy_of, source, to, sems, work):
    def step(chunk, carry):
        copy_of(chunk, source, to, sems).wait()

        @pl.when(chunk + AHEAD < CHUNKS)
        def _():
            copy_of(chunk + AHEAD, source, to, sems).start()

        work(chunk)
        return carry

    lax.fori_loop(0, CHUNKS, step, 0)


def start_first(copy_of, source, to, sems):
    for chunk in range(AHEAD):
        copy_of(chunk, source, to, sems).start()


def unpack_rows_body(codes_hbm, zeros_hbm, log_hbm, out_ref, zeros_ref, log_ref, table_sems, codes, sems):
    tables = tables_in((zeros_hbm, log_hbm), (zeros_ref, log_ref), table_sems)
    start_first(row_copy, codes_hbm, codes, sems)
    for table in tables:
        table.wait()
    streamed(
        row_copy, codes_hbm, codes, sems, lambda pair: unpack_rows_pair(pair, codes, zeros_ref, log_ref, out_ref)
    )


def unpack_rows(codes, zeros, log_scale):
    return call(
        unpack_rows_body,
        pltpu.VMEM((N_Z, N_X * N_Y, OWN, HIDDEN), jnp.bfloat16),
        [ANY] * 3,
        VMEM,
        [
            pltpu.VMEM((48, HIDDEN), jnp.int32),
            pltpu.VMEM((48, HIDDEN), jnp.float32),
            pltpu.SemaphoreType.DMA((2,)),
            pltpu.VMEM((BLOCKS * WORDS, HIDDEN), jnp.int32),
            pltpu.SemaphoreType.DMA((CHUNKS,)),
        ],
        flops=20000000,
        traffic=10500000,
    )(*from_hbm(codes, zeros, log_scale))


def field_order(transposed):
    feature = lax.broadcasted_iota(jnp.int32, (FEATURES, FEATURES), 1 if transposed else 0)
    column = lax.broadcasted_iota(jnp.int32, (FEATURES, FEATURES), 0 if transposed else 1)
    wanted = 3 * jnp.bitwise_and(column, 127) + jnp.right_shift(column, 7)
    return (feature == wanted).astype(jnp.float32)


def reorder(rows, transposed):
    return jnp.dot(
        rows, field_order(transposed), precision=lax.Precision.HIGHEST, preferred_element_type=jnp.float32
    )


def unpack_columns_pair(pair, codes, table_ref, out_ref):
    for part in range(2):
        block = pair * 2 + part
        table = table_ref[pl.ds(pl.multiple_of(8 * block, 8), 8), :]
        for g in range(4):
            words = codes[g * 128 : (g + 1) * 128, pl.ds(pl.multiple_of(block * WORDS, WORDS), WORDS)]
            for k in range(3):
                columns = slice(k * WORDS, (k + 1) * WORDS)
                zero, scale = table[g : g + 1, columns], table[4 + g : 5 + g, columns]
                weight = (scale * (field(words, k) - zero)).astype(jnp.bfloat16)
                to = slice(part * FEATURES + k * WORDS, part * FEATURES + (k + 1) * WORDS)
                out_ref[pair, g * 128 : (g + 1) * 128, to] = weight


def unpack_columns_body(
    codes_hbm, zeros_hbm, log_hbm, out_ref, table_ref, zeros_ref, log_ref, table_sems, natural, codes, sems
):
    tables = tables_in((zeros_hbm, log_hbm), (zeros_ref, log_ref), table_sems)
    start_first(column_copy, codes_hbm, codes, sems)
    for table in tables:
        table.wait()
    for b in range(BLOCKS):
        columns = slice(b * FEATURES, (b + 1) * FEATURES)
        natural[8 * b : 8 * b + 4, :] = zeros_ref[:, columns].astype(jnp.float32)
        natural[8 * b + 4 : 8 * b + 8, :] = jnp.exp(log_ref[:, columns])
    table_ref[...] = reorder(natural[...], False)
    streamed(column_copy, codes_hbm, codes, sems, lambda pair: unpack_columns_pair(pair, codes, table_ref, out_ref))


def unpack_columns(codes, zeros, log_scale):
    wide = (4, BLOCKS * FEATURES)
    return call(
        unpack_columns_body,
        (
            pltpu.VMEM((N_X * N_Y, HIDDEN, 2 * FEATURES), jnp.bfloat16),
            pltpu.HBM((8 * BLOCKS, FEATURES), jnp.float32),
        ),
        [ANY] * 3,
        (VMEM,) * 2,
        [
            pltpu.VMEM(wide, jnp.int32),
            pltpu.VMEM(wide, jnp.float32),
            pltpu.SemaphoreType.DMA((2,)),
            pltpu.VMEM((8 * BLOCKS, FEATURES), jnp.float32),
            pltpu.VMEM((HIDDEN, BLOCKS * WORDS), jnp.int32),
            pltpu.SemaphoreType.DMA((CHUNKS,)),
        ],
        flops=20000000,
        traffic=10500000,
    )(*from_hbm(codes, zeros, log_scale))


SLAB = 8 * OWN


def position():
    return tuple(lax.axis_index(axis) for axis in ("x", "y_lo", "z"))


def swapped_with(here, near):
    place = 3 - here if near // 2 else here
    return place + 1 - 2 * (place % 2) if near % 2 else place


def lay_tokens(place, source, far, to):
    x, y, z = place
    slab = (z + 4 - far) % 4
    for near in range(4):
        for dy in range(2):
            to[slab, swapped_with(x, near) * 2 + (y + dy) % 2, :, :] = source[near * 2 + dy]
    return slab


def lay_grad(place, source, far, to):
    x, y, z = place
    slab = (x + 4 - far) % 4
    for near in range(4):
        z_from = swapped_with(z, near)
        for dy in range(2):
            for k in range(3):
                row = pl.multiple_of((z_from // 2) * FEATURES + k * WORDS + (z_from % 2) * THIRD, THIRD)
                to[slab * 2 + (y + dy) % 2, pl.ds(row, THIRD), :] = source[
                    near * 2 + dy, k * THIRD : (k + 1) * THIRD, :
                ]
    return slab


def slab_out(slab, tokens_from, tokens_hbm, sems):
    return pltpu.make_async_copy(tokens_from.at[slab], tokens_hbm.at[slab], sems)


def pair_out(slab, grad_from, grad_hbm, sems):
    pairs = pl.ds(slab * 2, 2)
    return pltpu.make_async_copy(grad_from.at[pairs], grad_hbm.at[pairs], sems)


def slab_products(fars, tokens_refs, grad_refs, weights, scratch, hbm, totals):
    gate_ref, up_ref, down_ref = weights
    tokens_to, grad_to, tokens_sems, grad_sems = scratch
    tokens_hbm, grad_hbm = hbm
    place = position()
    gate_pre, up_pre, hidden_grad = totals
    copies, laid = [], []
    for i, far in enumerate(fars):
        slabs = lay_tokens(place, tokens_refs[i], far, tokens_to), lay_grad(place, grad_refs[i], far, grad_to)
        copies.append(slab_out(slabs[0], tokens_to, tokens_hbm, tokens_sems.at[i]))
        copies.append(pair_out(slabs[1], grad_to, grad_hbm, grad_sems.at[i]))
        laid.append(slabs)
    for copy in copies:
        copy.start()
    for slab, grad_slab in laid:
        features = tokens_to[slab].reshape(SLAB, LOCAL).T
        gate_pre += jnp.dot(features, gate_ref[slab].reshape(SLAB, HIDDEN), preferred_element_type=jnp.float32)
        up_pre += jnp.dot(features, up_ref[slab].reshape(SLAB, HIDDEN), preferred_element_type=jnp.float32)
        for dy in range(2):
            piece = grad_to[grad_slab * 2 + dy]
            hidden_grad += jnp.dot(down_ref[grad_slab * 2 + dy], piece, preferred_element_type=jnp.float32)
    return (gate_pre, up_pre, hidden_grad), copies


def forward_body(
    t0, t1, t3, o0, o1, o3, gate_ref, up_ref, down_ref,
    gate_pre_ref, up_pre_ref, hidden_grad_ref, tokens_hbm, grad_hbm,
    tokens_to, grad_to, tokens_sems, grad_sems,
):
    zero = jnp.zeros((LOCAL, HIDDEN), jnp.float32)
    core = lax.axis_index("core")
    (gate_pre_ref[...], up_pre_ref[...], hidden_grad_ref[...]), copies = slab_products(
        (0, 1 + 2 * core, 3 - 2 * core), (t0, t1, t3), (o0, o1, o3), (gate_ref, up_ref, down_ref),
        (tokens_to, grad_to, tokens_sems, grad_sems), (tokens_hbm, grad_hbm),
        (zero, zero, jnp.zeros((HIDDEN, LOCAL), jnp.float32)),
    )
    for copy in copies:
        copy.wait()


TOKENS_SHAPE = (N_Z, N_X * N_Y, OWN, LOCAL)
GRAD_SHAPE = (N_X * N_Y, 2 * FEATURES, LOCAL)


def slab_scratch(slabs):
    return [
        pltpu.VMEM(TOKENS_SHAPE, jnp.bfloat16),
        pltpu.VMEM(GRAD_SHAPE, jnp.bfloat16),
        pltpu.SemaphoreType.DMA((slabs,)),
        pltpu.SemaphoreType.DMA((slabs,)),
    ]


def forward(tokens_parts, grad_parts, gate, up, down):
    f32, bf16 = jnp.float32, jnp.bfloat16
    near = (0, 1, 3)
    return call(
        forward_body,
        (
            pltpu.VMEM((LOCAL, HIDDEN), f32),
            pltpu.VMEM((LOCAL, HIDDEN), f32),
            pltpu.VMEM((HIDDEN, LOCAL), f32),
            pltpu.HBM(TOKENS_SHAPE, bf16),
            pltpu.HBM(GRAD_SHAPE, bf16),
        ),
        [VMEM] * 9,
        (VMEM,) * 3 + (ANY,) * 2,
        slab_scratch(3),
        flops=3 * 3 * 2 * 128 * 1536 * 512,
        traffic=18000000,
    )(
        *from_vmem(*[tokens_parts[far] for far in near], *[grad_parts[far] for far in near]),
        *from_vmem(gate, up, down),
    )


def backward_body(
    t2, o2, gate_ref, up_ref, down_ref, gate_pre_ref, up_pre_ref, hidden_grad_ref, tokens_in, grad_in,
    partial_hbm, tokens_hbm, grad_hbm, gate_grad_hbm, up_grad_hbm, hidden_hbm,
    tokens_to, grad_to, tokens_sems, grad_sems, partial, partial_sems, gate_grad_ref, up_grad_ref, hidden_ref, small_sems,
):
    (gate_pre, up_pre, hidden_grad), copies = slab_products(
        (2,), (t2,), (o2,), (gate_ref, up_ref, down_ref),
        (tokens_to, grad_to, tokens_sems, grad_sems), (tokens_hbm, grad_hbm),
        (gate_pre_ref[...], up_pre_ref[...], hidden_grad_ref[...]),
    )
    hidden_grad = hidden_grad.T
    sigmoid_gate = jax.nn.sigmoid(gate_pre)
    silu_gate = gate_pre * sigmoid_gate
    hidden = silu_gate * up_pre
    gate_grad = hidden_grad * up_pre * sigmoid_gate * (1.0 + gate_pre * (1.0 - sigmoid_gate))
    up_grad = hidden_grad * silu_gate
    gate_grad_ref[...] = gate_grad.astype(jnp.bfloat16)
    up_grad_ref[...] = up_grad.astype(jnp.bfloat16)
    hidden_ref[...] = hidden.T.astype(jnp.bfloat16)
    copies += tables_in(
        (gate_grad_ref, up_grad_ref, hidden_ref), (gate_grad_hbm, up_grad_hbm, hidden_hbm), small_sems
    )
    gate_turned = gate_grad.T.astype(jnp.bfloat16)
    up_turned = up_grad.T.astype(jnp.bfloat16)
    for slab in range(N_Z):
        total = jnp.dot(gate_ref[slab].reshape(SLAB, HIDDEN), gate_turned, preferred_element_type=jnp.float32)
        total += jnp.dot(up_ref[slab].reshape(SLAB, HIDDEN), up_turned, preferred_element_type=jnp.float32)
        partial[slab] = total.astype(jnp.bfloat16).reshape(N_X * N_Y, OWN, LOCAL)
        copy = pltpu.make_async_copy(partial.at[slab], partial_hbm.at[:, slab], partial_sems.at[slab])
        copy.start()
        copies.append(copy)
    for copy in copies:
        copy.wait()


def backward(tokens_parts, grad_parts, gate, up, down, sums, all_tokens, all_grad):
    bf16 = jnp.bfloat16
    return call(
        backward_body,
        (
            pltpu.HBM((N_X * N_Y, N_Z, OWN, LOCAL), bf16),
            pltpu.HBM(TOKENS_SHAPE, bf16),
            pltpu.HBM(GRAD_SHAPE, bf16),
            pltpu.HBM((LOCAL, HIDDEN), bf16),
            pltpu.HBM((LOCAL, HIDDEN), bf16),
            pltpu.HBM((HIDDEN, LOCAL), bf16),
        ),
        [VMEM] * 8 + [ANY] * 2,
        (ANY,) * 6,
        slab_scratch(1)
        + [
            pltpu.VMEM(TOKENS_SHAPE, bf16),
            pltpu.SemaphoreType.DMA((N_Z,)),
            pltpu.VMEM((LOCAL, HIDDEN), bf16),
            pltpu.VMEM((LOCAL, HIDDEN), bf16),
            pltpu.VMEM((HIDDEN, LOCAL), bf16),
            pltpu.SemaphoreType.DMA((3,)),
        ],
        flops=3 * 2 * 128 * 6144 * 512,
        traffic=24000000,
        aliases={8: 1, 9: 2},
    )(
        *from_vmem(tokens_parts[2], grad_parts[2], gate, up, down, *sums),
        *from_hbm(all_tokens, all_grad),
    )


EXTRA = 16


def with_sums(rows, members):
    sums = jnp.dot(members, rows, preferred_element_type=jnp.float32)
    head = sums.astype(jnp.bfloat16)
    rest = (sums - head.astype(jnp.float32)).astype(jnp.bfloat16)
    return jnp.concatenate([rows, jnp.concatenate([head, rest], axis=0)], axis=0)


def block_members():
    group = lax.broadcasted_iota(jnp.int32, (8, FEATURES), 0)
    place = lax.broadcasted_iota(jnp.int32, (8, FEATURES), 1)
    half = (place >= OWN).astype(jnp.int32)
    place = place - OWN * half
    k = jnp.right_shift(place, 6)
    feature = 3 * (half * THIRD + place - THIRD * k) + k
    scale = jnp.where(k == 0, 1.0, jnp.where(k == 1, 16.0, 256.0))
    return jnp.where(jnp.right_shift(feature, 7) == group, scale, 0.0).astype(jnp.bfloat16)


def hidden_members():
    group = lax.broadcasted_iota(jnp.int32, (8, HIDDEN), 0)
    unit = lax.broadcasted_iota(jnp.int32, (8, HIDDEN), 1)
    return (jnp.right_shift(unit, 7) == group).astype(jnp.float32).astype(jnp.bfloat16)


MASKS = (15, 240, 3840)
SHRINK = (1.0, 1.0 / 16.0, 1.0 / 256.0)


def in_place(words, k):
    return jnp.bitwise_and(words, MASKS[k]).astype(jnp.float32)


def row_groups(block, codes, weight_grad, zeros_ref, log_ref, out_ref):
    weighted = [jnp.zeros((8, HIDDEN), jnp.float32)] * 3
    for start in range(0, WORDS, 8):
        words = codes[pl.ds(pl.multiple_of(block * WORDS + start, 8), 8), :]
        for k in range(3):
            product = in_place(words, k) * weight_grad[shard_row(k, start) : shard_row(k, start) + 8, :]
            first, last = (3 * start + k) // 128, (3 * (start + 7) + k) // 128
            if first == last:
                weighted[first] = weighted[first] + product
            else:
                low = start + lax.broadcasted_iota(jnp.int32, (8, 1), 0) < first_word(k, last)
                low_product = jnp.where(low, product, 0.0)
                weighted[first] = weighted[first] + low_product
                weighted[last] = weighted[last] + (product - low_product)
    for g in range(3):
        row = 3 * block + g
        scale = jnp.exp(log_ref[pl.ds(row, 1), :])
        zero = zeros_ref[pl.ds(row, 1), :].astype(jnp.float32)
        total = weight_grad[FEATURES + g : FEATURES + g + 1, :] + weight_grad[FEATURES + 8 + g : FEATURES + 9 + g, :]
        out_ref[pl.ds(row, 1), :] = scale * (jnp.sum(weighted[g], axis=0, keepdims=True) - zero * total)
        out_ref[pl.ds(48 + row, 1), :] = -scale * total


def column_groups(block, part, codes, weight_grad, table_ref, down_rows):
    here = pl.ds(pl.multiple_of(8 * block, 8), 8)
    table = table_ref[here, :]
    mine = slice(part * FEATURES, (part + 1) * FEATURES)
    totals = weight_grad[HIDDEN : HIDDEN + 4, mine] + weight_grad[HIDDEN + 8 : HIDDEN + 12, mine]
    for k in range(3):
        columns = slice(k * WORDS, (k + 1) * WORDS)
        sums = []
        for g in range(4):
            weighted = jnp.zeros((8, WORDS), jnp.float32)
            for start in range(g * 128, g * 128 + 128, 8):
                words = codes[start : start + 8, pl.ds(pl.multiple_of(block * WORDS, WORDS), WORDS)]
                value = weight_grad[start : start + 8, part * FEATURES + k * WORDS : part * FEATURES + (k + 1) * WORDS]
                weighted = weighted + in_place(words, k) * value
            sums.append(jnp.sum(weighted, axis=0, keepdims=True))
        zero, scale, total = table[0:4, columns], table[4:8, columns], totals[:, columns]
        scale_rows = scale * (jnp.concatenate(sums, axis=0) * SHRINK[k] - zero * total)
        down_rows[here, columns] = jnp.concatenate([scale_rows, -scale * total], axis=0)


def group_body(
    gate_hbm, up_hbm, down_hbm, tokens_hbm, grad_hbm, *small_hbm_and_rest
):
    small_hbm, rest = small_hbm_and_rest[:8], small_hbm_and_rest[8:]
    small, rest = rest[-8:], rest[:-8]
    group_work(gate_hbm, up_hbm, down_hbm, tokens_hbm, grad_hbm, small_hbm, small, *rest)


def group_work(
    gate_hbm, up_hbm, down_hbm, tokens_hbm, grad_hbm, small_hbm, small,
    own_ref, given_ref,
    gate_codes, up_codes, down_codes, gate_sems, up_sems, down_sems, tokens_ref, grad_ref, tokens_sems, grad_sems, small_sems,
    hidden_rows, gate_even, up_even, gate_odd, up_odd, down_pair, down_rows, halves,
):
    def copies(chunk):
        return (
            row_copy(chunk, gate_hbm, gate_codes, gate_sems),
            row_copy(chunk, up_hbm, up_codes, up_sems),
            column_copy(chunk, down_hbm, down_codes, down_sems),
        )

    def start(chunk):
        for copy in copies(chunk):
            copy.start()

    def rows_in(pair):
        return (
            pltpu.make_async_copy(tokens_hbm.at[:, pair], tokens_ref.at[:, pair], tokens_sems.at[pair]),
            pltpu.make_async_copy(grad_hbm.at[pair], grad_ref.at[pair], grad_sems.at[pair]),
        )

    gate_grad_ref, up_grad_ref, hidden_ref, gate_zeros, gate_log, up_zeros, up_log, table_ref = small
    arrivals = tables_in(small_hbm, small, small_sems)
    for copy in rows_in(0):
        copy.start()
    start(0)
    for pair in range(1, BLOCKS // 2):
        for copy in rows_in(pair):
            copy.start()
    start(1)
    for arrival in arrivals:
        arrival.wait()
    hidden_rows[...] = with_sums(hidden_ref[...], hidden_members())
    members = block_members()
    field_of_row = jnp.right_shift(lax.broadcasted_iota(jnp.int32, (OWN, 1), 0), 6)
    shrink = jnp.where(field_of_row == 0, SHRINK[0], jnp.where(field_of_row == 1, SHRINK[1], SHRINK[2]))
    shrink = jnp.broadcast_to(shrink, (OWN, LOCAL)).astype(jnp.bfloat16)

    def row_products(pair, part, gate_to, up_to):
        features = jnp.concatenate([tokens_ref[part * 2 + half, pair] * shrink for half in range(2)], axis=0)
        features = with_sums(features, members)
        gate_to[...] = jnp.dot(features, gate_grad_ref[...], preferred_element_type=jnp.float32)
        up_to[...] = jnp.dot(features, up_grad_ref[...], preferred_element_type=jnp.float32)

    def column_products(pair, down_to):
        down_to[...] = lax.dot_general(
            hidden_rows[...], grad_ref[pair], CONTRACT_LAST, preferred_element_type=jnp.float32
        )

    def groups(block, gate_from, up_from):
        row_groups(block, gate_codes, gate_from, gate_zeros, gate_log, halves.at[0])
        row_groups(block, up_codes, up_from, up_zeros, up_log, halves.at[1])

    for copy in rows_in(0):
        copy.wait()
    row_products(0, 0, gate_even, up_even)

    def pair_step(pair, carry):
        for copy in copies(pair):
            copy.wait()
        following = jnp.minimum(pair + 1, BLOCKS // 2 - 1)

        @pl.when(pair < BLOCKS // 2 - 1)
        def _():
            for copy in rows_in(following):
                copy.wait()

        @pl.when(pair + 2 < CHUNKS)
        def _():
            start(pair + 2)

        row_products(pair, 1, gate_odd, up_odd)
        groups(pair * 2, gate_even, up_even)
        column_products(pair, down_pair)
        groups(pair * 2 + 1, gate_odd, up_odd)
        row_products(following, 0, gate_even, up_even)
        for part in range(2):
            column_groups(pair * 2 + part, part, down_codes, down_pair, table_ref, down_rows)
        return carry

    lax.fori_loop(0, BLOCKS // 2, pair_step, 0)

    for half, begin in ((0, 0), (1, 48)):
        for j in range(3):
            halves[half, 96:144, j * 128 : (j + 1) * 128] = down_rows[begin : begin + 48, j * 128 : (j + 1) * 128]
    halves[0, 96:128, 384:] = down_rows[96:128, 0:128]
    halves[0, 128:144, 384:] = down_rows[96:112, 128:256]
    halves[1, 96:112, 384:] = down_rows[112:128, 128:256]
    halves[1, 112:144, 384:] = down_rows[96:128, 256:384]
    core = lax.axis_index("core")
    own_ref[...] = halves[core]
    given_ref[...] = halves[1 - core]


def group_grads(tokens, grad, gate_grad, up_grad, hidden, gate_tables, up_tables, down_codes, table):
    half = struct((144, HIDDEN), jnp.float32)
    gate_codes, *gate_tables = gate_tables
    up_codes, *up_tables = up_tables
    small = (gate_grad, up_grad, hidden, *gate_tables, *up_tables, table)
    rows, columns = (FEATURES + EXTRA, HIDDEN), (HIDDEN + EXTRA, 2 * FEATURES)
    return call(
        group_body,
        (half, half),
        [ANY] * 13,
        (VMEM, VMEM),
        [
            pltpu.VMEM((BLOCKS * WORDS, HIDDEN), jnp.int32),
            pltpu.VMEM((BLOCKS * WORDS, HIDDEN), jnp.int32),
            pltpu.VMEM((HIDDEN, BLOCKS * WORDS), jnp.int32),
        ]
        + [pltpu.SemaphoreType.DMA((CHUNKS,))] * 3
        + [
            pltpu.VMEM(TOKENS_SHAPE, jnp.bfloat16),
            pltpu.VMEM(GRAD_SHAPE, jnp.bfloat16),
            pltpu.SemaphoreType.DMA((BLOCKS // 2,)),
            pltpu.SemaphoreType.DMA((BLOCKS // 2,)),
            pltpu.SemaphoreType.DMA((8,)),
            pltpu.VMEM((HIDDEN + EXTRA, LOCAL), jnp.bfloat16),
        ]
        + [pltpu.VMEM(shape, jnp.float32) for shape in (rows,) * 4 + (columns,)]
        + [pltpu.VMEM((8 * BLOCKS, FEATURES), jnp.float32), pltpu.VMEM((2, 144, HIDDEN), jnp.float32)]
        + [pltpu.VMEM(array.shape, array.dtype) for array in small],
        flops=3 * 2 * 128 * 6144 * 512,
        traffic=17000000,
        vmem=40,
    )(
        *from_hbm(gate_codes, up_codes, down_codes, tokens, grad, *small),
    )


def split_body(mine_ref, other_ref, gs_ref, gz_ref, us_ref, uz_ref, ds_ref, dz_ref, halves, rows):
    core = lax.axis_index("core")
    halves[core] = mine_ref[...]
    halves[1 - core] = other_ref[...]
    for half, scale_ref, zero_ref in ((0, gs_ref, gz_ref), (1, us_ref, uz_ref)):
        scale_ref[...] = halves[half, 0:48, :]
        zero_ref[...] = halves[half, 48:96, :]
        for j in range(3):
            rows[48 * half : 48 * half + 48, j * 128 : (j + 1) * 128] = halves[half, 96:144, j * 128 : (j + 1) * 128]
    rows[96:128, 0:128] = halves[0, 96:128, 384:]
    rows[96:112, 128:256] = halves[0, 128:144, 384:]
    rows[112:128, 128:256] = halves[1, 96:112, 384:]
    rows[96:128, 256:384] = halves[1, 112:144, 384:]
    natural = reorder(rows[...], True)
    for b in range(BLOCKS):
        columns = slice(b * FEATURES, (b + 1) * FEATURES)
        ds_ref[:, columns] = natural[8 * b : 8 * b + 4, :]
        dz_ref[:, columns] = natural[8 * b + 4 : 8 * b + 8, :]


def split(mine, other):
    f32 = jnp.float32
    return call(
        split_body,
        (struct((48, HIDDEN), f32),) * 4 + (struct((4, BLOCKS * FEATURES), f32),) * 2,
        [VMEM, VMEM],
        (VMEM,) * 6,
        [pltpu.VMEM((2, 144, HIDDEN), f32), pltpu.VMEM((8 * BLOCKS, FEATURES), f32)],
        traffic=1200000,
    )(mine, other)


def sum_body(parts_ref, out_ref):
    total = parts_ref[0].astype(jnp.float32)
    for part in range(1, SHARDS):
        total = total + parts_ref[part].astype(jnp.float32)
    for k in range(3):
        out_ref[pl.ds(k, THIRD, stride=3), :] = total[k * THIRD : (k + 1) * THIRD, :]


def sum_parts(parts):
    return call(sum_body, struct((OWN, LOCAL), jnp.float32), [VMEM], VMEM, traffic=1700000)(parts)


NEAR, ACROSS = ((0, 1), (2, 3)), ((0, 3), (1, 2))


def paired(block, axis, pairs):
    other = lax.ppermute(block, axis, [pair for a, b in pairs for pair in ((a, b), (b, a))])
    return jnp.concatenate([block, other])


def turned(block, axis, way):
    pairs = [(place, (place + way) % 4) for place in range(4)]
    pairs += [(4 + place, 4 + (place - way) % 4) for place in range(4)]
    return lax.ppermute(block, ("core", axis), pairs)


def swap(value, axis):
    return lax.ppermute(value, axis, [(0, 1), (1, 0)])


def shards(
    tokens,
    out_grad,
    gate_codes,
    gate_zeros,
    gate_log_scale,
    up_codes,
    up_zeros,
    up_log_scale,
    down_codes,
    down_zeros,
    down_log_scale,
):
    tokens_near, grad_near = by_field(tokens, out_grad)
    tokens_near, grad_near = paired(tokens_near, "y_lo", ((0, 1),)), paired(grad_near, "y_lo", ((0, 1),))
    tokens_near, grad_near = paired(tokens_near, "x", NEAR), paired(grad_near, "z", NEAR)
    tokens_near, gate_zeros = lax.optimization_barrier((tokens_near, gate_zeros))
    tokens_near, grad_near = paired(tokens_near, "x", ACROSS), paired(grad_near, "z", ACROSS)
    gate = unpack_rows(gate_codes, gate_zeros, gate_log_scale)
    tokens_near, gate, up_zeros = lax.optimization_barrier((tokens_near, gate, up_zeros))
    grad_near, up_log_scale = lax.optimization_barrier((grad_near, up_log_scale))
    tokens_first, grad_first = turned(tokens_near, "z", 1), turned(grad_near, "x", 1)
    tokens_second, grad_second = turned(tokens_near, "z", -1), turned(grad_near, "x", -1)
    up = unpack_rows(up_codes, up_zeros, up_log_scale)
    tokens_first, grad_first, up, down_zeros = lax.optimization_barrier((tokens_first, grad_first, up, down_zeros))
    tokens_parts = tokens_near, tokens_first, turned(tokens_first, "z", 1), tokens_second
    grad_parts = grad_near, grad_first, turned(grad_first, "x", 1), grad_second
    down, table = unpack_columns(down_codes, down_zeros, down_log_scale)
    *sums, all_tokens, all_grad = forward(tokens_parts, grad_parts, gate, up, down)
    partial, all_tokens, all_grad, gate_grad, up_grad, hidden = backward(
        tokens_parts, grad_parts, gate, up, down, sums, all_tokens, all_grad
    )
    parts = lax.all_to_all(partial.reshape(SHARDS, OWN, LOCAL), ("x", "y_lo", "z"), 0, 0, tiled=True)
    own, given = group_grads(
        all_tokens,
        all_grad,
        gate_grad,
        up_grad,
        hidden,
        (gate_codes, gate_zeros, gate_log_scale),
        (up_codes, up_zeros, up_log_scale),
        down_codes,
        table,
    )
    own = own + swap(given, "core")
    own = own.astype(jnp.bfloat16)
    tokens_grad = sum_parts(parts).T
    far, tokens_grad = lax.optimization_barrier((swap(own, "y_hi"), tokens_grad))
    mine = own.astype(jnp.float32) + far.astype(jnp.float32)
    theirs = swap(mine, "core")
    return (tokens_grad, *split(mine, theirs))


def solution(mesh):
    axes = jax.sharding.Mesh(mesh.devices.reshape(2, 2, N_X, N_Y, N_Z), ("y_hi", "core", "x", "y_lo", "z"))
    dp, tensor = ("y_hi", "core"), ("x", "y_lo", "z")
    columns, rows = P(None, tensor), P(tensor, None)
    return jax.shard_map(
        shards,
        mesh=axes,
        in_specs=(P(dp, tensor),) * 2 + (columns,) * 6 + (rows,) * 3,
        out_specs=(P(dp, tensor),) + (columns,) * 4 + (rows,) * 2,
        check_vma=False,
    )
```

```python
import jax
import jax.numpy as jnp
from jax import lax
from jax.experimental import pallas as pl
from jax.experimental.pallas import tpu as pltpu
from jax.sharding import PartitionSpec as P

N_X, N_Y, N_Z = 4, 2, 4
SHARDS = 32
OWN = 192
THIRD = 64
BLOCKS = 16
WORDS = 128
FEATURES = 384
HIDDEN = 512
LOCAL = 128
MIB = 1 << 20

CONTRACT_LAST = (((1,), (1,)), ((), ()))
CONTRACT_FIRST = (((0,), (0,)), ((), ()))


def shard_row(k, word):
    return (word // THIRD) * OWN + k * THIRD + word % THIRD


def first_word(k, group):
    return -((k - 128 * group) // 3)


def spread_over_groups(k, start, rows, values):
    first, last = (3 * start + k) // 128, (3 * (start + rows - 1) + k) // 128
    if first == last:
        return values[first]
    row = start + lax.broadcasted_iota(jnp.int32, (rows, 1), 0)
    return jnp.where(row < first_word(k, last), values[first], values[last])


def call(body, out_shape, in_specs, out_specs, scratch=(), flops=0, traffic=0, vmem=16, aliases=None):
    return pl.pallas_call(
        body,
        out_shape=out_shape,
        in_specs=in_specs,
        out_specs=out_specs,
        scratch_shapes=list(scratch),
        input_output_aliases=aliases or {},
        compiler_params=pltpu.CompilerParams(vmem_limit_bytes=vmem * MIB),
        cost_estimate=pl.CostEstimate(flops=flops, bytes_accessed=traffic, transcendentals=0),
    )


def struct(shape, dtype):
    return jax.ShapeDtypeStruct(shape, dtype)


def from_hbm(*arrays):
    return [pltpu.with_memory_space_constraint(array, pltpu.HBM) for array in arrays]


def from_vmem(*arrays):
    return [pltpu.with_memory_space_constraint(array, pltpu.VMEM) for array in arrays]


VMEM = pl.BlockSpec(memory_space=pltpu.VMEM)
ANY = pl.BlockSpec(memory_space=pl.ANY)


def by_field_body(tokens_ref, grad_ref, tokens_out, grad_out, wide):
    for ref, out_ref in ((tokens_ref, tokens_out), (grad_ref, grad_out)):
        wide[...] = ref[...].astype(jnp.float32)
        for k in range(3):
            out_ref[0, k * THIRD : (k + 1) * THIRD, :] = wide[pl.ds(k, THIRD, stride=3), :].astype(jnp.bfloat16)


def by_field(tokens, out_grad):
    return call(
        by_field_body,
        (struct((1, OWN, LOCAL), jnp.bfloat16),) * 2,
        [VMEM, VMEM],
        (VMEM, VMEM),
        [pltpu.VMEM((OWN, LOCAL), jnp.float32)],
        traffic=200000,
    )(*from_hbm(tokens.T, out_grad.T))


def field(words, k):
    if k:
        words = jnp.right_shift(words, 4 * k)
    if k < 2:
        words = jnp.bitwise_and(words, 15)
    return words.astype(jnp.float32)


CHUNKS = 8
AHEAD = 3


def row_copy(chunk, source, to, sems):
    rows = pl.ds(pl.multiple_of(chunk * 2 * WORDS, 2 * WORDS), 2 * WORDS)
    return pltpu.make_async_copy(source.at[rows], to.at[rows], sems.at[chunk])


def column_copy(chunk, source, to, sems):
    columns = pl.ds(pl.multiple_of(chunk * 2 * WORDS, 2 * WORDS), 2 * WORDS)
    return pltpu.make_async_copy(source.at[:, columns], to.at[:, columns], sems.at[chunk])


def tables_in(sources, targets, sems):
    copies = [pltpu.make_async_copy(a, b, sems.at[i]) for i, (a, b) in enumerate(zip(sources, targets))]
    for copy in copies:
        copy.start()
    return copies


def unpack_rows_pair(pair, codes, zeros_ref, log_ref, out_ref):
    for part in range(2):
        block = pair * 2 + part
        zeros = [zeros_ref[pl.ds(3 * block + g, 1), :].astype(jnp.float32) for g in range(3)]
        scales = [jnp.exp(log_ref[pl.ds(3 * block + g, 1), :]) for g in range(3)]
        for start in range(0, WORDS, 16):
            words = codes[pl.ds(pl.multiple_of(block * WORDS + start, 16), 16), :]
            for k in range(3):
                zero = spread_over_groups(k, start, 16, zeros)
                scale = spread_over_groups(k, start, 16, scales)
                weight = (scale * (field(words, k) - zero)).astype(jnp.bfloat16)
                row = k * THIRD + start % THIRD
                out_ref[part * 2 + start // THIRD, pair, row : row + 16, :] = weight


def streamed(copy_of, source, to, sems, work):
    def step(chunk, carry):
        copy_of(chunk, source, to, sems).wait()

        @pl.when(chunk + AHEAD < CHUNKS)
        def _():
            copy_of(chunk + AHEAD, source, to, sems).start()

        work(chunk)
        return carry

    lax.fori_loop(0, CHUNKS, step, 0)


def start_first(copy_of, source, to, sems):
    for chunk in range(AHEAD):
        copy_of(chunk, source, to, sems).start()


def unpack_rows_body(codes_hbm, zeros_hbm, log_hbm, out_ref, zeros_ref, log_ref, table_sems, codes, sems):
    tables = tables_in((zeros_hbm, log_hbm), (zeros_ref, log_ref), table_sems)
    start_first(row_copy, codes_hbm, codes, sems)
    for table in tables:
        table.wait()
    streamed(
        row_copy, codes_hbm, codes, sems, lambda pair: unpack_rows_pair(pair, codes, zeros_ref, log_ref, out_ref)
    )


def unpack_rows(codes, zeros, log_scale):
    return call(
        unpack_rows_body,
        pltpu.VMEM((N_Z, N_X * N_Y, OWN, HIDDEN), jnp.bfloat16),
        [ANY] * 3,
        VMEM,
        [
            pltpu.VMEM((48, HIDDEN), jnp.int32),
            pltpu.VMEM((48, HIDDEN), jnp.float32),
            pltpu.SemaphoreType.DMA((2,)),
            pltpu.VMEM((BLOCKS * WORDS, HIDDEN), jnp.int32),
            pltpu.SemaphoreType.DMA((CHUNKS,)),
        ],
        flops=20000000,
        traffic=10500000,
    )(*from_hbm(codes, zeros, log_scale))


def field_order(transposed):
    feature = lax.broadcasted_iota(jnp.int32, (FEATURES, FEATURES), 1 if transposed else 0)
    column = lax.broadcasted_iota(jnp.int32, (FEATURES, FEATURES), 0 if transposed else 1)
    wanted = 3 * jnp.bitwise_and(column, 127) + jnp.right_shift(column, 7)
    return (feature == wanted).astype(jnp.float32)


def reorder(rows, transposed):
    return jnp.dot(
        rows, field_order(transposed), precision=lax.Precision.HIGHEST, preferred_element_type=jnp.float32
    )


def unpack_columns_pair(pair, codes, table_ref, out_ref):
    for part in range(2):
        block = pair * 2 + part
        table = table_ref[pl.ds(pl.multiple_of(8 * block, 8), 8), :]
        for g in range(4):
            words = codes[g * 128 : (g + 1) * 128, pl.ds(pl.multiple_of(block * WORDS, WORDS), WORDS)]
            for k in range(3):
                columns = slice(k * WORDS, (k + 1) * WORDS)
                zero, scale = table[g : g + 1, columns], table[4 + g : 5 + g, columns]
                weight = (scale * (field(words, k) - zero)).astype(jnp.bfloat16)
                to = slice(part * FEATURES + k * WORDS, part * FEATURES + (k + 1) * WORDS)
                out_ref[pair, g * 128 : (g + 1) * 128, to] = weight


def unpack_columns_body(
    codes_hbm, zeros_hbm, log_hbm, out_ref, table_ref, zeros_ref, log_ref, table_sems, natural, codes, sems
):
    tables = tables_in((zeros_hbm, log_hbm), (zeros_ref, log_ref), table_sems)
    start_first(column_copy, codes_hbm, codes, sems)
    for table in tables:
        table.wait()
    for b in range(BLOCKS):
        columns = slice(b * FEATURES, (b + 1) * FEATURES)
        natural[8 * b : 8 * b + 4, :] = zeros_ref[:, columns].astype(jnp.float32)
        natural[8 * b + 4 : 8 * b + 8, :] = jnp.exp(log_ref[:, columns])
    table_ref[...] = reorder(natural[...], False)
    streamed(column_copy, codes_hbm, codes, sems, lambda pair: unpack_columns_pair(pair, codes, table_ref, out_ref))


def unpack_columns(codes, zeros, log_scale):
    wide = (4, BLOCKS * FEATURES)
    return call(
        unpack_columns_body,
        (
            pltpu.VMEM((N_X * N_Y, HIDDEN, 2 * FEATURES), jnp.bfloat16),
            pltpu.HBM((8 * BLOCKS, FEATURES), jnp.float32),
        ),
        [ANY] * 3,
        (VMEM,) * 2,
        [
            pltpu.VMEM(wide, jnp.int32),
            pltpu.VMEM(wide, jnp.float32),
            pltpu.SemaphoreType.DMA((2,)),
            pltpu.VMEM((8 * BLOCKS, FEATURES), jnp.float32),
            pltpu.VMEM((HIDDEN, BLOCKS * WORDS), jnp.int32),
            pltpu.SemaphoreType.DMA((CHUNKS,)),
        ],
        flops=20000000,
        traffic=10500000,
    )(*from_hbm(codes, zeros, log_scale))


EXTRA = 16


def with_sums(rows, members):
    sums = jnp.dot(members, rows, preferred_element_type=jnp.float32)
    head = sums.astype(jnp.bfloat16)
    rest = (sums - head.astype(jnp.float32)).astype(jnp.bfloat16)
    return jnp.concatenate([rows, jnp.concatenate([head, rest], axis=0)], axis=0)


def block_members():
    group = lax.broadcasted_iota(jnp.int32, (8, FEATURES), 0)
    place = lax.broadcasted_iota(jnp.int32, (8, FEATURES), 1)
    half = (place >= OWN).astype(jnp.int32)
    place = place - OWN * half
    k = jnp.right_shift(place, 6)
    feature = 3 * (half * THIRD + place - THIRD * k) + k
    return (jnp.right_shift(feature, 7) == group).astype(jnp.float32).astype(jnp.bfloat16)


def hidden_members():
    group = lax.broadcasted_iota(jnp.int32, (8, HIDDEN), 0)
    unit = lax.broadcasted_iota(jnp.int32, (8, HIDDEN), 1)
    return (jnp.right_shift(unit, 7) == group).astype(jnp.float32).astype(jnp.bfloat16)


def folded(products):
    return products[0:8] + products[8:16]


def row_groups(pair, part, weight_of, weight_grad, sums, totals):
    weighted = [jnp.zeros((8, HIDDEN), jnp.float32)] * 3
    for start in range(0, WORDS, 16):
        for k in range(3):
            row = k * THIRD + start % THIRD
            weight = weight_of[part * 2 + start // THIRD, pair, row : row + 16, :].astype(jnp.float32)
            product = weight * weight_grad[shard_row(k, start) : shard_row(k, start) + 16, :]
            first, last = (3 * start + k) // 128, (3 * (start + 15) + k) // 128
            if first == last:
                weighted[first] = weighted[first] + folded(product)
            else:
                low = start + lax.broadcasted_iota(jnp.int32, (16, 1), 0) < first_word(k, last)
                low_product = jnp.where(low, product, 0.0)
                weighted[first] = weighted[first] + folded(low_product)
                weighted[last] = weighted[last] + folded(product - low_product)
    for g in range(3):
        row = pl.ds(3 * (pair * 2 + part) + g, 1)
        sums[row, :] = jnp.sum(weighted[g], axis=0, keepdims=True)
        totals[row, :] = (
            weight_grad[FEATURES + g : FEATURES + g + 1, :] + weight_grad[FEATURES + 8 + g : FEATURES + 9 + g, :]
        )


SLAB = 8 * OWN


def position():
    return tuple(lax.axis_index(axis) for axis in ("x", "y_lo", "z"))


def swapped_with(here, near):
    place = 3 - here if near // 2 else here
    return place + 1 - 2 * (place % 2) if near % 2 else place


def lay_tokens(place, source, far, to):
    x, y, z = place
    slab = (z + 4 - far) % 4
    for near in range(4):
        for dy in range(2):
            to[slab, swapped_with(x, near) * 2 + (y + dy) % 2, :, :] = source[near * 2 + dy]
    return slab


def lay_grad(place, source, far, to):
    x, y, z = place
    slab = (x + 4 - far) % 4
    for near in range(4):
        z_from = swapped_with(z, near)
        for dy in range(2):
            for k in range(3):
                row = pl.multiple_of((z_from // 2) * FEATURES + k * WORDS + (z_from % 2) * THIRD, THIRD)
                to[slab * 2 + (y + dy) % 2, pl.ds(row, THIRD), :] = source[
                    near * 2 + dy, k * THIRD : (k + 1) * THIRD, :
                ]
    return slab


def pair_out(slab, grad_from, grad_hbm, sems):
    pairs = pl.ds(slab * 2, 2)
    return pltpu.make_async_copy(grad_from.at[pairs], grad_hbm.at[pairs], sems)


def slab_products(fars, tokens_refs, grad_refs, weights, scratch, grad_hbm, totals):
    gate_ref, up_ref, down_ref = weights
    tokens_to, grad_to, grad_sems = scratch
    place = position()
    gate_pre, up_pre, hidden_grad = totals
    copies, laid = [], []
    for i, far in enumerate(fars):
        slabs = lay_tokens(place, tokens_refs[i], far, tokens_to), lay_grad(place, grad_refs[i], far, grad_to)
        copies.append(pair_out(slabs[1], grad_to, grad_hbm, grad_sems.at[i]))
        laid.append(slabs)
    for copy in copies:
        copy.start()
    for slab, grad_slab in laid:
        features = tokens_to[slab].reshape(SLAB, LOCAL).T
        gate_pre += jnp.dot(features, gate_ref[slab].reshape(SLAB, HIDDEN), preferred_element_type=jnp.float32)
        up_pre += jnp.dot(features, up_ref[slab].reshape(SLAB, HIDDEN), preferred_element_type=jnp.float32)
        for dy in range(2):
            piece = grad_to[grad_slab * 2 + dy]
            hidden_grad += jnp.dot(down_ref[grad_slab * 2 + dy], piece, preferred_element_type=jnp.float32)
    return (gate_pre, up_pre, hidden_grad), copies


def forward_body(
    t0, t1, t3, o0, o1, o3, gate_ref, up_ref, down_ref,
    gate_pre_ref, up_pre_ref, hidden_grad_ref, grad_hbm,
    tokens_to, grad_to, grad_sems,
):
    zero = jnp.zeros((LOCAL, HIDDEN), jnp.float32)
    core = lax.axis_index("core")
    (gate_pre_ref[...], up_pre_ref[...], hidden_grad_ref[...]), copies = slab_products(
        (0, 1 + 2 * core, 3 - 2 * core), (t0, t1, t3), (o0, o1, o3), (gate_ref, up_ref, down_ref),
        (tokens_to, grad_to, grad_sems), grad_hbm,
        (zero, zero, jnp.zeros((HIDDEN, LOCAL), jnp.float32)),
    )
    for copy in copies:
        copy.wait()


TOKENS_SHAPE = (N_Z, N_X * N_Y, OWN, LOCAL)
GRAD_SHAPE = (N_X * N_Y, 2 * FEATURES, LOCAL)


def slab_scratch(slabs):
    return [
        pltpu.VMEM(TOKENS_SHAPE, jnp.bfloat16),
        pltpu.VMEM(GRAD_SHAPE, jnp.bfloat16),
        pltpu.SemaphoreType.DMA((slabs,)),
    ]


def forward(tokens_parts, grad_parts, gate, up, down):
    f32, bf16 = jnp.float32, jnp.bfloat16
    near = (0, 1, 3)
    return call(
        forward_body,
        (
            pltpu.VMEM((LOCAL, HIDDEN), f32),
            pltpu.VMEM((LOCAL, HIDDEN), f32),
            pltpu.VMEM((HIDDEN, LOCAL), f32),
            pltpu.HBM(GRAD_SHAPE, bf16),
        ),
        [VMEM] * 9,
        (VMEM,) * 3 + (ANY,),
        slab_scratch(3),
        flops=3 * 3 * 2 * 128 * 1536 * 512,
        traffic=18000000,
    )(
        *from_vmem(*[tokens_parts[far] for far in near], *[grad_parts[far] for far in near]),
        *from_vmem(gate, up, down),
    )


def backward_body(
    t0, t1, t2, t3, o2, gate_ref, up_ref, down_ref, gate_pre_ref, up_pre_ref, hidden_grad_ref, gate_log_hbm, up_log_hbm, grad_in,
    partial_hbm, grad_hbm, hidden_hbm, gate_groups_hbm, up_groups_hbm,
    tokens_to, grad_to, grad_sems, partial, partial_sems, gate_grad_ref, up_grad_ref, hidden_ref, small_sems,
    gate_even, up_even, gate_odd, up_odd, gate_groups, up_groups, gate_log, up_log, log_sems,
):
    logs = tables_in((gate_log_hbm, up_log_hbm), (gate_log, up_log), log_sems)
    (gate_pre, up_pre, hidden_grad), copies = slab_products(
        (2,), (t2,), (o2,), (gate_ref, up_ref, down_ref),
        (tokens_to, grad_to, grad_sems), grad_hbm,
        (gate_pre_ref[...], up_pre_ref[...], hidden_grad_ref[...]),
    )
    hidden_grad = hidden_grad.T
    sigmoid_gate = jax.nn.sigmoid(gate_pre)
    silu_gate = gate_pre * sigmoid_gate
    hidden = silu_gate * up_pre
    gate_grad = hidden_grad * up_pre * sigmoid_gate * (1.0 + gate_pre * (1.0 - sigmoid_gate))
    up_grad = hidden_grad * silu_gate
    gate_grad_ref[...] = gate_grad.astype(jnp.bfloat16)
    up_grad_ref[...] = up_grad.astype(jnp.bfloat16)
    hidden_ref[...] = hidden.T.astype(jnp.bfloat16)
    copies += tables_in((hidden_ref,), (hidden_hbm,), small_sems)
    gate_turned = gate_grad.T.astype(jnp.bfloat16)
    up_turned = up_grad.T.astype(jnp.bfloat16)
    for slab in range(N_Z):
        total = jnp.dot(gate_ref[slab].reshape(SLAB, HIDDEN), gate_turned, preferred_element_type=jnp.float32)
        total += jnp.dot(up_ref[slab].reshape(SLAB, HIDDEN), up_turned, preferred_element_type=jnp.float32)
        partial[slab] = total.astype(jnp.bfloat16).reshape(N_X * N_Y, OWN, LOCAL)
        copy = pltpu.make_async_copy(partial.at[slab], partial_hbm.at[:, slab], partial_sems.at[slab])
        copy.start()
        copies.append(copy)
    core = lax.axis_index("core")
    for far, source in ((0, t0), (1 + 2 * core, t1), (3 - 2 * core, t3)):
        lay_tokens(position(), source, far, tokens_to)
    members = block_members()

    def products(pair, part, gate_to, up_to):
        features = jnp.concatenate([tokens_to[part * 2 + half, pair] for half in range(2)], axis=0)
        features = with_sums(features, members)
        gate_to[...] = jnp.dot(features, gate_grad_ref[...], preferred_element_type=jnp.float32)
        up_to[...] = jnp.dot(features, up_grad_ref[...], preferred_element_type=jnp.float32)

    def groups(pair, part, gate_from, up_from):
        row_groups(pair, part, gate_ref, gate_from, gate_groups.at[0], gate_groups.at[1])
        row_groups(pair, part, up_ref, up_from, up_groups.at[0], up_groups.at[1])

    products(0, 0, gate_even, up_even)

    def pair_step(pair, carry):
        products(pair, 1, gate_odd, up_odd)
        groups(pair, 0, gate_even, up_even)
        products(jnp.minimum(pair + 1, BLOCKS // 2 - 1), 0, gate_even, up_even)
        groups(pair, 1, gate_odd, up_odd)
        return carry

    lax.fori_loop(0, BLOCKS // 2, pair_step, 0)
    for log in logs:
        log.wait()
    for results, log_ref in ((gate_groups, gate_log), (up_groups, up_log)):
        results[1] = -jnp.exp(log_ref[...]) * results[1]
    copies += tables_in((gate_groups, up_groups), (gate_groups_hbm, up_groups_hbm), small_sems.at[pl.ds(1, 2)])
    for copy in copies:
        copy.wait()


def backward(tokens_parts, grad_parts, gate, up, down, sums, gate_log, up_log, all_grad):
    bf16 = jnp.bfloat16
    return call(
        backward_body,
        (
            pltpu.HBM((N_X * N_Y, N_Z, OWN, LOCAL), bf16),
            pltpu.HBM(GRAD_SHAPE, bf16),
            pltpu.HBM((HIDDEN, LOCAL), bf16),
            pltpu.HBM((2, 48, HIDDEN), jnp.float32),
            pltpu.HBM((2, 48, HIDDEN), jnp.float32),
        ),
        [VMEM] * 11 + [ANY] * 3,
        (ANY,) * 5,
        slab_scratch(1)
        + [
            pltpu.VMEM(TOKENS_SHAPE, bf16),
            pltpu.SemaphoreType.DMA((N_Z,)),
            pltpu.VMEM((LOCAL, HIDDEN), bf16),
            pltpu.VMEM((LOCAL, HIDDEN), bf16),
            pltpu.VMEM((HIDDEN, LOCAL), bf16),
            pltpu.SemaphoreType.DMA((3,)),
        ]
        + [pltpu.VMEM((FEATURES + EXTRA, HIDDEN), jnp.float32)] * 4
        + [pltpu.VMEM((2, 48, HIDDEN), jnp.float32)] * 2
        + [pltpu.VMEM((48, HIDDEN), jnp.float32)] * 2
        + [pltpu.SemaphoreType.DMA((2,))],
        flops=5 * 2 * 128 * 6144 * 512,
        traffic=24000000,
        aliases={13: 1},
    )(
        *from_vmem(*tokens_parts, grad_parts[2], gate, up, down, *sums),
        *from_hbm(gate_log, up_log, all_grad),
    )


MASKS = (15, 240, 3840)
SHRINK = (1.0, 1.0 / 16.0, 1.0 / 256.0)


def in_place(words, k):
    return jnp.bitwise_and(words, MASKS[k]).astype(jnp.float32)


def column_groups(pair, part, codes, weight_grad, raw):
    here = pl.ds(pl.multiple_of(8 * (pair * 2 + part), 8), 8)
    mine = slice(part * FEATURES, (part + 1) * FEATURES)
    totals = weight_grad[HIDDEN : HIDDEN + 4, mine] + weight_grad[HIDDEN + 8 : HIDDEN + 12, mine]
    for k in range(3):
        sums = []
        for g in range(4):
            weighted = jnp.zeros((8, WORDS), jnp.float32)
            for start in range(g * 128, g * 128 + 128, 8):
                words = codes[start : start + 8, pl.ds(pl.multiple_of((pair * 2 + part) * WORDS, WORDS), WORDS)]
                value = weight_grad[start : start + 8, part * FEATURES + k * WORDS : part * FEATURES + (k + 1) * WORDS]
                weighted = weighted + in_place(words, k) * value
            sums.append(jnp.sum(weighted, axis=0, keepdims=True))
        columns = slice(k * WORDS, (k + 1) * WORDS)
        raw[here, columns] = jnp.concatenate([jnp.concatenate(sums, axis=0) * SHRINK[k], totals[:, columns]], axis=0)


def group_body(
    down_hbm, grad_hbm, hidden_hbm, table_hbm, gate_groups_hbm, up_groups_hbm,
    own_ref, given_ref,
    down_codes, down_sems, grad_ref, grad_sems, hidden_ref, table_ref, gate_groups, up_groups, small_sems,
    hidden_rows, down_even, down_odd, raw, halves,
):
    def grad_in(pair):
        return pltpu.make_async_copy(grad_hbm.at[pair], grad_ref.at[pair], grad_sems.at[pair])

    def codes_in(chunk):
        return column_copy(chunk, down_hbm, down_codes, down_sems)

    hidden_in, *later = tables_in(
        (hidden_hbm, table_hbm, gate_groups_hbm, up_groups_hbm), (hidden_ref, table_ref, gate_groups, up_groups), small_sems
    )
    for pair in range(2):
        grad_in(pair).start()
        codes_in(pair).start()
    for pair in range(2, BLOCKS // 2):
        grad_in(pair).start()
    codes_in(2).start()
    hidden_in.wait()
    hidden_rows[...] = with_sums(hidden_ref[...], hidden_members())

    def products(pair, to):
        to[...] = lax.dot_general(hidden_rows[...], grad_ref[pair], CONTRACT_LAST, preferred_element_type=jnp.float32)

    def groups(pair, weight_grad):
        for part in range(2):
            column_groups(pair, part, down_codes, weight_grad, raw)

    grad_in(0).wait()
    products(0, down_even)

    def two_pairs(step, carry):
        pair = step * 2
        following = jnp.minimum(pair + 2, BLOCKS // 2 - 1)
        for near in range(2):
            codes_in(pair + near).wait()
        grad_in(pair + 1).wait()

        @pl.when(pair + 2 < BLOCKS // 2)
        def _():
            grad_in(following).wait()

        @pl.when(step == 0)
        def _():
            codes_in(3).start()

        @pl.when(step == 1)
        def _():
            for chunk in range(6, 8):
                codes_in(chunk).start()

        @pl.when(step == 0)
        def _():
            for chunk in range(4, 6):
                codes_in(chunk).start()

        products(pair + 1, down_odd)
        groups(pair, down_even)
        products(following, down_even)
        groups(pair + 1, down_odd)
        return carry

    lax.fori_loop(0, BLOCKS // 4, two_pairs, 0)
    for copy in later:
        copy.wait()
    found, table = raw[...].reshape(BLOCKS, 8, FEATURES), table_ref[...].reshape(BLOCKS, 8, FEATURES)
    sums, totals, zero, scale = found[:, 0:4], found[:, 4:8], table[:, 0:4], table[:, 4:8]
    down_rows = jnp.concatenate([scale * (sums - zero * totals), -scale * totals], axis=1)
    raw[...] = down_rows.reshape(8 * BLOCKS, FEATURES)
    for half, begin, results in ((0, 0, gate_groups), (1, 48, up_groups)):
        halves[half, 0:48] = results[0]
        halves[half, 48:96] = results[1]
        for j in range(3):
            halves[half, 96:144, j * 128 : (j + 1) * 128] = raw[begin : begin + 48, j * 128 : (j + 1) * 128]
    halves[0, 96:128, 384:] = raw[96:128, 0:128]
    halves[0, 128:144, 384:] = raw[96:112, 128:256]
    halves[1, 96:112, 384:] = raw[112:128, 128:256]
    halves[1, 112:144, 384:] = raw[96:128, 256:384]
    core = lax.axis_index("core")
    own_ref[...] = halves[core]
    given_ref[...] = halves[1 - core]


def group_grads(down_codes, grad, hidden, table, gate_groups, up_groups):
    f32, bf16 = jnp.float32, jnp.bfloat16
    half = struct((144, HIDDEN), f32)
    columns = (HIDDEN + EXTRA, 2 * FEATURES)
    return call(
        group_body,
        (half, half),
        [ANY] * 6,
        (VMEM, VMEM),
        [
            pltpu.VMEM((HIDDEN, BLOCKS * WORDS), jnp.int32),
            pltpu.SemaphoreType.DMA((CHUNKS,)),
            pltpu.VMEM(GRAD_SHAPE, bf16),
            pltpu.SemaphoreType.DMA((BLOCKS // 2,)),
            pltpu.VMEM((HIDDEN, LOCAL), bf16),
            pltpu.VMEM((8 * BLOCKS, FEATURES), f32),
            pltpu.VMEM((2, 48, HIDDEN), f32),
            pltpu.VMEM((2, 48, HIDDEN), f32),
            pltpu.SemaphoreType.DMA((4,)),
            pltpu.VMEM((HIDDEN + EXTRA, LOCAL), bf16),
            pltpu.VMEM(columns, f32),
            pltpu.VMEM(columns, f32),
            pltpu.VMEM((8 * BLOCKS, FEATURES), f32),
            pltpu.VMEM((2, 144, HIDDEN), f32),
        ],
        flops=2 * 128 * 6144 * 512,
        traffic=7000000,
        vmem=24,
    )(*from_hbm(down_codes, grad, hidden, table, gate_groups, up_groups))


def split_body(mine_ref, other_ref, gs_ref, gz_ref, us_ref, uz_ref, ds_ref, dz_ref, halves, rows):
    core = lax.axis_index("core")
    halves[core] = mine_ref[...]
    halves[1 - core] = other_ref[...]
    for half, scale_ref, zero_ref in ((0, gs_ref, gz_ref), (1, us_ref, uz_ref)):
        scale_ref[...] = halves[half, 0:48, :]
        zero_ref[...] = halves[half, 48:96, :]
        for j in range(3):
            rows[48 * half : 48 * half + 48, j * 128 : (j + 1) * 128] = halves[half, 96:144, j * 128 : (j + 1) * 128]
    rows[96:128, 0:128] = halves[0, 96:128, 384:]
    rows[96:112, 128:256] = halves[0, 128:144, 384:]
    rows[112:128, 128:256] = halves[1, 96:112, 384:]
    rows[96:128, 256:384] = halves[1, 112:144, 384:]
    natural = reorder(rows[...], True)
    for b in range(BLOCKS):
        columns = slice(b * FEATURES, (b + 1) * FEATURES)
        ds_ref[:, columns] = natural[8 * b : 8 * b + 4, :]
        dz_ref[:, columns] = natural[8 * b + 4 : 8 * b + 8, :]


def split(mine, other):
    f32 = jnp.float32
    return call(
        split_body,
        (struct((48, HIDDEN), f32),) * 4 + (struct((4, BLOCKS * FEATURES), f32),) * 2,
        [VMEM, VMEM],
        (VMEM,) * 6,
        [pltpu.VMEM((2, 144, HIDDEN), f32), pltpu.VMEM((8 * BLOCKS, FEATURES), f32)],
        traffic=1200000,
    )(mine, other)


def sum_body(parts_ref, out_ref):
    total = parts_ref[0].astype(jnp.float32)
    for part in range(1, SHARDS):
        total = total + parts_ref[part].astype(jnp.float32)
    for k in range(3):
        out_ref[pl.ds(k, THIRD, stride=3), :] = total[k * THIRD : (k + 1) * THIRD, :]


def sum_parts(parts):
    return call(sum_body, struct((OWN, LOCAL), jnp.float32), [VMEM], VMEM, traffic=1700000)(parts)


NEAR, ACROSS = ((0, 1), (2, 3)), ((0, 3), (1, 2))


def paired(block, axis, pairs):
    other = lax.ppermute(block, axis, [pair for a, b in pairs for pair in ((a, b), (b, a))])
    return jnp.concatenate([block, other])


def turned(block, axis, way):
    pairs = [(place, (place + way) % 4) for place in range(4)]
    pairs += [(4 + place, 4 + (place - way) % 4) for place in range(4)]
    return lax.ppermute(block, ("core", axis), pairs)


def swap(value, axis):
    return lax.ppermute(value, axis, [(0, 1), (1, 0)])


def shards(
    tokens,
    out_grad,
    gate_codes,
    gate_zeros,
    gate_log_scale,
    up_codes,
    up_zeros,
    up_log_scale,
    down_codes,
    down_zeros,
    down_log_scale,
):
    tokens_near, grad_near = by_field(tokens, out_grad)
    tokens_near, grad_near = paired(tokens_near, "y_lo", ((0, 1),)), paired(grad_near, "y_lo", ((0, 1),))
    tokens_near, grad_near = paired(tokens_near, "x", NEAR), paired(grad_near, "z", NEAR)
    tokens_near, gate_zeros = lax.optimization_barrier((tokens_near, gate_zeros))
    tokens_near, grad_near = paired(tokens_near, "x", ACROSS), paired(grad_near, "z", ACROSS)
    gate = unpack_rows(gate_codes, gate_zeros, gate_log_scale)
    tokens_near, gate, up_zeros = lax.optimization_barrier((tokens_near, gate, up_zeros))
    grad_near, up_log_scale = lax.optimization_barrier((grad_near, up_log_scale))
    tokens_first, grad_first = turned(tokens_near, "z", 1), turned(grad_near, "x", 1)
    tokens_second, grad_second = turned(tokens_near, "z", -1), turned(grad_near, "x", -1)
    up = unpack_rows(up_codes, up_zeros, up_log_scale)
    tokens_first, grad_first, up, down_zeros = lax.optimization_barrier((tokens_first, grad_first, up, down_zeros))
    tokens_parts = tokens_near, tokens_first, turned(tokens_first, "z", 1), tokens_second
    grad_parts = grad_near, grad_first, turned(grad_first, "x", 1), grad_second
    down, table = unpack_columns(down_codes, down_zeros, down_log_scale)
    *sums, all_grad = forward(tokens_parts, grad_parts, gate, up, down)
    partial, all_grad, hidden, gate_groups, up_groups = backward(
        tokens_parts, grad_parts, gate, up, down, sums, gate_log_scale, up_log_scale, all_grad
    )
    parts = lax.all_to_all(partial.reshape(SHARDS, OWN, LOCAL), ("x", "y_lo", "z"), 0, 0, tiled=True)
    own, given = group_grads(down_codes, all_grad, hidden, table, gate_groups, up_groups)
    own = own + swap(given, "core")
    own = own.astype(jnp.bfloat16)
    tokens_grad = sum_parts(parts).T
    far, tokens_grad = lax.optimization_barrier((swap(own, "y_hi"), tokens_grad))
    mine = own.astype(jnp.float32) + far.astype(jnp.float32)
    theirs = swap(mine, "core")
    return (tokens_grad, *split(mine, theirs))


def solution(mesh):
    axes = jax.sharding.Mesh(mesh.devices.reshape(2, 2, N_X, N_Y, N_Z), ("y_hi", "core", "x", "y_lo", "z"))
    dp, tensor = ("y_hi", "core"), ("x", "y_lo", "z")
    columns, rows = P(None, tensor), P(tensor, None)
    return jax.shard_map(
        shards,
        mesh=axes,
        in_specs=(P(dp, tensor),) * 2 + (columns,) * 6 + (rows,) * 3,
        out_specs=(P(dp, tensor),) + (columns,) * 4 + (rows,) * 2,
        check_vma=False,
    )
```

```python
import jax
import jax.numpy as jnp
from jax import lax
from jax.experimental import pallas as pl
from jax.experimental.pallas import tpu as pltpu
from jax.sharding import PartitionSpec as P

N_X, N_Y, N_Z = 4, 2, 4
SHARDS = 32
OWN = 192
THIRD = 64
BLOCKS = 16
WORDS = 128
FEATURES = 384
HIDDEN = 512
LOCAL = 128
MIB = 1 << 20

CONTRACT_LAST = (((1,), (1,)), ((), ()))
CONTRACT_FIRST = (((0,), (0,)), ((), ()))


def shard_row(k, word):
    return (word // THIRD) * OWN + k * THIRD + word % THIRD


def first_word(k, group):
    return -((k - 128 * group) // 3)


def spread_over_groups(k, start, rows, values):
    first, last = (3 * start + k) // 128, (3 * (start + rows - 1) + k) // 128
    if first == last:
        return values[first]
    row = start + lax.broadcasted_iota(jnp.int32, (rows, 1), 0)
    return jnp.where(row < first_word(k, last), values[first], values[last])


def call(body, out_shape, in_specs, out_specs, scratch=(), flops=0, traffic=0, vmem=16, aliases=None):
    return pl.pallas_call(
        body,
        out_shape=out_shape,
        in_specs=in_specs,
        out_specs=out_specs,
        scratch_shapes=list(scratch),
        input_output_aliases=aliases or {},
        compiler_params=pltpu.CompilerParams(vmem_limit_bytes=vmem * MIB),
        cost_estimate=pl.CostEstimate(flops=flops, bytes_accessed=traffic, transcendentals=0),
    )


def struct(shape, dtype):
    return jax.ShapeDtypeStruct(shape, dtype)


def from_hbm(*arrays):
    return [pltpu.with_memory_space_constraint(array, pltpu.HBM) for array in arrays]


def from_vmem(*arrays):
    return [pltpu.with_memory_space_constraint(array, pltpu.VMEM) for array in arrays]


VMEM = pl.BlockSpec(memory_space=pltpu.VMEM)
ANY = pl.BlockSpec(memory_space=pl.ANY)


def by_field_body(tokens_ref, grad_ref, tokens_out, grad_out, wide):
    for ref, out_ref in ((tokens_ref, tokens_out), (grad_ref, grad_out)):
        wide[...] = ref[...].astype(jnp.float32)
        for k in range(3):
            out_ref[0, k * THIRD : (k + 1) * THIRD, :] = wide[pl.ds(k, THIRD, stride=3), :].astype(jnp.bfloat16)


def by_field(tokens, out_grad):
    return call(
        by_field_body,
        (struct((1, OWN, LOCAL), jnp.bfloat16),) * 2,
        [VMEM, VMEM],
        (VMEM, VMEM),
        [pltpu.VMEM((OWN, LOCAL), jnp.float32)],
        traffic=200000,
    )(*from_hbm(tokens.T, out_grad.T))


def field(words, k):
    if k:
        words = jnp.right_shift(words, 4 * k)
    if k < 2:
        words = jnp.bitwise_and(words, 15)
    return words.astype(jnp.float32)


CHUNKS = 8
AHEAD = 3


def row_copy(chunk, source, to, sems):
    rows = pl.ds(pl.multiple_of(chunk * 2 * WORDS, 2 * WORDS), 2 * WORDS)
    return pltpu.make_async_copy(source.at[rows], to.at[rows], sems.at[chunk])


def column_copy(chunk, source, to, sems):
    columns = pl.ds(pl.multiple_of(chunk * 2 * WORDS, 2 * WORDS), 2 * WORDS)
    return pltpu.make_async_copy(source.at[:, columns], to.at[:, columns], sems.at[chunk])


def tables_in(sources, targets, sems):
    copies = [pltpu.make_async_copy(a, b, sems.at[i]) for i, (a, b) in enumerate(zip(sources, targets))]
    for copy in copies:
        copy.start()
    return copies


def unpack_rows_pair(pair, codes, zeros_ref, log_ref, out_ref):
    for part in range(2):
        block = pair * 2 + part
        zeros = [zeros_ref[pl.ds(3 * block + g, 1), :].astype(jnp.float32) for g in range(3)]
        scales = [jnp.exp(log_ref[pl.ds(3 * block + g, 1), :]) for g in range(3)]
        for start in range(0, WORDS, 16):
            words = codes[pl.ds(pl.multiple_of(block * WORDS + start, 16), 16), :]
            for k in range(3):
                zero = spread_over_groups(k, start, 16, zeros)
                scale = spread_over_groups(k, start, 16, scales)
                weight = (scale * (field(words, k) - zero)).astype(jnp.bfloat16)
                row = k * THIRD + start % THIRD
                out_ref[part * 2 + start // THIRD, pair, row : row + 16, :] = weight


def streamed(copy_of, source, to, sems, work):
    def step(chunk, carry):
        copy_of(chunk, source, to, sems).wait()

        @pl.when(chunk + AHEAD < CHUNKS)
        def _():
            copy_of(chunk + AHEAD, source, to, sems).start()

        work(chunk)
        return carry

    lax.fori_loop(0, CHUNKS, step, 0)


def start_first(copy_of, source, to, sems):
    for chunk in range(AHEAD):
        copy_of(chunk, source, to, sems).start()


def unpack_rows_body(codes_hbm, zeros_hbm, log_hbm, out_ref, zeros_ref, log_ref, table_sems, codes, sems):
    tables = tables_in((zeros_hbm, log_hbm), (zeros_ref, log_ref), table_sems)
    start_first(row_copy, codes_hbm, codes, sems)
    for table in tables:
        table.wait()
    streamed(
        row_copy, codes_hbm, codes, sems, lambda pair: unpack_rows_pair(pair, codes, zeros_ref, log_ref, out_ref)
    )


def unpack_rows(codes, zeros, log_scale):
    return call(
        unpack_rows_body,
        pltpu.VMEM((N_Z, N_X * N_Y, OWN, HIDDEN), jnp.bfloat16),
        [ANY] * 3,
        VMEM,
        [
            pltpu.VMEM((48, HIDDEN), jnp.int32),
            pltpu.VMEM((48, HIDDEN), jnp.float32),
            pltpu.SemaphoreType.DMA((2,)),
            pltpu.VMEM((BLOCKS * WORDS, HIDDEN), jnp.int32),
            pltpu.SemaphoreType.DMA((CHUNKS,)),
        ],
        flops=20000000,
        traffic=10500000,
    )(*from_hbm(codes, zeros, log_scale))


def field_order(transposed):
    feature = lax.broadcasted_iota(jnp.int32, (FEATURES, FEATURES), 1 if transposed else 0)
    column = lax.broadcasted_iota(jnp.int32, (FEATURES, FEATURES), 0 if transposed else 1)
    wanted = 3 * jnp.bitwise_and(column, 127) + jnp.right_shift(column, 7)
    return (feature == wanted).astype(jnp.float32)


def reorder(rows, transposed):
    return jnp.dot(
        rows, field_order(transposed), precision=lax.Precision.HIGHEST, preferred_element_type=jnp.float32
    )


def unpack_columns_pair(pair, codes, table_ref, out_ref):
    for part in range(2):
        block = pair * 2 + part
        table = table_ref[pl.ds(pl.multiple_of(8 * block, 8), 8), :]
        for g in range(4):
            words = codes[g * 128 : (g + 1) * 128, pl.ds(pl.multiple_of(block * WORDS, WORDS), WORDS)]
            for k in range(3):
                columns = slice(k * WORDS, (k + 1) * WORDS)
                zero, scale = table[g : g + 1, columns], table[4 + g : 5 + g, columns]
                weight = (scale * (field(words, k) - zero)).astype(jnp.bfloat16)
                to = slice(part * FEATURES + k * WORDS, part * FEATURES + (k + 1) * WORDS)
                out_ref[pair, g * 128 : (g + 1) * 128, to] = weight


def unpack_columns_body(
    codes_hbm, zeros_hbm, log_hbm, out_ref, table_ref, zeros_ref, log_ref, table_sems, natural, codes, sems
):
    tables = tables_in((zeros_hbm, log_hbm), (zeros_ref, log_ref), table_sems)
    start_first(column_copy, codes_hbm, codes, sems)
    for table in tables:
        table.wait()
    for b in range(BLOCKS):
        columns = slice(b * FEATURES, (b + 1) * FEATURES)
        natural[8 * b : 8 * b + 4, :] = zeros_ref[:, columns].astype(jnp.float32)
        natural[8 * b + 4 : 8 * b + 8, :] = jnp.exp(log_ref[:, columns])
    table_ref[...] = reorder(natural[...], False)
    streamed(column_copy, codes_hbm, codes, sems, lambda pair: unpack_columns_pair(pair, codes, table_ref, out_ref))


def unpack_columns(codes, zeros, log_scale):
    wide = (4, BLOCKS * FEATURES)
    return call(
        unpack_columns_body,
        (
            pltpu.VMEM((N_X * N_Y, HIDDEN, 2 * FEATURES), jnp.bfloat16),
            pltpu.HBM((8 * BLOCKS, FEATURES), jnp.float32),
        ),
        [ANY] * 3,
        (VMEM,) * 2,
        [
            pltpu.VMEM(wide, jnp.int32),
            pltpu.VMEM(wide, jnp.float32),
            pltpu.SemaphoreType.DMA((2,)),
            pltpu.VMEM((8 * BLOCKS, FEATURES), jnp.float32),
            pltpu.VMEM((HIDDEN, BLOCKS * WORDS), jnp.int32),
            pltpu.SemaphoreType.DMA((CHUNKS,)),
        ],
        flops=20000000,
        traffic=10500000,
    )(*from_hbm(codes, zeros, log_scale))


SLAB = 8 * OWN


def position():
    return tuple(lax.axis_index(axis) for axis in ("x", "y_lo", "z"))


def swapped_with(here, near):
    place = 3 - here if near // 2 else here
    return place + 1 - 2 * (place % 2) if near % 2 else place


def lay_tokens(place, source, far, to):
    x, y, z = place
    slab = (z + 4 - far) % 4
    for near in range(4):
        for dy in range(2):
            to[slab, swapped_with(x, near) * 2 + (y + dy) % 2, :, :] = source[near * 2 + dy]
    return slab


def lay_grad(place, source, far, to):
    x, y, z = place
    slab = (x + 4 - far) % 4
    for near in range(4):
        z_from = swapped_with(z, near)
        for dy in range(2):
            for k in range(3):
                row = pl.multiple_of((z_from // 2) * FEATURES + k * WORDS + (z_from % 2) * THIRD, THIRD)
                to[slab * 2 + (y + dy) % 2, pl.ds(row, THIRD), :] = source[
                    near * 2 + dy, k * THIRD : (k + 1) * THIRD, :
                ]
    return slab


def slab_out(slab, tokens_from, tokens_hbm, sems):
    return pltpu.make_async_copy(tokens_from.at[slab], tokens_hbm.at[slab], sems)


def pair_out(slab, grad_from, grad_hbm, sems):
    pairs = pl.ds(slab * 2, 2)
    return pltpu.make_async_copy(grad_from.at[pairs], grad_hbm.at[pairs], sems)


def slab_products(fars, tokens_refs, grad_refs, weights, scratch, hbm, totals):
    gate_ref, up_ref, down_ref = weights
    tokens_to, grad_to, tokens_sems, grad_sems = scratch
    tokens_hbm, grad_hbm = hbm
    place = position()
    gate_pre, up_pre, hidden_grad = totals
    copies, laid = [], []
    for i, far in enumerate(fars):
        slabs = lay_tokens(place, tokens_refs[i], far, tokens_to), lay_grad(place, grad_refs[i], far, grad_to)
        copies.append(slab_out(slabs[0], tokens_to, tokens_hbm, tokens_sems.at[i]))
        copies.append(pair_out(slabs[1], grad_to, grad_hbm, grad_sems.at[i]))
        laid.append(slabs)
    for copy in copies:
        copy.start()
    for slab, grad_slab in laid:
        features = tokens_to[slab].reshape(SLAB, LOCAL).T
        gate_pre += jnp.dot(features, gate_ref[slab].reshape(SLAB, HIDDEN), preferred_element_type=jnp.float32)
        up_pre += jnp.dot(features, up_ref[slab].reshape(SLAB, HIDDEN), preferred_element_type=jnp.float32)
        for dy in range(2):
            piece = grad_to[grad_slab * 2 + dy]
            hidden_grad += jnp.dot(down_ref[grad_slab * 2 + dy], piece, preferred_element_type=jnp.float32)
    return (gate_pre, up_pre, hidden_grad), copies


def forward_body(
    t0, t1, t3, o0, o1, o3, gate_ref, up_ref, down_ref,
    gate_pre_ref, up_pre_ref, hidden_grad_ref, tokens_hbm, grad_hbm,
    tokens_to, grad_to, tokens_sems, grad_sems,
):
    zero = jnp.zeros((LOCAL, HIDDEN), jnp.float32)
    core = lax.axis_index("core")
    (gate_pre_ref[...], up_pre_ref[...], hidden_grad_ref[...]), copies = slab_products(
        (0, 1 + 2 * core, 3 - 2 * core), (t0, t1, t3), (o0, o1, o3), (gate_ref, up_ref, down_ref),
        (tokens_to, grad_to, tokens_sems, grad_sems), (tokens_hbm, grad_hbm),
        (zero, zero, jnp.zeros((HIDDEN, LOCAL), jnp.float32)),
    )
    for copy in copies:
        copy.wait()


TOKENS_SHAPE = (N_Z, N_X * N_Y, OWN, LOCAL)
GRAD_SHAPE = (N_X * N_Y, 2 * FEATURES, LOCAL)


def slab_scratch(slabs):
    return [
        pltpu.VMEM(TOKENS_SHAPE, jnp.bfloat16),
        pltpu.VMEM(GRAD_SHAPE, jnp.bfloat16),
        pltpu.SemaphoreType.DMA((slabs,)),
        pltpu.SemaphoreType.DMA((slabs,)),
    ]


def forward(tokens_parts, grad_parts, gate, up, down):
    f32, bf16 = jnp.float32, jnp.bfloat16
    near = (0, 1, 3)
    return call(
        forward_body,
        (
            pltpu.VMEM((LOCAL, HIDDEN), f32),
            pltpu.VMEM((LOCAL, HIDDEN), f32),
            pltpu.VMEM((HIDDEN, LOCAL), f32),
            pltpu.HBM(TOKENS_SHAPE, bf16),
            pltpu.HBM(GRAD_SHAPE, bf16),
        ),
        [VMEM] * 9,
        (VMEM,) * 3 + (ANY,) * 2,
        slab_scratch(3),
        flops=3 * 3 * 2 * 128 * 1536 * 512,
        traffic=18000000,
    )(
        *from_vmem(*[tokens_parts[far] for far in near], *[grad_parts[far] for far in near]),
        *from_vmem(gate, up, down),
    )


def backward_body(
    t2, o2, gate_ref, up_ref, down_ref, gate_pre_ref, up_pre_ref, hidden_grad_ref, tokens_in, grad_in,
    partial_hbm, tokens_hbm, grad_hbm, gate_grad_hbm, up_grad_hbm, hidden_hbm,
    tokens_to, grad_to, tokens_sems, grad_sems, partial, partial_sems, gate_grad_ref, up_grad_ref, hidden_ref, small_sems,
):
    (gate_pre, up_pre, hidden_grad), copies = slab_products(
        (2,), (t2,), (o2,), (gate_ref, up_ref, down_ref),
        (tokens_to, grad_to, tokens_sems, grad_sems), (tokens_hbm, grad_hbm),
        (gate_pre_ref[...], up_pre_ref[...], hidden_grad_ref[...]),
    )
    hidden_grad = hidden_grad.T
    sigmoid_gate = jax.nn.sigmoid(gate_pre)
    silu_gate = gate_pre * sigmoid_gate
    hidden = silu_gate * up_pre
    gate_grad = hidden_grad * up_pre * sigmoid_gate * (1.0 + gate_pre * (1.0 - sigmoid_gate))
    up_grad = hidden_grad * silu_gate
    gate_grad_ref[...] = gate_grad.astype(jnp.bfloat16)
    up_grad_ref[...] = up_grad.astype(jnp.bfloat16)
    hidden_ref[...] = hidden.T.astype(jnp.bfloat16)
    copies += tables_in(
        (gate_grad_ref, up_grad_ref, hidden_ref), (gate_grad_hbm, up_grad_hbm, hidden_hbm), small_sems
    )
    gate_turned = gate_grad.T.astype(jnp.bfloat16)
    up_turned = up_grad.T.astype(jnp.bfloat16)
    for slab in range(N_Z):
        total = jnp.dot(gate_ref[slab].reshape(SLAB, HIDDEN), gate_turned, preferred_element_type=jnp.float32)
        total += jnp.dot(up_ref[slab].reshape(SLAB, HIDDEN), up_turned, preferred_element_type=jnp.float32)
        partial[slab] = total.astype(jnp.bfloat16).reshape(N_X * N_Y, OWN, LOCAL)
        copy = pltpu.make_async_copy(partial.at[slab], partial_hbm.at[:, slab], partial_sems.at[slab])
        copy.start()
        copies.append(copy)
    for copy in copies:
        copy.wait()


def backward(tokens_parts, grad_parts, gate, up, down, sums, all_tokens, all_grad):
    bf16 = jnp.bfloat16
    return call(
        backward_body,
        (
            pltpu.HBM((N_X * N_Y, N_Z, OWN, LOCAL), bf16),
            pltpu.HBM(TOKENS_SHAPE, bf16),
            pltpu.HBM(GRAD_SHAPE, bf16),
            pltpu.HBM((LOCAL, HIDDEN), bf16),
            pltpu.HBM((LOCAL, HIDDEN), bf16),
            pltpu.HBM((HIDDEN, LOCAL), bf16),
        ),
        [VMEM] * 8 + [ANY] * 2,
        (ANY,) * 6,
        slab_scratch(1)
        + [
            pltpu.VMEM(TOKENS_SHAPE, bf16),
            pltpu.SemaphoreType.DMA((N_Z,)),
            pltpu.VMEM((LOCAL, HIDDEN), bf16),
            pltpu.VMEM((LOCAL, HIDDEN), bf16),
            pltpu.VMEM((HIDDEN, LOCAL), bf16),
            pltpu.SemaphoreType.DMA((3,)),
        ],
        flops=3 * 2 * 128 * 6144 * 512,
        traffic=24000000,
        aliases={8: 1, 9: 2},
    )(
        *from_vmem(tokens_parts[2], grad_parts[2], gate, up, down, *sums),
        *from_hbm(all_tokens, all_grad),
    )


EXTRA = 16


def with_sums(rows, members):
    sums = jnp.dot(members, rows, preferred_element_type=jnp.float32)
    head = sums.astype(jnp.bfloat16)
    rest = (sums - head.astype(jnp.float32)).astype(jnp.bfloat16)
    return jnp.concatenate([rows, jnp.concatenate([head, rest], axis=0)], axis=0)


def block_members():
    group = lax.broadcasted_iota(jnp.int32, (8, FEATURES), 0)
    place = lax.broadcasted_iota(jnp.int32, (8, FEATURES), 1)
    half = (place >= OWN).astype(jnp.int32)
    place = place - OWN * half
    k = jnp.right_shift(place, 6)
    feature = 3 * (half * THIRD + place - THIRD * k) + k
    scale = jnp.where(k == 0, 1.0, jnp.where(k == 1, 16.0, 256.0))
    return jnp.where(jnp.right_shift(feature, 7) == group, scale, 0.0).astype(jnp.bfloat16)


def hidden_members():
    group = lax.broadcasted_iota(jnp.int32, (8, HIDDEN), 0)
    unit = lax.broadcasted_iota(jnp.int32, (8, HIDDEN), 1)
    return (jnp.right_shift(unit, 7) == group).astype(jnp.float32).astype(jnp.bfloat16)


MASKS = (15, 240, 3840)
SHRINK = (1.0, 1.0 / 16.0, 1.0 / 256.0)


def in_place(words, k):
    return jnp.bitwise_and(words, MASKS[k]).astype(jnp.float32)


def in_turn(*streams):
    running = list(streams)
    while running:
        for stream in list(running):
            if next(stream, None) is None:
                running.remove(stream)


def row_groups(block, codes, weight_grad, sums, totals):
    weighted = [jnp.zeros((8, HIDDEN), jnp.float32)] * 3
    for start in range(0, WORDS, 8):
        words = codes[pl.ds(pl.multiple_of(block * WORDS + start, 8), 8), :]
        for k in range(3):
            product = in_place(words, k) * weight_grad[shard_row(k, start) : shard_row(k, start) + 8, :]
            first, last = (3 * start + k) // 128, (3 * (start + 7) + k) // 128
            if first == last:
                weighted[first] = weighted[first] + product
            else:
                low = start + lax.broadcasted_iota(jnp.int32, (8, 1), 0) < first_word(k, last)
                low_product = jnp.where(low, product, 0.0)
                weighted[first] = weighted[first] + low_product
                weighted[last] = weighted[last] + (product - low_product)
        yield True
    for g in range(3):
        row = pl.ds(3 * block + g, 1)
        sums[row, :] = jnp.sum(weighted[g], axis=0, keepdims=True)
        totals[row, :] = (
            weight_grad[FEATURES + g : FEATURES + g + 1, :] + weight_grad[FEATURES + 8 + g : FEATURES + 9 + g, :]
        )
    yield True


def column_groups(block, part, codes, weight_grad, raw):
    here = pl.ds(pl.multiple_of(8 * block, 8), 8)
    mine = slice(part * FEATURES, (part + 1) * FEATURES)
    totals = weight_grad[HIDDEN : HIDDEN + 4, mine] + weight_grad[HIDDEN + 8 : HIDDEN + 12, mine]
    for k in range(3):
        sums = []
        for g in range(4):
            weighted = jnp.zeros((8, WORDS), jnp.float32)
            for start in range(g * 128, g * 128 + 128, 8):
                words = codes[start : start + 8, pl.ds(pl.multiple_of(block * WORDS, WORDS), WORDS)]
                value = weight_grad[start : start + 8, part * FEATURES + k * WORDS : part * FEATURES + (k + 1) * WORDS]
                weighted = weighted + in_place(words, k) * value
            sums.append(jnp.sum(weighted, axis=0, keepdims=True))
            yield True
        columns = slice(k * WORDS, (k + 1) * WORDS)
        raw[here, columns] = jnp.concatenate([jnp.concatenate(sums, axis=0) * SHRINK[k], totals[:, columns]], axis=0)


def group_body(
    gate_hbm, up_hbm, down_hbm, tokens_hbm, grad_hbm, *small_hbm_and_rest
):
    small_hbm, rest = small_hbm_and_rest[:8], small_hbm_and_rest[8:]
    small, rest = rest[-8:], rest[:-8]
    group_work(gate_hbm, up_hbm, down_hbm, tokens_hbm, grad_hbm, small_hbm, small, *rest)


def group_work(
    gate_hbm, up_hbm, down_hbm, tokens_hbm, grad_hbm, small_hbm, small,
    own_ref, given_ref,
    gate_codes, up_codes, down_codes, gate_sems, up_sems, down_sems, tokens_ref, grad_ref, tokens_sems, grad_sems, small_sems,
    hidden_rows, gate_even, up_even, gate_odd, up_odd, down_pair, down_rows, halves, sums, totals,
):
    def copies(chunk):
        return (
            row_copy(chunk, gate_hbm, gate_codes, gate_sems),
            row_copy(chunk, up_hbm, up_codes, up_sems),
            column_copy(chunk, down_hbm, down_codes, down_sems),
        )

    def start(chunk):
        for copy in copies(chunk):
            copy.start()

    def rows_in(pair):
        return (
            pltpu.make_async_copy(tokens_hbm.at[:, pair], tokens_ref.at[:, pair], tokens_sems.at[pair]),
            pltpu.make_async_copy(grad_hbm.at[pair], grad_ref.at[pair], grad_sems.at[pair]),
        )

    gate_grad_ref, up_grad_ref, hidden_ref, gate_zeros, gate_log, up_zeros, up_log, table_ref = small
    arrivals = tables_in(small_hbm, small, small_sems)
    for copy in rows_in(0):
        copy.start()
    start(0)
    for pair in range(1, BLOCKS // 2):
        for copy in rows_in(pair):
            copy.start()
    start(1)
    for arrival in arrivals:
        arrival.wait()
    hidden_rows[...] = with_sums(hidden_ref[...], hidden_members())
    members = block_members()
    field_of_row = jnp.right_shift(lax.broadcasted_iota(jnp.int32, (OWN, 1), 0), 6)
    shrink = jnp.where(field_of_row == 0, SHRINK[0], jnp.where(field_of_row == 1, SHRINK[1], SHRINK[2]))
    shrink = jnp.broadcast_to(shrink, (OWN, LOCAL)).astype(jnp.bfloat16)

    def row_products(pair, part, gate_to, up_to):
        features = jnp.concatenate([tokens_ref[part * 2 + half, pair] * shrink for half in range(2)], axis=0)
        features = with_sums(features, members)
        for grad, to in ((gate_grad_ref, gate_to), (up_grad_ref, up_to)):
            for row in range(0, FEATURES + EXTRA, 80):
                to[row : row + 80, :] = jnp.dot(
                    features[row : row + 80, :], grad[...], preferred_element_type=jnp.float32
                )
                yield True

    def column_products(pair, down_to):
        for row in range(0, HIDDEN + EXTRA, 176):
            down_to[row : row + 176, :] = lax.dot_general(
                hidden_rows[row : row + 176, :], grad_ref[pair], CONTRACT_LAST, preferred_element_type=jnp.float32
            )
            yield True

    def groups(block, gate_from, up_from):
        yield from row_groups(block, gate_codes, gate_from, sums.at[0], totals.at[0])
        yield from row_groups(block, up_codes, up_from, sums.at[1], totals.at[1])

    def down_groups(pair):
        for part in range(2):
            yield from column_groups(pair * 2 + part, part, down_codes, down_pair, down_rows)

    for copy in rows_in(0):
        copy.wait()
    in_turn(row_products(0, 0, gate_even, up_even))

    def pair_step(pair, carry):
        for copy in copies(pair):
            copy.wait()
        following = jnp.minimum(pair + 1, BLOCKS // 2 - 1)

        @pl.when(pair < BLOCKS // 2 - 1)
        def _():
            for copy in rows_in(following):
                copy.wait()

        @pl.when(pair + 2 < CHUNKS)
        def _():
            start(pair + 2)

        in_turn(row_products(pair, 1, gate_odd, up_odd), groups(pair * 2, gate_even, up_even))
        in_turn(column_products(pair, down_pair), groups(pair * 2 + 1, gate_odd, up_odd))
        in_turn(row_products(following, 0, gate_even, up_even), down_groups(pair))
        return carry

    lax.fori_loop(0, BLOCKS // 2, pair_step, 0)

    for half, (zeros_ref, log_ref) in enumerate(((gate_zeros, gate_log), (up_zeros, up_log))):
        scale = jnp.exp(log_ref[...])
        halves[half, 0:48] = scale * (sums[half] - zeros_ref[...].astype(jnp.float32) * totals[half])
        halves[half, 48:96] = -scale * totals[half]
    found, table = down_rows[...].reshape(BLOCKS, 8, FEATURES), table_ref[...].reshape(BLOCKS, 8, FEATURES)
    found, total, zero, scale = found[:, 0:4], found[:, 4:8], table[:, 0:4], table[:, 4:8]
    finished = jnp.concatenate([scale * (found - zero * total), -scale * total], axis=1)
    down_rows[...] = finished.reshape(8 * BLOCKS, FEATURES)
    for half, begin in ((0, 0), (1, 48)):
        for j in range(3):
            halves[half, 96:144, j * 128 : (j + 1) * 128] = down_rows[begin : begin + 48, j * 128 : (j + 1) * 128]
    halves[0, 96:128, 384:] = down_rows[96:128, 0:128]
    halves[0, 128:144, 384:] = down_rows[96:112, 128:256]
    halves[1, 96:112, 384:] = down_rows[112:128, 128:256]
    halves[1, 112:144, 384:] = down_rows[96:128, 256:384]
    core = lax.axis_index("core")
    own_ref[...] = halves[core]
    given_ref[...] = halves[1 - core]


def group_grads(tokens, grad, gate_grad, up_grad, hidden, gate_tables, up_tables, down_codes, table):
    half = struct((144, HIDDEN), jnp.float32)
    gate_codes, *gate_tables = gate_tables
    up_codes, *up_tables = up_tables
    small = (gate_grad, up_grad, hidden, *gate_tables, *up_tables, table)
    rows, columns = (FEATURES + EXTRA, HIDDEN), (HIDDEN + EXTRA, 2 * FEATURES)
    return call(
        group_body,
        (half, half),
        [ANY] * 13,
        (VMEM, VMEM),
        [
            pltpu.VMEM((BLOCKS * WORDS, HIDDEN), jnp.int32),
            pltpu.VMEM((BLOCKS * WORDS, HIDDEN), jnp.int32),
            pltpu.VMEM((HIDDEN, BLOCKS * WORDS), jnp.int32),
        ]
        + [pltpu.SemaphoreType.DMA((CHUNKS,))] * 3
        + [
            pltpu.VMEM(TOKENS_SHAPE, jnp.bfloat16),
            pltpu.VMEM(GRAD_SHAPE, jnp.bfloat16),
            pltpu.SemaphoreType.DMA((BLOCKS // 2,)),
            pltpu.SemaphoreType.DMA((BLOCKS // 2,)),
            pltpu.SemaphoreType.DMA((8,)),
            pltpu.VMEM((HIDDEN + EXTRA, LOCAL), jnp.bfloat16),
        ]
        + [pltpu.VMEM(shape, jnp.float32) for shape in (rows,) * 4 + (columns,)]
        + [pltpu.VMEM((8 * BLOCKS, FEATURES), jnp.float32), pltpu.VMEM((2, 144, HIDDEN), jnp.float32)]
        + [pltpu.VMEM((2, 48, HIDDEN), jnp.float32)] * 2
        + [pltpu.VMEM(array.shape, array.dtype) for array in small],
        flops=3 * 2 * 128 * 6144 * 512,
        traffic=17000000,
        vmem=40,
    )(
        *from_hbm(gate_codes, up_codes, down_codes, tokens, grad, *small),
    )


def split_body(mine_ref, other_ref, gs_ref, gz_ref, us_ref, uz_ref, ds_ref, dz_ref, halves, rows):
    core = lax.axis_index("core")
    halves[core] = mine_ref[...]
    halves[1 - core] = other_ref[...]
    for half, scale_ref, zero_ref in ((0, gs_ref, gz_ref), (1, us_ref, uz_ref)):
        scale_ref[...] = halves[half, 0:48, :]
        zero_ref[...] = halves[half, 48:96, :]
        for j in range(3):
            rows[48 * half : 48 * half + 48, j * 128 : (j + 1) * 128] = halves[half, 96:144, j * 128 : (j + 1) * 128]
    rows[96:128, 0:128] = halves[0, 96:128, 384:]
    rows[96:112, 128:256] = halves[0, 128:144, 384:]
    rows[112:128, 128:256] = halves[1, 96:112, 384:]
    rows[96:128, 256:384] = halves[1, 112:144, 384:]
    natural = reorder(rows[...], True)
    for b in range(BLOCKS):
        columns = slice(b * FEATURES, (b + 1) * FEATURES)
        ds_ref[:, columns] = natural[8 * b : 8 * b + 4, :]
        dz_ref[:, columns] = natural[8 * b + 4 : 8 * b + 8, :]


def split(mine, other):
    f32 = jnp.float32
    return call(
        split_body,
        (struct((48, HIDDEN), f32),) * 4 + (struct((4, BLOCKS * FEATURES), f32),) * 2,
        [VMEM, VMEM],
        (VMEM,) * 6,
        [pltpu.VMEM((2, 144, HIDDEN), f32), pltpu.VMEM((8 * BLOCKS, FEATURES), f32)],
        traffic=1200000,
    )(mine, other)


def sum_body(parts_ref, out_ref):
    total = parts_ref[0].astype(jnp.float32)
    for part in range(1, SHARDS):
        total = total + parts_ref[part].astype(jnp.float32)
    for k in range(3):
        out_ref[pl.ds(k, THIRD, stride=3), :] = total[k * THIRD : (k + 1) * THIRD, :]


def sum_parts(parts):
    return call(sum_body, struct((OWN, LOCAL), jnp.float32), [VMEM], VMEM, traffic=1700000)(parts)


NEAR, ACROSS = ((0, 1), (2, 3)), ((0, 3), (1, 2))


def paired(block, axis, pairs):
    other = lax.ppermute(block, axis, [pair for a, b in pairs for pair in ((a, b), (b, a))])
    return jnp.concatenate([block, other])


def turned(block, axis, way):
    pairs = [(place, (place + way) % 4) for place in range(4)]
    pairs += [(4 + place, 4 + (place - way) % 4) for place in range(4)]
    return lax.ppermute(block, ("core", axis), pairs)


def swap(value, axis):
    return lax.ppermute(value, axis, [(0, 1), (1, 0)])


def shards(
    tokens,
    out_grad,
    gate_codes,
    gate_zeros,
    gate_log_scale,
    up_codes,
    up_zeros,
    up_log_scale,
    down_codes,
    down_zeros,
    down_log_scale,
):
    tokens_near, grad_near = by_field(tokens, out_grad)
    tokens_near, grad_near = paired(tokens_near, "y_lo", ((0, 1),)), paired(grad_near, "y_lo", ((0, 1),))
    tokens_near, grad_near = paired(tokens_near, "x", NEAR), paired(grad_near, "z", NEAR)
    tokens_near, gate_zeros = lax.optimization_barrier((tokens_near, gate_zeros))
    tokens_near, grad_near = paired(tokens_near, "x", ACROSS), paired(grad_near, "z", ACROSS)
    gate = unpack_rows(gate_codes, gate_zeros, gate_log_scale)
    tokens_near, gate, up_zeros = lax.optimization_barrier((tokens_near, gate, up_zeros))
    grad_near, up_log_scale = lax.optimization_barrier((grad_near, up_log_scale))
    tokens_first, grad_first = turned(tokens_near, "z", 1), turned(grad_near, "x", 1)
    tokens_second, grad_second = turned(tokens_near, "z", -1), turned(grad_near, "x", -1)
    up = unpack_rows(up_codes, up_zeros, up_log_scale)
    tokens_first, grad_first, up, down_zeros = lax.optimization_barrier((tokens_first, grad_first, up, down_zeros))
    tokens_parts = tokens_near, tokens_first, turned(tokens_first, "z", 1), tokens_second
    grad_parts = grad_near, grad_first, turned(grad_first, "x", 1), grad_second
    down, table = unpack_columns(down_codes, down_zeros, down_log_scale)
    *sums, all_tokens, all_grad = forward(tokens_parts, grad_parts, gate, up, down)
    partial, all_tokens, all_grad, gate_grad, up_grad, hidden = backward(
        tokens_parts, grad_parts, gate, up, down, sums, all_tokens, all_grad
    )
    parts = lax.all_to_all(partial.reshape(SHARDS, OWN, LOCAL), ("x", "y_lo", "z"), 0, 0, tiled=True)
    own, given = group_grads(
        all_tokens,
        all_grad,
        gate_grad,
        up_grad,
        hidden,
        (gate_codes, gate_zeros, gate_log_scale),
        (up_codes, up_zeros, up_log_scale),
        down_codes,
        table,
    )
    own = own + swap(given, "core")
    own = own.astype(jnp.bfloat16)
    tokens_grad = sum_parts(parts).T
    far, tokens_grad = lax.optimization_barrier((swap(own, "y_hi"), tokens_grad))
    mine = own.astype(jnp.float32) + far.astype(jnp.float32)
    theirs = swap(mine, "core")
    return (tokens_grad, *split(mine, theirs))


def solution(mesh):
    axes = jax.sharding.Mesh(mesh.devices.reshape(2, 2, N_X, N_Y, N_Z), ("y_hi", "core", "x", "y_lo", "z"))
    dp, tensor = ("y_hi", "core"), ("x", "y_lo", "z")
    columns, rows = P(None, tensor), P(tensor, None)
    return jax.shard_map(
        shards,
        mesh=axes,
        in_specs=(P(dp, tensor),) * 2 + (columns,) * 6 + (rows,) * 3,
        out_specs=(P(dp, tensor),) + (columns,) * 4 + (rows,) * 2,
        check_vma=False,
    )
```

```python
import jax
import jax.numpy as jnp
from jax import lax
from jax.experimental import pallas as pl
from jax.experimental.pallas import tpu as pltpu
from jax.sharding import PartitionSpec as P

N_X, N_Y, N_Z = 4, 2, 4
SHARDS = 32
OWN = 192
THIRD = 64
BLOCKS = 16
WORDS = 128
FEATURES = 384
HIDDEN = 512
LOCAL = 128
MIB = 1 << 20

CONTRACT_LAST = (((1,), (1,)), ((), ()))
CONTRACT_FIRST = (((0,), (0,)), ((), ()))


def shard_row(k, word):
    return (word // THIRD) * OWN + k * THIRD + word % THIRD


def first_word(k, group):
    return -((k - 128 * group) // 3)


def spread_over_groups(k, start, rows, values):
    first, last = (3 * start + k) // 128, (3 * (start + rows - 1) + k) // 128
    if first == last:
        return values[first]
    row = start + lax.broadcasted_iota(jnp.int32, (rows, 1), 0)
    return jnp.where(row < first_word(k, last), values[first], values[last])


def call(body, out_shape, in_specs, out_specs, scratch=(), flops=0, traffic=0, vmem=16, aliases=None):
    return pl.pallas_call(
        body,
        out_shape=out_shape,
        in_specs=in_specs,
        out_specs=out_specs,
        scratch_shapes=list(scratch),
        input_output_aliases=aliases or {},
        compiler_params=pltpu.CompilerParams(vmem_limit_bytes=vmem * MIB),
        cost_estimate=pl.CostEstimate(flops=flops, bytes_accessed=traffic, transcendentals=0),
    )


def struct(shape, dtype):
    return jax.ShapeDtypeStruct(shape, dtype)


def from_hbm(*arrays):
    return [pltpu.with_memory_space_constraint(array, pltpu.HBM) for array in arrays]


def from_vmem(*arrays):
    return [pltpu.with_memory_space_constraint(array, pltpu.VMEM) for array in arrays]


VMEM = pl.BlockSpec(memory_space=pltpu.VMEM)
ANY = pl.BlockSpec(memory_space=pl.ANY)


def by_field_body(tokens_ref, grad_ref, tokens_out, grad_out, wide):
    for ref, out_ref in ((tokens_ref, tokens_out), (grad_ref, grad_out)):
        wide[...] = ref[...].astype(jnp.float32)
        for k in range(3):
            out_ref[0, k * THIRD : (k + 1) * THIRD, :] = wide[pl.ds(k, THIRD, stride=3), :].astype(jnp.bfloat16)


def by_field(tokens, out_grad):
    return call(
        by_field_body,
        (struct((1, OWN, LOCAL), jnp.bfloat16),) * 2,
        [VMEM, VMEM],
        (VMEM, VMEM),
        [pltpu.VMEM((OWN, LOCAL), jnp.float32)],
        traffic=200000,
    )(*from_hbm(tokens.T, out_grad.T))


def field(words, k):
    if k:
        words = jnp.right_shift(words, 4 * k)
    if k < 2:
        words = jnp.bitwise_and(words, 15)
    return words.astype(jnp.float32)


CHUNKS = 8
AHEAD = 6


def row_copy(chunk, source, to, sems):
    rows = pl.ds(pl.multiple_of(chunk * 2 * WORDS, 2 * WORDS), 2 * WORDS)
    return pltpu.make_async_copy(source.at[rows], to.at[rows], sems.at[chunk])


def column_copy(chunk, source, to, sems):
    columns = pl.ds(pl.multiple_of(chunk * 2 * WORDS, 2 * WORDS), 2 * WORDS)
    return pltpu.make_async_copy(source.at[:, columns], to.at[:, columns], sems.at[chunk])


def tables_in(sources, targets, sems):
    copies = [pltpu.make_async_copy(a, b, sems.at[i]) for i, (a, b) in enumerate(zip(sources, targets))]
    for copy in copies:
        copy.start()
    return copies


def unpack_rows_pair(pair, codes, zeros_ref, log_ref, out_ref):
    for part in range(2):
        block = pair * 2 + part
        zeros = [zeros_ref[pl.ds(3 * block + g, 1), :].astype(jnp.float32) for g in range(3)]
        scales = [jnp.exp(log_ref[pl.ds(3 * block + g, 1), :]) for g in range(3)]
        for start in range(0, WORDS, 16):
            words = codes[pl.ds(pl.multiple_of(block * WORDS + start, 16), 16), :]
            for k in range(3):
                zero = spread_over_groups(k, start, 16, zeros)
                scale = spread_over_groups(k, start, 16, scales)
                weight = (scale * (field(words, k) - zero)).astype(jnp.bfloat16)
                row = k * THIRD + start % THIRD
                out_ref[part * 2 + start // THIRD, pair, row : row + 16, :] = weight


def streamed(copy_of, source, to, sems, work):
    def step(chunk, carry):
        copy_of(chunk, source, to, sems).wait()

        @pl.when(chunk + AHEAD < CHUNKS)
        def _():
            copy_of(chunk + AHEAD, source, to, sems).start()

        work(chunk)
        return carry

    lax.fori_loop(0, CHUNKS, step, 0)


def start_first(copy_of, source, to, sems):
    for chunk in range(AHEAD):
        copy_of(chunk, source, to, sems).start()


def unpack_rows_body(codes_hbm, zeros_hbm, log_hbm, out_ref, zeros_ref, log_ref, table_sems, codes, sems):
    tables = tables_in((zeros_hbm, log_hbm), (zeros_ref, log_ref), table_sems)
    start_first(row_copy, codes_hbm, codes, sems)
    for table in tables:
        table.wait()
    streamed(
        row_copy, codes_hbm, codes, sems, lambda pair: unpack_rows_pair(pair, codes, zeros_ref, log_ref, out_ref)
    )


def unpack_rows(codes, zeros, log_scale):
    return call(
        unpack_rows_body,
        pltpu.VMEM((N_Z, N_X * N_Y, OWN, HIDDEN), jnp.bfloat16),
        [ANY] * 3,
        VMEM,
        [
            pltpu.VMEM((48, HIDDEN), jnp.int32),
            pltpu.VMEM((48, HIDDEN), jnp.float32),
            pltpu.SemaphoreType.DMA((2,)),
            pltpu.VMEM((BLOCKS * WORDS, HIDDEN), jnp.int32),
            pltpu.SemaphoreType.DMA((CHUNKS,)),
        ],
        flops=20000000,
        traffic=10500000,
    )(*from_hbm(codes, zeros, log_scale))


def field_order(transposed):
    feature = lax.broadcasted_iota(jnp.int32, (FEATURES, FEATURES), 1 if transposed else 0)
    column = lax.broadcasted_iota(jnp.int32, (FEATURES, FEATURES), 0 if transposed else 1)
    wanted = 3 * jnp.bitwise_and(column, 127) + jnp.right_shift(column, 7)
    return (feature == wanted).astype(jnp.float32)


def reorder(rows, transposed):
    return jnp.dot(
        rows, field_order(transposed), precision=lax.Precision.HIGHEST, preferred_element_type=jnp.float32
    )


def unpack_columns_pair(pair, codes, table_ref, out_ref):
    for part in range(2):
        block = pair * 2 + part
        table = table_ref[pl.ds(pl.multiple_of(8 * block, 8), 8), :]
        for g in range(4):
            words = codes[g * 128 : (g + 1) * 128, pl.ds(pl.multiple_of(block * WORDS, WORDS), WORDS)]
            for k in range(3):
                columns = slice(k * WORDS, (k + 1) * WORDS)
                zero, scale = table[g : g + 1, columns], table[4 + g : 5 + g, columns]
                weight = (scale * (field(words, k) - zero)).astype(jnp.bfloat16)
                to = slice(part * FEATURES + k * WORDS, part * FEATURES + (k + 1) * WORDS)
                out_ref[pair, g * 128 : (g + 1) * 128, to] = weight


def unpack_columns_body(
    codes_hbm, zeros_hbm, log_hbm, out_ref, table_ref, zeros_ref, log_ref, table_sems, natural, codes, sems
):
    tables = tables_in((zeros_hbm, log_hbm), (zeros_ref, log_ref), table_sems)
    start_first(column_copy, codes_hbm, codes, sems)
    for table in tables:
        table.wait()
    for b in range(BLOCKS):
        columns = slice(b * FEATURES, (b + 1) * FEATURES)
        natural[8 * b : 8 * b + 4, :] = zeros_ref[:, columns].astype(jnp.float32)
        natural[8 * b + 4 : 8 * b + 8, :] = jnp.exp(log_ref[:, columns])
    table_ref[...] = reorder(natural[...], False)
    streamed(column_copy, codes_hbm, codes, sems, lambda pair: unpack_columns_pair(pair, codes, table_ref, out_ref))


def unpack_columns(codes, zeros, log_scale):
    wide = (4, BLOCKS * FEATURES)
    return call(
        unpack_columns_body,
        (
            pltpu.VMEM((N_X * N_Y, HIDDEN, 2 * FEATURES), jnp.bfloat16),
            pltpu.HBM((8 * BLOCKS, FEATURES), jnp.float32),
        ),
        [ANY] * 3,
        (VMEM,) * 2,
        [
            pltpu.VMEM(wide, jnp.int32),
            pltpu.VMEM(wide, jnp.float32),
            pltpu.SemaphoreType.DMA((2,)),
            pltpu.VMEM((8 * BLOCKS, FEATURES), jnp.float32),
            pltpu.VMEM((HIDDEN, BLOCKS * WORDS), jnp.int32),
            pltpu.SemaphoreType.DMA((CHUNKS,)),
        ],
        flops=20000000,
        traffic=10500000,
    )(*from_hbm(codes, zeros, log_scale))


SLAB = 8 * OWN


def position():
    return tuple(lax.axis_index(axis) for axis in ("x", "y_lo", "z"))


def swapped_with(here, near):
    place = 3 - here if near // 2 else here
    return place + 1 - 2 * (place % 2) if near % 2 else place


def lay_tokens(place, source, far, to):
    x, y, z = place
    slab = (z + 4 - far) % 4
    for near in range(4):
        for dy in range(2):
            to[slab, swapped_with(x, near) * 2 + (y + dy) % 2, :, :] = source[near * 2 + dy]
    return slab


def lay_grad(place, source, far, to):
    x, y, z = place
    slab = (x + 4 - far) % 4
    for near in range(4):
        z_from = swapped_with(z, near)
        for dy in range(2):
            for k in range(3):
                row = pl.multiple_of((z_from // 2) * FEATURES + k * WORDS + (z_from % 2) * THIRD, THIRD)
                to[slab * 2 + (y + dy) % 2, pl.ds(row, THIRD), :] = source[
                    near * 2 + dy, k * THIRD : (k + 1) * THIRD, :
                ]
    return slab


def slab_out(slab, tokens_from, tokens_hbm, sems):
    return pltpu.make_async_copy(tokens_from.at[slab], tokens_hbm.at[slab], sems)


def pair_out(slab, grad_from, grad_hbm, sems):
    pairs = pl.ds(slab * 2, 2)
    return pltpu.make_async_copy(grad_from.at[pairs], grad_hbm.at[pairs], sems)


def slab_products(fars, tokens_refs, grad_refs, weights, scratch, hbm, totals):
    gate_ref, up_ref, down_ref = weights
    tokens_to, grad_to, tokens_sems, grad_sems = scratch
    tokens_hbm, grad_hbm = hbm
    place = position()
    gate_pre, up_pre, hidden_grad = totals
    copies, laid = [], []
    for i, far in enumerate(fars):
        slabs = lay_tokens(place, tokens_refs[i], far, tokens_to), lay_grad(place, grad_refs[i], far, grad_to)
        copies.append(slab_out(slabs[0], tokens_to, tokens_hbm, tokens_sems.at[i]))
        copies.append(pair_out(slabs[1], grad_to, grad_hbm, grad_sems.at[i]))
        laid.append(slabs)
    for copy in copies:
        copy.start()
    for slab, grad_slab in laid:
        features = tokens_to[slab].reshape(SLAB, LOCAL).T
        gate_pre += jnp.dot(features, gate_ref[slab].reshape(SLAB, HIDDEN), preferred_element_type=jnp.float32)
        up_pre += jnp.dot(features, up_ref[slab].reshape(SLAB, HIDDEN), preferred_element_type=jnp.float32)
        for dy in range(2):
            piece = grad_to[grad_slab * 2 + dy]
            hidden_grad += jnp.dot(down_ref[grad_slab * 2 + dy], piece, preferred_element_type=jnp.float32)
    return (gate_pre, up_pre, hidden_grad), copies


def forward_body(
    t0, t1, t3, o0, o1, o3, gate_ref, up_ref, down_ref,
    gate_pre_ref, up_pre_ref, hidden_grad_ref, tokens_hbm, grad_hbm,
    tokens_to, grad_to, tokens_sems, grad_sems,
):
    zero = jnp.zeros((LOCAL, HIDDEN), jnp.float32)
    core = lax.axis_index("core")
    (gate_pre_ref[...], up_pre_ref[...], hidden_grad_ref[...]), copies = slab_products(
        (0, 1 + 2 * core, 3 - 2 * core), (t0, t1, t3), (o0, o1, o3), (gate_ref, up_ref, down_ref),
        (tokens_to, grad_to, tokens_sems, grad_sems), (tokens_hbm, grad_hbm),
        (zero, zero, jnp.zeros((HIDDEN, LOCAL), jnp.float32)),
    )
    for copy in copies:
        copy.wait()


TOKENS_SHAPE = (N_Z, N_X * N_Y, OWN, LOCAL)
GRAD_SHAPE = (N_X * N_Y, 2 * FEATURES, LOCAL)


def slab_scratch(slabs):
    return [
        pltpu.VMEM(TOKENS_SHAPE, jnp.bfloat16),
        pltpu.VMEM(GRAD_SHAPE, jnp.bfloat16),
        pltpu.SemaphoreType.DMA((slabs,)),
        pltpu.SemaphoreType.DMA((slabs,)),
    ]


def forward(tokens_parts, grad_parts, gate, up, down):
    f32, bf16 = jnp.float32, jnp.bfloat16
    near = (0, 1, 3)
    return call(
        forward_body,
        (
            pltpu.VMEM((LOCAL, HIDDEN), f32),
            pltpu.VMEM((LOCAL, HIDDEN), f32),
            pltpu.VMEM((HIDDEN, LOCAL), f32),
            pltpu.HBM(TOKENS_SHAPE, bf16),
            pltpu.HBM(GRAD_SHAPE, bf16),
        ),
        [VMEM] * 9,
        (VMEM,) * 3 + (ANY,) * 2,
        slab_scratch(3),
        flops=3 * 3 * 2 * 128 * 1536 * 512,
        traffic=18000000,
    )(
        *from_vmem(*[tokens_parts[far] for far in near], *[grad_parts[far] for far in near]),
        *from_vmem(gate, up, down),
    )


def backward_body(
    t2, o2, gate_ref, up_ref, down_ref, gate_pre_ref, up_pre_ref, hidden_grad_ref, tokens_in, grad_in,
    partial_hbm, tokens_hbm, grad_hbm, gate_grad_hbm, up_grad_hbm, hidden_hbm,
    tokens_to, grad_to, tokens_sems, grad_sems, partial, partial_sems, gate_grad_ref, up_grad_ref, hidden_ref, small_sems,
):
    (gate_pre, up_pre, hidden_grad), copies = slab_products(
        (2,), (t2,), (o2,), (gate_ref, up_ref, down_ref),
        (tokens_to, grad_to, tokens_sems, grad_sems), (tokens_hbm, grad_hbm),
        (gate_pre_ref[...], up_pre_ref[...], hidden_grad_ref[...]),
    )
    hidden_grad = hidden_grad.T
    sigmoid_gate = jax.nn.sigmoid(gate_pre)
    silu_gate = gate_pre * sigmoid_gate
    hidden = silu_gate * up_pre
    gate_grad = hidden_grad * up_pre * sigmoid_gate * (1.0 + gate_pre * (1.0 - sigmoid_gate))
    up_grad = hidden_grad * silu_gate
    gate_grad_ref[...] = gate_grad.astype(jnp.bfloat16)
    up_grad_ref[...] = up_grad.astype(jnp.bfloat16)
    hidden_ref[...] = hidden.T.astype(jnp.bfloat16)
    copies += tables_in(
        (gate_grad_ref, up_grad_ref, hidden_ref), (gate_grad_hbm, up_grad_hbm, hidden_hbm), small_sems
    )
    gate_turned = gate_grad.T.astype(jnp.bfloat16)
    up_turned = up_grad.T.astype(jnp.bfloat16)
    for slab in range(N_Z):
        total = jnp.dot(gate_ref[slab].reshape(SLAB, HIDDEN), gate_turned, preferred_element_type=jnp.float32)
        total += jnp.dot(up_ref[slab].reshape(SLAB, HIDDEN), up_turned, preferred_element_type=jnp.float32)
        partial[slab] = total.astype(jnp.bfloat16).reshape(N_X * N_Y, OWN, LOCAL)
        copy = pltpu.make_async_copy(partial.at[slab], partial_hbm.at[:, slab], partial_sems.at[slab])
        copy.start()
        copies.append(copy)
    for copy in copies:
        copy.wait()


def backward(tokens_parts, grad_parts, gate, up, down, sums, all_tokens, all_grad):
    bf16 = jnp.bfloat16
    return call(
        backward_body,
        (
            pltpu.HBM((N_X * N_Y, N_Z, OWN, LOCAL), bf16),
            pltpu.HBM(TOKENS_SHAPE, bf16),
            pltpu.HBM(GRAD_SHAPE, bf16),
            pltpu.HBM((LOCAL, HIDDEN), bf16),
            pltpu.HBM((LOCAL, HIDDEN), bf16),
            pltpu.HBM((HIDDEN, LOCAL), bf16),
        ),
        [VMEM] * 8 + [ANY] * 2,
        (ANY,) * 6,
        slab_scratch(1)
        + [
            pltpu.VMEM(TOKENS_SHAPE, bf16),
            pltpu.SemaphoreType.DMA((N_Z,)),
            pltpu.VMEM((LOCAL, HIDDEN), bf16),
            pltpu.VMEM((LOCAL, HIDDEN), bf16),
            pltpu.VMEM((HIDDEN, LOCAL), bf16),
            pltpu.SemaphoreType.DMA((3,)),
        ],
        flops=3 * 2 * 128 * 6144 * 512,
        traffic=24000000,
        aliases={8: 1, 9: 2},
    )(
        *from_vmem(tokens_parts[2], grad_parts[2], gate, up, down, *sums),
        *from_hbm(all_tokens, all_grad),
    )


EXTRA = 16


def with_sums(rows, members):
    sums = jnp.dot(members, rows, preferred_element_type=jnp.float32)
    head = sums.astype(jnp.bfloat16)
    rest = (sums - head.astype(jnp.float32)).astype(jnp.bfloat16)
    return jnp.concatenate([rows, jnp.concatenate([head, rest], axis=0)], axis=0)


def block_members():
    group = lax.broadcasted_iota(jnp.int32, (8, FEATURES), 0)
    place = lax.broadcasted_iota(jnp.int32, (8, FEATURES), 1)
    half = (place >= OWN).astype(jnp.int32)
    place = place - OWN * half
    k = jnp.right_shift(place, 6)
    feature = 3 * (half * THIRD + place - THIRD * k) + k
    scale = jnp.where(k == 0, 1.0, jnp.where(k == 1, 16.0, 256.0))
    return jnp.where(jnp.right_shift(feature, 7) == group, scale, 0.0).astype(jnp.bfloat16)


def hidden_members():
    group = lax.broadcasted_iota(jnp.int32, (8, HIDDEN), 0)
    unit = lax.broadcasted_iota(jnp.int32, (8, HIDDEN), 1)
    return (jnp.right_shift(unit, 7) == group).astype(jnp.float32).astype(jnp.bfloat16)


MASKS = (15, 240, 3840)
SHRINK = (1.0, 1.0 / 16.0, 1.0 / 256.0)


def in_place(words, k):
    return jnp.bitwise_and(words, MASKS[k]).astype(jnp.float32)


def in_turn(*streams):
    running = list(streams)
    while running:
        for stream in list(running):
            if next(stream, None) is None:
                running.remove(stream)


def row_groups(block, codes, weight_grad, sums, totals):
    weighted = [jnp.zeros((8, HIDDEN), jnp.float32)] * 3
    for start in range(0, WORDS, 8):
        words = codes[pl.ds(pl.multiple_of(block * WORDS + start, 8), 8), :]
        for k in range(3):
            product = in_place(words, k) * weight_grad[shard_row(k, start) : shard_row(k, start) + 8, :]
            first, last = (3 * start + k) // 128, (3 * (start + 7) + k) // 128
            if first == last:
                weighted[first] = weighted[first] + product
            else:
                low = start + lax.broadcasted_iota(jnp.int32, (8, 1), 0) < first_word(k, last)
                low_product = jnp.where(low, product, 0.0)
                weighted[first] = weighted[first] + low_product
                weighted[last] = weighted[last] + (product - low_product)
        yield True
    for g in range(3):
        row = pl.ds(3 * block + g, 1)
        sums[row, :] = jnp.sum(weighted[g], axis=0, keepdims=True)
        totals[row, :] = (
            weight_grad[FEATURES + g : FEATURES + g + 1, :] + weight_grad[FEATURES + 8 + g : FEATURES + 9 + g, :]
        )
    yield True


def column_groups(block, part, codes, weight_grad, raw):
    here = pl.ds(pl.multiple_of(8 * block, 8), 8)
    mine = slice(part * FEATURES, (part + 1) * FEATURES)
    totals = weight_grad[HIDDEN : HIDDEN + 4, mine] + weight_grad[HIDDEN + 8 : HIDDEN + 12, mine]
    for k in range(3):
        sums = []
        for g in range(4):
            weighted = jnp.zeros((8, WORDS), jnp.float32)
            for start in range(g * 128, g * 128 + 128, 8):
                words = codes[start : start + 8, pl.ds(pl.multiple_of(block * WORDS, WORDS), WORDS)]
                value = weight_grad[start : start + 8, part * FEATURES + k * WORDS : part * FEATURES + (k + 1) * WORDS]
                weighted = weighted + in_place(words, k) * value
            sums.append(jnp.sum(weighted, axis=0, keepdims=True))
            yield True
        columns = slice(k * WORDS, (k + 1) * WORDS)
        raw[here, columns] = jnp.concatenate([jnp.concatenate(sums, axis=0) * SHRINK[k], totals[:, columns]], axis=0)


DEEP = 4


def group_body(
    gate_hbm, up_hbm, down_hbm, tokens_hbm, grad_hbm, *small_hbm_and_rest
):
    small_hbm, rest = small_hbm_and_rest[:8], small_hbm_and_rest[8:]
    small, rest = rest[-8:], rest[:-8]
    group_work(gate_hbm, up_hbm, down_hbm, tokens_hbm, grad_hbm, small_hbm, small, *rest)


def group_work(
    gate_hbm, up_hbm, down_hbm, tokens_hbm, grad_hbm, small_hbm, small,
    own_ref, given_ref,
    gate_codes, up_codes, down_codes, gate_sems, up_sems, down_sems, tokens_ref, grad_ref, tokens_sems, grad_sems, small_sems,
    hidden_rows, gate_even, up_even, gate_odd, up_odd, down_pair, down_rows, halves, sums, totals,
):
    def copies(chunk):
        return (
            row_copy(chunk, gate_hbm, gate_codes, gate_sems),
            row_copy(chunk, up_hbm, up_codes, up_sems),
            column_copy(chunk, down_hbm, down_codes, down_sems),
        )

    def start(chunk):
        for copy in copies(chunk):
            copy.start()

    def rows_in(pair):
        return (
            pltpu.make_async_copy(tokens_hbm.at[:, pair], tokens_ref.at[:, pair], tokens_sems.at[pair]),
            pltpu.make_async_copy(grad_hbm.at[pair], grad_ref.at[pair], grad_sems.at[pair]),
        )

    gate_grad_ref, up_grad_ref, hidden_ref, gate_zeros, gate_log, up_zeros, up_log, table_ref = small
    arrivals = tables_in(small_hbm, small, small_sems)
    for pair in range(DEEP):
        for copy in rows_in(pair):
            copy.start()
        start(pair)
    for pair in range(DEEP, BLOCKS // 2):
        for copy in rows_in(pair):
            copy.start()
    for arrival in arrivals:
        arrival.wait()
    hidden_rows[...] = with_sums(hidden_ref[...], hidden_members())
    members = block_members()
    field_of_row = jnp.right_shift(lax.broadcasted_iota(jnp.int32, (OWN, 1), 0), 6)
    shrink = jnp.where(field_of_row == 0, SHRINK[0], jnp.where(field_of_row == 1, SHRINK[1], SHRINK[2]))
    shrink = jnp.broadcast_to(shrink, (OWN, LOCAL)).astype(jnp.bfloat16)

    def row_products(pair, part, gate_to, up_to):
        features = jnp.concatenate([tokens_ref[part * 2 + half, pair] * shrink for half in range(2)], axis=0)
        features = with_sums(features, members)
        for grad, to in ((gate_grad_ref, gate_to), (up_grad_ref, up_to)):
            for row in range(0, FEATURES + EXTRA, 80):
                to[row : row + 80, :] = jnp.dot(
                    features[row : row + 80, :], grad[...], preferred_element_type=jnp.float32
                )
                yield True

    def column_products(pair, down_to):
        for row in range(0, HIDDEN + EXTRA, 176):
            down_to[row : row + 176, :] = lax.dot_general(
                hidden_rows[row : row + 176, :], grad_ref[pair], CONTRACT_LAST, preferred_element_type=jnp.float32
            )
            yield True

    def groups(block, gate_from, up_from):
        yield from row_groups(block, gate_codes, gate_from, sums.at[0], totals.at[0])
        yield from row_groups(block, up_codes, up_from, sums.at[1], totals.at[1])

    def down_groups(pair):
        for part in range(2):
            yield from column_groups(pair * 2 + part, part, down_codes, down_pair, down_rows)

    for copy in rows_in(0):
        copy.wait()
    in_turn(row_products(0, 0, gate_even, up_even))

    def pair_step(pair, carry):
        for copy in copies(pair):
            copy.wait()
        following = jnp.minimum(pair + 1, BLOCKS // 2 - 1)

        @pl.when(pair < BLOCKS // 2 - 1)
        def _():
            for copy in rows_in(following):
                copy.wait()

        @pl.when(pair + DEEP < CHUNKS)
        def _():
            start(pair + DEEP)

        in_turn(row_products(pair, 1, gate_odd, up_odd), groups(pair * 2, gate_even, up_even))
        in_turn(column_products(pair, down_pair), groups(pair * 2 + 1, gate_odd, up_odd))
        in_turn(row_products(following, 0, gate_even, up_even), down_groups(pair))
        return carry

    lax.fori_loop(0, BLOCKS // 2, pair_step, 0)

    for half, (zeros_ref, log_ref) in enumerate(((gate_zeros, gate_log), (up_zeros, up_log))):
        scale = jnp.exp(log_ref[...])
        halves[half, 0:48] = scale * (sums[half] - zeros_ref[...].astype(jnp.float32) * totals[half])
        halves[half, 48:96] = -scale * totals[half]
    found, table = down_rows[...].reshape(BLOCKS, 8, FEATURES), table_ref[...].reshape(BLOCKS, 8, FEATURES)
    found, total, zero, scale = found[:, 0:4], found[:, 4:8], table[:, 0:4], table[:, 4:8]
    finished = jnp.concatenate([scale * (found - zero * total), -scale * total], axis=1)
    down_rows[...] = finished.reshape(8 * BLOCKS, FEATURES)
    for half, begin in ((0, 0), (1, 48)):
        for j in range(3):
            halves[half, 96:144, j * 128 : (j + 1) * 128] = down_rows[begin : begin + 48, j * 128 : (j + 1) * 128]
    halves[0, 96:128, 384:] = down_rows[96:128, 0:128]
    halves[0, 128:144, 384:] = down_rows[96:112, 128:256]
    halves[1, 96:112, 384:] = down_rows[112:128, 128:256]
    halves[1, 112:144, 384:] = down_rows[96:128, 256:384]
    core = lax.axis_index("core")
    own_ref[...] = halves[core]
    given_ref[...] = halves[1 - core]


def group_grads(tokens, grad, gate_grad, up_grad, hidden, gate_tables, up_tables, down_codes, table):
    half = struct((144, HIDDEN), jnp.float32)
    gate_codes, *gate_tables = gate_tables
    up_codes, *up_tables = up_tables
    small = (gate_grad, up_grad, hidden, *gate_tables, *up_tables, table)
    rows, columns = (FEATURES + EXTRA, HIDDEN), (HIDDEN + EXTRA, 2 * FEATURES)
    return call(
        group_body,
        (half, half),
        [ANY] * 13,
        (VMEM, VMEM),
        [
            pltpu.VMEM((BLOCKS * WORDS, HIDDEN), jnp.int32),
            pltpu.VMEM((BLOCKS * WORDS, HIDDEN), jnp.int32),
            pltpu.VMEM((HIDDEN, BLOCKS * WORDS), jnp.int32),
        ]
        + [pltpu.SemaphoreType.DMA((CHUNKS,))] * 3
        + [
            pltpu.VMEM(TOKENS_SHAPE, jnp.bfloat16),
            pltpu.VMEM(GRAD_SHAPE, jnp.bfloat16),
            pltpu.SemaphoreType.DMA((BLOCKS // 2,)),
            pltpu.SemaphoreType.DMA((BLOCKS // 2,)),
            pltpu.SemaphoreType.DMA((8,)),
            pltpu.VMEM((HIDDEN + EXTRA, LOCAL), jnp.bfloat16),
        ]
        + [pltpu.VMEM(shape, jnp.float32) for shape in (rows,) * 4 + (columns,)]
        + [pltpu.VMEM((8 * BLOCKS, FEATURES), jnp.float32), pltpu.VMEM((2, 144, HIDDEN), jnp.float32)]
        + [pltpu.VMEM((2, 48, HIDDEN), jnp.float32)] * 2
        + [pltpu.VMEM(array.shape, array.dtype) for array in small],
        flops=3 * 2 * 128 * 6144 * 512,
        traffic=17000000,
        vmem=40,
    )(
        *from_hbm(gate_codes, up_codes, down_codes, tokens, grad, *small),
    )


def split_body(mine_ref, other_ref, gs_ref, gz_ref, us_ref, uz_ref, ds_ref, dz_ref, halves, rows):
    core = lax.axis_index("core")
    halves[core] = mine_ref[...]
    halves[1 - core] = other_ref[...]
    for half, scale_ref, zero_ref in ((0, gs_ref, gz_ref), (1, us_ref, uz_ref)):
        scale_ref[...] = halves[half, 0:48, :]
        zero_ref[...] = halves[half, 48:96, :]
        for j in range(3):
            rows[48 * half : 48 * half + 48, j * 128 : (j + 1) * 128] = halves[half, 96:144, j * 128 : (j + 1) * 128]
    rows[96:128, 0:128] = halves[0, 96:128, 384:]
    rows[96:112, 128:256] = halves[0, 128:144, 384:]
    rows[112:128, 128:256] = halves[1, 96:112, 384:]
    rows[96:128, 256:384] = halves[1, 112:144, 384:]
    natural = reorder(rows[...], True)
    for b in range(BLOCKS):
        columns = slice(b * FEATURES, (b + 1) * FEATURES)
        ds_ref[:, columns] = natural[8 * b : 8 * b + 4, :]
        dz_ref[:, columns] = natural[8 * b + 4 : 8 * b + 8, :]


def split(mine, other):
    f32 = jnp.float32
    return call(
        split_body,
        (struct((48, HIDDEN), f32),) * 4 + (struct((4, BLOCKS * FEATURES), f32),) * 2,
        [VMEM, VMEM],
        (VMEM,) * 6,
        [pltpu.VMEM((2, 144, HIDDEN), f32), pltpu.VMEM((8 * BLOCKS, FEATURES), f32)],
        traffic=1200000,
    )(mine, other)


def sum_body(parts_ref, out_ref):
    total = parts_ref[0].astype(jnp.float32)
    for part in range(1, SHARDS):
        total = total + parts_ref[part].astype(jnp.float32)
    for k in range(3):
        out_ref[pl.ds(k, THIRD, stride=3), :] = total[k * THIRD : (k + 1) * THIRD, :]


def sum_parts(parts):
    return call(sum_body, struct((OWN, LOCAL), jnp.float32), [VMEM], VMEM, traffic=1700000)(parts)


NEAR, ACROSS = ((0, 1), (2, 3)), ((0, 3), (1, 2))


def paired(block, axis, pairs):
    other = lax.ppermute(block, axis, [pair for a, b in pairs for pair in ((a, b), (b, a))])
    return jnp.concatenate([block, other])


def turned(block, axis, way):
    pairs = [(place, (place + way) % 4) for place in range(4)]
    pairs += [(4 + place, 4 + (place - way) % 4) for place in range(4)]
    return lax.ppermute(block, ("core", axis), pairs)


def swap(value, axis):
    return lax.ppermute(value, axis, [(0, 1), (1, 0)])


def shards(
    tokens,
    out_grad,
    gate_codes,
    gate_zeros,
    gate_log_scale,
    up_codes,
    up_zeros,
    up_log_scale,
    down_codes,
    down_zeros,
    down_log_scale,
):
    tokens_near, grad_near = by_field(tokens, out_grad)
    tokens_near, grad_near = paired(tokens_near, "y_lo", ((0, 1),)), paired(grad_near, "y_lo", ((0, 1),))
    tokens_near, grad_near = paired(tokens_near, "x", NEAR), paired(grad_near, "z", NEAR)
    tokens_near, gate_zeros = lax.optimization_barrier((tokens_near, gate_zeros))
    tokens_near, grad_near = paired(tokens_near, "x", ACROSS), paired(grad_near, "z", ACROSS)
    gate = unpack_rows(gate_codes, gate_zeros, gate_log_scale)
    tokens_near, gate, up_zeros = lax.optimization_barrier((tokens_near, gate, up_zeros))
    grad_near, up_log_scale = lax.optimization_barrier((grad_near, up_log_scale))
    tokens_first, grad_first = turned(tokens_near, "z", 1), turned(grad_near, "x", 1)
    tokens_second, grad_second = turned(tokens_near, "z", -1), turned(grad_near, "x", -1)
    up = unpack_rows(up_codes, up_zeros, up_log_scale)
    tokens_first, grad_first, up, down_zeros = lax.optimization_barrier((tokens_first, grad_first, up, down_zeros))
    tokens_parts = tokens_near, tokens_first, turned(tokens_first, "z", 1), tokens_second
    grad_parts = grad_near, grad_first, turned(grad_first, "x", 1), grad_second
    down, table = unpack_columns(down_codes, down_zeros, down_log_scale)
    *sums, all_tokens, all_grad = forward(tokens_parts, grad_parts, gate, up, down)
    partial, all_tokens, all_grad, gate_grad, up_grad, hidden = backward(
        tokens_parts, grad_parts, gate, up, down, sums, all_tokens, all_grad
    )
    parts = lax.all_to_all(partial.reshape(SHARDS, OWN, LOCAL), ("x", "y_lo", "z"), 0, 0, tiled=True)
    own, given = group_grads(
        all_tokens,
        all_grad,
        gate_grad,
        up_grad,
        hidden,
        (gate_codes, gate_zeros, gate_log_scale),
        (up_codes, up_zeros, up_log_scale),
        down_codes,
        table,
    )
    own = own + swap(given, "core")
    own = own.astype(jnp.bfloat16)
    tokens_grad = sum_parts(parts).T
    far, tokens_grad = lax.optimization_barrier((swap(own, "y_hi"), tokens_grad))
    mine = own.astype(jnp.float32) + far.astype(jnp.float32)
    theirs = swap(mine, "core")
    return (tokens_grad, *split(mine, theirs))


def solution(mesh):
    axes = jax.sharding.Mesh(mesh.devices.reshape(2, 2, N_X, N_Y, N_Z), ("y_hi", "core", "x", "y_lo", "z"))
    dp, tensor = ("y_hi", "core"), ("x", "y_lo", "z")
    columns, rows = P(None, tensor), P(tensor, None)
    return jax.shard_map(
        shards,
        mesh=axes,
        in_specs=(P(dp, tensor),) * 2 + (columns,) * 6 + (rows,) * 3,
        out_specs=(P(dp, tensor),) + (columns,) * 4 + (rows,) * 2,
        check_vma=False,
    )
```

```python
import jax
import jax.numpy as jnp
from jax import lax
from jax.experimental import pallas as pl
from jax.experimental.pallas import tpu as pltpu
from jax.sharding import PartitionSpec as P

N_X, N_Y, N_Z = 4, 2, 4
SHARDS = 32
OWN = 192
THIRD = 64
BLOCKS = 16
WORDS = 128
FEATURES = 384
HIDDEN = 512
LOCAL = 128
MIB = 1 << 20

CONTRACT_LAST = (((1,), (1,)), ((), ()))
CONTRACT_FIRST = (((0,), (0,)), ((), ()))


def shard_row(k, word):
    return (word // THIRD) * OWN + k * THIRD + word % THIRD


def first_word(k, group):
    return -((k - 128 * group) // 3)


def spread_over_groups(k, start, rows, values):
    first, last = (3 * start + k) // 128, (3 * (start + rows - 1) + k) // 128
    if first == last:
        return values[first]
    row = start + lax.broadcasted_iota(jnp.int32, (rows, 1), 0)
    return jnp.where(row < first_word(k, last), values[first], values[last])


def call(body, out_shape, in_specs, out_specs, scratch=(), flops=0, traffic=0, vmem=16, aliases=None):
    return pl.pallas_call(
        body,
        out_shape=out_shape,
        in_specs=in_specs,
        out_specs=out_specs,
        scratch_shapes=list(scratch),
        input_output_aliases=aliases or {},
        compiler_params=pltpu.CompilerParams(vmem_limit_bytes=vmem * MIB),
        cost_estimate=pl.CostEstimate(flops=flops, bytes_accessed=traffic, transcendentals=0),
    )


def struct(shape, dtype):
    return jax.ShapeDtypeStruct(shape, dtype)


def from_hbm(*arrays):
    return [pltpu.with_memory_space_constraint(array, pltpu.HBM) for array in arrays]


def from_vmem(*arrays):
    return [pltpu.with_memory_space_constraint(array, pltpu.VMEM) for array in arrays]


VMEM = pl.BlockSpec(memory_space=pltpu.VMEM)
ANY = pl.BlockSpec(memory_space=pl.ANY)


def by_field_body(tokens_ref, grad_ref, tokens_out, grad_out, wide):
    for ref, out_ref in ((tokens_ref, tokens_out), (grad_ref, grad_out)):
        wide[...] = ref[...].astype(jnp.float32)
        for k in range(3):
            out_ref[0, k * THIRD : (k + 1) * THIRD, :] = wide[pl.ds(k, THIRD, stride=3), :].astype(jnp.bfloat16)


def by_field(tokens, out_grad):
    return call(
        by_field_body,
        (struct((1, OWN, LOCAL), jnp.bfloat16),) * 2,
        [VMEM, VMEM],
        (VMEM, VMEM),
        [pltpu.VMEM((OWN, LOCAL), jnp.float32)],
        traffic=200000,
    )(*from_hbm(tokens.T, out_grad.T))


def field(words, k):
    if k:
        words = jnp.right_shift(words, 4 * k)
    if k < 2:
        words = jnp.bitwise_and(words, 15)
    return words.astype(jnp.float32)


CHUNKS = 8
AHEAD = 3


def row_copy(chunk, source, to, sems):
    rows = pl.ds(pl.multiple_of(chunk * 2 * WORDS, 2 * WORDS), 2 * WORDS)
    return pltpu.make_async_copy(source.at[rows], to.at[rows], sems.at[chunk])


def column_copy(chunk, source, to, sems):
    columns = pl.ds(pl.multiple_of(chunk * 2 * WORDS, 2 * WORDS), 2 * WORDS)
    return pltpu.make_async_copy(source.at[:, columns], to.at[:, columns], sems.at[chunk])


def tables_in(sources, targets, sems):
    copies = [pltpu.make_async_copy(a, b, sems.at[i]) for i, (a, b) in enumerate(zip(sources, targets))]
    for copy in copies:
        copy.start()
    return copies


def unpack_rows_pair(pair, codes, zeros_ref, log_ref, out_ref):
    for part in range(2):
        block = pair * 2 + part
        zeros = [zeros_ref[pl.ds(3 * block + g, 1), :].astype(jnp.float32) for g in range(3)]
        scales = [jnp.exp(log_ref[pl.ds(3 * block + g, 1), :]) for g in range(3)]
        for start in range(0, WORDS, 16):
            words = codes[pl.ds(pl.multiple_of(block * WORDS + start, 16), 16), :]
            for k in range(3):
                zero = spread_over_groups(k, start, 16, zeros)
                scale = spread_over_groups(k, start, 16, scales)
                weight = (scale * (field(words, k) - zero)).astype(jnp.bfloat16)
                row = k * THIRD + start % THIRD
                out_ref[part * 2 + start // THIRD, pair, row : row + 16, :] = weight


def streamed(copy_of, source, to, sems, work):
    def step(chunk, carry):
        copy_of(chunk, source, to, sems).wait()

        @pl.when(chunk + AHEAD < CHUNKS)
        def _():
            copy_of(chunk + AHEAD, source, to, sems).start()

        work(chunk)
        return carry

    lax.fori_loop(0, CHUNKS, step, 0)


def start_first(copy_of, source, to, sems):
    for chunk in range(AHEAD):
        copy_of(chunk, source, to, sems).start()


def unpack_rows_body(codes_hbm, zeros_hbm, log_hbm, out_ref, zeros_ref, log_ref, table_sems, codes, sems):
    tables = tables_in((zeros_hbm, log_hbm), (zeros_ref, log_ref), table_sems)
    start_first(row_copy, codes_hbm, codes, sems)
    for table in tables:
        table.wait()
    streamed(
        row_copy, codes_hbm, codes, sems, lambda pair: unpack_rows_pair(pair, codes, zeros_ref, log_ref, out_ref)
    )


def unpack_rows(codes, zeros, log_scale):
    return call(
        unpack_rows_body,
        pltpu.VMEM((N_Z, N_X * N_Y, OWN, HIDDEN), jnp.bfloat16),
        [ANY] * 3,
        VMEM,
        [
            pltpu.VMEM((48, HIDDEN), jnp.int32),
            pltpu.VMEM((48, HIDDEN), jnp.float32),
            pltpu.SemaphoreType.DMA((2,)),
            pltpu.VMEM((BLOCKS * WORDS, HIDDEN), jnp.int32),
            pltpu.SemaphoreType.DMA((CHUNKS,)),
        ],
        flops=20000000,
        traffic=10500000,
    )(*from_hbm(codes, zeros, log_scale))


def field_order(transposed):
    feature = lax.broadcasted_iota(jnp.int32, (FEATURES, FEATURES), 1 if transposed else 0)
    column = lax.broadcasted_iota(jnp.int32, (FEATURES, FEATURES), 0 if transposed else 1)
    wanted = 3 * jnp.bitwise_and(column, 127) + jnp.right_shift(column, 7)
    return (feature == wanted).astype(jnp.float32)


def reorder(rows, transposed):
    return jnp.dot(
        rows, field_order(transposed), precision=lax.Precision.HIGHEST, preferred_element_type=jnp.float32
    )


def unpack_columns_pair(pair, codes, table_ref, out_ref):
    for part in range(2):
        block = pair * 2 + part
        table = table_ref[pl.ds(pl.multiple_of(8 * block, 8), 8), :]
        for g in range(4):
            words = codes[g * 128 : (g + 1) * 128, pl.ds(pl.multiple_of(block * WORDS, WORDS), WORDS)]
            for k in range(3):
                columns = slice(k * WORDS, (k + 1) * WORDS)
                zero, scale = table[g : g + 1, columns], table[4 + g : 5 + g, columns]
                weight = (scale * (field(words, k) - zero)).astype(jnp.bfloat16)
                to = slice(part * FEATURES + k * WORDS, part * FEATURES + (k + 1) * WORDS)
                out_ref[pair, g * 128 : (g + 1) * 128, to] = weight


def column_tables_body(zeros_hbm, log_hbm, table_ref, zeros_ref, log_ref, table_sems, natural):
    for table in tables_in((zeros_hbm, log_hbm), (zeros_ref, log_ref), table_sems):
        table.wait()
    for b in range(BLOCKS):
        columns = slice(b * FEATURES, (b + 1) * FEATURES)
        natural[8 * b : 8 * b + 4, :] = zeros_ref[:, columns].astype(jnp.float32)
        natural[8 * b + 4 : 8 * b + 8, :] = jnp.exp(log_ref[:, columns])
    table_ref[...] = reorder(natural[...], False)


def column_tables(zeros, log_scale):
    wide = (4, BLOCKS * FEATURES)
    return call(
        column_tables_body,
        pltpu.HBM((8 * BLOCKS, FEATURES), jnp.float32),
        [ANY] * 2,
        VMEM,
        [
            pltpu.VMEM(wide, jnp.int32),
            pltpu.VMEM(wide, jnp.float32),
            pltpu.SemaphoreType.DMA((2,)),
            pltpu.VMEM((8 * BLOCKS, FEATURES), jnp.float32),
        ],
        traffic=400000,
    )(*from_hbm(zeros, log_scale))


def unpack_columns_body(codes_hbm, table_hbm, out_ref, table_ref, table_sems, codes, sems):
    tables = tables_in((table_hbm,), (table_ref,), table_sems)
    start_first(column_copy, codes_hbm, codes, sems)
    for table in tables:
        table.wait()
    streamed(column_copy, codes_hbm, codes, sems, lambda pair: unpack_columns_pair(pair, codes, table_ref, out_ref))


def unpack_columns(codes, table):
    return call(
        unpack_columns_body,
        pltpu.VMEM((N_X * N_Y, HIDDEN, 2 * FEATURES), jnp.bfloat16),
        [ANY] * 2,
        VMEM,
        [
            pltpu.VMEM((8 * BLOCKS, FEATURES), jnp.float32),
            pltpu.SemaphoreType.DMA((1,)),
            pltpu.VMEM((HIDDEN, BLOCKS * WORDS), jnp.int32),
            pltpu.SemaphoreType.DMA((CHUNKS,)),
        ],
        flops=20000000,
        traffic=10500000,
    )(*from_hbm(codes, table))


SLAB = 8 * OWN


def position():
    return tuple(lax.axis_index(axis) for axis in ("x", "y_lo", "z"))


def swapped_with(here, near):
    place = 3 - here if near // 2 else here
    return place + 1 - 2 * (place % 2) if near % 2 else place


def lay_tokens(place, source, far, to):
    x, y, z = place
    slab = (z + 4 - far) % 4
    for near in range(4):
        for dy in range(2):
            to[slab, swapped_with(x, near) * 2 + (y + dy) % 2, :, :] = source[near * 2 + dy]
    return slab


def lay_grad(place, source, far, to):
    x, y, z = place
    slab = (x + 4 - far) % 4
    for near in range(4):
        z_from = swapped_with(z, near)
        for dy in range(2):
            for k in range(3):
                row = pl.multiple_of((z_from // 2) * FEATURES + k * WORDS + (z_from % 2) * THIRD, THIRD)
                to[slab * 2 + (y + dy) % 2, pl.ds(row, THIRD), :] = source[
                    near * 2 + dy, k * THIRD : (k + 1) * THIRD, :
                ]
    return slab


def slab_out(slab, tokens_from, tokens_hbm, sems):
    return pltpu.make_async_copy(tokens_from.at[slab], tokens_hbm.at[slab], sems)


def pair_out(slab, grad_from, grad_hbm, sems):
    pairs = pl.ds(slab * 2, 2)
    return pltpu.make_async_copy(grad_from.at[pairs], grad_hbm.at[pairs], sems)


def slab_products(fars, tokens_refs, grad_refs, weights, scratch, hbm, totals):
    gate_ref, up_ref, down_ref = weights
    tokens_to, grad_to, tokens_sems, grad_sems = scratch
    tokens_hbm, grad_hbm = hbm
    place = position()
    gate_pre, up_pre, hidden_grad = totals
    copies, laid = [], []
    for i, far in enumerate(fars):
        slabs = lay_tokens(place, tokens_refs[i], far, tokens_to), lay_grad(place, grad_refs[i], far, grad_to)
        copies.append(slab_out(slabs[0], tokens_to, tokens_hbm, tokens_sems.at[i]))
        copies.append(pair_out(slabs[1], grad_to, grad_hbm, grad_sems.at[i]))
        laid.append(slabs)
    for copy in copies:
        copy.start()
    for slab, grad_slab in laid:
        features = tokens_to[slab].reshape(SLAB, LOCAL).T
        gate_pre += jnp.dot(features, gate_ref[slab].reshape(SLAB, HIDDEN), preferred_element_type=jnp.float32)
        up_pre += jnp.dot(features, up_ref[slab].reshape(SLAB, HIDDEN), preferred_element_type=jnp.float32)
        for dy in range(2):
            piece = grad_to[grad_slab * 2 + dy]
            hidden_grad += jnp.dot(down_ref[grad_slab * 2 + dy], piece, preferred_element_type=jnp.float32)
    return (gate_pre, up_pre, hidden_grad), copies


def forward_body(
    t0, t1, t3, o0, o1, o3, gate_ref, up_ref, down_ref,
    gate_pre_ref, up_pre_ref, hidden_grad_ref, tokens_hbm, grad_hbm,
    tokens_to, grad_to, tokens_sems, grad_sems,
):
    zero = jnp.zeros((LOCAL, HIDDEN), jnp.float32)
    core = lax.axis_index("core")
    (gate_pre_ref[...], up_pre_ref[...], hidden_grad_ref[...]), copies = slab_products(
        (0, 1 + 2 * core, 3 - 2 * core), (t0, t1, t3), (o0, o1, o3), (gate_ref, up_ref, down_ref),
        (tokens_to, grad_to, tokens_sems, grad_sems), (tokens_hbm, grad_hbm),
        (zero, zero, jnp.zeros((HIDDEN, LOCAL), jnp.float32)),
    )
    for copy in copies:
        copy.wait()


TOKENS_SHAPE = (N_Z, N_X * N_Y, OWN, LOCAL)
GRAD_SHAPE = (N_X * N_Y, 2 * FEATURES, LOCAL)


def slab_scratch(slabs):
    return [
        pltpu.VMEM(TOKENS_SHAPE, jnp.bfloat16),
        pltpu.VMEM(GRAD_SHAPE, jnp.bfloat16),
        pltpu.SemaphoreType.DMA((slabs,)),
        pltpu.SemaphoreType.DMA((slabs,)),
    ]


def forward(tokens_parts, grad_parts, gate, up, down):
    f32, bf16 = jnp.float32, jnp.bfloat16
    near = (0, 1, 3)
    return call(
        forward_body,
        (
            pltpu.VMEM((LOCAL, HIDDEN), f32),
            pltpu.VMEM((LOCAL, HIDDEN), f32),
            pltpu.VMEM((HIDDEN, LOCAL), f32),
            pltpu.HBM(TOKENS_SHAPE, bf16),
            pltpu.HBM(GRAD_SHAPE, bf16),
        ),
        [VMEM] * 9,
        (VMEM,) * 3 + (ANY,) * 2,
        slab_scratch(3),
        flops=3 * 3 * 2 * 128 * 1536 * 512,
        traffic=18000000,
    )(
        *from_vmem(*[tokens_parts[far] for far in near], *[grad_parts[far] for far in near]),
        *from_vmem(gate, up, down),
    )


def backward_body(
    t2, o2, gate_ref, up_ref, down_ref, gate_pre_ref, up_pre_ref, hidden_grad_ref, tokens_in, grad_in,
    partial_hbm, tokens_hbm, grad_hbm, gate_grad_hbm, up_grad_hbm, hidden_hbm,
    tokens_to, grad_to, tokens_sems, grad_sems, partial, partial_sems, gate_grad_ref, up_grad_ref, hidden_ref, small_sems,
):
    (gate_pre, up_pre, hidden_grad), copies = slab_products(
        (2,), (t2,), (o2,), (gate_ref, up_ref, down_ref),
        (tokens_to, grad_to, tokens_sems, grad_sems), (tokens_hbm, grad_hbm),
        (gate_pre_ref[...], up_pre_ref[...], hidden_grad_ref[...]),
    )
    hidden_grad = hidden_grad.T
    sigmoid_gate = jax.nn.sigmoid(gate_pre)
    silu_gate = gate_pre * sigmoid_gate
    hidden = silu_gate * up_pre
    gate_grad = hidden_grad * up_pre * sigmoid_gate * (1.0 + gate_pre * (1.0 - sigmoid_gate))
    up_grad = hidden_grad * silu_gate
    gate_grad_ref[...] = gate_grad.astype(jnp.bfloat16)
    up_grad_ref[...] = up_grad.astype(jnp.bfloat16)
    hidden_ref[...] = hidden.T.astype(jnp.bfloat16)
    copies += tables_in(
        (gate_grad_ref, up_grad_ref, hidden_ref), (gate_grad_hbm, up_grad_hbm, hidden_hbm), small_sems
    )
    gate_turned = gate_grad.T.astype(jnp.bfloat16)
    up_turned = up_grad.T.astype(jnp.bfloat16)
    for slab in range(N_Z):
        total = jnp.dot(gate_ref[slab].reshape(SLAB, HIDDEN), gate_turned, preferred_element_type=jnp.float32)
        total += jnp.dot(up_ref[slab].reshape(SLAB, HIDDEN), up_turned, preferred_element_type=jnp.float32)
        partial[slab] = total.astype(jnp.bfloat16).reshape(N_X * N_Y, OWN, LOCAL)
        copy = pltpu.make_async_copy(partial.at[slab], partial_hbm.at[:, slab], partial_sems.at[slab])
        copy.start()
        copies.append(copy)
    for copy in copies:
        copy.wait()


def backward(tokens_parts, grad_parts, gate, up, down, sums, all_tokens, all_grad):
    bf16 = jnp.bfloat16
    return call(
        backward_body,
        (
            pltpu.HBM((N_X * N_Y, N_Z, OWN, LOCAL), bf16),
            pltpu.HBM(TOKENS_SHAPE, bf16),
            pltpu.HBM(GRAD_SHAPE, bf16),
            pltpu.HBM((LOCAL, HIDDEN), bf16),
            pltpu.HBM((LOCAL, HIDDEN), bf16),
            pltpu.HBM((HIDDEN, LOCAL), bf16),
        ),
        [VMEM] * 8 + [ANY] * 2,
        (ANY,) * 6,
        slab_scratch(1)
        + [
            pltpu.VMEM(TOKENS_SHAPE, bf16),
            pltpu.SemaphoreType.DMA((N_Z,)),
            pltpu.VMEM((LOCAL, HIDDEN), bf16),
            pltpu.VMEM((LOCAL, HIDDEN), bf16),
            pltpu.VMEM((HIDDEN, LOCAL), bf16),
            pltpu.SemaphoreType.DMA((3,)),
        ],
        flops=3 * 2 * 128 * 6144 * 512,
        traffic=24000000,
        aliases={8: 1, 9: 2},
    )(
        *from_vmem(tokens_parts[2], grad_parts[2], gate, up, down, *sums),
        *from_hbm(all_tokens, all_grad),
    )


EXTRA = 16


def with_sums(rows, members):
    sums = jnp.dot(members, rows, preferred_element_type=jnp.float32)
    head = sums.astype(jnp.bfloat16)
    rest = (sums - head.astype(jnp.float32)).astype(jnp.bfloat16)
    return jnp.concatenate([rows, jnp.concatenate([head, rest], axis=0)], axis=0)


def block_members():
    group = lax.broadcasted_iota(jnp.int32, (8, FEATURES), 0)
    place = lax.broadcasted_iota(jnp.int32, (8, FEATURES), 1)
    half = (place >= OWN).astype(jnp.int32)
    place = place - OWN * half
    k = jnp.right_shift(place, 6)
    feature = 3 * (half * THIRD + place - THIRD * k) + k
    scale = jnp.where(k == 0, 1.0, jnp.where(k == 1, 16.0, 256.0))
    return jnp.where(jnp.right_shift(feature, 7) == group, scale, 0.0).astype(jnp.bfloat16)


def hidden_members():
    group = lax.broadcasted_iota(jnp.int32, (8, HIDDEN), 0)
    unit = lax.broadcasted_iota(jnp.int32, (8, HIDDEN), 1)
    return (jnp.right_shift(unit, 7) == group).astype(jnp.float32).astype(jnp.bfloat16)


MASKS = (15, 240, 3840)
SHRINK = (1.0, 1.0 / 16.0, 1.0 / 256.0)


def in_place(words, k):
    return jnp.bitwise_and(words, MASKS[k]).astype(jnp.float32)


def in_turn(*streams):
    running = list(streams)
    while running:
        for stream in list(running):
            if next(stream, None) is None:
                running.remove(stream)


def row_groups(block, codes, weight_grad, sums, totals):
    weighted = [jnp.zeros((8, HIDDEN), jnp.float32)] * 3
    for start in range(0, WORDS, 8):
        words = codes[pl.ds(pl.multiple_of(block * WORDS + start, 8), 8), :]
        for k in range(3):
            product = in_place(words, k) * weight_grad[shard_row(k, start) : shard_row(k, start) + 8, :]
            first, last = (3 * start + k) // 128, (3 * (start + 7) + k) // 128
            if first == last:
                weighted[first] = weighted[first] + product
            else:
                low = start + lax.broadcasted_iota(jnp.int32, (8, 1), 0) < first_word(k, last)
                low_product = jnp.where(low, product, 0.0)
                weighted[first] = weighted[first] + low_product
                weighted[last] = weighted[last] + (product - low_product)
        yield True
    for g in range(3):
        row = pl.ds(3 * block + g, 1)
        sums[row, :] = jnp.sum(weighted[g], axis=0, keepdims=True)
        totals[row, :] = (
            weight_grad[FEATURES + g : FEATURES + g + 1, :] + weight_grad[FEATURES + 8 + g : FEATURES + 9 + g, :]
        )
    yield True


def column_groups(block, part, codes, weight_grad, raw):
    here = pl.ds(pl.multiple_of(8 * block, 8), 8)
    mine = slice(part * FEATURES, (part + 1) * FEATURES)
    totals = weight_grad[HIDDEN : HIDDEN + 4, mine] + weight_grad[HIDDEN + 8 : HIDDEN + 12, mine]
    for k in range(3):
        sums = []
        for g in range(4):
            weighted = jnp.zeros((8, WORDS), jnp.float32)
            for start in range(g * 128, g * 128 + 128, 8):
                words = codes[start : start + 8, pl.ds(pl.multiple_of(block * WORDS, WORDS), WORDS)]
                value = weight_grad[start : start + 8, part * FEATURES + k * WORDS : part * FEATURES + (k + 1) * WORDS]
                weighted = weighted + in_place(words, k) * value
            sums.append(jnp.sum(weighted, axis=0, keepdims=True))
            yield True
        columns = slice(k * WORDS, (k + 1) * WORDS)
        raw[here, columns] = jnp.concatenate([jnp.concatenate(sums, axis=0) * SHRINK[k], totals[:, columns]], axis=0)


def group_body(
    gate_hbm, up_hbm, down_hbm, tokens_hbm, grad_hbm, *small_hbm_and_rest
):
    small_hbm, rest = small_hbm_and_rest[:8], small_hbm_and_rest[8:]
    small, rest = rest[-8:], rest[:-8]
    group_work(gate_hbm, up_hbm, down_hbm, tokens_hbm, grad_hbm, small_hbm, small, *rest)


def group_work(
    gate_hbm, up_hbm, down_hbm, tokens_hbm, grad_hbm, small_hbm, small,
    own_ref, given_ref,
    gate_codes, up_codes, down_codes, gate_sems, up_sems, down_sems, tokens_ref, grad_ref, tokens_sems, grad_sems, small_sems,
    hidden_rows, gate_even, up_even, gate_odd, up_odd, down_pair, down_rows, halves, sums, totals,
):
    def copies(chunk):
        return (
            row_copy(chunk, gate_hbm, gate_codes, gate_sems),
            row_copy(chunk, up_hbm, up_codes, up_sems),
            column_copy(chunk, down_hbm, down_codes, down_sems),
        )

    def start(chunk):
        for copy in copies(chunk):
            copy.start()

    def rows_in(pair):
        return (
            pltpu.make_async_copy(tokens_hbm.at[:, pair], tokens_ref.at[:, pair], tokens_sems.at[pair]),
            pltpu.make_async_copy(grad_hbm.at[pair], grad_ref.at[pair], grad_sems.at[pair]),
        )

    gate_grad_ref, up_grad_ref, hidden_ref, gate_zeros, gate_log, up_zeros, up_log, table_ref = small
    for copy in rows_in(0):
        copy.start()
    arrivals = tables_in(small_hbm[:3], small[:3], small_sems)
    start(0)
    members = block_members()
    field_of_row = jnp.right_shift(lax.broadcasted_iota(jnp.int32, (OWN, 1), 0), 6)
    shrink = jnp.where(field_of_row == 0, SHRINK[0], jnp.where(field_of_row == 1, SHRINK[1], SHRINK[2]))
    shrink = jnp.broadcast_to(shrink, (OWN, LOCAL)).astype(jnp.bfloat16)
    for arrival in arrivals:
        arrival.wait()
    hidden_rows[...] = with_sums(hidden_ref[...], hidden_members())

    def row_products(pair, part, gate_to, up_to):
        features = jnp.concatenate([tokens_ref[part * 2 + half, pair] * shrink for half in range(2)], axis=0)
        features = with_sums(features, members)
        for grad, to in ((gate_grad_ref, gate_to), (up_grad_ref, up_to)):
            for row in range(0, FEATURES + EXTRA, 80):
                to[row : row + 80, :] = jnp.dot(
                    features[row : row + 80, :], grad[...], preferred_element_type=jnp.float32
                )
                yield True

    def column_products(pair, down_to):
        for row in range(0, HIDDEN + EXTRA, 176):
            down_to[row : row + 176, :] = lax.dot_general(
                hidden_rows[row : row + 176, :], grad_ref[pair], CONTRACT_LAST, preferred_element_type=jnp.float32
            )
            yield True

    def groups(block, gate_from, up_from):
        yield from row_groups(block, gate_codes, gate_from, sums.at[0], totals.at[0])
        yield from row_groups(block, up_codes, up_from, sums.at[1], totals.at[1])

    def down_groups(pair):
        for part in range(2):
            yield from column_groups(pair * 2 + part, part, down_codes, down_pair, down_rows)

    for copy in rows_in(0):
        copy.wait()
    for copy in rows_in(1):
        copy.start()
    start(1)
    tables = tables_in(small_hbm[3:], small[3:], small_sems.at[pl.ds(3, 5)])
    in_turn(row_products(0, 0, gate_even, up_even))

    def pair_step(pair, carry):
        for copy in copies(pair):
            copy.wait()
        following = jnp.minimum(pair + 1, BLOCKS // 2 - 1)

        @pl.when(pair < BLOCKS // 2 - 1)
        def _():
            for copy in rows_in(following):
                copy.wait()

        @pl.when(pair + 2 < CHUNKS)
        def _():
            start(pair + 2)
            for copy in rows_in(pair + 2):
                copy.start()

        in_turn(row_products(pair, 1, gate_odd, up_odd), groups(pair * 2, gate_even, up_even))
        in_turn(column_products(pair, down_pair), groups(pair * 2 + 1, gate_odd, up_odd))
        in_turn(row_products(following, 0, gate_even, up_even), down_groups(pair))
        return carry

    lax.fori_loop(0, BLOCKS // 2, pair_step, 0)

    for table in tables:
        table.wait()
    for half, (zeros_ref, log_ref) in enumerate(((gate_zeros, gate_log), (up_zeros, up_log))):
        scale = jnp.exp(log_ref[...])
        halves[half, 0:48] = scale * (sums[half] - zeros_ref[...].astype(jnp.float32) * totals[half])
        halves[half, 48:96] = -scale * totals[half]
    found, table = down_rows[...].reshape(BLOCKS, 8, FEATURES), table_ref[...].reshape(BLOCKS, 8, FEATURES)
    found, total, zero, scale = found[:, 0:4], found[:, 4:8], table[:, 0:4], table[:, 4:8]
    finished = jnp.concatenate([scale * (found - zero * total), -scale * total], axis=1)
    down_rows[...] = finished.reshape(8 * BLOCKS, FEATURES)
    for half, begin in ((0, 0), (1, 48)):
        for j in range(3):
            halves[half, 96:144, j * 128 : (j + 1) * 128] = down_rows[begin : begin + 48, j * 128 : (j + 1) * 128]
    halves[0, 96:128, 384:] = down_rows[96:128, 0:128]
    halves[0, 128:144, 384:] = down_rows[96:112, 128:256]
    halves[1, 96:112, 384:] = down_rows[112:128, 128:256]
    halves[1, 112:144, 384:] = down_rows[96:128, 256:384]
    core = lax.axis_index("core")
    own_ref[...] = halves[core]
    given_ref[...] = halves[1 - core]


def group_grads(tokens, grad, gate_grad, up_grad, hidden, gate_tables, up_tables, down_codes, table):
    half = struct((144, HIDDEN), jnp.float32)
    gate_codes, *gate_tables = gate_tables
    up_codes, *up_tables = up_tables
    small = (gate_grad, up_grad, hidden, *gate_tables, *up_tables, table)
    rows, columns = (FEATURES + EXTRA, HIDDEN), (HIDDEN + EXTRA, 2 * FEATURES)
    return call(
        group_body,
        (half, half),
        [ANY] * 13,
        (VMEM, VMEM),
        [
            pltpu.VMEM((BLOCKS * WORDS, HIDDEN), jnp.int32),
            pltpu.VMEM((BLOCKS * WORDS, HIDDEN), jnp.int32),
            pltpu.VMEM((HIDDEN, BLOCKS * WORDS), jnp.int32),
        ]
        + [pltpu.SemaphoreType.DMA((CHUNKS,))] * 3
        + [
            pltpu.VMEM(TOKENS_SHAPE, jnp.bfloat16),
            pltpu.VMEM(GRAD_SHAPE, jnp.bfloat16),
            pltpu.SemaphoreType.DMA((BLOCKS // 2,)),
            pltpu.SemaphoreType.DMA((BLOCKS // 2,)),
            pltpu.SemaphoreType.DMA((8,)),
            pltpu.VMEM((HIDDEN + EXTRA, LOCAL), jnp.bfloat16),
        ]
        + [pltpu.VMEM(shape, jnp.float32) for shape in (rows,) * 4 + (columns,)]
        + [pltpu.VMEM((8 * BLOCKS, FEATURES), jnp.float32), pltpu.VMEM((2, 144, HIDDEN), jnp.float32)]
        + [pltpu.VMEM((2, 48, HIDDEN), jnp.float32)] * 2
        + [pltpu.VMEM(array.shape, array.dtype) for array in small],
        flops=3 * 2 * 128 * 6144 * 512,
        traffic=17000000,
        vmem=40,
    )(
        *from_hbm(gate_codes, up_codes, down_codes, tokens, grad, *small),
    )


def split_body(mine_ref, other_ref, gs_ref, gz_ref, us_ref, uz_ref, ds_ref, dz_ref, halves, rows):
    core = lax.axis_index("core")
    halves[core] = mine_ref[...]
    halves[1 - core] = other_ref[...]
    for half, scale_ref, zero_ref in ((0, gs_ref, gz_ref), (1, us_ref, uz_ref)):
        scale_ref[...] = halves[half, 0:48, :]
        zero_ref[...] = halves[half, 48:96, :]
        for j in range(3):
            rows[48 * half : 48 * half + 48, j * 128 : (j + 1) * 128] = halves[half, 96:144, j * 128 : (j + 1) * 128]
    rows[96:128, 0:128] = halves[0, 96:128, 384:]
    rows[96:112, 128:256] = halves[0, 128:144, 384:]
    rows[112:128, 128:256] = halves[1, 96:112, 384:]
    rows[96:128, 256:384] = halves[1, 112:144, 384:]
    natural = reorder(rows[...], True)
    for b in range(BLOCKS):
        columns = slice(b * FEATURES, (b + 1) * FEATURES)
        ds_ref[:, columns] = natural[8 * b : 8 * b + 4, :]
        dz_ref[:, columns] = natural[8 * b + 4 : 8 * b + 8, :]


def split(mine, other):
    f32 = jnp.float32
    return call(
        split_body,
        (struct((48, HIDDEN), f32),) * 4 + (struct((4, BLOCKS * FEATURES), f32),) * 2,
        [VMEM, VMEM],
        (VMEM,) * 6,
        [pltpu.VMEM((2, 144, HIDDEN), f32), pltpu.VMEM((8 * BLOCKS, FEATURES), f32)],
        traffic=1200000,
    )(mine, other)


def sum_body(parts_ref, out_ref):
    total = parts_ref[0].astype(jnp.float32)
    for part in range(1, SHARDS):
        total = total + parts_ref[part].astype(jnp.float32)
    for k in range(3):
        out_ref[pl.ds(k, THIRD, stride=3), :] = total[k * THIRD : (k + 1) * THIRD, :]


def sum_parts(parts):
    return call(sum_body, struct((OWN, LOCAL), jnp.float32), [VMEM], VMEM, traffic=1700000)(parts)


NEAR, ACROSS = ((0, 1), (2, 3)), ((0, 3), (1, 2))


def paired(block, axis, pairs):
    other = lax.ppermute(block, axis, [pair for a, b in pairs for pair in ((a, b), (b, a))])
    return jnp.concatenate([block, other])


def turned(block, axis, way):
    pairs = [(place, (place + way) % 4) for place in range(4)]
    pairs += [(4 + place, 4 + (place - way) % 4) for place in range(4)]
    return lax.ppermute(block, ("core", axis), pairs)


def swap(value, axis):
    return lax.ppermute(value, axis, [(0, 1), (1, 0)])


def shards(
    tokens,
    out_grad,
    gate_codes,
    gate_zeros,
    gate_log_scale,
    up_codes,
    up_zeros,
    up_log_scale,
    down_codes,
    down_zeros,
    down_log_scale,
):
    tokens_near, grad_near = by_field(tokens, out_grad)
    tokens_near, grad_near = paired(tokens_near, "y_lo", ((0, 1),)), paired(grad_near, "y_lo", ((0, 1),))
    table = column_tables(down_zeros, down_log_scale)
    tokens_near, grad_near, table = lax.optimization_barrier((tokens_near, grad_near, table))
    tokens_near, grad_near = paired(tokens_near, "x", NEAR), paired(grad_near, "z", NEAR)
    tokens_near, gate_zeros = lax.optimization_barrier((tokens_near, gate_zeros))
    tokens_near, grad_near = paired(tokens_near, "x", ACROSS), paired(grad_near, "z", ACROSS)
    gate = unpack_rows(gate_codes, gate_zeros, gate_log_scale)
    tokens_near, gate, up_zeros = lax.optimization_barrier((tokens_near, gate, up_zeros))
    grad_near, up_log_scale = lax.optimization_barrier((grad_near, up_log_scale))
    tokens_first, grad_first = turned(tokens_near, "z", 1), turned(grad_near, "x", 1)
    tokens_second, grad_second = turned(tokens_near, "z", -1), turned(grad_near, "x", -1)
    up = unpack_rows(up_codes, up_zeros, up_log_scale)
    tokens_first, grad_first, up, table = lax.optimization_barrier((tokens_first, grad_first, up, table))
    tokens_parts = tokens_near, tokens_first, turned(tokens_first, "z", 1), tokens_second
    grad_parts = grad_near, grad_first, turned(grad_first, "x", 1), grad_second
    down = unpack_columns(down_codes, table)
    *sums, all_tokens, all_grad = forward(tokens_parts, grad_parts, gate, up, down)
    partial, all_tokens, all_grad, gate_grad, up_grad, hidden = backward(
        tokens_parts, grad_parts, gate, up, down, sums, all_tokens, all_grad
    )
    parts = lax.all_to_all(partial.reshape(SHARDS, OWN, LOCAL), ("x", "y_lo", "z"), 0, 0, tiled=True)
    own, given = group_grads(
        all_tokens,
        all_grad,
        gate_grad,
        up_grad,
        hidden,
        (gate_codes, gate_zeros, gate_log_scale),
        (up_codes, up_zeros, up_log_scale),
        down_codes,
        table,
    )
    own = own + swap(given, "core")
    own = own.astype(jnp.bfloat16)
    tokens_grad = sum_parts(parts).T
    far, tokens_grad = lax.optimization_barrier((swap(own, "y_hi"), tokens_grad))
    mine = own.astype(jnp.float32) + far.astype(jnp.float32)
    theirs = swap(mine, "core")
    return (tokens_grad, *split(mine, theirs))


def solution(mesh):
    axes = jax.sharding.Mesh(mesh.devices.reshape(2, 2, N_X, N_Y, N_Z), ("y_hi", "core", "x", "y_lo", "z"))
    dp, tensor = ("y_hi", "core"), ("x", "y_lo", "z")
    columns, rows = P(None, tensor), P(tensor, None)
    return jax.shard_map(
        shards,
        mesh=axes,
        in_specs=(P(dp, tensor),) * 2 + (columns,) * 6 + (rows,) * 3,
        out_specs=(P(dp, tensor),) + (columns,) * 4 + (rows,) * 2,
        check_vma=False,
    )
```

```python
import jax
import jax.numpy as jnp
from jax import lax
from jax.experimental import pallas as pl
from jax.experimental.pallas import tpu as pltpu
from jax.sharding import PartitionSpec as P

N_X, N_Y, N_Z = 4, 2, 4
SHARDS = 32
OWN = 192
THIRD = 64
BLOCKS = 16
WORDS = 128
FEATURES = 384
HIDDEN = 512
LOCAL = 128
MIB = 1 << 20

CONTRACT_LAST = (((1,), (1,)), ((), ()))
CONTRACT_FIRST = (((0,), (0,)), ((), ()))


def shard_row(k, word):
    return (word // THIRD) * OWN + k * THIRD + word % THIRD


def first_word(k, group):
    return -((k - 128 * group) // 3)


def spread_over_groups(k, start, rows, values):
    first, last = (3 * start + k) // 128, (3 * (start + rows - 1) + k) // 128
    if first == last:
        return values[first]
    row = start + lax.broadcasted_iota(jnp.int32, (rows, 1), 0)
    return jnp.where(row < first_word(k, last), values[first], values[last])


def call(body, out_shape, in_specs, out_specs, scratch=(), flops=0, traffic=0, vmem=16, aliases=None):
    return pl.pallas_call(
        body,
        out_shape=out_shape,
        in_specs=in_specs,
        out_specs=out_specs,
        scratch_shapes=list(scratch),
        input_output_aliases=aliases or {},
        compiler_params=pltpu.CompilerParams(vmem_limit_bytes=vmem * MIB),
        cost_estimate=pl.CostEstimate(flops=flops, bytes_accessed=traffic, transcendentals=0),
    )


def struct(shape, dtype):
    return jax.ShapeDtypeStruct(shape, dtype)


def from_hbm(*arrays):
    return [pltpu.with_memory_space_constraint(array, pltpu.HBM) for array in arrays]


def from_vmem(*arrays):
    return [pltpu.with_memory_space_constraint(array, pltpu.VMEM) for array in arrays]


VMEM = pl.BlockSpec(memory_space=pltpu.VMEM)
ANY = pl.BlockSpec(memory_space=pl.ANY)


def by_field_body(tokens_ref, grad_ref, tokens_out, grad_out, wide):
    for ref, out_ref in ((tokens_ref, tokens_out), (grad_ref, grad_out)):
        wide[...] = ref[...].astype(jnp.float32)
        for k in range(3):
            out_ref[0, k * THIRD : (k + 1) * THIRD, :] = wide[pl.ds(k, THIRD, stride=3), :].astype(jnp.bfloat16)


def by_field(tokens, out_grad):
    return call(
        by_field_body,
        (struct((1, OWN, LOCAL), jnp.bfloat16),) * 2,
        [VMEM, VMEM],
        (VMEM, VMEM),
        [pltpu.VMEM((OWN, LOCAL), jnp.float32)],
        traffic=200000,
    )(*from_hbm(tokens.T, out_grad.T))


def field(words, k):
    if k:
        words = jnp.right_shift(words, 4 * k)
    if k < 2:
        words = jnp.bitwise_and(words, 15)
    return words.astype(jnp.float32)


CHUNKS = 8
AHEAD = 3


def row_copy(chunk, source, to, sems):
    rows = pl.ds(pl.multiple_of(chunk * 2 * WORDS, 2 * WORDS), 2 * WORDS)
    return pltpu.make_async_copy(source.at[rows], to.at[rows], sems.at[chunk])


def column_copy(chunk, source, to, sems):
    columns = pl.ds(pl.multiple_of(chunk * 2 * WORDS, 2 * WORDS), 2 * WORDS)
    return pltpu.make_async_copy(source.at[:, columns], to.at[:, columns], sems.at[chunk])


def tables_in(sources, targets, sems):
    copies = [pltpu.make_async_copy(a, b, sems.at[i]) for i, (a, b) in enumerate(zip(sources, targets))]
    for copy in copies:
        copy.start()
    return copies


def unpack_rows_pair(pair, codes, zeros_ref, log_ref, out_ref, short_ref):
    for part in range(2):
        block = pair * 2 + part
        zeros = [zeros_ref[pl.ds(3 * block + g, 1), :].astype(jnp.float32) for g in range(3)]
        scales = [jnp.exp(log_ref[pl.ds(3 * block + g, 1), :]) for g in range(3)]
        for start in range(0, WORDS, 16):
            here = pl.ds(pl.multiple_of(block * WORDS + start, 16), 16)
            words = codes[here, :]
            short_ref[here, :] = words.astype(jnp.int16)
            for k in range(3):
                zero = spread_over_groups(k, start, 16, zeros)
                scale = spread_over_groups(k, start, 16, scales)
                weight = (scale * (field(words, k) - zero)).astype(jnp.bfloat16)
                row = k * THIRD + start % THIRD
                out_ref[part * 2 + start // THIRD, pair, row : row + 16, :] = weight


def streamed(copy_of, source, to, sems, work):
    def step(chunk, carry):
        copy_of(chunk, source, to, sems).wait()

        @pl.when(chunk + AHEAD < CHUNKS)
        def _():
            copy_of(chunk + AHEAD, source, to, sems).start()

        work(chunk)
        return carry

    lax.fori_loop(0, CHUNKS, step, 0)


def start_first(copy_of, source, to, sems):
    for chunk in range(AHEAD):
        copy_of(chunk, source, to, sems).start()


def unpack_rows_body(codes_hbm, zeros_hbm, log_hbm, out_ref, short_ref, zeros_ref, log_ref, table_sems, codes, sems):
    tables = tables_in((zeros_hbm, log_hbm), (zeros_ref, log_ref), table_sems)
    start_first(row_copy, codes_hbm, codes, sems)
    for table in tables:
        table.wait()
    streamed(
        row_copy, codes_hbm, codes, sems, lambda pair: unpack_rows_pair(pair, codes, zeros_ref, log_ref, out_ref, short_ref)
    )


def unpack_rows(codes, zeros, log_scale):
    return call(
        unpack_rows_body,
        (
            pltpu.VMEM((N_Z, N_X * N_Y, OWN, HIDDEN), jnp.bfloat16),
            pltpu.VMEM((BLOCKS * WORDS, HIDDEN), jnp.int16),
        ),
        [ANY] * 3,
        (VMEM, VMEM),
        [
            pltpu.VMEM((48, HIDDEN), jnp.int32),
            pltpu.VMEM((48, HIDDEN), jnp.float32),
            pltpu.SemaphoreType.DMA((2,)),
            pltpu.VMEM((BLOCKS * WORDS, HIDDEN), jnp.int32),
            pltpu.SemaphoreType.DMA((CHUNKS,)),
        ],
        flops=20000000,
        traffic=10500000,
    )(*from_hbm(codes, zeros, log_scale))


def field_order(transposed):
    feature = lax.broadcasted_iota(jnp.int32, (FEATURES, FEATURES), 1 if transposed else 0)
    column = lax.broadcasted_iota(jnp.int32, (FEATURES, FEATURES), 0 if transposed else 1)
    wanted = 3 * jnp.bitwise_and(column, 127) + jnp.right_shift(column, 7)
    return (feature == wanted).astype(jnp.float32)


def reorder(rows, transposed):
    return jnp.dot(
        rows, field_order(transposed), precision=lax.Precision.HIGHEST, preferred_element_type=jnp.float32
    )


def unpack_columns_pair(pair, codes, table_ref, out_ref, short_ref):
    for part in range(2):
        block = pair * 2 + part
        table = table_ref[pl.ds(pl.multiple_of(8 * block, 8), 8), :]
        for g in range(4):
            here = slice(g * 128, (g + 1) * 128), pl.ds(pl.multiple_of(block * WORDS, WORDS), WORDS)
            words = codes[here]
            short_ref[here] = words.astype(jnp.int16)
            for k in range(3):
                columns = slice(k * WORDS, (k + 1) * WORDS)
                zero, scale = table[g : g + 1, columns], table[4 + g : 5 + g, columns]
                weight = (scale * (field(words, k) - zero)).astype(jnp.bfloat16)
                to = slice(part * FEATURES + k * WORDS, part * FEATURES + (k + 1) * WORDS)
                out_ref[pair, g * 128 : (g + 1) * 128, to] = weight


def unpack_columns_body(
    codes_hbm, zeros_hbm, log_hbm, out_ref, table_ref, short_ref, zeros_ref, log_ref, table_sems, natural, codes, sems
):
    tables = tables_in((zeros_hbm, log_hbm), (zeros_ref, log_ref), table_sems)
    start_first(column_copy, codes_hbm, codes, sems)
    for table in tables:
        table.wait()
    for b in range(BLOCKS):
        columns = slice(b * FEATURES, (b + 1) * FEATURES)
        natural[8 * b : 8 * b + 4, :] = zeros_ref[:, columns].astype(jnp.float32)
        natural[8 * b + 4 : 8 * b + 8, :] = jnp.exp(log_ref[:, columns])
    table_ref[...] = reorder(natural[...], False)
    streamed(column_copy, codes_hbm, codes, sems, lambda pair: unpack_columns_pair(pair, codes, table_ref, out_ref, short_ref))


def unpack_columns(codes, zeros, log_scale):
    wide = (4, BLOCKS * FEATURES)
    return call(
        unpack_columns_body,
        (
            pltpu.VMEM((N_X * N_Y, HIDDEN, 2 * FEATURES), jnp.bfloat16),
            pltpu.HBM((8 * BLOCKS, FEATURES), jnp.float32),
            pltpu.VMEM((HIDDEN, BLOCKS * WORDS), jnp.int16),
        ),
        [ANY] * 3,
        (VMEM,) * 3,
        [
            pltpu.VMEM(wide, jnp.int32),
            pltpu.VMEM(wide, jnp.float32),
            pltpu.SemaphoreType.DMA((2,)),
            pltpu.VMEM((8 * BLOCKS, FEATURES), jnp.float32),
            pltpu.VMEM((HIDDEN, BLOCKS * WORDS), jnp.int32),
            pltpu.SemaphoreType.DMA((CHUNKS,)),
        ],
        flops=20000000,
        traffic=10500000,
    )(*from_hbm(codes, zeros, log_scale))


SLAB = 8 * OWN


def position():
    return tuple(lax.axis_index(axis) for axis in ("x", "y_lo", "z"))


def swapped_with(here, near):
    place = 3 - here if near // 2 else here
    return place + 1 - 2 * (place % 2) if near % 2 else place


def lay_tokens(place, source, far, to):
    x, y, z = place
    slab = (z + 4 - far) % 4
    for near in range(4):
        for dy in range(2):
            to[slab, swapped_with(x, near) * 2 + (y + dy) % 2, :, :] = source[near * 2 + dy]
    return slab


def lay_grad(place, source, far, to):
    x, y, z = place
    slab = (x + 4 - far) % 4
    for near in range(4):
        z_from = swapped_with(z, near)
        for dy in range(2):
            for k in range(3):
                row = pl.multiple_of((z_from // 2) * FEATURES + k * WORDS + (z_from % 2) * THIRD, THIRD)
                to[slab * 2 + (y + dy) % 2, pl.ds(row, THIRD), :] = source[
                    near * 2 + dy, k * THIRD : (k + 1) * THIRD, :
                ]
    return slab


def slab_out(slab, tokens_from, tokens_hbm, sems):
    return pltpu.make_async_copy(tokens_from.at[slab], tokens_hbm.at[slab], sems)


def pair_out(slab, grad_from, grad_hbm, sems):
    pairs = pl.ds(slab * 2, 2)
    return pltpu.make_async_copy(grad_from.at[pairs], grad_hbm.at[pairs], sems)


def slab_products(fars, tokens_refs, grad_refs, weights, scratch, hbm, totals):
    gate_ref, up_ref, down_ref = weights
    tokens_to, grad_to, tokens_sems, grad_sems = scratch
    tokens_hbm, grad_hbm = hbm
    place = position()
    gate_pre, up_pre, hidden_grad = totals
    copies, laid = [], []
    for i, far in enumerate(fars):
        slabs = lay_tokens(place, tokens_refs[i], far, tokens_to), lay_grad(place, grad_refs[i], far, grad_to)
        copies.append(slab_out(slabs[0], tokens_to, tokens_hbm, tokens_sems.at[i]))
        copies.append(pair_out(slabs[1], grad_to, grad_hbm, grad_sems.at[i]))
        laid.append(slabs)
    for copy in copies:
        copy.start()
    for slab, grad_slab in laid:
        features = tokens_to[slab].reshape(SLAB, LOCAL).T
        gate_pre += jnp.dot(features, gate_ref[slab].reshape(SLAB, HIDDEN), preferred_element_type=jnp.float32)
        up_pre += jnp.dot(features, up_ref[slab].reshape(SLAB, HIDDEN), preferred_element_type=jnp.float32)
        for dy in range(2):
            piece = grad_to[grad_slab * 2 + dy]
            hidden_grad += jnp.dot(down_ref[grad_slab * 2 + dy], piece, preferred_element_type=jnp.float32)
    return (gate_pre, up_pre, hidden_grad), copies


def forward_body(
    t0, t1, t3, o0, o1, o3, gate_ref, up_ref, down_ref, gate_short,
    gate_pre_ref, up_pre_ref, hidden_grad_ref, tokens_hbm, grad_hbm, gate_codes_hbm,
    tokens_to, grad_to, tokens_sems, grad_sems, short_sems,
):
    short = tables_in((gate_short,), (gate_codes_hbm,), short_sems)
    zero = jnp.zeros((LOCAL, HIDDEN), jnp.float32)
    core = lax.axis_index("core")
    (gate_pre_ref[...], up_pre_ref[...], hidden_grad_ref[...]), copies = slab_products(
        (0, 1 + 2 * core, 3 - 2 * core), (t0, t1, t3), (o0, o1, o3), (gate_ref, up_ref, down_ref),
        (tokens_to, grad_to, tokens_sems, grad_sems), (tokens_hbm, grad_hbm),
        (zero, zero, jnp.zeros((HIDDEN, LOCAL), jnp.float32)),
    )
    for copy in copies + short:
        copy.wait()


TOKENS_SHAPE = (N_Z, N_X * N_Y, OWN, LOCAL)
GRAD_SHAPE = (N_X * N_Y, 2 * FEATURES, LOCAL)


def slab_scratch(slabs):
    return [
        pltpu.VMEM(TOKENS_SHAPE, jnp.bfloat16),
        pltpu.VMEM(GRAD_SHAPE, jnp.bfloat16),
        pltpu.SemaphoreType.DMA((slabs,)),
        pltpu.SemaphoreType.DMA((slabs,)),
    ]


def forward(tokens_parts, grad_parts, gate, up, down, gate_short):
    f32, bf16 = jnp.float32, jnp.bfloat16
    near = (0, 1, 3)
    return call(
        forward_body,
        (
            pltpu.VMEM((LOCAL, HIDDEN), f32),
            pltpu.VMEM((LOCAL, HIDDEN), f32),
            pltpu.VMEM((HIDDEN, LOCAL), f32),
            pltpu.HBM(TOKENS_SHAPE, bf16),
            pltpu.HBM(GRAD_SHAPE, bf16),
            pltpu.HBM(gate_short.shape, gate_short.dtype),
        ),
        [VMEM] * 10,
        (VMEM,) * 3 + (ANY,) * 3,
        slab_scratch(3) + [pltpu.SemaphoreType.DMA((1,))],
        flops=3 * 3 * 2 * 128 * 1536 * 512,
        traffic=18000000,
    )(
        *from_vmem(*[tokens_parts[far] for far in near], *[grad_parts[far] for far in near]),
        *from_vmem(gate, up, down, gate_short),
    )


def backward_body(
    t2, o2, gate_ref, up_ref, down_ref, gate_pre_ref, up_pre_ref, hidden_grad_ref, up_short, down_short, tokens_in, grad_in,
    partial_hbm, tokens_hbm, grad_hbm, gate_grad_hbm, up_grad_hbm, hidden_hbm, up_codes_hbm, down_codes_hbm,
    tokens_to, grad_to, tokens_sems, grad_sems, partial, partial_sems, gate_grad_ref, up_grad_ref, hidden_ref, small_sems, short_sems,
):
    short = tables_in((up_short, down_short), (up_codes_hbm, down_codes_hbm), short_sems)
    (gate_pre, up_pre, hidden_grad), copies = slab_products(
        (2,), (t2,), (o2,), (gate_ref, up_ref, down_ref),
        (tokens_to, grad_to, tokens_sems, grad_sems), (tokens_hbm, grad_hbm),
        (gate_pre_ref[...], up_pre_ref[...], hidden_grad_ref[...]),
    )
    hidden_grad = hidden_grad.T
    sigmoid_gate = jax.nn.sigmoid(gate_pre)
    silu_gate = gate_pre * sigmoid_gate
    hidden = silu_gate * up_pre
    gate_grad = hidden_grad * up_pre * sigmoid_gate * (1.0 + gate_pre * (1.0 - sigmoid_gate))
    up_grad = hidden_grad * silu_gate
    gate_grad_ref[...] = gate_grad.astype(jnp.bfloat16)
    up_grad_ref[...] = up_grad.astype(jnp.bfloat16)
    hidden_ref[...] = hidden.T.astype(jnp.bfloat16)
    copies += tables_in(
        (gate_grad_ref, up_grad_ref, hidden_ref), (gate_grad_hbm, up_grad_hbm, hidden_hbm), small_sems
    )
    gate_turned = gate_grad.T.astype(jnp.bfloat16)
    up_turned = up_grad.T.astype(jnp.bfloat16)
    for slab in range(N_Z):
        total = jnp.dot(gate_ref[slab].reshape(SLAB, HIDDEN), gate_turned, preferred_element_type=jnp.float32)
        total += jnp.dot(up_ref[slab].reshape(SLAB, HIDDEN), up_turned, preferred_element_type=jnp.float32)
        partial[slab] = total.astype(jnp.bfloat16).reshape(N_X * N_Y, OWN, LOCAL)
        copy = pltpu.make_async_copy(partial.at[slab], partial_hbm.at[:, slab], partial_sems.at[slab])
        copy.start()
        copies.append(copy)
    for copy in copies + short:
        copy.wait()


def backward(tokens_parts, grad_parts, gate, up, down, sums, up_short, down_short, all_tokens, all_grad):
    bf16 = jnp.bfloat16
    return call(
        backward_body,
        (
            pltpu.HBM((N_X * N_Y, N_Z, OWN, LOCAL), bf16),
            pltpu.HBM(TOKENS_SHAPE, bf16),
            pltpu.HBM(GRAD_SHAPE, bf16),
            pltpu.HBM((LOCAL, HIDDEN), bf16),
            pltpu.HBM((LOCAL, HIDDEN), bf16),
            pltpu.HBM((HIDDEN, LOCAL), bf16),
            pltpu.HBM(up_short.shape, up_short.dtype),
            pltpu.HBM(down_short.shape, down_short.dtype),
        ),
        [VMEM] * 10 + [ANY] * 2,
        (ANY,) * 8,
        slab_scratch(1)
        + [
            pltpu.VMEM(TOKENS_SHAPE, bf16),
            pltpu.SemaphoreType.DMA((N_Z,)),
            pltpu.VMEM((LOCAL, HIDDEN), bf16),
            pltpu.VMEM((LOCAL, HIDDEN), bf16),
            pltpu.VMEM((HIDDEN, LOCAL), bf16),
            pltpu.SemaphoreType.DMA((3,)),
            pltpu.SemaphoreType.DMA((2,)),
        ],
        flops=3 * 2 * 128 * 6144 * 512,
        traffic=24000000,
        aliases={10: 1, 11: 2},
    )(
        *from_vmem(tokens_parts[2], grad_parts[2], gate, up, down, *sums, up_short, down_short),
        *from_hbm(all_tokens, all_grad),
    )


EXTRA = 16


def with_sums(rows, members):
    sums = jnp.dot(members, rows, preferred_element_type=jnp.float32)
    head = sums.astype(jnp.bfloat16)
    rest = (sums - head.astype(jnp.float32)).astype(jnp.bfloat16)
    return jnp.concatenate([rows, jnp.concatenate([head, rest], axis=0)], axis=0)


def block_members():
    group = lax.broadcasted_iota(jnp.int32, (8, FEATURES), 0)
    place = lax.broadcasted_iota(jnp.int32, (8, FEATURES), 1)
    half = (place >= OWN).astype(jnp.int32)
    place = place - OWN * half
    k = jnp.right_shift(place, 6)
    feature = 3 * (half * THIRD + place - THIRD * k) + k
    scale = jnp.where(k == 0, 1.0, jnp.where(k == 1, 16.0, 256.0))
    return jnp.where(jnp.right_shift(feature, 7) == group, scale, 0.0).astype(jnp.bfloat16)


def hidden_members():
    group = lax.broadcasted_iota(jnp.int32, (8, HIDDEN), 0)
    unit = lax.broadcasted_iota(jnp.int32, (8, HIDDEN), 1)
    return (jnp.right_shift(unit, 7) == group).astype(jnp.float32).astype(jnp.bfloat16)


MASKS = (15, 240, 3840)
SHRINK = (1.0, 1.0 / 16.0, 1.0 / 256.0)


def in_place(words, k):
    return jnp.bitwise_and(words, MASKS[k]).astype(jnp.float32)


def in_turn(*streams):
    running = list(streams)
    while running:
        for stream in list(running):
            if next(stream, None) is None:
                running.remove(stream)


def folded(products):
    return products[0:8] + products[8:16]


def row_groups(block, codes, weight_grad, sums, totals):
    weighted = [jnp.zeros((8, HIDDEN), jnp.float32)] * 3
    for start in range(0, WORDS, 16):
        words = codes[pl.ds(pl.multiple_of(block * WORDS + start, 16), 16), :].astype(jnp.int32)
        for k in range(3):
            product = in_place(words, k) * weight_grad[shard_row(k, start) : shard_row(k, start) + 16, :]
            first, last = (3 * start + k) // 128, (3 * (start + 15) + k) // 128
            if first == last:
                weighted[first] = weighted[first] + folded(product)
            else:
                low = start + lax.broadcasted_iota(jnp.int32, (16, 1), 0) < first_word(k, last)
                low_product = jnp.where(low, product, 0.0)
                weighted[first] = weighted[first] + folded(low_product)
                weighted[last] = weighted[last] + folded(product - low_product)
        yield True
    for g in range(3):
        row = pl.ds(3 * block + g, 1)
        sums[row, :] = jnp.sum(weighted[g], axis=0, keepdims=True)
        totals[row, :] = (
            weight_grad[FEATURES + g : FEATURES + g + 1, :] + weight_grad[FEATURES + 8 + g : FEATURES + 9 + g, :]
        )
    yield True


def column_groups(block, part, codes, weight_grad, raw):
    here = pl.ds(pl.multiple_of(8 * block, 8), 8)
    mine = slice(part * FEATURES, (part + 1) * FEATURES)
    totals = weight_grad[HIDDEN : HIDDEN + 4, mine] + weight_grad[HIDDEN + 8 : HIDDEN + 12, mine]
    for k in range(3):
        sums = []
        for g in range(4):
            weighted = jnp.zeros((8, WORDS), jnp.float32)
            for start in range(g * 128, g * 128 + 128, 16):
                words = codes[start : start + 16, pl.ds(pl.multiple_of(block * WORDS, WORDS), WORDS)].astype(jnp.int32)
                value = weight_grad[start : start + 16, part * FEATURES + k * WORDS : part * FEATURES + (k + 1) * WORDS]
                weighted = weighted + folded(in_place(words, k) * value)
            sums.append(jnp.sum(weighted, axis=0, keepdims=True))
            yield True
        columns = slice(k * WORDS, (k + 1) * WORDS)
        raw[here, columns] = jnp.concatenate([jnp.concatenate(sums, axis=0) * SHRINK[k], totals[:, columns]], axis=0)


def group_body(
    gate_hbm, up_hbm, down_hbm, tokens_hbm, grad_hbm, *small_hbm_and_rest
):
    small_hbm, rest = small_hbm_and_rest[:8], small_hbm_and_rest[8:]
    small, rest = rest[-8:], rest[:-8]
    group_work(gate_hbm, up_hbm, down_hbm, tokens_hbm, grad_hbm, small_hbm, small, *rest)


def group_work(
    gate_hbm, up_hbm, down_hbm, tokens_hbm, grad_hbm, small_hbm, small,
    own_ref, given_ref,
    gate_codes, up_codes, down_codes, gate_sems, up_sems, down_sems, tokens_ref, grad_ref, tokens_sems, grad_sems, small_sems,
    hidden_rows, gate_even, up_even, gate_odd, up_odd, down_pair, down_rows, halves, sums, totals,
):
    def copies(chunk):
        return (
            row_copy(chunk, gate_hbm, gate_codes, gate_sems),
            row_copy(chunk, up_hbm, up_codes, up_sems),
            column_copy(chunk, down_hbm, down_codes, down_sems),
        )

    def start(chunk):
        for copy in copies(chunk):
            copy.start()

    def rows_in(pair):
        return (
            pltpu.make_async_copy(tokens_hbm.at[:, pair], tokens_ref.at[:, pair], tokens_sems.at[pair]),
            pltpu.make_async_copy(grad_hbm.at[pair], grad_ref.at[pair], grad_sems.at[pair]),
        )

    gate_grad_ref, up_grad_ref, hidden_ref, gate_zeros, gate_log, up_zeros, up_log, table_ref = small
    arrivals = tables_in(small_hbm, small, small_sems)
    for copy in rows_in(0):
        copy.start()
    start(0)
    for pair in range(1, BLOCKS // 2):
        for copy in rows_in(pair):
            copy.start()
    start(1)
    for arrival in arrivals:
        arrival.wait()
    hidden_rows[...] = with_sums(hidden_ref[...], hidden_members())
    members = block_members()
    field_of_row = jnp.right_shift(lax.broadcasted_iota(jnp.int32, (OWN, 1), 0), 6)
    shrink = jnp.where(field_of_row == 0, SHRINK[0], jnp.where(field_of_row == 1, SHRINK[1], SHRINK[2]))
    shrink = jnp.broadcast_to(shrink, (OWN, LOCAL)).astype(jnp.bfloat16)

    def row_products(pair, part, gate_to, up_to):
        features = jnp.concatenate([tokens_ref[part * 2 + half, pair] * shrink for half in range(2)], axis=0)
        features = with_sums(features, members)
        for grad, to in ((gate_grad_ref, gate_to), (up_grad_ref, up_to)):
            for row in range(0, FEATURES + EXTRA, 80):
                to[row : row + 80, :] = jnp.dot(
                    features[row : row + 80, :], grad[...], preferred_element_type=jnp.float32
                )
                yield True

    def column_products(pair, down_to):
        for row in range(0, HIDDEN + EXTRA, 176):
            down_to[row : row + 176, :] = lax.dot_general(
                hidden_rows[row : row + 176, :], grad_ref[pair], CONTRACT_LAST, preferred_element_type=jnp.float32
            )
            yield True

    def groups(block, gate_from, up_from):
        yield from row_groups(block, gate_codes, gate_from, sums.at[0], totals.at[0])
        yield from row_groups(block, up_codes, up_from, sums.at[1], totals.at[1])

    def down_groups(pair):
        for part in range(2):
            yield from column_groups(pair * 2 + part, part, down_codes, down_pair, down_rows)

    for copy in rows_in(0):
        copy.wait()
    in_turn(row_products(0, 0, gate_even, up_even))

    def pair_step(pair, carry):
        for copy in copies(pair):
            copy.wait()
        following = jnp.minimum(pair + 1, BLOCKS // 2 - 1)

        @pl.when(pair < BLOCKS // 2 - 1)
        def _():
            for copy in rows_in(following):
                copy.wait()

        @pl.when(pair + 2 < CHUNKS)
        def _():
            start(pair + 2)

        in_turn(row_products(pair, 1, gate_odd, up_odd), groups(pair * 2, gate_even, up_even))
        in_turn(column_products(pair, down_pair), groups(pair * 2 + 1, gate_odd, up_odd))
        in_turn(row_products(following, 0, gate_even, up_even), down_groups(pair))
        return carry

    lax.fori_loop(0, BLOCKS // 2, pair_step, 0)

    for half, (zeros_ref, log_ref) in enumerate(((gate_zeros, gate_log), (up_zeros, up_log))):
        scale = jnp.exp(log_ref[...])
        halves[half, 0:48] = scale * (sums[half] - zeros_ref[...].astype(jnp.float32) * totals[half])
        halves[half, 48:96] = -scale * totals[half]
    found, table = down_rows[...].reshape(BLOCKS, 8, FEATURES), table_ref[...].reshape(BLOCKS, 8, FEATURES)
    found, total, zero, scale = found[:, 0:4], found[:, 4:8], table[:, 0:4], table[:, 4:8]
    finished = jnp.concatenate([scale * (found - zero * total), -scale * total], axis=1)
    down_rows[...] = finished.reshape(8 * BLOCKS, FEATURES)
    for half, begin in ((0, 0), (1, 48)):
        for j in range(3):
            halves[half, 96:144, j * 128 : (j + 1) * 128] = down_rows[begin : begin + 48, j * 128 : (j + 1) * 128]
    halves[0, 96:128, 384:] = down_rows[96:128, 0:128]
    halves[0, 128:144, 384:] = down_rows[96:112, 128:256]
    halves[1, 96:112, 384:] = down_rows[112:128, 128:256]
    halves[1, 112:144, 384:] = down_rows[96:128, 256:384]
    core = lax.axis_index("core")
    own_ref[...] = halves[core]
    given_ref[...] = halves[1 - core]


def group_grads(tokens, grad, gate_grad, up_grad, hidden, gate_tables, up_tables, down_codes, table):
    half = struct((144, HIDDEN), jnp.float32)
    gate_codes, *gate_tables = gate_tables
    up_codes, *up_tables = up_tables
    small = (gate_grad, up_grad, hidden, *gate_tables, *up_tables, table)
    rows, columns = (FEATURES + EXTRA, HIDDEN), (HIDDEN + EXTRA, 2 * FEATURES)
    return call(
        group_body,
        (half, half),
        [ANY] * 13,
        (VMEM, VMEM),
        [
            pltpu.VMEM((BLOCKS * WORDS, HIDDEN), jnp.int16),
            pltpu.VMEM((BLOCKS * WORDS, HIDDEN), jnp.int16),
            pltpu.VMEM((HIDDEN, BLOCKS * WORDS), jnp.int16),
        ]
        + [pltpu.SemaphoreType.DMA((CHUNKS,))] * 3
        + [
            pltpu.VMEM(TOKENS_SHAPE, jnp.bfloat16),
            pltpu.VMEM(GRAD_SHAPE, jnp.bfloat16),
            pltpu.SemaphoreType.DMA((BLOCKS // 2,)),
            pltpu.SemaphoreType.DMA((BLOCKS // 2,)),
            pltpu.SemaphoreType.DMA((8,)),
            pltpu.VMEM((HIDDEN + EXTRA, LOCAL), jnp.bfloat16),
        ]
        + [pltpu.VMEM(shape, jnp.float32) for shape in (rows,) * 4 + (columns,)]
        + [pltpu.VMEM((8 * BLOCKS, FEATURES), jnp.float32), pltpu.VMEM((2, 144, HIDDEN), jnp.float32)]
        + [pltpu.VMEM((2, 48, HIDDEN), jnp.float32)] * 2
        + [pltpu.VMEM(array.shape, array.dtype) for array in small],
        flops=3 * 2 * 128 * 6144 * 512,
        traffic=17000000,
        vmem=40,
    )(
        *from_hbm(gate_codes, up_codes, down_codes, tokens, grad, *small),
    )


def split_body(mine_ref, other_ref, gs_ref, gz_ref, us_ref, uz_ref, ds_ref, dz_ref, halves, rows):
    core = lax.axis_index("core")
    halves[core] = mine_ref[...]
    halves[1 - core] = other_ref[...]
    for half, scale_ref, zero_ref in ((0, gs_ref, gz_ref), (1, us_ref, uz_ref)):
        scale_ref[...] = halves[half, 0:48, :]
        zero_ref[...] = halves[half, 48:96, :]
        for j in range(3):
            rows[48 * half : 48 * half + 48, j * 128 : (j + 1) * 128] = halves[half, 96:144, j * 128 : (j + 1) * 128]
    rows[96:128, 0:128] = halves[0, 96:128, 384:]
    rows[96:112, 128:256] = halves[0, 128:144, 384:]
    rows[112:128, 128:256] = halves[1, 96:112, 384:]
    rows[96:128, 256:384] = halves[1, 112:144, 384:]
    natural = reorder(rows[...], True)
    for b in range(BLOCKS):
        columns = slice(b * FEATURES, (b + 1) * FEATURES)
        ds_ref[:, columns] = natural[8 * b : 8 * b + 4, :]
        dz_ref[:, columns] = natural[8 * b + 4 : 8 * b + 8, :]


def split(mine, other):
    f32 = jnp.float32
    return call(
        split_body,
        (struct((48, HIDDEN), f32),) * 4 + (struct((4, BLOCKS * FEATURES), f32),) * 2,
        [VMEM, VMEM],
        (VMEM,) * 6,
        [pltpu.VMEM((2, 144, HIDDEN), f32), pltpu.VMEM((8 * BLOCKS, FEATURES), f32)],
        traffic=1200000,
    )(mine, other)


def sum_body(parts_ref, out_ref):
    total = parts_ref[0].astype(jnp.float32)
    for part in range(1, SHARDS):
        total = total + parts_ref[part].astype(jnp.float32)
    for k in range(3):
        out_ref[pl.ds(k, THIRD, stride=3), :] = total[k * THIRD : (k + 1) * THIRD, :]


def sum_parts(parts):
    return call(sum_body, struct((OWN, LOCAL), jnp.float32), [VMEM], VMEM, traffic=1700000)(parts)


NEAR, ACROSS = ((0, 1), (2, 3)), ((0, 3), (1, 2))


def paired(block, axis, pairs):
    other = lax.ppermute(block, axis, [pair for a, b in pairs for pair in ((a, b), (b, a))])
    return jnp.concatenate([block, other])


def turned(block, axis, way):
    pairs = [(place, (place + way) % 4) for place in range(4)]
    pairs += [(4 + place, 4 + (place - way) % 4) for place in range(4)]
    return lax.ppermute(block, ("core", axis), pairs)


def swap(value, axis):
    return lax.ppermute(value, axis, [(0, 1), (1, 0)])


def shards(
    tokens,
    out_grad,
    gate_codes,
    gate_zeros,
    gate_log_scale,
    up_codes,
    up_zeros,
    up_log_scale,
    down_codes,
    down_zeros,
    down_log_scale,
):
    tokens_near, grad_near = by_field(tokens, out_grad)
    tokens_near, grad_near = paired(tokens_near, "y_lo", ((0, 1),)), paired(grad_near, "y_lo", ((0, 1),))
    tokens_near, grad_near = paired(tokens_near, "x", NEAR), paired(grad_near, "z", NEAR)
    tokens_near, gate_zeros = lax.optimization_barrier((tokens_near, gate_zeros))
    tokens_near, grad_near = paired(tokens_near, "x", ACROSS), paired(grad_near, "z", ACROSS)
    gate, gate_short = unpack_rows(gate_codes, gate_zeros, gate_log_scale)
    tokens_near, gate, up_zeros = lax.optimization_barrier((tokens_near, gate, up_zeros))
    grad_near, up_log_scale = lax.optimization_barrier((grad_near, up_log_scale))
    tokens_first, grad_first = turned(tokens_near, "z", 1), turned(grad_near, "x", 1)
    tokens_second, grad_second = turned(tokens_near, "z", -1), turned(grad_near, "x", -1)
    up, up_short = unpack_rows(up_codes, up_zeros, up_log_scale)
    tokens_first, grad_first, up, down_zeros = lax.optimization_barrier((tokens_first, grad_first, up, down_zeros))
    tokens_parts = tokens_near, tokens_first, turned(tokens_first, "z", 1), tokens_second
    grad_parts = grad_near, grad_first, turned(grad_first, "x", 1), grad_second
    down, table, down_short = unpack_columns(down_codes, down_zeros, down_log_scale)
    *sums, all_tokens, all_grad, gate_short = forward(tokens_parts, grad_parts, gate, up, down, gate_short)
    partial, all_tokens, all_grad, gate_grad, up_grad, hidden, up_short, down_short = backward(
        tokens_parts, grad_parts, gate, up, down, sums, up_short, down_short, all_tokens, all_grad
    )
    parts = lax.all_to_all(partial.reshape(SHARDS, OWN, LOCAL), ("x", "y_lo", "z"), 0, 0, tiled=True)
    own, given = group_grads(
        all_tokens,
        all_grad,
        gate_grad,
        up_grad,
        hidden,
        (gate_short, gate_zeros, gate_log_scale),
        (up_short, up_zeros, up_log_scale),
        down_short,
        table,
    )
    own = own + swap(given, "core")
    own = own.astype(jnp.bfloat16)
    tokens_grad = sum_parts(parts).T
    far, tokens_grad = lax.optimization_barrier((swap(own, "y_hi"), tokens_grad))
    mine = own.astype(jnp.float32) + far.astype(jnp.float32)
    theirs = swap(mine, "core")
    return (tokens_grad, *split(mine, theirs))


def solution(mesh):
    axes = jax.sharding.Mesh(mesh.devices.reshape(2, 2, N_X, N_Y, N_Z), ("y_hi", "core", "x", "y_lo", "z"))
    dp, tensor = ("y_hi", "core"), ("x", "y_lo", "z")
    columns, rows = P(None, tensor), P(tensor, None)
    return jax.shard_map(
        shards,
        mesh=axes,
        in_specs=(P(dp, tensor),) * 2 + (columns,) * 6 + (rows,) * 3,
        out_specs=(P(dp, tensor),) + (columns,) * 4 + (rows,) * 2,
        check_vma=False,
    )
```

```python
import jax
import jax.numpy as jnp
from jax import lax
from jax.experimental import pallas as pl
from jax.experimental.pallas import tpu as pltpu
from jax.sharding import PartitionSpec as P

N_X, N_Y, N_Z = 4, 2, 4
SHARDS = 32
OWN = 192
THIRD = 64
BLOCKS = 16
WORDS = 128
FEATURES = 384
HIDDEN = 512
LOCAL = 128
MIB = 1 << 20

CONTRACT_LAST = (((1,), (1,)), ((), ()))
CONTRACT_FIRST = (((0,), (0,)), ((), ()))


def shard_row(k, word):
    return (word // THIRD) * OWN + k * THIRD + word % THIRD


def first_word(k, group):
    return -((k - 128 * group) // 3)


def spread_over_groups(k, start, rows, values):
    first, last = (3 * start + k) // 128, (3 * (start + rows - 1) + k) // 128
    if first == last:
        return values[first]
    row = start + lax.broadcasted_iota(jnp.int32, (rows, 1), 0)
    return jnp.where(row < first_word(k, last), values[first], values[last])


def call(body, out_shape, in_specs, out_specs, scratch=(), flops=0, traffic=0, vmem=16, aliases=None):
    return pl.pallas_call(
        body,
        out_shape=out_shape,
        in_specs=in_specs,
        out_specs=out_specs,
        scratch_shapes=list(scratch),
        input_output_aliases=aliases or {},
        compiler_params=pltpu.CompilerParams(vmem_limit_bytes=vmem * MIB),
        cost_estimate=pl.CostEstimate(flops=flops, bytes_accessed=traffic, transcendentals=0),
    )


def struct(shape, dtype):
    return jax.ShapeDtypeStruct(shape, dtype)


def from_hbm(*arrays):
    return [pltpu.with_memory_space_constraint(array, pltpu.HBM) for array in arrays]


def from_vmem(*arrays):
    return [pltpu.with_memory_space_constraint(array, pltpu.VMEM) for array in arrays]


VMEM = pl.BlockSpec(memory_space=pltpu.VMEM)
ANY = pl.BlockSpec(memory_space=pl.ANY)


def by_field_body(tokens_ref, grad_ref, tokens_out, grad_out, wide):
    for ref, out_ref in ((tokens_ref, tokens_out), (grad_ref, grad_out)):
        wide[...] = ref[...].astype(jnp.float32)
        for k in range(3):
            out_ref[0, k * THIRD : (k + 1) * THIRD, :] = wide[pl.ds(k, THIRD, stride=3), :].astype(jnp.bfloat16)


def by_field(tokens, out_grad):
    return call(
        by_field_body,
        (struct((1, OWN, LOCAL), jnp.bfloat16),) * 2,
        [VMEM, VMEM],
        (VMEM, VMEM),
        [pltpu.VMEM((OWN, LOCAL), jnp.float32)],
        traffic=200000,
    )(*from_hbm(tokens.T, out_grad.T))


def field(words, k):
    if k:
        words = jnp.right_shift(words, 4 * k)
    if k < 2:
        words = jnp.bitwise_and(words, 15)
    return words.astype(jnp.float32)


CHUNKS = 8
AHEAD = 3


def row_copy(chunk, source, to, sems):
    rows = pl.ds(pl.multiple_of(chunk * 2 * WORDS, 2 * WORDS), 2 * WORDS)
    return pltpu.make_async_copy(source.at[rows], to.at[rows], sems.at[chunk])


def column_copy(chunk, source, to, sems):
    columns = pl.ds(pl.multiple_of(chunk * 2 * WORDS, 2 * WORDS), 2 * WORDS)
    return pltpu.make_async_copy(source.at[:, columns], to.at[:, columns], sems.at[chunk])


def tables_in(sources, targets, sems):
    copies = [pltpu.make_async_copy(a, b, sems.at[i]) for i, (a, b) in enumerate(zip(sources, targets))]
    for copy in copies:
        copy.start()
    return copies


def unpack_rows_pair(pair, codes, zeros_ref, log_ref, out_ref):
    for part in range(2):
        block = pair * 2 + part
        zeros = [zeros_ref[pl.ds(3 * block + g, 1), :].astype(jnp.float32) for g in range(3)]
        scales = [jnp.exp(log_ref[pl.ds(3 * block + g, 1), :]) for g in range(3)]
        for start in range(0, WORDS, 16):
            words = codes[pl.ds(pl.multiple_of(block * WORDS + start, 16), 16), :]
            for k in range(3):
                zero = spread_over_groups(k, start, 16, zeros)
                scale = spread_over_groups(k, start, 16, scales)
                weight = (scale * (field(words, k) - zero)).astype(jnp.bfloat16)
                row = k * THIRD + start % THIRD
                out_ref[part * 2 + start // THIRD, pair, row : row + 16, :] = weight


def streamed(copy_of, source, to, sems, work):
    def step(chunk, carry):
        copy_of(chunk, source, to, sems).wait()

        @pl.when(chunk + AHEAD < CHUNKS)
        def _():
            copy_of(chunk + AHEAD, source, to, sems).start()

        work(chunk)
        return carry

    lax.fori_loop(0, CHUNKS, step, 0)


def start_first(copy_of, source, to, sems):
    for chunk in range(AHEAD):
        copy_of(chunk, source, to, sems).start()


def unpack_rows_body(codes_hbm, zeros_hbm, log_hbm, out_ref, zeros_ref, log_ref, table_sems, codes, sems):
    tables = tables_in((zeros_hbm, log_hbm), (zeros_ref, log_ref), table_sems)
    start_first(row_copy, codes_hbm, codes, sems)
    for table in tables:
        table.wait()
    streamed(
        row_copy, codes_hbm, codes, sems, lambda pair: unpack_rows_pair(pair, codes, zeros_ref, log_ref, out_ref)
    )


def unpack_rows(codes, zeros, log_scale):
    return call(
        unpack_rows_body,
        pltpu.VMEM((N_Z, N_X * N_Y, OWN, HIDDEN), jnp.bfloat16),
        [ANY] * 3,
        VMEM,
        [
            pltpu.VMEM((48, HIDDEN), jnp.int32),
            pltpu.VMEM((48, HIDDEN), jnp.float32),
            pltpu.SemaphoreType.DMA((2,)),
            pltpu.VMEM((BLOCKS * WORDS, HIDDEN), jnp.int32),
            pltpu.SemaphoreType.DMA((CHUNKS,)),
        ],
        flops=20000000,
        traffic=10500000,
    )(*from_hbm(codes, zeros, log_scale))


def field_order(transposed):
    feature = lax.broadcasted_iota(jnp.int32, (FEATURES, FEATURES), 1 if transposed else 0)
    column = lax.broadcasted_iota(jnp.int32, (FEATURES, FEATURES), 0 if transposed else 1)
    wanted = 3 * jnp.bitwise_and(column, 127) + jnp.right_shift(column, 7)
    return (feature == wanted).astype(jnp.float32)


def reorder(rows, transposed):
    return jnp.dot(
        rows, field_order(transposed), precision=lax.Precision.HIGHEST, preferred_element_type=jnp.float32
    )


def unpack_columns_pair(pair, codes, table_ref, out_ref):
    for part in range(2):
        block = pair * 2 + part
        table = table_ref[pl.ds(pl.multiple_of(8 * block, 8), 8), :]
        for g in range(4):
            words = codes[g * 128 : (g + 1) * 128, pl.ds(pl.multiple_of(block * WORDS, WORDS), WORDS)]
            for k in range(3):
                columns = slice(k * WORDS, (k + 1) * WORDS)
                zero, scale = table[g : g + 1, columns], table[4 + g : 5 + g, columns]
                weight = (scale * (field(words, k) - zero)).astype(jnp.bfloat16)
                to = slice(part * FEATURES + k * WORDS, part * FEATURES + (k + 1) * WORDS)
                out_ref[pair, g * 128 : (g + 1) * 128, to] = weight


def unpack_columns_body(
    codes_hbm, zeros_hbm, log_hbm, out_ref, table_ref, zeros_ref, log_ref, table_sems, natural, codes, sems
):
    tables = tables_in((zeros_hbm, log_hbm), (zeros_ref, log_ref), table_sems)
    start_first(column_copy, codes_hbm, codes, sems)
    for table in tables:
        table.wait()
    for b in range(BLOCKS):
        columns = slice(b * FEATURES, (b + 1) * FEATURES)
        natural[8 * b : 8 * b + 4, :] = zeros_ref[:, columns].astype(jnp.float32)
        natural[8 * b + 4 : 8 * b + 8, :] = jnp.exp(log_ref[:, columns])
    table_ref[...] = reorder(natural[...], False)
    streamed(column_copy, codes_hbm, codes, sems, lambda pair: unpack_columns_pair(pair, codes, table_ref, out_ref))


def unpack_columns(codes, zeros, log_scale):
    wide = (4, BLOCKS * FEATURES)
    return call(
        unpack_columns_body,
        (
            pltpu.VMEM((N_X * N_Y, HIDDEN, 2 * FEATURES), jnp.bfloat16),
            pltpu.HBM((8 * BLOCKS, FEATURES), jnp.float32),
        ),
        [ANY] * 3,
        (VMEM,) * 2,
        [
            pltpu.VMEM(wide, jnp.int32),
            pltpu.VMEM(wide, jnp.float32),
            pltpu.SemaphoreType.DMA((2,)),
            pltpu.VMEM((8 * BLOCKS, FEATURES), jnp.float32),
            pltpu.VMEM((HIDDEN, BLOCKS * WORDS), jnp.int32),
            pltpu.SemaphoreType.DMA((CHUNKS,)),
        ],
        flops=20000000,
        traffic=10500000,
    )(*from_hbm(codes, zeros, log_scale))


EXTRA = 16


def with_sums(rows, members):
    sums = jnp.dot(members, rows, preferred_element_type=jnp.float32)
    head = sums.astype(jnp.bfloat16)
    rest = (sums - head.astype(jnp.float32)).astype(jnp.bfloat16)
    return jnp.concatenate([rows, jnp.concatenate([head, rest], axis=0)], axis=0)


def block_members():
    group = lax.broadcasted_iota(jnp.int32, (8, FEATURES), 0)
    place = lax.broadcasted_iota(jnp.int32, (8, FEATURES), 1)
    half = (place >= OWN).astype(jnp.int32)
    place = place - OWN * half
    k = jnp.right_shift(place, 6)
    feature = 3 * (half * THIRD + place - THIRD * k) + k
    return (jnp.right_shift(feature, 7) == group).astype(jnp.float32).astype(jnp.bfloat16)


def hidden_members():
    group = lax.broadcasted_iota(jnp.int32, (8, HIDDEN), 0)
    unit = lax.broadcasted_iota(jnp.int32, (8, HIDDEN), 1)
    return (jnp.right_shift(unit, 7) == group).astype(jnp.float32).astype(jnp.bfloat16)


def folded(products):
    return products[0:8] + products[8:16]


def row_groups(pair, part, weight_of, weight_grad, sums, totals):
    weighted = [jnp.zeros((8, HIDDEN), jnp.float32)] * 3
    for start in range(0, WORDS, 16):
        for k in range(3):
            row = k * THIRD + start % THIRD
            weight = weight_of[part * 2 + start // THIRD, pair, row : row + 16, :].astype(jnp.float32)
            product = weight * weight_grad[shard_row(k, start) : shard_row(k, start) + 16, :]
            first, last = (3 * start + k) // 128, (3 * (start + 15) + k) // 128
            if first == last:
                weighted[first] = weighted[first] + folded(product)
            else:
                low = start + lax.broadcasted_iota(jnp.int32, (16, 1), 0) < first_word(k, last)
                low_product = jnp.where(low, product, 0.0)
                weighted[first] = weighted[first] + folded(low_product)
                weighted[last] = weighted[last] + folded(product - low_product)
    for g in range(3):
        row = pl.ds(3 * (pair * 2 + part) + g, 1)
        sums[row, :] = jnp.sum(weighted[g], axis=0, keepdims=True)
        totals[row, :] = (
            weight_grad[FEATURES + g : FEATURES + g + 1, :] + weight_grad[FEATURES + 8 + g : FEATURES + 9 + g, :]
        )


SLAB = 8 * OWN


def position():
    return tuple(lax.axis_index(axis) for axis in ("x", "y_lo", "z"))


def swapped_with(here, near):
    place = 3 - here if near // 2 else here
    return place + 1 - 2 * (place % 2) if near % 2 else place


def lay_tokens(place, source, far, to):
    x, y, z = place
    slab = (z + 4 - far) % 4
    for near in range(4):
        for dy in range(2):
            to[slab, swapped_with(x, near) * 2 + (y + dy) % 2, :, :] = source[near * 2 + dy]
    return slab


def lay_grad(place, source, far, to):
    x, y, z = place
    slab = (x + 4 - far) % 4
    for near in range(4):
        z_from = swapped_with(z, near)
        for dy in range(2):
            for k in range(3):
                row = pl.multiple_of((z_from // 2) * FEATURES + k * WORDS + (z_from % 2) * THIRD, THIRD)
                to[slab * 2 + (y + dy) % 2, pl.ds(row, THIRD), :] = source[
                    near * 2 + dy, k * THIRD : (k + 1) * THIRD, :
                ]
    return slab


def pair_out(slab, grad_from, grad_hbm, sems):
    pairs = pl.ds(slab * 2, 2)
    return pltpu.make_async_copy(grad_from.at[pairs], grad_hbm.at[pairs], sems)


def slab_products(fars, tokens_refs, grad_refs, weights, scratch, grad_hbm, totals):
    gate_ref, up_ref, down_ref = weights
    tokens_to, grad_to, grad_sems = scratch
    place = position()
    gate_pre, up_pre, hidden_grad = totals
    copies, laid = [], []
    for i, far in enumerate(fars):
        slabs = lay_tokens(place, tokens_refs[i], far, tokens_to), lay_grad(place, grad_refs[i], far, grad_to)
        copies.append(pair_out(slabs[1], grad_to, grad_hbm, grad_sems.at[i]))
        laid.append(slabs)
    for copy in copies:
        copy.start()
    for slab, grad_slab in laid:
        features = tokens_to[slab].reshape(SLAB, LOCAL).T
        gate_pre += jnp.dot(features, gate_ref[slab].reshape(SLAB, HIDDEN), preferred_element_type=jnp.float32)
        up_pre += jnp.dot(features, up_ref[slab].reshape(SLAB, HIDDEN), preferred_element_type=jnp.float32)
        for dy in range(2):
            piece = grad_to[grad_slab * 2 + dy]
            hidden_grad += jnp.dot(down_ref[grad_slab * 2 + dy], piece, preferred_element_type=jnp.float32)
    return (gate_pre, up_pre, hidden_grad), copies


def forward_body(
    t0, t1, t3, o0, o1, o3, gate_ref, up_ref, down_ref,
    gate_pre_ref, up_pre_ref, hidden_grad_ref, grad_hbm,
    tokens_to, grad_to, grad_sems,
):
    zero = jnp.zeros((LOCAL, HIDDEN), jnp.float32)
    core = lax.axis_index("core")
    (gate_pre_ref[...], up_pre_ref[...], hidden_grad_ref[...]), copies = slab_products(
        (0, 1 + 2 * core, 3 - 2 * core), (t0, t1, t3), (o0, o1, o3), (gate_ref, up_ref, down_ref),
        (tokens_to, grad_to, grad_sems), grad_hbm,
        (zero, zero, jnp.zeros((HIDDEN, LOCAL), jnp.float32)),
    )
    for copy in copies:
        copy.wait()


TOKENS_SHAPE = (N_Z, N_X * N_Y, OWN, LOCAL)
GRAD_SHAPE = (N_X * N_Y, 2 * FEATURES, LOCAL)


def slab_scratch(slabs):
    return [
        pltpu.VMEM(TOKENS_SHAPE, jnp.bfloat16),
        pltpu.VMEM(GRAD_SHAPE, jnp.bfloat16),
        pltpu.SemaphoreType.DMA((slabs,)),
    ]


def forward(tokens_parts, grad_parts, gate, up, down):
    f32, bf16 = jnp.float32, jnp.bfloat16
    near = (0, 1, 3)
    return call(
        forward_body,
        (
            pltpu.VMEM((LOCAL, HIDDEN), f32),
            pltpu.VMEM((LOCAL, HIDDEN), f32),
            pltpu.VMEM((HIDDEN, LOCAL), f32),
            pltpu.HBM(GRAD_SHAPE, bf16),
        ),
        [VMEM] * 9,
        (VMEM,) * 3 + (ANY,),
        slab_scratch(3),
        flops=3 * 3 * 2 * 128 * 1536 * 512,
        traffic=18000000,
    )(
        *from_vmem(*[tokens_parts[far] for far in near], *[grad_parts[far] for far in near]),
        *from_vmem(gate, up, down),
    )


def backward_body(
    t0, t1, t2, t3, o2, gate_ref, up_ref, down_ref, gate_pre_ref, up_pre_ref, hidden_grad_ref, gate_log_hbm, up_log_hbm, grad_in,
    partial_hbm, grad_hbm, hidden_hbm, gate_groups_hbm, up_groups_hbm,
    tokens_to, grad_to, grad_sems, partial, partial_sems, gate_grad_ref, up_grad_ref, hidden_ref, small_sems,
    gate_even, up_even, gate_odd, up_odd, gate_groups, up_groups, gate_log, up_log, log_sems,
):
    logs = tables_in((gate_log_hbm, up_log_hbm), (gate_log, up_log), log_sems)
    (gate_pre, up_pre, hidden_grad), copies = slab_products(
        (2,), (t2,), (o2,), (gate_ref, up_ref, down_ref),
        (tokens_to, grad_to, grad_sems), grad_hbm,
        (gate_pre_ref[...], up_pre_ref[...], hidden_grad_ref[...]),
    )
    hidden_grad = hidden_grad.T
    sigmoid_gate = jax.nn.sigmoid(gate_pre)
    silu_gate = gate_pre * sigmoid_gate
    hidden = silu_gate * up_pre
    gate_grad = hidden_grad * up_pre * sigmoid_gate * (1.0 + gate_pre * (1.0 - sigmoid_gate))
    up_grad = hidden_grad * silu_gate
    gate_grad_ref[...] = gate_grad.astype(jnp.bfloat16)
    up_grad_ref[...] = up_grad.astype(jnp.bfloat16)
    hidden_ref[...] = hidden.T.astype(jnp.bfloat16)
    copies += tables_in((hidden_ref,), (hidden_hbm,), small_sems)
    gate_turned = gate_grad.T.astype(jnp.bfloat16)
    up_turned = up_grad.T.astype(jnp.bfloat16)
    for slab in range(N_Z):
        total = jnp.dot(gate_ref[slab].reshape(SLAB, HIDDEN), gate_turned, preferred_element_type=jnp.float32)
        total += jnp.dot(up_ref[slab].reshape(SLAB, HIDDEN), up_turned, preferred_element_type=jnp.float32)
        partial[slab] = total.astype(jnp.bfloat16).reshape(N_X * N_Y, OWN, LOCAL)
        copy = pltpu.make_async_copy(partial.at[slab], partial_hbm.at[:, slab], partial_sems.at[slab])
        copy.start()
        copies.append(copy)
    core = lax.axis_index("core")
    for far, source in ((0, t0), (1 + 2 * core, t1), (3 - 2 * core, t3)):
        lay_tokens(position(), source, far, tokens_to)
    members = block_members()

    def products(pair, part, gate_to, up_to):
        features = jnp.concatenate([tokens_to[part * 2 + half, pair] for half in range(2)], axis=0)
        features = with_sums(features, members)
        gate_to[...] = jnp.dot(features, gate_grad_ref[...], preferred_element_type=jnp.float32)
        up_to[...] = jnp.dot(features, up_grad_ref[...], preferred_element_type=jnp.float32)

    def groups(pair, part, gate_from, up_from):
        row_groups(pair, part, gate_ref, gate_from, gate_groups.at[0], gate_groups.at[1])
        row_groups(pair, part, up_ref, up_from, up_groups.at[0], up_groups.at[1])

    products(0, 0, gate_even, up_even)

    def pair_step(pair, carry):
        products(pair, 1, gate_odd, up_odd)
        groups(pair, 0, gate_even, up_even)
        products(jnp.minimum(pair + 1, BLOCKS // 2 - 1), 0, gate_even, up_even)
        groups(pair, 1, gate_odd, up_odd)
        return carry

    lax.fori_loop(0, BLOCKS // 2, pair_step, 0)
    for log in logs:
        log.wait()
    for results, log_ref in ((gate_groups, gate_log), (up_groups, up_log)):
        results[1] = -jnp.exp(log_ref[...]) * results[1]
    copies += tables_in((gate_groups, up_groups), (gate_groups_hbm, up_groups_hbm), small_sems.at[pl.ds(1, 2)])
    for copy in copies:
        copy.wait()


def backward(tokens_parts, grad_parts, gate, up, down, sums, gate_log, up_log, all_grad):
    bf16 = jnp.bfloat16
    return call(
        backward_body,
        (
            pltpu.HBM((N_X * N_Y, N_Z, OWN, LOCAL), bf16),
            pltpu.HBM(GRAD_SHAPE, bf16),
            pltpu.HBM((HIDDEN, LOCAL), bf16),
            pltpu.HBM((2, 48, HIDDEN), jnp.float32),
            pltpu.HBM((2, 48, HIDDEN), jnp.float32),
        ),
        [VMEM] * 11 + [ANY] * 3,
        (ANY,) * 5,
        slab_scratch(1)
        + [
            pltpu.VMEM(TOKENS_SHAPE, bf16),
            pltpu.SemaphoreType.DMA((N_Z,)),
            pltpu.VMEM((LOCAL, HIDDEN), bf16),
            pltpu.VMEM((LOCAL, HIDDEN), bf16),
            pltpu.VMEM((HIDDEN, LOCAL), bf16),
            pltpu.SemaphoreType.DMA((3,)),
        ]
        + [pltpu.VMEM((FEATURES + EXTRA, HIDDEN), jnp.float32)] * 4
        + [pltpu.VMEM((2, 48, HIDDEN), jnp.float32)] * 2
        + [pltpu.VMEM((48, HIDDEN), jnp.float32)] * 2
        + [pltpu.SemaphoreType.DMA((2,))],
        flops=5 * 2 * 128 * 6144 * 512,
        traffic=24000000,
        aliases={13: 1},
    )(
        *from_vmem(*tokens_parts, grad_parts[2], gate, up, down, *sums),
        *from_hbm(gate_log, up_log, all_grad),
    )


MASKS = (15, 240, 3840)
SHRINK = (1.0, 1.0 / 16.0, 1.0 / 256.0)


def in_place(words, k):
    return jnp.bitwise_and(words, MASKS[k]).astype(jnp.float32)


def column_groups(pair, part, codes, weight_grad, raw):
    here = pl.ds(pl.multiple_of(8 * (pair * 2 + part), 8), 8)
    mine = slice(part * FEATURES, (part + 1) * FEATURES)
    totals = weight_grad[HIDDEN : HIDDEN + 4, mine] + weight_grad[HIDDEN + 8 : HIDDEN + 12, mine]
    for k in range(3):
        sums = []
        for g in range(4):
            weighted = jnp.zeros((8, WORDS), jnp.float32)
            for start in range(g * 128, g * 128 + 128, 8):
                words = codes[start : start + 8, pl.ds(pl.multiple_of((pair * 2 + part) * WORDS, WORDS), WORDS)]
                value = weight_grad[start : start + 8, part * FEATURES + k * WORDS : part * FEATURES + (k + 1) * WORDS]
                weighted = weighted + in_place(words, k) * value
            sums.append(jnp.sum(weighted, axis=0, keepdims=True))
        columns = slice(k * WORDS, (k + 1) * WORDS)
        raw[here, columns] = jnp.concatenate([jnp.concatenate(sums, axis=0) * SHRINK[k], totals[:, columns]], axis=0)


def group_body(
    down_hbm, grad_hbm, hidden_hbm, table_hbm, gate_groups_hbm, up_groups_hbm,
    own_ref, given_ref,
    down_codes, down_sems, grad_ref, grad_sems, hidden_ref, table_ref, gate_groups, up_groups, small_sems,
    hidden_rows, down_even, down_odd, raw, halves,
):
    def grad_in(pair):
        return pltpu.make_async_copy(grad_hbm.at[pair], grad_ref.at[pair], grad_sems.at[pair])

    def codes_in(chunk):
        return column_copy(chunk, down_hbm, down_codes, down_sems)

    hidden_in, *later = tables_in(
        (hidden_hbm, table_hbm, gate_groups_hbm, up_groups_hbm), (hidden_ref, table_ref, gate_groups, up_groups), small_sems
    )
    for pair in range(2):
        grad_in(pair).start()
        codes_in(pair).start()
    for pair in range(2, BLOCKS // 2):
        grad_in(pair).start()
    codes_in(2).start()
    hidden_in.wait()
    hidden_rows[...] = with_sums(hidden_ref[...], hidden_members())

    def products(pair, to):
        to[...] = lax.dot_general(hidden_rows[...], grad_ref[pair], CONTRACT_LAST, preferred_element_type=jnp.float32)

    def groups(pair, weight_grad):
        for part in range(2):
            column_groups(pair, part, down_codes, weight_grad, raw)

    grad_in(0).wait()
    products(0, down_even)

    def two_pairs(step, carry):
        pair = step * 2
        following = jnp.minimum(pair + 2, BLOCKS // 2 - 1)
        for near in range(2):
            codes_in(pair + near).wait()
        grad_in(pair + 1).wait()

        @pl.when(pair + 2 < BLOCKS // 2)
        def _():
            grad_in(following).wait()

        @pl.when(step == 0)
        def _():
            codes_in(3).start()

        @pl.when(step == 1)
        def _():
            for chunk in range(6, 8):
                codes_in(chunk).start()

        @pl.when(step == 0)
        def _():
            for chunk in range(4, 6):
                codes_in(chunk).start()

        products(pair + 1, down_odd)
        groups(pair, down_even)
        products(following, down_even)
        groups(pair + 1, down_odd)
        return carry

    lax.fori_loop(0, BLOCKS // 4, two_pairs, 0)
    for copy in later:
        copy.wait()
    found, table = raw[...].reshape(BLOCKS, 8, FEATURES), table_ref[...].reshape(BLOCKS, 8, FEATURES)
    sums, totals, zero, scale = found[:, 0:4], found[:, 4:8], table[:, 0:4], table[:, 4:8]
    down_rows = jnp.concatenate([scale * (sums - zero * totals), -scale * totals], axis=1)
    raw[...] = down_rows.reshape(8 * BLOCKS, FEATURES)
    for half, begin, results in ((0, 0, gate_groups), (1, 48, up_groups)):
        halves[half, 0:48] = results[0]
        halves[half, 48:96] = results[1]
        for j in range(3):
            halves[half, 96:144, j * 128 : (j + 1) * 128] = raw[begin : begin + 48, j * 128 : (j + 1) * 128]
    halves[0, 96:128, 384:] = raw[96:128, 0:128]
    halves[0, 128:144, 384:] = raw[96:112, 128:256]
    halves[1, 96:112, 384:] = raw[112:128, 128:256]
    halves[1, 112:144, 384:] = raw[96:128, 256:384]
    core = lax.axis_index("core")
    own_ref[...] = halves[core]
    given_ref[...] = halves[1 - core]


def group_grads(down_codes, grad, hidden, table, gate_groups, up_groups):
    f32, bf16 = jnp.float32, jnp.bfloat16
    half = struct((144, HIDDEN), f32)
    columns = (HIDDEN + EXTRA, 2 * FEATURES)
    return call(
        group_body,
        (half, half),
        [ANY] * 6,
        (VMEM, VMEM),
        [
            pltpu.VMEM((HIDDEN, BLOCKS * WORDS), jnp.int32),
            pltpu.SemaphoreType.DMA((CHUNKS,)),
            pltpu.VMEM(GRAD_SHAPE, bf16),
            pltpu.SemaphoreType.DMA((BLOCKS // 2,)),
            pltpu.VMEM((HIDDEN, LOCAL), bf16),
            pltpu.VMEM((8 * BLOCKS, FEATURES), f32),
            pltpu.VMEM((2, 48, HIDDEN), f32),
            pltpu.VMEM((2, 48, HIDDEN), f32),
            pltpu.SemaphoreType.DMA((4,)),
            pltpu.VMEM((HIDDEN + EXTRA, LOCAL), bf16),
            pltpu.VMEM(columns, f32),
            pltpu.VMEM(columns, f32),
            pltpu.VMEM((8 * BLOCKS, FEATURES), f32),
            pltpu.VMEM((2, 144, HIDDEN), f32),
        ],
        flops=2 * 128 * 6144 * 512,
        traffic=7000000,
        vmem=24,
    )(*from_hbm(down_codes, grad, hidden, table, gate_groups, up_groups))


def finish_body(mine_ref, other_ref, parts_ref, tokens_grad_ref, gs_ref, gz_ref, us_ref, uz_ref, ds_ref, dz_ref, halves, rows):
    core = lax.axis_index("core")
    halves[core] = mine_ref[...]
    halves[1 - core] = other_ref[...]
    for half, scale_ref, zero_ref in ((0, gs_ref, gz_ref), (1, us_ref, uz_ref)):
        scale_ref[...] = halves[half, 0:48, :]
        zero_ref[...] = halves[half, 48:96, :]
        for j in range(3):
            rows[48 * half : 48 * half + 48, j * 128 : (j + 1) * 128] = halves[half, 96:144, j * 128 : (j + 1) * 128]
    rows[96:128, 0:128] = halves[0, 96:128, 384:]
    rows[96:112, 128:256] = halves[0, 128:144, 384:]
    rows[112:128, 128:256] = halves[1, 96:112, 384:]
    rows[96:128, 256:384] = halves[1, 112:144, 384:]
    natural = reorder(rows[...], True)
    for b in range(BLOCKS):
        columns = slice(b * FEATURES, (b + 1) * FEATURES)
        ds_ref[:, columns] = natural[8 * b : 8 * b + 4, :]
        dz_ref[:, columns] = natural[8 * b + 4 : 8 * b + 8, :]
    total = parts_ref[0].astype(jnp.float32)
    for part in range(1, SHARDS):
        total = total + parts_ref[part].astype(jnp.float32)
    for k in range(3):
        tokens_grad_ref[pl.ds(k, THIRD, stride=3), :] = total[k * THIRD : (k + 1) * THIRD, :]


def finish(mine, other, parts):
    f32 = jnp.float32
    return call(
        finish_body,
        (struct((OWN, LOCAL), f32),)
        + (struct((48, HIDDEN), f32),) * 4
        + (struct((4, BLOCKS * FEATURES), f32),) * 2,
        [VMEM] * 3,
        (VMEM,) * 7,
        [pltpu.VMEM((2, 144, HIDDEN), f32), pltpu.VMEM((8 * BLOCKS, FEATURES), f32)],
        traffic=2900000,
    )(mine, other, parts)


NEAR, ACROSS = ((0, 1), (2, 3)), ((0, 3), (1, 2))


def paired(block, axis, pairs):
    other = lax.ppermute(block, axis, [pair for a, b in pairs for pair in ((a, b), (b, a))])
    return jnp.concatenate([block, other])


def turned(block, axis, way):
    pairs = [(place, (place + way) % 4) for place in range(4)]
    pairs += [(4 + place, 4 + (place - way) % 4) for place in range(4)]
    return lax.ppermute(block, ("core", axis), pairs)


def swap(value, axis):
    return lax.ppermute(value, axis, [(0, 1), (1, 0)])


def shards(
    tokens,
    out_grad,
    gate_codes,
    gate_zeros,
    gate_log_scale,
    up_codes,
    up_zeros,
    up_log_scale,
    down_codes,
    down_zeros,
    down_log_scale,
):
    tokens_near, grad_near = by_field(tokens, out_grad)
    tokens_near, grad_near = paired(tokens_near, "y_lo", ((0, 1),)), paired(grad_near, "y_lo", ((0, 1),))
    tokens_near, grad_near = paired(tokens_near, "x", NEAR), paired(grad_near, "z", NEAR)
    tokens_near, gate_zeros = lax.optimization_barrier((tokens_near, gate_zeros))
    tokens_near, grad_near = paired(tokens_near, "x", ACROSS), paired(grad_near, "z", ACROSS)
    gate = unpack_rows(gate_codes, gate_zeros, gate_log_scale)
    tokens_near, gate, up_zeros = lax.optimization_barrier((tokens_near, gate, up_zeros))
    grad_near, up_log_scale = lax.optimization_barrier((grad_near, up_log_scale))
    tokens_first, grad_first = turned(tokens_near, "z", 1), turned(grad_near, "x", 1)
    tokens_second, grad_second = turned(tokens_near, "z", -1), turned(grad_near, "x", -1)
    up = unpack_rows(up_codes, up_zeros, up_log_scale)
    tokens_first, grad_first, up, down_zeros = lax.optimization_barrier((tokens_first, grad_first, up, down_zeros))
    tokens_parts = tokens_near, tokens_first, turned(tokens_first, "z", 1), tokens_second
    grad_parts = grad_near, grad_first, turned(grad_first, "x", 1), grad_second
    down, table = unpack_columns(down_codes, down_zeros, down_log_scale)
    *sums, all_grad = forward(tokens_parts, grad_parts, gate, up, down)
    partial, all_grad, hidden, gate_groups, up_groups = backward(
        tokens_parts, grad_parts, gate, up, down, sums, gate_log_scale, up_log_scale, all_grad
    )
    parts = lax.all_to_all(partial.reshape(SHARDS, OWN, LOCAL), ("x", "y_lo", "z"), 0, 0, tiled=True)
    own, given = group_grads(down_codes, all_grad, hidden, table, gate_groups, up_groups)
    own = own + swap(given, "core")
    own = own.astype(jnp.bfloat16)
    mine = own.astype(jnp.float32) + swap(own, "y_hi").astype(jnp.float32)
    tokens_grad, *group_results = finish(mine, swap(mine, "core"), parts)
    return (tokens_grad.T, *group_results)


def solution(mesh):
    axes = jax.sharding.Mesh(mesh.devices.reshape(2, 2, N_X, N_Y, N_Z), ("y_hi", "core", "x", "y_lo", "z"))
    dp, tensor = ("y_hi", "core"), ("x", "y_lo", "z")
    columns, rows = P(None, tensor), P(tensor, None)
    return jax.shard_map(
        shards,
        mesh=axes,
        in_specs=(P(dp, tensor),) * 2 + (columns,) * 6 + (rows,) * 3,
        out_specs=(P(dp, tensor),) + (columns,) * 4 + (rows,) * 2,
        check_vma=False,
    )
```

```python
import jax
import jax.numpy as jnp
from jax import lax
from jax.experimental import pallas as pl
from jax.experimental.pallas import tpu as pltpu
from jax.sharding import PartitionSpec as P

N_X, N_Y, N_Z = 4, 2, 4
SHARDS = 32
OWN = 192
THIRD = 64
BLOCKS = 16
WORDS = 128
FEATURES = 384
HIDDEN = 512
LOCAL = 128
MIB = 1 << 20

CONTRACT_LAST = (((1,), (1,)), ((), ()))
CONTRACT_FIRST = (((0,), (0,)), ((), ()))


def shard_row(k, word):
    return (word // THIRD) * OWN + k * THIRD + word % THIRD


def first_word(k, group):
    return -((k - 128 * group) // 3)


def spread_over_groups(k, start, rows, values):
    first, last = (3 * start + k) // 128, (3 * (start + rows - 1) + k) // 128
    if first == last:
        return values[first]
    row = start + lax.broadcasted_iota(jnp.int32, (rows, 1), 0)
    return jnp.where(row < first_word(k, last), values[first], values[last])


def call(body, out_shape, in_specs, out_specs, scratch=(), flops=0, traffic=0, vmem=16, aliases=None):
    return pl.pallas_call(
        body,
        out_shape=out_shape,
        in_specs=in_specs,
        out_specs=out_specs,
        scratch_shapes=list(scratch),
        input_output_aliases=aliases or {},
        compiler_params=pltpu.CompilerParams(vmem_limit_bytes=vmem * MIB),
        cost_estimate=pl.CostEstimate(flops=flops, bytes_accessed=traffic, transcendentals=0),
    )


def struct(shape, dtype):
    return jax.ShapeDtypeStruct(shape, dtype)


def from_hbm(*arrays):
    return [pltpu.with_memory_space_constraint(array, pltpu.HBM) for array in arrays]


def from_vmem(*arrays):
    return [pltpu.with_memory_space_constraint(array, pltpu.VMEM) for array in arrays]


VMEM = pl.BlockSpec(memory_space=pltpu.VMEM)
ANY = pl.BlockSpec(memory_space=pl.ANY)


def by_field_body(tokens_ref, grad_ref, tokens_out, grad_out, wide):
    for ref, out_ref in ((tokens_ref, tokens_out), (grad_ref, grad_out)):
        wide[...] = ref[...].astype(jnp.float32)
        for k in range(3):
            out_ref[0, k * THIRD : (k + 1) * THIRD, :] = wide[pl.ds(k, THIRD, stride=3), :].astype(jnp.bfloat16)


def by_field(tokens, out_grad):
    return call(
        by_field_body,
        (struct((1, OWN, LOCAL), jnp.bfloat16),) * 2,
        [VMEM, VMEM],
        (VMEM, VMEM),
        [pltpu.VMEM((OWN, LOCAL), jnp.float32)],
        traffic=200000,
    )(*from_hbm(tokens.T, out_grad.T))


def field(words, k):
    if k:
        words = jnp.right_shift(words, 4 * k)
    if k < 2:
        words = jnp.bitwise_and(words, 15)
    return words.astype(jnp.float32)


CHUNKS = 8
AHEAD = 3


def row_copy(chunk, source, to, sems):
    rows = pl.ds(pl.multiple_of(chunk * 2 * WORDS, 2 * WORDS), 2 * WORDS)
    return pltpu.make_async_copy(source.at[rows], to.at[rows], sems.at[chunk])


def column_copy(chunk, source, to, sems):
    columns = pl.ds(pl.multiple_of(chunk * 2 * WORDS, 2 * WORDS), 2 * WORDS)
    return pltpu.make_async_copy(source.at[:, columns], to.at[:, columns], sems.at[chunk])


def tables_in(sources, targets, sems):
    copies = [pltpu.make_async_copy(a, b, sems.at[i]) for i, (a, b) in enumerate(zip(sources, targets))]
    for copy in copies:
        copy.start()
    return copies


def unpack_rows_pair(pair, codes, zeros_ref, log_ref, out_ref):
    for part in range(2):
        block = pair * 2 + part
        zeros = [zeros_ref[pl.ds(3 * block + g, 1), :].astype(jnp.float32) for g in range(3)]
        scales = [jnp.exp(log_ref[pl.ds(3 * block + g, 1), :]) for g in range(3)]
        for start in range(0, WORDS, 16):
            words = codes[pl.ds(pl.multiple_of(block * WORDS + start, 16), 16), :]
            for k in range(3):
                zero = spread_over_groups(k, start, 16, zeros)
                scale = spread_over_groups(k, start, 16, scales)
                weight = (scale * (field(words, k) - zero)).astype(jnp.bfloat16)
                row = k * THIRD + start % THIRD
                out_ref[part * 2 + start // THIRD, pair, row : row + 16, :] = weight


def streamed(copy_of, source, to, sems, work):
    def step(chunk, carry):
        copy_of(chunk, source, to, sems).wait()

        @pl.when(chunk + AHEAD < CHUNKS)
        def _():
            copy_of(chunk + AHEAD, source, to, sems).start()

        work(chunk)
        return carry

    lax.fori_loop(0, CHUNKS, step, 0)


def start_first(copy_of, source, to, sems):
    for chunk in range(AHEAD):
        copy_of(chunk, source, to, sems).start()


def unpack_rows_body(codes_hbm, zeros_hbm, log_hbm, out_ref, zeros_ref, log_ref, table_sems, codes, sems):
    tables = tables_in((zeros_hbm, log_hbm), (zeros_ref, log_ref), table_sems)
    start_first(row_copy, codes_hbm, codes, sems)
    for table in tables:
        table.wait()
    streamed(
        row_copy, codes_hbm, codes, sems, lambda pair: unpack_rows_pair(pair, codes, zeros_ref, log_ref, out_ref)
    )


def unpack_rows(codes, zeros, log_scale):
    return call(
        unpack_rows_body,
        pltpu.VMEM((N_Z, N_X * N_Y, OWN, HIDDEN), jnp.bfloat16),
        [ANY] * 3,
        VMEM,
        [
            pltpu.VMEM((48, HIDDEN), jnp.int32),
            pltpu.VMEM((48, HIDDEN), jnp.float32),
            pltpu.SemaphoreType.DMA((2,)),
            pltpu.VMEM((BLOCKS * WORDS, HIDDEN), jnp.int32),
            pltpu.SemaphoreType.DMA((CHUNKS,)),
        ],
        flops=20000000,
        traffic=10500000,
    )(*from_hbm(codes, zeros, log_scale))


def field_order(transposed):
    feature = lax.broadcasted_iota(jnp.int32, (FEATURES, FEATURES), 1 if transposed else 0)
    column = lax.broadcasted_iota(jnp.int32, (FEATURES, FEATURES), 0 if transposed else 1)
    wanted = 3 * jnp.bitwise_and(column, 127) + jnp.right_shift(column, 7)
    return (feature == wanted).astype(jnp.float32)


def reorder(rows, transposed):
    return jnp.dot(
        rows, field_order(transposed), precision=lax.Precision.HIGHEST, preferred_element_type=jnp.float32
    )


def unpack_columns_pair(pair, codes, table_ref, out_ref):
    for part in range(2):
        block = pair * 2 + part
        table = table_ref[pl.ds(pl.multiple_of(8 * block, 8), 8), :]
        for g in range(4):
            words = codes[g * 128 : (g + 1) * 128, pl.ds(pl.multiple_of(block * WORDS, WORDS), WORDS)]
            for k in range(3):
                columns = slice(k * WORDS, (k + 1) * WORDS)
                zero, scale = table[g : g + 1, columns], table[4 + g : 5 + g, columns]
                weight = (scale * (field(words, k) - zero)).astype(jnp.bfloat16)
                to = slice(part * FEATURES + k * WORDS, part * FEATURES + (k + 1) * WORDS)
                out_ref[pair, g * 128 : (g + 1) * 128, to] = weight


def unpack_columns_body(
    codes_hbm, zeros_hbm, log_hbm, out_ref, table_ref, zeros_ref, log_ref, table_sems, natural, codes, sems
):
    tables = tables_in((zeros_hbm, log_hbm), (zeros_ref, log_ref), table_sems)
    start_first(column_copy, codes_hbm, codes, sems)
    for table in tables:
        table.wait()
    for b in range(BLOCKS):
        columns = slice(b * FEATURES, (b + 1) * FEATURES)
        natural[8 * b : 8 * b + 4, :] = zeros_ref[:, columns].astype(jnp.float32)
        natural[8 * b + 4 : 8 * b + 8, :] = jnp.exp(log_ref[:, columns])
    table_ref[...] = reorder(natural[...], False)
    streamed(column_copy, codes_hbm, codes, sems, lambda pair: unpack_columns_pair(pair, codes, table_ref, out_ref))


def unpack_columns(codes, zeros, log_scale):
    wide = (4, BLOCKS * FEATURES)
    return call(
        unpack_columns_body,
        (
            pltpu.VMEM((N_X * N_Y, HIDDEN, 2 * FEATURES), jnp.bfloat16),
            pltpu.HBM((8 * BLOCKS, FEATURES), jnp.float32),
        ),
        [ANY] * 3,
        (VMEM,) * 2,
        [
            pltpu.VMEM(wide, jnp.int32),
            pltpu.VMEM(wide, jnp.float32),
            pltpu.SemaphoreType.DMA((2,)),
            pltpu.VMEM((8 * BLOCKS, FEATURES), jnp.float32),
            pltpu.VMEM((HIDDEN, BLOCKS * WORDS), jnp.int32),
            pltpu.SemaphoreType.DMA((CHUNKS,)),
        ],
        flops=20000000,
        traffic=10500000,
    )(*from_hbm(codes, zeros, log_scale))


SLAB = 8 * OWN


def position():
    return tuple(lax.axis_index(axis) for axis in ("x", "y_lo", "z"))


def swapped_with(here, near):
    place = 3 - here if near // 2 else here
    return place + 1 - 2 * (place % 2) if near % 2 else place


def lay_tokens(place, source, far, to):
    x, y, z = place
    slab = (z + 4 - far) % 4
    for near in range(4):
        for dy in range(2):
            to[slab, swapped_with(x, near) * 2 + (y + dy) % 2, :, :] = source[near * 2 + dy]
    return slab


def lay_grad(place, source, far, to):
    x, y, z = place
    slab = (x + 4 - far) % 4
    for near in range(4):
        z_from = swapped_with(z, near)
        for dy in range(2):
            for k in range(3):
                row = pl.multiple_of((z_from // 2) * FEATURES + k * WORDS + (z_from % 2) * THIRD, THIRD)
                to[slab * 2 + (y + dy) % 2, pl.ds(row, THIRD), :] = source[
                    near * 2 + dy, k * THIRD : (k + 1) * THIRD, :
                ]
    return slab


def slab_out(slab, tokens_from, tokens_hbm, sems):
    return pltpu.make_async_copy(tokens_from.at[slab], tokens_hbm.at[slab], sems)


def pair_out(slab, grad_from, grad_hbm, sems):
    pairs = pl.ds(slab * 2, 2)
    return pltpu.make_async_copy(grad_from.at[pairs], grad_hbm.at[pairs], sems)


def slab_products(fars, tokens_refs, grad_refs, weights, scratch, hbm, totals):
    gate_ref, up_ref, down_ref = weights
    tokens_to, grad_to, tokens_sems, grad_sems = scratch
    tokens_hbm, grad_hbm = hbm
    place = position()
    gate_pre, up_pre, hidden_grad = totals
    copies, laid = [], []
    for i, far in enumerate(fars):
        slabs = lay_tokens(place, tokens_refs[i], far, tokens_to), lay_grad(place, grad_refs[i], far, grad_to)
        copies.append(slab_out(slabs[0], tokens_to, tokens_hbm, tokens_sems.at[i]))
        copies.append(pair_out(slabs[1], grad_to, grad_hbm, grad_sems.at[i]))
        laid.append(slabs)
    for copy in copies:
        copy.start()
    for slab, grad_slab in laid:
        features = tokens_to[slab].reshape(SLAB, LOCAL).T
        gate_pre += jnp.dot(features, gate_ref[slab].reshape(SLAB, HIDDEN), preferred_element_type=jnp.float32)
        up_pre += jnp.dot(features, up_ref[slab].reshape(SLAB, HIDDEN), preferred_element_type=jnp.float32)
        for dy in range(2):
            piece = grad_to[grad_slab * 2 + dy]
            hidden_grad += jnp.dot(down_ref[grad_slab * 2 + dy], piece, preferred_element_type=jnp.float32)
    return (gate_pre, up_pre, hidden_grad), copies


def forward_body(
    t0, t1, t3, o0, o1, o3, gate_ref, up_ref, down_ref,
    gate_pre_ref, up_pre_ref, hidden_grad_ref, tokens_hbm, grad_hbm,
    tokens_to, grad_to, tokens_sems, grad_sems,
):
    zero = jnp.zeros((LOCAL, HIDDEN), jnp.float32)
    core = lax.axis_index("core")
    (gate_pre_ref[...], up_pre_ref[...], hidden_grad_ref[...]), copies = slab_products(
        (0, 1 + 2 * core, 3 - 2 * core), (t0, t1, t3), (o0, o1, o3), (gate_ref, up_ref, down_ref),
        (tokens_to, grad_to, tokens_sems, grad_sems), (tokens_hbm, grad_hbm),
        (zero, zero, jnp.zeros((HIDDEN, LOCAL), jnp.float32)),
    )
    for copy in copies:
        copy.wait()


TOKENS_SHAPE = (N_Z, N_X * N_Y, OWN, LOCAL)
GRAD_SHAPE = (N_X * N_Y, 2 * FEATURES, LOCAL)


def slab_scratch(slabs):
    return [
        pltpu.VMEM(TOKENS_SHAPE, jnp.bfloat16),
        pltpu.VMEM(GRAD_SHAPE, jnp.bfloat16),
        pltpu.SemaphoreType.DMA((slabs,)),
        pltpu.SemaphoreType.DMA((slabs,)),
    ]


def forward(tokens_parts, grad_parts, gate, up, down):
    f32, bf16 = jnp.float32, jnp.bfloat16
    near = (0, 1, 3)
    return call(
        forward_body,
        (
            pltpu.VMEM((LOCAL, HIDDEN), f32),
            pltpu.VMEM((LOCAL, HIDDEN), f32),
            pltpu.VMEM((HIDDEN, LOCAL), f32),
            pltpu.HBM(TOKENS_SHAPE, bf16),
            pltpu.HBM(GRAD_SHAPE, bf16),
        ),
        [VMEM] * 9,
        (VMEM,) * 3 + (ANY,) * 2,
        slab_scratch(3),
        flops=3 * 3 * 2 * 128 * 1536 * 512,
        traffic=18000000,
    )(
        *from_vmem(*[tokens_parts[far] for far in near], *[grad_parts[far] for far in near]),
        *from_vmem(gate, up, down),
    )


def backward_body(
    t2, o2, gate_ref, up_ref, down_ref, gate_pre_ref, up_pre_ref, hidden_grad_ref, tokens_in, grad_in,
    partial_hbm, tokens_hbm, grad_hbm, gate_grad_hbm, up_grad_hbm, hidden_hbm,
    tokens_to, grad_to, tokens_sems, grad_sems, partial, partial_sems, gate_grad_ref, up_grad_ref, hidden_ref, small_sems,
):
    (gate_pre, up_pre, hidden_grad), copies = slab_products(
        (2,), (t2,), (o2,), (gate_ref, up_ref, down_ref),
        (tokens_to, grad_to, tokens_sems, grad_sems), (tokens_hbm, grad_hbm),
        (gate_pre_ref[...], up_pre_ref[...], hidden_grad_ref[...]),
    )
    hidden_grad = hidden_grad.T
    sigmoid_gate = jax.nn.sigmoid(gate_pre)
    silu_gate = gate_pre * sigmoid_gate
    hidden = silu_gate * up_pre
    gate_grad = hidden_grad * up_pre * sigmoid_gate * (1.0 + gate_pre * (1.0 - sigmoid_gate))
    up_grad = hidden_grad * silu_gate
    gate_grad_ref[...] = gate_grad.astype(jnp.bfloat16)
    up_grad_ref[...] = up_grad.astype(jnp.bfloat16)
    hidden_ref[...] = hidden.T.astype(jnp.bfloat16)
    copies += tables_in(
        (gate_grad_ref, up_grad_ref, hidden_ref), (gate_grad_hbm, up_grad_hbm, hidden_hbm), small_sems
    )
    gate_turned = gate_grad.T.astype(jnp.bfloat16)
    up_turned = up_grad.T.astype(jnp.bfloat16)
    for slab in range(N_Z):
        total = jnp.dot(gate_ref[slab].reshape(SLAB, HIDDEN), gate_turned, preferred_element_type=jnp.float32)
        total += jnp.dot(up_ref[slab].reshape(SLAB, HIDDEN), up_turned, preferred_element_type=jnp.float32)
        partial[slab] = total.astype(jnp.bfloat16).reshape(N_X, N_Y, OWN, LOCAL)
        copy = pltpu.make_async_copy(partial.at[slab], partial_hbm.at[:, slab], partial_sems.at[slab])
        copy.start()
        copies.append(copy)
    for copy in copies:
        copy.wait()


def backward(tokens_parts, grad_parts, gate, up, down, sums, all_tokens, all_grad):
    bf16 = jnp.bfloat16
    return call(
        backward_body,
        (
            pltpu.HBM((N_X, N_Z, N_Y, OWN, LOCAL), bf16),
            pltpu.HBM(TOKENS_SHAPE, bf16),
            pltpu.HBM(GRAD_SHAPE, bf16),
            pltpu.HBM((LOCAL, HIDDEN), bf16),
            pltpu.HBM((LOCAL, HIDDEN), bf16),
            pltpu.HBM((HIDDEN, LOCAL), bf16),
        ),
        [VMEM] * 8 + [ANY] * 2,
        (ANY,) * 6,
        slab_scratch(1)
        + [
            pltpu.VMEM((N_Z, N_X, N_Y, OWN, LOCAL), bf16),
            pltpu.SemaphoreType.DMA((N_Z,)),
            pltpu.VMEM((LOCAL, HIDDEN), bf16),
            pltpu.VMEM((LOCAL, HIDDEN), bf16),
            pltpu.VMEM((HIDDEN, LOCAL), bf16),
            pltpu.SemaphoreType.DMA((3,)),
        ],
        flops=3 * 2 * 128 * 6144 * 512,
        traffic=24000000,
        aliases={8: 1, 9: 2},
    )(
        *from_vmem(tokens_parts[2], grad_parts[2], gate, up, down, *sums),
        *from_hbm(all_tokens, all_grad),
    )


EXTRA = 16


def with_sums(rows, members):
    sums = jnp.dot(members, rows, preferred_element_type=jnp.float32)
    head = sums.astype(jnp.bfloat16)
    rest = (sums - head.astype(jnp.float32)).astype(jnp.bfloat16)
    return jnp.concatenate([rows, jnp.concatenate([head, rest], axis=0)], axis=0)


def block_members():
    group = lax.broadcasted_iota(jnp.int32, (8, FEATURES), 0)
    place = lax.broadcasted_iota(jnp.int32, (8, FEATURES), 1)
    half = (place >= OWN).astype(jnp.int32)
    place = place - OWN * half
    k = jnp.right_shift(place, 6)
    feature = 3 * (half * THIRD + place - THIRD * k) + k
    scale = jnp.where(k == 0, 1.0, jnp.where(k == 1, 16.0, 256.0))
    return jnp.where(jnp.right_shift(feature, 7) == group, scale, 0.0).astype(jnp.bfloat16)


def hidden_members():
    group = lax.broadcasted_iota(jnp.int32, (8, HIDDEN), 0)
    unit = lax.broadcasted_iota(jnp.int32, (8, HIDDEN), 1)
    return (jnp.right_shift(unit, 7) == group).astype(jnp.float32).astype(jnp.bfloat16)


MASKS = (15, 240, 3840)
SHRINK = (1.0, 1.0 / 16.0, 1.0 / 256.0)


def in_place(words, k):
    return jnp.bitwise_and(words, MASKS[k]).astype(jnp.float32)


def in_turn(*streams):
    running = list(streams)
    while running:
        for stream in list(running):
            if next(stream, None) is None:
                running.remove(stream)


def row_groups(block, codes, weight_grad, sums, totals):
    weighted = [jnp.zeros((8, HIDDEN), jnp.float32)] * 3
    for start in range(0, WORDS, 8):
        words = codes[pl.ds(pl.multiple_of(block * WORDS + start, 8), 8), :]
        for k in range(3):
            product = in_place(words, k) * weight_grad[shard_row(k, start) : shard_row(k, start) + 8, :]
            first, last = (3 * start + k) // 128, (3 * (start + 7) + k) // 128
            if first == last:
                weighted[first] = weighted[first] + product
            else:
                low = start + lax.broadcasted_iota(jnp.int32, (8, 1), 0) < first_word(k, last)
                low_product = jnp.where(low, product, 0.0)
                weighted[first] = weighted[first] + low_product
                weighted[last] = weighted[last] + (product - low_product)
        yield True
    for g in range(3):
        row = pl.ds(3 * block + g, 1)
        sums[row, :] = jnp.sum(weighted[g], axis=0, keepdims=True)
        totals[row, :] = (
            weight_grad[FEATURES + g : FEATURES + g + 1, :] + weight_grad[FEATURES + 8 + g : FEATURES + 9 + g, :]
        )
    yield True


def column_groups(block, part, codes, weight_grad, raw):
    here = pl.ds(pl.multiple_of(8 * block, 8), 8)
    mine = slice(part * FEATURES, (part + 1) * FEATURES)
    totals = weight_grad[HIDDEN : HIDDEN + 4, mine] + weight_grad[HIDDEN + 8 : HIDDEN + 12, mine]
    for k in range(3):
        sums = []
        for g in range(4):
            weighted = jnp.zeros((8, WORDS), jnp.float32)
            for start in range(g * 128, g * 128 + 128, 8):
                words = codes[start : start + 8, pl.ds(pl.multiple_of(block * WORDS, WORDS), WORDS)]
                value = weight_grad[start : start + 8, part * FEATURES + k * WORDS : part * FEATURES + (k + 1) * WORDS]
                weighted = weighted + in_place(words, k) * value
            sums.append(jnp.sum(weighted, axis=0, keepdims=True))
            yield True
        columns = slice(k * WORDS, (k + 1) * WORDS)
        raw[here, columns] = jnp.concatenate([jnp.concatenate(sums, axis=0) * SHRINK[k], totals[:, columns]], axis=0)


def group_body(
    gate_hbm, up_hbm, down_hbm, tokens_hbm, grad_hbm, *small_hbm_and_rest
):
    small_hbm, rest = small_hbm_and_rest[:8], small_hbm_and_rest[8:]
    small, rest = rest[-8:], rest[:-8]
    group_work(gate_hbm, up_hbm, down_hbm, tokens_hbm, grad_hbm, small_hbm, small, *rest)


def group_work(
    gate_hbm, up_hbm, down_hbm, tokens_hbm, grad_hbm, small_hbm, small,
    own_ref, given_ref,
    gate_codes, up_codes, down_codes, gate_sems, up_sems, down_sems, tokens_ref, grad_ref, tokens_sems, grad_sems, small_sems,
    hidden_rows, gate_even, up_even, gate_odd, up_odd, down_pair, down_rows, halves, sums, totals,
):
    def copies(chunk):
        return (
            row_copy(chunk, gate_hbm, gate_codes, gate_sems),
            row_copy(chunk, up_hbm, up_codes, up_sems),
            column_copy(chunk, down_hbm, down_codes, down_sems),
        )

    def start(chunk):
        for copy in copies(chunk):
            copy.start()

    def rows_in(pair):
        return (
            pltpu.make_async_copy(tokens_hbm.at[:, pair], tokens_ref.at[:, pair], tokens_sems.at[pair]),
            pltpu.make_async_copy(grad_hbm.at[pair], grad_ref.at[pair], grad_sems.at[pair]),
        )

    gate_grad_ref, up_grad_ref, hidden_ref, gate_zeros, gate_log, up_zeros, up_log, table_ref = small
    arrivals = tables_in(small_hbm, small, small_sems)
    for copy in rows_in(0):
        copy.start()
    start(0)
    for pair in range(1, BLOCKS // 2):
        for copy in rows_in(pair):
            copy.start()
    start(1)
    for arrival in arrivals:
        arrival.wait()
    hidden_rows[...] = with_sums(hidden_ref[...], hidden_members())
    members = block_members()
    field_of_row = jnp.right_shift(lax.broadcasted_iota(jnp.int32, (OWN, 1), 0), 6)
    shrink = jnp.where(field_of_row == 0, SHRINK[0], jnp.where(field_of_row == 1, SHRINK[1], SHRINK[2]))
    shrink = jnp.broadcast_to(shrink, (OWN, LOCAL)).astype(jnp.bfloat16)

    def row_products(pair, part, gate_to, up_to):
        features = jnp.concatenate([tokens_ref[part * 2 + half, pair] * shrink for half in range(2)], axis=0)
        features = with_sums(features, members)
        for grad, to in ((gate_grad_ref, gate_to), (up_grad_ref, up_to)):
            for row in range(0, FEATURES + EXTRA, 80):
                to[row : row + 80, :] = jnp.dot(
                    features[row : row + 80, :], grad[...], preferred_element_type=jnp.float32
                )
                yield True

    def column_products(pair, down_to):
        for row in range(0, HIDDEN + EXTRA, 176):
            down_to[row : row + 176, :] = lax.dot_general(
                hidden_rows[row : row + 176, :], grad_ref[pair], CONTRACT_LAST, preferred_element_type=jnp.float32
            )
            yield True

    def groups(block, gate_from, up_from):
        yield from row_groups(block, gate_codes, gate_from, sums.at[0], totals.at[0])
        yield from row_groups(block, up_codes, up_from, sums.at[1], totals.at[1])

    def down_groups(pair):
        for part in range(2):
            yield from column_groups(pair * 2 + part, part, down_codes, down_pair, down_rows)

    for copy in rows_in(0):
        copy.wait()
    in_turn(row_products(0, 0, gate_even, up_even))

    def pair_step(pair, carry):
        for copy in copies(pair):
            copy.wait()
        following = jnp.minimum(pair + 1, BLOCKS // 2 - 1)

        @pl.when(pair < BLOCKS // 2 - 1)
        def _():
            for copy in rows_in(following):
                copy.wait()

        @pl.when(pair + 2 < CHUNKS)
        def _():
            start(pair + 2)

        in_turn(row_products(pair, 1, gate_odd, up_odd), groups(pair * 2, gate_even, up_even))
        in_turn(column_products(pair, down_pair), groups(pair * 2 + 1, gate_odd, up_odd))
        in_turn(row_products(following, 0, gate_even, up_even), down_groups(pair))
        return carry

    lax.fori_loop(0, BLOCKS // 2, pair_step, 0)

    for half, (zeros_ref, log_ref) in enumerate(((gate_zeros, gate_log), (up_zeros, up_log))):
        scale = jnp.exp(log_ref[...])
        halves[half, 0:48] = scale * (sums[half] - zeros_ref[...].astype(jnp.float32) * totals[half])
        halves[half, 48:96] = -scale * totals[half]
    found, table = down_rows[...].reshape(BLOCKS, 8, FEATURES), table_ref[...].reshape(BLOCKS, 8, FEATURES)
    found, total, zero, scale = found[:, 0:4], found[:, 4:8], table[:, 0:4], table[:, 4:8]
    finished = jnp.concatenate([scale * (found - zero * total), -scale * total], axis=1)
    down_rows[...] = finished.reshape(8 * BLOCKS, FEATURES)
    for half, begin in ((0, 0), (1, 48)):
        for j in range(3):
            halves[half, 96:144, j * 128 : (j + 1) * 128] = down_rows[begin : begin + 48, j * 128 : (j + 1) * 128]
    halves[0, 96:128, 384:] = down_rows[96:128, 0:128]
    halves[0, 128:144, 384:] = down_rows[96:112, 128:256]
    halves[1, 96:112, 384:] = down_rows[112:128, 128:256]
    halves[1, 112:144, 384:] = down_rows[96:128, 256:384]
    core = lax.axis_index("core")
    own_ref[...] = halves[core]
    given_ref[...] = halves[1 - core]


def group_grads(tokens, grad, gate_grad, up_grad, hidden, gate_tables, up_tables, down_codes, table):
    half = struct((144, HIDDEN), jnp.float32)
    gate_codes, *gate_tables = gate_tables
    up_codes, *up_tables = up_tables
    small = (gate_grad, up_grad, hidden, *gate_tables, *up_tables, table)
    rows, columns = (FEATURES + EXTRA, HIDDEN), (HIDDEN + EXTRA, 2 * FEATURES)
    return call(
        group_body,
        (half, half),
        [ANY] * 13,
        (VMEM, VMEM),
        [
            pltpu.VMEM((BLOCKS * WORDS, HIDDEN), jnp.int32),
            pltpu.VMEM((BLOCKS * WORDS, HIDDEN), jnp.int32),
            pltpu.VMEM((HIDDEN, BLOCKS * WORDS), jnp.int32),
        ]
        + [pltpu.SemaphoreType.DMA((CHUNKS,))] * 3
        + [
            pltpu.VMEM(TOKENS_SHAPE, jnp.bfloat16),
            pltpu.VMEM(GRAD_SHAPE, jnp.bfloat16),
            pltpu.SemaphoreType.DMA((BLOCKS // 2,)),
            pltpu.SemaphoreType.DMA((BLOCKS // 2,)),
            pltpu.SemaphoreType.DMA((8,)),
            pltpu.VMEM((HIDDEN + EXTRA, LOCAL), jnp.bfloat16),
        ]
        + [pltpu.VMEM(shape, jnp.float32) for shape in (rows,) * 4 + (columns,)]
        + [pltpu.VMEM((8 * BLOCKS, FEATURES), jnp.float32), pltpu.VMEM((2, 144, HIDDEN), jnp.float32)]
        + [pltpu.VMEM((2, 48, HIDDEN), jnp.float32)] * 2
        + [pltpu.VMEM(array.shape, array.dtype) for array in small],
        flops=3 * 2 * 128 * 6144 * 512,
        traffic=17000000,
        vmem=40,
    )(
        *from_hbm(gate_codes, up_codes, down_codes, tokens, grad, *small),
    )


def finish_body(mine_ref, other_ref, kept_ref, came_ref, tokens_grad_ref, gs_ref, gz_ref, us_ref, uz_ref, ds_ref, dz_ref, halves, rows):
    core = lax.axis_index("core")
    halves[core] = mine_ref[...]
    halves[1 - core] = other_ref[...]
    for half, scale_ref, zero_ref in ((0, gs_ref, gz_ref), (1, us_ref, uz_ref)):
        scale_ref[...] = halves[half, 0:48, :]
        zero_ref[...] = halves[half, 48:96, :]
        for j in range(3):
            rows[48 * half : 48 * half + 48, j * 128 : (j + 1) * 128] = halves[half, 96:144, j * 128 : (j + 1) * 128]
    rows[96:128, 0:128] = halves[0, 96:128, 384:]
    rows[96:112, 128:256] = halves[0, 128:144, 384:]
    rows[112:128, 128:256] = halves[1, 96:112, 384:]
    rows[96:128, 256:384] = halves[1, 112:144, 384:]
    natural = reorder(rows[...], True)
    for b in range(BLOCKS):
        columns = slice(b * FEATURES, (b + 1) * FEATURES)
        ds_ref[:, columns] = natural[8 * b : 8 * b + 4, :]
        dz_ref[:, columns] = natural[8 * b + 4 : 8 * b + 8, :]
    total = kept_ref[...] + came_ref[...]
    for k in range(3):
        tokens_grad_ref[pl.ds(k, THIRD, stride=3), :] = total[k * THIRD : (k + 1) * THIRD, :]


def finish(mine, other, kept, came):
    f32 = jnp.float32
    return call(
        finish_body,
        (struct((OWN, LOCAL), f32),)
        + (struct((48, HIDDEN), f32),) * 4
        + (struct((4, BLOCKS * FEATURES), f32),) * 2,
        [VMEM] * 4,
        (VMEM,) * 7,
        [pltpu.VMEM((2, 144, HIDDEN), f32), pltpu.VMEM((8 * BLOCKS, FEATURES), f32)],
        traffic=1400000,
    )(mine, other, kept, came)


def sum_body(parts_ref, kept_ref, given_ref, totals):
    total = parts_ref[0].astype(jnp.float32)
    for part in range(1, N_X * N_Z):
        total = total + parts_ref[part].astype(jnp.float32)
    totals[...] = total
    y = lax.axis_index("y_lo")
    kept_ref[...] = totals[y]
    given_ref[...] = totals[1 - y]


def sum_parts(parts):
    shard = struct((OWN, LOCAL), jnp.float32)
    return call(
        sum_body, (shard, shard), [VMEM], (VMEM, VMEM), [pltpu.VMEM((N_Y, OWN, LOCAL), jnp.float32)], traffic=1700000
    )(parts)


NEAR, ACROSS = ((0, 1), (2, 3)), ((0, 3), (1, 2))


def paired(block, axis, pairs):
    other = lax.ppermute(block, axis, [pair for a, b in pairs for pair in ((a, b), (b, a))])
    return jnp.concatenate([block, other])


def turned(block, axis, way):
    pairs = [(place, (place + way) % 4) for place in range(4)]
    pairs += [(4 + place, 4 + (place - way) % 4) for place in range(4)]
    return lax.ppermute(block, ("core", axis), pairs)


def swap(value, axis):
    return lax.ppermute(value, axis, [(0, 1), (1, 0)])


def shards(
    tokens,
    out_grad,
    gate_codes,
    gate_zeros,
    gate_log_scale,
    up_codes,
    up_zeros,
    up_log_scale,
    down_codes,
    down_zeros,
    down_log_scale,
):
    tokens_near, grad_near = by_field(tokens, out_grad)
    tokens_near, grad_near = paired(tokens_near, "y_lo", ((0, 1),)), paired(grad_near, "y_lo", ((0, 1),))
    tokens_near, grad_near = paired(tokens_near, "x", NEAR), paired(grad_near, "z", NEAR)
    tokens_near, gate_zeros = lax.optimization_barrier((tokens_near, gate_zeros))
    tokens_near, grad_near = paired(tokens_near, "x", ACROSS), paired(grad_near, "z", ACROSS)
    gate = unpack_rows(gate_codes, gate_zeros, gate_log_scale)
    tokens_near, gate, up_zeros = lax.optimization_barrier((tokens_near, gate, up_zeros))
    grad_near, up_log_scale = lax.optimization_barrier((grad_near, up_log_scale))
    tokens_first, grad_first = turned(tokens_near, "z", 1), turned(grad_near, "x", 1)
    tokens_second, grad_second = turned(tokens_near, "z", -1), turned(grad_near, "x", -1)
    up = unpack_rows(up_codes, up_zeros, up_log_scale)
    tokens_first, grad_first, up, down_zeros = lax.optimization_barrier((tokens_first, grad_first, up, down_zeros))
    tokens_parts = tokens_near, tokens_first, turned(tokens_first, "z", 1), tokens_second
    grad_parts = grad_near, grad_first, turned(grad_first, "x", 1), grad_second
    down, table = unpack_columns(down_codes, down_zeros, down_log_scale)
    *sums, all_tokens, all_grad = forward(tokens_parts, grad_parts, gate, up, down)
    partial, all_tokens, all_grad, gate_grad, up_grad, hidden = backward(
        tokens_parts, grad_parts, gate, up, down, sums, all_tokens, all_grad
    )
    parts = lax.all_to_all(partial.reshape(N_X * N_Z, N_Y, OWN, LOCAL), ("x", "z"), 0, 0, tiled=True)
    own, given = group_grads(
        all_tokens,
        all_grad,
        gate_grad,
        up_grad,
        hidden,
        (gate_codes, gate_zeros, gate_log_scale),
        (up_codes, up_zeros, up_log_scale),
        down_codes,
        table,
    )
    own = own + swap(given, "core")
    own = own.astype(jnp.bfloat16)
    kept, handed = sum_parts(parts)
    far, kept, came = lax.optimization_barrier((swap(own, "y_hi"), kept, swap(handed, "y_lo")))
    mine = own.astype(jnp.float32) + far.astype(jnp.float32)
    tokens_grad, *group_results = finish(mine, swap(mine, "core"), kept, came)
    return (tokens_grad.T, *group_results)


def solution(mesh):
    axes = jax.sharding.Mesh(mesh.devices.reshape(2, 2, N_X, N_Y, N_Z), ("y_hi", "core", "x", "y_lo", "z"))
    dp, tensor = ("y_hi", "core"), ("x", "y_lo", "z")
    columns, rows = P(None, tensor), P(tensor, None)
    return jax.shard_map(
        shards,
        mesh=axes,
        in_specs=(P(dp, tensor),) * 2 + (columns,) * 6 + (rows,) * 3,
        out_specs=(P(dp, tensor),) + (columns,) * 4 + (rows,) * 2,
        check_vma=False,
    )
```

```python
import jax
import jax.numpy as jnp
from jax import lax
from jax.experimental import pallas as pl
from jax.experimental.pallas import tpu as pltpu
from jax.sharding import PartitionSpec as P

N_X, N_Y, N_Z = 4, 2, 4
SHARDS = 32
OWN = 192
THIRD = 64
BLOCKS = 16
WORDS = 128
FEATURES = 384
HIDDEN = 512
LOCAL = 128
MIB = 1 << 20

CONTRACT_LAST = (((1,), (1,)), ((), ()))
CONTRACT_FIRST = (((0,), (0,)), ((), ()))


def shard_row(k, word):
    return (word // THIRD) * OWN + k * THIRD + word % THIRD


def first_word(k, group):
    return -((k - 128 * group) // 3)


def spread_over_groups(k, start, rows, values):
    first, last = (3 * start + k) // 128, (3 * (start + rows - 1) + k) // 128
    if first == last:
        return values[first]
    row = start + lax.broadcasted_iota(jnp.int32, (rows, 1), 0)
    return jnp.where(row < first_word(k, last), values[first], values[last])


def call(body, out_shape, in_specs, out_specs, scratch=(), flops=0, traffic=0, vmem=16, aliases=None):
    return pl.pallas_call(
        body,
        out_shape=out_shape,
        in_specs=in_specs,
        out_specs=out_specs,
        scratch_shapes=list(scratch),
        input_output_aliases=aliases or {},
        compiler_params=pltpu.CompilerParams(vmem_limit_bytes=vmem * MIB),
        cost_estimate=pl.CostEstimate(flops=flops, bytes_accessed=traffic, transcendentals=0),
    )


def struct(shape, dtype):
    return jax.ShapeDtypeStruct(shape, dtype)


def from_hbm(*arrays):
    return [pltpu.with_memory_space_constraint(array, pltpu.HBM) for array in arrays]


def from_vmem(*arrays):
    return [pltpu.with_memory_space_constraint(array, pltpu.VMEM) for array in arrays]


VMEM = pl.BlockSpec(memory_space=pltpu.VMEM)
ANY = pl.BlockSpec(memory_space=pl.ANY)


def by_field_body(tokens_ref, grad_ref, tokens_out, grad_out, wide):
    for ref, out_ref in ((tokens_ref, tokens_out), (grad_ref, grad_out)):
        wide[...] = ref[...].astype(jnp.float32)
        for k in range(3):
            out_ref[0, k * THIRD : (k + 1) * THIRD, :] = wide[pl.ds(k, THIRD, stride=3), :].astype(jnp.bfloat16)


def by_field(tokens, out_grad):
    return call(
        by_field_body,
        (struct((1, OWN, LOCAL), jnp.bfloat16),) * 2,
        [VMEM, VMEM],
        (VMEM, VMEM),
        [pltpu.VMEM((OWN, LOCAL), jnp.float32)],
        traffic=200000,
    )(*from_hbm(tokens.T, out_grad.T))


def field(words, k):
    if k:
        words = jnp.right_shift(words, 4 * k)
    if k < 2:
        words = jnp.bitwise_and(words, 15)
    return words.astype(jnp.float32)


CHUNKS = 8
AHEAD = 3


def row_copy(chunk, source, to, sems):
    rows = pl.ds(pl.multiple_of(chunk * 2 * WORDS, 2 * WORDS), 2 * WORDS)
    return pltpu.make_async_copy(source.at[rows], to.at[rows], sems.at[chunk])


def column_copy(chunk, source, to, sems):
    columns = pl.ds(pl.multiple_of(chunk * 2 * WORDS, 2 * WORDS), 2 * WORDS)
    return pltpu.make_async_copy(source.at[:, columns], to.at[:, columns], sems.at[chunk])


def tables_in(sources, targets, sems):
    copies = [pltpu.make_async_copy(a, b, sems.at[i]) for i, (a, b) in enumerate(zip(sources, targets))]
    for copy in copies:
        copy.start()
    return copies


def unpack_rows_pair(pair, codes, zeros_ref, log_ref, out_ref):
    for part in range(2):
        block = pair * 2 + part
        zeros = [zeros_ref[pl.ds(3 * block + g, 1), :].astype(jnp.float32) for g in range(3)]
        scales = [jnp.exp(log_ref[pl.ds(3 * block + g, 1), :]) for g in range(3)]
        for start in range(0, WORDS, 16):
            words = codes[pl.ds(pl.multiple_of(block * WORDS + start, 16), 16), :]
            for k in range(3):
                zero = spread_over_groups(k, start, 16, zeros)
                scale = spread_over_groups(k, start, 16, scales)
                weight = (scale * (field(words, k) - zero)).astype(jnp.bfloat16)
                row = k * THIRD + start % THIRD
                out_ref[part * 2 + start // THIRD, pair, row : row + 16, :] = weight


def streamed(copy_of, source, to, sems, work):
    def step(chunk, carry):
        copy_of(chunk, source, to, sems).wait()

        @pl.when(chunk + AHEAD < CHUNKS)
        def _():
            copy_of(chunk + AHEAD, source, to, sems).start()

        work(chunk)
        return carry

    lax.fori_loop(0, CHUNKS, step, 0)


def start_first(copy_of, source, to, sems):
    for chunk in range(AHEAD):
        copy_of(chunk, source, to, sems).start()


def unpack_rows_body(codes_hbm, zeros_hbm, log_hbm, out_ref, zeros_ref, log_ref, table_sems, codes, sems):
    tables = tables_in((zeros_hbm, log_hbm), (zeros_ref, log_ref), table_sems)
    start_first(row_copy, codes_hbm, codes, sems)
    for table in tables:
        table.wait()
    streamed(
        row_copy, codes_hbm, codes, sems, lambda pair: unpack_rows_pair(pair, codes, zeros_ref, log_ref, out_ref)
    )


def unpack_rows(codes, zeros, log_scale):
    return call(
        unpack_rows_body,
        pltpu.VMEM((N_Z, N_X * N_Y, OWN, HIDDEN), jnp.bfloat16),
        [ANY] * 3,
        VMEM,
        [
            pltpu.VMEM((48, HIDDEN), jnp.int32),
            pltpu.VMEM((48, HIDDEN), jnp.float32),
            pltpu.SemaphoreType.DMA((2,)),
            pltpu.VMEM((BLOCKS * WORDS, HIDDEN), jnp.int32),
            pltpu.SemaphoreType.DMA((CHUNKS,)),
        ],
        flops=20000000,
        traffic=10500000,
    )(*from_hbm(codes, zeros, log_scale))


def field_order(transposed):
    feature = lax.broadcasted_iota(jnp.int32, (FEATURES, FEATURES), 1 if transposed else 0)
    column = lax.broadcasted_iota(jnp.int32, (FEATURES, FEATURES), 0 if transposed else 1)
    wanted = 3 * jnp.bitwise_and(column, 127) + jnp.right_shift(column, 7)
    return (feature == wanted).astype(jnp.float32)


def reorder(rows, transposed):
    return jnp.dot(
        rows, field_order(transposed), precision=lax.Precision.HIGHEST, preferred_element_type=jnp.float32
    )


def unpack_columns_pair(pair, codes, table_ref, out_ref):
    for part in range(2):
        block = pair * 2 + part
        table = table_ref[pl.ds(pl.multiple_of(8 * block, 8), 8), :]
        for g in range(4):
            words = codes[g * 128 : (g + 1) * 128, pl.ds(pl.multiple_of(block * WORDS, WORDS), WORDS)]
            for k in range(3):
                columns = slice(k * WORDS, (k + 1) * WORDS)
                zero, scale = table[g : g + 1, columns], table[4 + g : 5 + g, columns]
                weight = (scale * (field(words, k) - zero)).astype(jnp.bfloat16)
                to = slice(part * FEATURES + k * WORDS, part * FEATURES + (k + 1) * WORDS)
                out_ref[pair, g * 128 : (g + 1) * 128, to] = weight


def unpack_columns_body(
    codes_hbm, zeros_hbm, log_hbm, out_ref, table_ref, zeros_ref, log_ref, table_sems, natural, codes, sems
):
    tables = tables_in((zeros_hbm, log_hbm), (zeros_ref, log_ref), table_sems)
    start_first(column_copy, codes_hbm, codes, sems)
    for table in tables:
        table.wait()
    for b in range(BLOCKS):
        columns = slice(b * FEATURES, (b + 1) * FEATURES)
        natural[8 * b : 8 * b + 4, :] = zeros_ref[:, columns].astype(jnp.float32)
        natural[8 * b + 4 : 8 * b + 8, :] = jnp.exp(log_ref[:, columns])
    table_ref[...] = reorder(natural[...], False)
    streamed(column_copy, codes_hbm, codes, sems, lambda pair: unpack_columns_pair(pair, codes, table_ref, out_ref))


def unpack_columns(codes, zeros, log_scale):
    wide = (4, BLOCKS * FEATURES)
    return call(
        unpack_columns_body,
        (
            pltpu.VMEM((N_X * N_Y, HIDDEN, 2 * FEATURES), jnp.bfloat16),
            pltpu.HBM((8 * BLOCKS, FEATURES), jnp.float32),
        ),
        [ANY] * 3,
        (VMEM,) * 2,
        [
            pltpu.VMEM(wide, jnp.int32),
            pltpu.VMEM(wide, jnp.float32),
            pltpu.SemaphoreType.DMA((2,)),
            pltpu.VMEM((8 * BLOCKS, FEATURES), jnp.float32),
            pltpu.VMEM((HIDDEN, BLOCKS * WORDS), jnp.int32),
            pltpu.SemaphoreType.DMA((CHUNKS,)),
        ],
        flops=20000000,
        traffic=10500000,
    )(*from_hbm(codes, zeros, log_scale))


SLAB = 8 * OWN


def position():
    return tuple(lax.axis_index(axis) for axis in ("x", "y_lo", "z"))


def swapped_with(here, near):
    place = 3 - here if near // 2 else here
    return place + 1 - 2 * (place % 2) if near % 2 else place


def lay_tokens(place, source, far, to):
    x, y, z = place
    slab = (z + 4 - far) % 4
    for near in range(4):
        for dy in range(2):
            to[slab, swapped_with(x, near) * 2 + (y + dy) % 2, :, :] = source[near * 2 + dy]
    return slab


def lay_grad(place, source, far, to):
    x, y, z = place
    slab = (x + 4 - far) % 4
    for near in range(4):
        z_from = swapped_with(z, near)
        for dy in range(2):
            for k in range(3):
                row = pl.multiple_of((z_from // 2) * FEATURES + k * WORDS + (z_from % 2) * THIRD, THIRD)
                to[slab * 2 + (y + dy) % 2, pl.ds(row, THIRD), :] = source[
                    near * 2 + dy, k * THIRD : (k + 1) * THIRD, :
                ]
    return slab


def slab_out(slab, tokens_from, tokens_hbm, sems):
    return pltpu.make_async_copy(tokens_from.at[slab], tokens_hbm.at[slab], sems)


def pair_out(slab, grad_from, grad_hbm, sems):
    pairs = pl.ds(slab * 2, 2)
    return pltpu.make_async_copy(grad_from.at[pairs], grad_hbm.at[pairs], sems)


def slab_products(fars, tokens_refs, grad_refs, weights, scratch, hbm, totals):
    gate_ref, up_ref, down_ref = weights
    tokens_to, grad_to, tokens_sems, grad_sems = scratch
    tokens_hbm, grad_hbm = hbm
    place = position()
    gate_pre, up_pre, hidden_grad = totals
    copies, laid = [], []
    for i, far in enumerate(fars):
        slabs = lay_tokens(place, tokens_refs[i], far, tokens_to), lay_grad(place, grad_refs[i], far, grad_to)
        copies.append(slab_out(slabs[0], tokens_to, tokens_hbm, tokens_sems.at[i]))
        copies.append(pair_out(slabs[1], grad_to, grad_hbm, grad_sems.at[i]))
        laid.append(slabs)
    for copy in copies:
        copy.start()
    for slab, grad_slab in laid:
        features = tokens_to[slab].reshape(SLAB, LOCAL).T
        gate_pre += jnp.dot(features, gate_ref[slab].reshape(SLAB, HIDDEN), preferred_element_type=jnp.float32)
        up_pre += jnp.dot(features, up_ref[slab].reshape(SLAB, HIDDEN), preferred_element_type=jnp.float32)
        for dy in range(2):
            piece = grad_to[grad_slab * 2 + dy]
            hidden_grad += jnp.dot(down_ref[grad_slab * 2 + dy], piece, preferred_element_type=jnp.float32)
    return (gate_pre, up_pre, hidden_grad), copies


def forward_body(
    t0, t1, t3, o0, o1, o3, gate_ref, up_ref, down_ref,
    gate_pre_ref, up_pre_ref, hidden_grad_ref, tokens_hbm, grad_hbm,
    tokens_to, grad_to, tokens_sems, grad_sems,
):
    zero = jnp.zeros((LOCAL, HIDDEN), jnp.float32)
    core = lax.axis_index("core")
    (gate_pre_ref[...], up_pre_ref[...], hidden_grad_ref[...]), copies = slab_products(
        (0, 1 + 2 * core, 3 - 2 * core), (t0, t1, t3), (o0, o1, o3), (gate_ref, up_ref, down_ref),
        (tokens_to, grad_to, tokens_sems, grad_sems), (tokens_hbm, grad_hbm),
        (zero, zero, jnp.zeros((HIDDEN, LOCAL), jnp.float32)),
    )
    for copy in copies:
        copy.wait()


TOKENS_SHAPE = (N_Z, N_X * N_Y, OWN, LOCAL)
GRAD_SHAPE = (N_X * N_Y, 2 * FEATURES, LOCAL)


def slab_scratch(slabs):
    return [
        pltpu.VMEM(TOKENS_SHAPE, jnp.bfloat16),
        pltpu.VMEM(GRAD_SHAPE, jnp.bfloat16),
        pltpu.SemaphoreType.DMA((slabs,)),
        pltpu.SemaphoreType.DMA((slabs,)),
    ]


def forward(tokens_parts, grad_parts, gate, up, down):
    f32, bf16 = jnp.float32, jnp.bfloat16
    near = (0, 1, 3)
    return call(
        forward_body,
        (
            pltpu.VMEM((LOCAL, HIDDEN), f32),
            pltpu.VMEM((LOCAL, HIDDEN), f32),
            pltpu.VMEM((HIDDEN, LOCAL), f32),
            pltpu.HBM(TOKENS_SHAPE, bf16),
            pltpu.HBM(GRAD_SHAPE, bf16),
        ),
        [VMEM] * 9,
        (VMEM,) * 3 + (ANY,) * 2,
        slab_scratch(3),
        flops=3 * 3 * 2 * 128 * 1536 * 512,
        traffic=18000000,
    )(
        *from_vmem(*[tokens_parts[far] for far in near], *[grad_parts[far] for far in near]),
        *from_vmem(gate, up, down),
    )


def backward_body(
    t2, o2, gate_ref, up_ref, down_ref, gate_pre_ref, up_pre_ref, hidden_grad_ref, tokens_in, grad_in,
    partial_hbm, tokens_hbm, grad_hbm, gate_grad_hbm, up_grad_hbm, hidden_hbm,
    tokens_to, grad_to, tokens_sems, grad_sems, partial, partial_sems, gate_grad_ref, up_grad_ref, hidden_ref, small_sems,
):
    (gate_pre, up_pre, hidden_grad), copies = slab_products(
        (2,), (t2,), (o2,), (gate_ref, up_ref, down_ref),
        (tokens_to, grad_to, tokens_sems, grad_sems), (tokens_hbm, grad_hbm),
        (gate_pre_ref[...], up_pre_ref[...], hidden_grad_ref[...]),
    )
    hidden_grad = hidden_grad.T
    sigmoid_gate = jax.nn.sigmoid(gate_pre)
    silu_gate = gate_pre * sigmoid_gate
    hidden = silu_gate * up_pre
    gate_grad = hidden_grad * up_pre * sigmoid_gate * (1.0 + gate_pre * (1.0 - sigmoid_gate))
    up_grad = hidden_grad * silu_gate
    gate_grad_ref[...] = gate_grad.astype(jnp.bfloat16)
    up_grad_ref[...] = up_grad.astype(jnp.bfloat16)
    hidden_ref[...] = hidden.T.astype(jnp.bfloat16)
    copies += tables_in(
        (gate_grad_ref, up_grad_ref, hidden_ref), (gate_grad_hbm, up_grad_hbm, hidden_hbm), small_sems
    )
    gate_turned = gate_grad.T.astype(jnp.bfloat16)
    up_turned = up_grad.T.astype(jnp.bfloat16)
    for slab in range(N_Z):
        total = jnp.dot(gate_ref[slab].reshape(SLAB, HIDDEN), gate_turned, preferred_element_type=jnp.float32)
        total += jnp.dot(up_ref[slab].reshape(SLAB, HIDDEN), up_turned, preferred_element_type=jnp.float32)
        partial[slab] = total.astype(jnp.bfloat16).reshape(N_X, N_Y, OWN, LOCAL)
        copy = pltpu.make_async_copy(partial.at[slab], partial_hbm.at[:, slab], partial_sems.at[slab])
        copy.start()
        copies.append(copy)
    for copy in copies:
        copy.wait()


def backward(tokens_parts, grad_parts, gate, up, down, sums, all_tokens, all_grad):
    bf16 = jnp.bfloat16
    return call(
        backward_body,
        (
            pltpu.HBM((N_X, N_Z, N_Y, OWN, LOCAL), bf16),
            pltpu.HBM(TOKENS_SHAPE, bf16),
            pltpu.HBM(GRAD_SHAPE, bf16),
            pltpu.HBM((LOCAL, HIDDEN), bf16),
            pltpu.HBM((LOCAL, HIDDEN), bf16),
            pltpu.HBM((HIDDEN, LOCAL), bf16),
        ),
        [VMEM] * 8 + [ANY] * 2,
        (ANY,) * 6,
        slab_scratch(1)
        + [
            pltpu.VMEM((N_Z, N_X, N_Y, OWN, LOCAL), bf16),
            pltpu.SemaphoreType.DMA((N_Z,)),
            pltpu.VMEM((LOCAL, HIDDEN), bf16),
            pltpu.VMEM((LOCAL, HIDDEN), bf16),
            pltpu.VMEM((HIDDEN, LOCAL), bf16),
            pltpu.SemaphoreType.DMA((3,)),
        ],
        flops=3 * 2 * 128 * 6144 * 512,
        traffic=24000000,
        aliases={8: 1, 9: 2},
    )(
        *from_vmem(tokens_parts[2], grad_parts[2], gate, up, down, *sums),
        *from_hbm(all_tokens, all_grad),
    )


EXTRA = 16


def with_sums(rows, members):
    sums = jnp.dot(members, rows, preferred_element_type=jnp.float32)
    head = sums.astype(jnp.bfloat16)
    rest = (sums - head.astype(jnp.float32)).astype(jnp.bfloat16)
    return jnp.concatenate([rows, jnp.concatenate([head, rest], axis=0)], axis=0)


def block_members():
    group = lax.broadcasted_iota(jnp.int32, (8, FEATURES), 0)
    place = lax.broadcasted_iota(jnp.int32, (8, FEATURES), 1)
    half = (place >= OWN).astype(jnp.int32)
    place = place - OWN * half
    k = jnp.right_shift(place, 6)
    feature = 3 * (half * THIRD + place - THIRD * k) + k
    scale = jnp.where(k == 0, 1.0, jnp.where(k == 1, 16.0, 256.0))
    return jnp.where(jnp.right_shift(feature, 7) == group, scale, 0.0).astype(jnp.bfloat16)


def hidden_members():
    group = lax.broadcasted_iota(jnp.int32, (8, HIDDEN), 0)
    unit = lax.broadcasted_iota(jnp.int32, (8, HIDDEN), 1)
    return (jnp.right_shift(unit, 7) == group).astype(jnp.float32).astype(jnp.bfloat16)


MASKS = (15, 240, 3840)
SHRINK = (1.0, 1.0 / 16.0, 1.0 / 256.0)


def in_place(words, k):
    return jnp.bitwise_and(words, MASKS[k]).astype(jnp.float32)


def in_turn(*streams):
    running = list(streams)
    while running:
        for stream in list(running):
            if next(stream, None) is None:
                running.remove(stream)


def row_groups(block, codes, weight_grad, sums, totals):
    weighted = [jnp.zeros((8, HIDDEN), jnp.float32)] * 3
    for start in range(0, WORDS, 8):
        words = codes[pl.ds(pl.multiple_of(block * WORDS + start, 8), 8), :]
        for k in range(3):
            product = in_place(words, k) * weight_grad[shard_row(k, start) : shard_row(k, start) + 8, :]
            first, last = (3 * start + k) // 128, (3 * (start + 7) + k) // 128
            if first == last:
                weighted[first] = weighted[first] + product
            else:
                low = start + lax.broadcasted_iota(jnp.int32, (8, 1), 0) < first_word(k, last)
                low_product = jnp.where(low, product, 0.0)
                weighted[first] = weighted[first] + low_product
                weighted[last] = weighted[last] + (product - low_product)
        yield True
    for g in range(3):
        row = pl.ds(3 * block + g, 1)
        sums[row, :] = jnp.sum(weighted[g], axis=0, keepdims=True)
        totals[row, :] = (
            weight_grad[FEATURES + g : FEATURES + g + 1, :] + weight_grad[FEATURES + 8 + g : FEATURES + 9 + g, :]
        )
    yield True


def column_groups(block, part, codes, weight_grad, raw):
    here = pl.ds(pl.multiple_of(8 * block, 8), 8)
    mine = slice(part * FEATURES, (part + 1) * FEATURES)
    totals = weight_grad[HIDDEN : HIDDEN + 4, mine] + weight_grad[HIDDEN + 8 : HIDDEN + 12, mine]
    for k in range(3):
        sums = []
        for g in range(4):
            weighted = jnp.zeros((8, WORDS), jnp.float32)
            for start in range(g * 128, g * 128 + 128, 8):
                words = codes[start : start + 8, pl.ds(pl.multiple_of(block * WORDS, WORDS), WORDS)]
                value = weight_grad[start : start + 8, part * FEATURES + k * WORDS : part * FEATURES + (k + 1) * WORDS]
                weighted = weighted + in_place(words, k) * value
            sums.append(jnp.sum(weighted, axis=0, keepdims=True))
            yield True
        columns = slice(k * WORDS, (k + 1) * WORDS)
        raw[here, columns] = jnp.concatenate([jnp.concatenate(sums, axis=0) * SHRINK[k], totals[:, columns]], axis=0)


def group_body(
    gate_hbm, up_hbm, down_hbm, tokens_hbm, grad_hbm, *small_hbm_and_rest
):
    small_hbm, rest = small_hbm_and_rest[:8], small_hbm_and_rest[8:]
    small, rest = rest[-8:], rest[:-8]
    group_work(gate_hbm, up_hbm, down_hbm, tokens_hbm, grad_hbm, small_hbm, small, *rest)


def group_work(
    gate_hbm, up_hbm, down_hbm, tokens_hbm, grad_hbm, small_hbm, small,
    own_ref, given_ref,
    gate_codes, up_codes, down_codes, gate_sems, up_sems, down_sems, tokens_ref, grad_ref, tokens_sems, grad_sems, small_sems,
    hidden_rows, gate_even, up_even, gate_odd, up_odd, down_pair, down_rows, halves, sums, totals,
):
    def copies(chunk):
        return (
            row_copy(chunk, gate_hbm, gate_codes, gate_sems),
            row_copy(chunk, up_hbm, up_codes, up_sems),
            column_copy(chunk, down_hbm, down_codes, down_sems),
        )

    def start(chunk):
        for copy in copies(chunk):
            copy.start()

    def rows_in(pair):
        return (
            pltpu.make_async_copy(tokens_hbm.at[:, pair], tokens_ref.at[:, pair], tokens_sems.at[pair]),
            pltpu.make_async_copy(grad_hbm.at[pair], grad_ref.at[pair], grad_sems.at[pair]),
        )

    gate_grad_ref, up_grad_ref, hidden_ref, gate_zeros, gate_log, up_zeros, up_log, table_ref = small
    arrivals = tables_in(small_hbm, small, small_sems)
    for copy in rows_in(0):
        copy.start()
    start(0)
    for pair in range(1, BLOCKS // 2):
        for copy in rows_in(pair):
            copy.start()
    start(1)
    for arrival in arrivals:
        arrival.wait()
    hidden_rows[...] = with_sums(hidden_ref[...], hidden_members())
    members = block_members()
    field_of_row = jnp.right_shift(lax.broadcasted_iota(jnp.int32, (OWN, 1), 0), 6)
    shrink = jnp.where(field_of_row == 0, SHRINK[0], jnp.where(field_of_row == 1, SHRINK[1], SHRINK[2]))
    shrink = jnp.broadcast_to(shrink, (OWN, LOCAL)).astype(jnp.bfloat16)

    def row_products(pair, part, gate_to, up_to):
        features = jnp.concatenate([tokens_ref[part * 2 + half, pair] * shrink for half in range(2)], axis=0)
        features = with_sums(features, members)
        for grad, to in ((gate_grad_ref, gate_to), (up_grad_ref, up_to)):
            for row in range(0, FEATURES + EXTRA, 80):
                to[row : row + 80, :] = jnp.dot(
                    features[row : row + 80, :], grad[...], preferred_element_type=jnp.float32
                )
                yield True

    def column_products(pair, down_to):
        for row in range(0, HIDDEN + EXTRA, 176):
            down_to[row : row + 176, :] = lax.dot_general(
                hidden_rows[row : row + 176, :], grad_ref[pair], CONTRACT_LAST, preferred_element_type=jnp.float32
            )
            yield True

    def groups(block, gate_from, up_from):
        yield from row_groups(block, gate_codes, gate_from, sums.at[0], totals.at[0])
        yield from row_groups(block, up_codes, up_from, sums.at[1], totals.at[1])

    def down_groups(pair):
        for part in range(2):
            yield from column_groups(pair * 2 + part, part, down_codes, down_pair, down_rows)

    for copy in rows_in(0):
        copy.wait()
    in_turn(row_products(0, 0, gate_even, up_even))

    def pair_step(pair, carry):
        for copy in copies(pair):
            copy.wait()
        following = jnp.minimum(pair + 1, BLOCKS // 2 - 1)

        @pl.when(pair < BLOCKS // 2 - 1)
        def _():
            for copy in rows_in(following):
                copy.wait()

        @pl.when(pair + 2 < CHUNKS)
        def _():
            start(pair + 2)

        in_turn(row_products(pair, 1, gate_odd, up_odd), groups(pair * 2, gate_even, up_even))
        in_turn(column_products(pair, down_pair), groups(pair * 2 + 1, gate_odd, up_odd))
        in_turn(row_products(following, 0, gate_even, up_even), down_groups(pair))
        return carry

    lax.fori_loop(0, BLOCKS // 2, pair_step, 0)

    for half, (zeros_ref, log_ref) in enumerate(((gate_zeros, gate_log), (up_zeros, up_log))):
        scale = jnp.exp(log_ref[...])
        halves[half, 0:48] = scale * (sums[half] - zeros_ref[...].astype(jnp.float32) * totals[half])
        halves[half, 48:96] = -scale * totals[half]
    found, table = down_rows[...].reshape(BLOCKS, 8, FEATURES), table_ref[...].reshape(BLOCKS, 8, FEATURES)
    found, total, zero, scale = found[:, 0:4], found[:, 4:8], table[:, 0:4], table[:, 4:8]
    finished = jnp.concatenate([scale * (found - zero * total), -scale * total], axis=1)
    down_rows[...] = finished.reshape(8 * BLOCKS, FEATURES)
    for half, begin in ((0, 0), (1, 48)):
        for j in range(3):
            halves[half, 96:144, j * 128 : (j + 1) * 128] = down_rows[begin : begin + 48, j * 128 : (j + 1) * 128]
    halves[0, 96:128, 384:] = down_rows[96:128, 0:128]
    halves[0, 128:144, 384:] = down_rows[96:112, 128:256]
    halves[1, 96:112, 384:] = down_rows[112:128, 128:256]
    halves[1, 112:144, 384:] = down_rows[96:128, 256:384]
    core = lax.axis_index("core")
    own_ref[...] = halves[core]
    given_ref[...] = halves[1 - core].astype(jnp.bfloat16)


def group_grads(tokens, grad, gate_grad, up_grad, hidden, gate_tables, up_tables, down_codes, table):
    half = struct((144, HIDDEN), jnp.float32)
    gate_codes, *gate_tables = gate_tables
    up_codes, *up_tables = up_tables
    small = (gate_grad, up_grad, hidden, *gate_tables, *up_tables, table)
    rows, columns = (FEATURES + EXTRA, HIDDEN), (HIDDEN + EXTRA, 2 * FEATURES)
    return call(
        group_body,
        (half, struct((144, HIDDEN), jnp.bfloat16)),
        [ANY] * 13,
        (VMEM, VMEM),
        [
            pltpu.VMEM((BLOCKS * WORDS, HIDDEN), jnp.int32),
            pltpu.VMEM((BLOCKS * WORDS, HIDDEN), jnp.int32),
            pltpu.VMEM((HIDDEN, BLOCKS * WORDS), jnp.int32),
        ]
        + [pltpu.SemaphoreType.DMA((CHUNKS,))] * 3
        + [
            pltpu.VMEM(TOKENS_SHAPE, jnp.bfloat16),
            pltpu.VMEM(GRAD_SHAPE, jnp.bfloat16),
            pltpu.SemaphoreType.DMA((BLOCKS // 2,)),
            pltpu.SemaphoreType.DMA((BLOCKS // 2,)),
            pltpu.SemaphoreType.DMA((8,)),
            pltpu.VMEM((HIDDEN + EXTRA, LOCAL), jnp.bfloat16),
        ]
        + [pltpu.VMEM(shape, jnp.float32) for shape in (rows,) * 4 + (columns,)]
        + [pltpu.VMEM((8 * BLOCKS, FEATURES), jnp.float32), pltpu.VMEM((2, 144, HIDDEN), jnp.float32)]
        + [pltpu.VMEM((2, 48, HIDDEN), jnp.float32)] * 2
        + [pltpu.VMEM(array.shape, array.dtype) for array in small],
        flops=3 * 2 * 128 * 6144 * 512,
        traffic=17000000,
        vmem=40,
    )(
        *from_hbm(gate_codes, up_codes, down_codes, tokens, grad, *small),
    )


def finish_body(mine_ref, other_ref, kept_ref, came_ref, tokens_grad_ref, gs_ref, gz_ref, us_ref, uz_ref, ds_ref, dz_ref, halves, rows):
    core = lax.axis_index("core")
    halves[core] = mine_ref[...]
    halves[1 - core] = other_ref[...]
    for half, scale_ref, zero_ref in ((0, gs_ref, gz_ref), (1, us_ref, uz_ref)):
        scale_ref[...] = halves[half, 0:48, :]
        zero_ref[...] = halves[half, 48:96, :]
        for j in range(3):
            rows[48 * half : 48 * half + 48, j * 128 : (j + 1) * 128] = halves[half, 96:144, j * 128 : (j + 1) * 128]
    rows[96:128, 0:128] = halves[0, 96:128, 384:]
    rows[96:112, 128:256] = halves[0, 128:144, 384:]
    rows[112:128, 128:256] = halves[1, 96:112, 384:]
    rows[96:128, 256:384] = halves[1, 112:144, 384:]
    natural = reorder(rows[...], True)
    for b in range(BLOCKS):
        columns = slice(b * FEATURES, (b + 1) * FEATURES)
        ds_ref[:, columns] = natural[8 * b : 8 * b + 4, :]
        dz_ref[:, columns] = natural[8 * b + 4 : 8 * b + 8, :]
    total = kept_ref[...] + came_ref[...].astype(jnp.float32)
    for k in range(3):
        tokens_grad_ref[pl.ds(k, THIRD, stride=3), :] = total[k * THIRD : (k + 1) * THIRD, :]


def finish(mine, other, kept, came):
    f32 = jnp.float32
    return call(
        finish_body,
        (struct((OWN, LOCAL), f32),)
        + (struct((48, HIDDEN), f32),) * 4
        + (struct((4, BLOCKS * FEATURES), f32),) * 2,
        [VMEM] * 4,
        (VMEM,) * 7,
        [pltpu.VMEM((2, 144, HIDDEN), f32), pltpu.VMEM((8 * BLOCKS, FEATURES), f32)],
        traffic=1400000,
    )(mine, other, kept, came)


def sum_body(parts_ref, kept_ref, given_ref, totals):
    total = parts_ref[0].astype(jnp.float32)
    for part in range(1, N_X * N_Z):
        total = total + parts_ref[part].astype(jnp.float32)
    totals[...] = total
    y = lax.axis_index("y_lo")
    kept_ref[...] = totals[y]
    given_ref[...] = totals[1 - y].astype(jnp.bfloat16)


def sum_parts(parts):
    shard = (OWN, LOCAL)
    return call(
        sum_body,
        (struct(shard, jnp.float32), struct(shard, jnp.bfloat16)),
        [VMEM],
        (VMEM, VMEM),
        [pltpu.VMEM((N_Y, OWN, LOCAL), jnp.float32)],
        traffic=1700000,
    )(parts)


NEAR, ACROSS = ((0, 1), (2, 3)), ((0, 3), (1, 2))


def paired(block, axis, pairs):
    other = lax.ppermute(block, axis, [pair for a, b in pairs for pair in ((a, b), (b, a))])
    return jnp.concatenate([block, other])


def turned(block, axis, way):
    pairs = [(place, (place + way) % 4) for place in range(4)]
    pairs += [(4 + place, 4 + (place - way) % 4) for place in range(4)]
    return lax.ppermute(block, ("core", axis), pairs)


def swap(value, axis):
    return lax.ppermute(value, axis, [(0, 1), (1, 0)])


def shards(
    tokens,
    out_grad,
    gate_codes,
    gate_zeros,
    gate_log_scale,
    up_codes,
    up_zeros,
    up_log_scale,
    down_codes,
    down_zeros,
    down_log_scale,
):
    tokens_near, grad_near = by_field(tokens, out_grad)
    tokens_near, grad_near = paired(tokens_near, "y_lo", ((0, 1),)), paired(grad_near, "y_lo", ((0, 1),))
    tokens_near, grad_near = paired(tokens_near, "x", NEAR), paired(grad_near, "z", NEAR)
    tokens_near, gate_zeros = lax.optimization_barrier((tokens_near, gate_zeros))
    tokens_near, grad_near = paired(tokens_near, "x", ACROSS), paired(grad_near, "z", ACROSS)
    gate = unpack_rows(gate_codes, gate_zeros, gate_log_scale)
    tokens_near, gate, up_zeros = lax.optimization_barrier((tokens_near, gate, up_zeros))
    grad_near, up_log_scale = lax.optimization_barrier((grad_near, up_log_scale))
    tokens_first, grad_first = turned(tokens_near, "z", 1), turned(grad_near, "x", 1)
    tokens_second, grad_second = turned(tokens_near, "z", -1), turned(grad_near, "x", -1)
    up = unpack_rows(up_codes, up_zeros, up_log_scale)
    tokens_first, grad_first, up, down_zeros = lax.optimization_barrier((tokens_first, grad_first, up, down_zeros))
    tokens_parts = tokens_near, tokens_first, turned(tokens_first, "z", 1), tokens_second
    grad_parts = grad_near, grad_first, turned(grad_first, "x", 1), grad_second
    down, table = unpack_columns(down_codes, down_zeros, down_log_scale)
    *sums, all_tokens, all_grad = forward(tokens_parts, grad_parts, gate, up, down)
    partial, all_tokens, all_grad, gate_grad, up_grad, hidden = backward(
        tokens_parts, grad_parts, gate, up, down, sums, all_tokens, all_grad
    )
    parts = lax.all_to_all(partial.reshape(N_X * N_Z, N_Y, OWN, LOCAL), ("x", "z"), 0, 0, tiled=True)
    own, given = group_grads(
        all_tokens,
        all_grad,
        gate_grad,
        up_grad,
        hidden,
        (gate_codes, gate_zeros, gate_log_scale),
        (up_codes, up_zeros, up_log_scale),
        down_codes,
        table,
    )
    own = own + swap(given, "core").astype(jnp.float32)
    own = own.astype(jnp.bfloat16)
    kept, handed = sum_parts(parts)
    came = swap(handed, "y_lo")
    far, kept = lax.optimization_barrier((swap(own, "y_hi"), kept))
    mine = own.astype(jnp.float32) + far.astype(jnp.float32)
    tokens_grad, *group_results = finish(mine, swap(mine, "core"), kept, came)
    return (tokens_grad.T, *group_results)


def solution(mesh):
    axes = jax.sharding.Mesh(mesh.devices.reshape(2, 2, N_X, N_Y, N_Z), ("y_hi", "core", "x", "y_lo", "z"))
    dp, tensor = ("y_hi", "core"), ("x", "y_lo", "z")
    columns, rows = P(None, tensor), P(tensor, None)
    return jax.shard_map(
        shards,
        mesh=axes,
        in_specs=(P(dp, tensor),) * 2 + (columns,) * 6 + (rows,) * 3,
        out_specs=(P(dp, tensor),) + (columns,) * 4 + (rows,) * 2,
        check_vma=False,
    )
```

```python
import jax
import jax.numpy as jnp
from jax import lax
from jax.experimental import pallas as pl
from jax.experimental.pallas import tpu as pltpu
from jax.sharding import PartitionSpec as P

N_X, N_Y, N_Z = 4, 2, 4
SHARDS = 32
OWN = 192
THIRD = 64
BLOCKS = 16
WORDS = 128
FEATURES = 384
HIDDEN = 512
LOCAL = 128
MIB = 1 << 20

CONTRACT_LAST = (((1,), (1,)), ((), ()))
CONTRACT_FIRST = (((0,), (0,)), ((), ()))


def shard_row(k, word):
    return (word // THIRD) * OWN + k * THIRD + word % THIRD


def first_word(k, group):
    return -((k - 128 * group) // 3)


def spread_over_groups(k, start, rows, values):
    first, last = (3 * start + k) // 128, (3 * (start + rows - 1) + k) // 128
    if first == last:
        return values[first]
    row = start + lax.broadcasted_iota(jnp.int32, (rows, 1), 0)
    return jnp.where(row < first_word(k, last), values[first], values[last])


def call(body, out_shape, in_specs, out_specs, scratch=(), flops=0, traffic=0, vmem=16, aliases=None):
    return pl.pallas_call(
        body,
        out_shape=out_shape,
        in_specs=in_specs,
        out_specs=out_specs,
        scratch_shapes=list(scratch),
        input_output_aliases=aliases or {},
        compiler_params=pltpu.CompilerParams(vmem_limit_bytes=vmem * MIB),
        cost_estimate=pl.CostEstimate(flops=flops, bytes_accessed=traffic, transcendentals=0),
    )


def struct(shape, dtype):
    return jax.ShapeDtypeStruct(shape, dtype)


def from_hbm(*arrays):
    return [pltpu.with_memory_space_constraint(array, pltpu.HBM) for array in arrays]


def from_vmem(*arrays):
    return [pltpu.with_memory_space_constraint(array, pltpu.VMEM) for array in arrays]


VMEM = pl.BlockSpec(memory_space=pltpu.VMEM)
ANY = pl.BlockSpec(memory_space=pl.ANY)


def by_field_body(tokens_ref, grad_ref, tokens_out, grad_out, wide):
    for ref, out_ref in ((tokens_ref, tokens_out), (grad_ref, grad_out)):
        wide[...] = ref[...].astype(jnp.float32)
        for k in range(3):
            out_ref[0, k * THIRD : (k + 1) * THIRD, :] = wide[pl.ds(k, THIRD, stride=3), :].astype(jnp.bfloat16)


def by_field(tokens, out_grad):
    return call(
        by_field_body,
        (struct((1, OWN, LOCAL), jnp.bfloat16),) * 2,
        [VMEM, VMEM],
        (VMEM, VMEM),
        [pltpu.VMEM((OWN, LOCAL), jnp.float32)],
        traffic=200000,
    )(*from_hbm(tokens.T, out_grad.T))


def field(words, k):
    if k:
        words = jnp.right_shift(words, 4 * k)
    if k < 2:
        words = jnp.bitwise_and(words, 15)
    return words.astype(jnp.float32)


CHUNKS = 8
AHEAD = 3


def row_copy(chunk, source, to, sems):
    rows = pl.ds(pl.multiple_of(chunk * 2 * WORDS, 2 * WORDS), 2 * WORDS)
    return pltpu.make_async_copy(source.at[rows], to.at[rows], sems.at[chunk])


def column_copy(chunk, source, to, sems):
    columns = pl.ds(pl.multiple_of(chunk * 2 * WORDS, 2 * WORDS), 2 * WORDS)
    return pltpu.make_async_copy(source.at[:, columns], to.at[:, columns], sems.at[chunk])


def tables_in(sources, targets, sems):
    copies = [pltpu.make_async_copy(a, b, sems.at[i]) for i, (a, b) in enumerate(zip(sources, targets))]
    for copy in copies:
        copy.start()
    return copies


def unpack_rows_pair(pair, codes, zeros_ref, log_ref, out_ref):
    for part in range(2):
        block = pair * 2 + part
        zeros = [zeros_ref[pl.ds(3 * block + g, 1), :].astype(jnp.float32) for g in range(3)]
        scales = [jnp.exp(log_ref[pl.ds(3 * block + g, 1), :]) for g in range(3)]
        for start in range(0, WORDS, 16):
            words = codes[pl.ds(pl.multiple_of(block * WORDS + start, 16), 16), :]
            for k in range(3):
                zero = spread_over_groups(k, start, 16, zeros)
                scale = spread_over_groups(k, start, 16, scales)
                weight = (scale * (field(words, k) - zero)).astype(jnp.bfloat16)
                row = k * THIRD + start % THIRD
                out_ref[part * 2 + start // THIRD, pair, row : row + 16, :] = weight


def streamed(copy_of, source, to, sems, work):
    def step(chunk, carry):
        copy_of(chunk, source, to, sems).wait()

        @pl.when(chunk + AHEAD < CHUNKS)
        def _():
            copy_of(chunk + AHEAD, source, to, sems).start()

        work(chunk)
        return carry

    lax.fori_loop(0, CHUNKS, step, 0)


def start_first(copy_of, source, to, sems):
    for chunk in range(AHEAD):
        copy_of(chunk, source, to, sems).start()


def unpack_rows_body(codes_hbm, zeros_hbm, log_hbm, out_ref, zeros_ref, log_ref, table_sems, codes, sems):
    tables = tables_in((zeros_hbm, log_hbm), (zeros_ref, log_ref), table_sems)
    start_first(row_copy, codes_hbm, codes, sems)
    for table in tables:
        table.wait()
    streamed(
        row_copy, codes_hbm, codes, sems, lambda pair: unpack_rows_pair(pair, codes, zeros_ref, log_ref, out_ref)
    )


def unpack_rows(codes, zeros, log_scale):
    return call(
        unpack_rows_body,
        pltpu.VMEM((N_Z, N_X * N_Y, OWN, HIDDEN), jnp.bfloat16),
        [ANY] * 3,
        VMEM,
        [
            pltpu.VMEM((48, HIDDEN), jnp.int32),
            pltpu.VMEM((48, HIDDEN), jnp.float32),
            pltpu.SemaphoreType.DMA((2,)),
            pltpu.VMEM((BLOCKS * WORDS, HIDDEN), jnp.int32),
            pltpu.SemaphoreType.DMA((CHUNKS,)),
        ],
        flops=20000000,
        traffic=10500000,
    )(*from_hbm(codes, zeros, log_scale))


def field_order(transposed):
    feature = lax.broadcasted_iota(jnp.int32, (FEATURES, FEATURES), 1 if transposed else 0)
    column = lax.broadcasted_iota(jnp.int32, (FEATURES, FEATURES), 0 if transposed else 1)
    wanted = 3 * jnp.bitwise_and(column, 127) + jnp.right_shift(column, 7)
    return (feature == wanted).astype(jnp.float32)


def reorder(rows, transposed):
    return jnp.dot(
        rows, field_order(transposed), precision=lax.Precision.HIGHEST, preferred_element_type=jnp.float32
    )


def unpack_columns_pair(pair, codes, table_ref, out_ref):
    for part in range(2):
        block = pair * 2 + part
        table = table_ref[pl.ds(pl.multiple_of(8 * block, 8), 8), :]
        for g in range(4):
            words = codes[g * 128 : (g + 1) * 128, pl.ds(pl.multiple_of(block * WORDS, WORDS), WORDS)]
            for k in range(3):
                columns = slice(k * WORDS, (k + 1) * WORDS)
                zero, scale = table[g : g + 1, columns], table[4 + g : 5 + g, columns]
                weight = (scale * (field(words, k) - zero)).astype(jnp.bfloat16)
                to = slice(part * FEATURES + k * WORDS, part * FEATURES + (k + 1) * WORDS)
                out_ref[pair, g * 128 : (g + 1) * 128, to] = weight


def unpack_columns_body(
    codes_hbm, zeros_hbm, log_hbm, out_ref, table_ref, zeros_ref, log_ref, table_sems, natural, codes, sems
):
    tables = tables_in((zeros_hbm, log_hbm), (zeros_ref, log_ref), table_sems)
    start_first(column_copy, codes_hbm, codes, sems)
    for table in tables:
        table.wait()
    for b in range(BLOCKS):
        columns = slice(b * FEATURES, (b + 1) * FEATURES)
        natural[8 * b : 8 * b + 4, :] = zeros_ref[:, columns].astype(jnp.float32)
        natural[8 * b + 4 : 8 * b + 8, :] = jnp.exp(log_ref[:, columns])
    table_ref[...] = reorder(natural[...], False)
    streamed(column_copy, codes_hbm, codes, sems, lambda pair: unpack_columns_pair(pair, codes, table_ref, out_ref))


def unpack_columns(codes, zeros, log_scale):
    wide = (4, BLOCKS * FEATURES)
    return call(
        unpack_columns_body,
        (
            pltpu.VMEM((N_X * N_Y, HIDDEN, 2 * FEATURES), jnp.bfloat16),
            pltpu.HBM((8 * BLOCKS, FEATURES), jnp.float32),
        ),
        [ANY] * 3,
        (VMEM,) * 2,
        [
            pltpu.VMEM(wide, jnp.int32),
            pltpu.VMEM(wide, jnp.float32),
            pltpu.SemaphoreType.DMA((2,)),
            pltpu.VMEM((8 * BLOCKS, FEATURES), jnp.float32),
            pltpu.VMEM((HIDDEN, BLOCKS * WORDS), jnp.int32),
            pltpu.SemaphoreType.DMA((CHUNKS,)),
        ],
        flops=20000000,
        traffic=10500000,
    )(*from_hbm(codes, zeros, log_scale))


SLAB = 8 * OWN


def position():
    return tuple(lax.axis_index(axis) for axis in ("x", "y_lo", "z"))


def swapped_with(here, near):
    place = 3 - here if near // 2 else here
    return place + 1 - 2 * (place % 2) if near % 2 else place


def lay_tokens(place, source, far, to):
    x, y, z = place
    slab = (z + 4 - far) % 4
    for near in range(4):
        for dy in range(2):
            to[slab, swapped_with(x, near) * 2 + (y + dy) % 2, :, :] = source[near * 2 + dy]
    return slab


def lay_grad(place, source, far, to):
    x, y, z = place
    slab = (x + 4 - far) % 4
    for near in range(4):
        z_from = swapped_with(z, near)
        for dy in range(2):
            for k in range(3):
                row = pl.multiple_of((z_from // 2) * FEATURES + k * WORDS + (z_from % 2) * THIRD, THIRD)
                to[slab * 2 + (y + dy) % 2, pl.ds(row, THIRD), :] = source[
                    near * 2 + dy, k * THIRD : (k + 1) * THIRD, :
                ]
    return slab


def slab_out(slab, tokens_from, tokens_hbm, sems):
    return pltpu.make_async_copy(tokens_from.at[slab], tokens_hbm.at[slab], sems)


def pair_out(slab, grad_from, grad_hbm, sems):
    pairs = pl.ds(slab * 2, 2)
    return pltpu.make_async_copy(grad_from.at[pairs], grad_hbm.at[pairs], sems)


def slab_products(fars, tokens_refs, grad_refs, weights, scratch, hbm, totals):
    gate_ref, up_ref, down_ref = weights
    tokens_to, grad_to, tokens_sems, grad_sems = scratch
    tokens_hbm, grad_hbm = hbm
    place = position()
    gate_pre, up_pre, hidden_grad = totals
    copies, laid = [], []
    for i, far in enumerate(fars):
        slabs = lay_tokens(place, tokens_refs[i], far, tokens_to), lay_grad(place, grad_refs[i], far, grad_to)
        copies.append(slab_out(slabs[0], tokens_to, tokens_hbm, tokens_sems.at[i]))
        copies.append(pair_out(slabs[1], grad_to, grad_hbm, grad_sems.at[i]))
        laid.append(slabs)
    for copy in copies:
        copy.start()
    for slab, grad_slab in laid:
        features = tokens_to[slab].reshape(SLAB, LOCAL).T
        gate_pre += jnp.dot(features, gate_ref[slab].reshape(SLAB, HIDDEN), preferred_element_type=jnp.float32)
        up_pre += jnp.dot(features, up_ref[slab].reshape(SLAB, HIDDEN), preferred_element_type=jnp.float32)
        for dy in range(2):
            piece = grad_to[grad_slab * 2 + dy]
            hidden_grad += jnp.dot(down_ref[grad_slab * 2 + dy], piece, preferred_element_type=jnp.float32)
    return (gate_pre, up_pre, hidden_grad), copies


def forward_body(
    t0, t1, t3, o0, o1, o3, gate_ref, up_ref, down_ref,
    gate_pre_ref, up_pre_ref, hidden_grad_ref, tokens_hbm, grad_hbm,
    tokens_to, grad_to, tokens_sems, grad_sems,
):
    zero = jnp.zeros((LOCAL, HIDDEN), jnp.float32)
    core = lax.axis_index("core")
    (gate_pre_ref[...], up_pre_ref[...], hidden_grad_ref[...]), copies = slab_products(
        (0, 1 + 2 * core, 3 - 2 * core), (t0, t1, t3), (o0, o1, o3), (gate_ref, up_ref, down_ref),
        (tokens_to, grad_to, tokens_sems, grad_sems), (tokens_hbm, grad_hbm),
        (zero, zero, jnp.zeros((HIDDEN, LOCAL), jnp.float32)),
    )
    for copy in copies:
        copy.wait()


TOKENS_SHAPE = (N_Z, N_X * N_Y, OWN, LOCAL)
GRAD_SHAPE = (N_X * N_Y, 2 * FEATURES, LOCAL)


def slab_scratch(slabs):
    return [
        pltpu.VMEM(TOKENS_SHAPE, jnp.bfloat16),
        pltpu.VMEM(GRAD_SHAPE, jnp.bfloat16),
        pltpu.SemaphoreType.DMA((slabs,)),
        pltpu.SemaphoreType.DMA((slabs,)),
    ]


def forward(tokens_parts, grad_parts, gate, up, down):
    f32, bf16 = jnp.float32, jnp.bfloat16
    near = (0, 1, 3)
    return call(
        forward_body,
        (
            pltpu.VMEM((LOCAL, HIDDEN), f32),
            pltpu.VMEM((LOCAL, HIDDEN), f32),
            pltpu.VMEM((HIDDEN, LOCAL), f32),
            pltpu.HBM(TOKENS_SHAPE, bf16),
            pltpu.HBM(GRAD_SHAPE, bf16),
        ),
        [VMEM] * 9,
        (VMEM,) * 3 + (ANY,) * 2,
        slab_scratch(3),
        flops=3 * 3 * 2 * 128 * 1536 * 512,
        traffic=18000000,
    )(
        *from_vmem(*[tokens_parts[far] for far in near], *[grad_parts[far] for far in near]),
        *from_vmem(gate, up, down),
    )


def backward_body(
    t2, o2, gate_ref, up_ref, down_ref, gate_pre_ref, up_pre_ref, hidden_grad_ref, tokens_in, grad_in,
    partial_hbm, tokens_hbm, grad_hbm, gate_grad_hbm, up_grad_hbm, hidden_hbm,
    tokens_to, grad_to, tokens_sems, grad_sems, partial, partial_sems, gate_grad_ref, up_grad_ref, hidden_ref, small_sems,
):
    (gate_pre, up_pre, hidden_grad), copies = slab_products(
        (2,), (t2,), (o2,), (gate_ref, up_ref, down_ref),
        (tokens_to, grad_to, tokens_sems, grad_sems), (tokens_hbm, grad_hbm),
        (gate_pre_ref[...], up_pre_ref[...], hidden_grad_ref[...]),
    )
    hidden_grad = hidden_grad.T
    sigmoid_gate = jax.nn.sigmoid(gate_pre)
    silu_gate = gate_pre * sigmoid_gate
    hidden = silu_gate * up_pre
    gate_grad = hidden_grad * up_pre * sigmoid_gate * (1.0 + gate_pre * (1.0 - sigmoid_gate))
    up_grad = hidden_grad * silu_gate
    gate_grad_ref[...] = gate_grad.astype(jnp.bfloat16)
    up_grad_ref[...] = up_grad.astype(jnp.bfloat16)
    hidden_ref[...] = hidden.T.astype(jnp.bfloat16)
    copies += tables_in(
        (gate_grad_ref, up_grad_ref, hidden_ref), (gate_grad_hbm, up_grad_hbm, hidden_hbm), small_sems
    )
    gate_turned = gate_grad.T.astype(jnp.bfloat16)
    up_turned = up_grad.T.astype(jnp.bfloat16)
    for slab in range(N_Z):
        total = jnp.dot(gate_ref[slab].reshape(SLAB, HIDDEN), gate_turned, preferred_element_type=jnp.float32)
        total += jnp.dot(up_ref[slab].reshape(SLAB, HIDDEN), up_turned, preferred_element_type=jnp.float32)
        partial[slab] = total.astype(jnp.bfloat16).reshape(N_X * N_Y, OWN, LOCAL)
        copy = pltpu.make_async_copy(partial.at[slab], partial_hbm.at[:, slab], partial_sems.at[slab])
        copy.start()
        copies.append(copy)
    for copy in copies:
        copy.wait()


def backward(tokens_parts, grad_parts, gate, up, down, sums, all_tokens, all_grad):
    bf16 = jnp.bfloat16
    return call(
        backward_body,
        (
            pltpu.HBM((N_X * N_Y, N_Z, OWN, LOCAL), bf16),
            pltpu.HBM(TOKENS_SHAPE, bf16),
            pltpu.HBM(GRAD_SHAPE, bf16),
            pltpu.HBM((LOCAL, HIDDEN), bf16),
            pltpu.HBM((LOCAL, HIDDEN), bf16),
            pltpu.HBM((HIDDEN, LOCAL), bf16),
        ),
        [VMEM] * 8 + [ANY] * 2,
        (ANY,) * 6,
        slab_scratch(1)
        + [
            pltpu.VMEM(TOKENS_SHAPE, bf16),
            pltpu.SemaphoreType.DMA((N_Z,)),
            pltpu.VMEM((LOCAL, HIDDEN), bf16),
            pltpu.VMEM((LOCAL, HIDDEN), bf16),
            pltpu.VMEM((HIDDEN, LOCAL), bf16),
            pltpu.SemaphoreType.DMA((3,)),
        ],
        flops=3 * 2 * 128 * 6144 * 512,
        traffic=24000000,
        aliases={8: 1, 9: 2},
    )(
        *from_vmem(tokens_parts[2], grad_parts[2], gate, up, down, *sums),
        *from_hbm(all_tokens, all_grad),
    )


EXTRA = 16


def with_sums(rows, members):
    sums = jnp.dot(members, rows, preferred_element_type=jnp.float32)
    head = sums.astype(jnp.bfloat16)
    rest = (sums - head.astype(jnp.float32)).astype(jnp.bfloat16)
    return jnp.concatenate([rows, jnp.concatenate([head, rest], axis=0)], axis=0)


def block_members():
    group = lax.broadcasted_iota(jnp.int32, (8, FEATURES), 0)
    place = lax.broadcasted_iota(jnp.int32, (8, FEATURES), 1)
    half = (place >= OWN).astype(jnp.int32)
    place = place - OWN * half
    k = jnp.right_shift(place, 6)
    feature = 3 * (half * THIRD + place - THIRD * k) + k
    scale = jnp.where(k == 0, 1.0, jnp.where(k == 1, 16.0, 256.0))
    return jnp.where(jnp.right_shift(feature, 7) == group, scale, 0.0).astype(jnp.bfloat16)


def hidden_members():
    group = lax.broadcasted_iota(jnp.int32, (8, HIDDEN), 0)
    unit = lax.broadcasted_iota(jnp.int32, (8, HIDDEN), 1)
    return (jnp.right_shift(unit, 7) == group).astype(jnp.float32).astype(jnp.bfloat16)


MASKS = (15, 240, 3840)
SHRINK = (1.0, 1.0 / 16.0, 1.0 / 256.0)


def in_place(words, k):
    return jnp.bitwise_and(words, MASKS[k]).astype(jnp.float32)


def in_turn(*streams):
    running = list(streams)
    while running:
        for stream in list(running):
            if next(stream, None) is None:
                running.remove(stream)


def row_groups(block, codes, weight_grad, sums, totals):
    weighted = [jnp.zeros((8, HIDDEN), jnp.float32)] * 3
    for start in range(0, WORDS, 8):
        words = codes[pl.ds(pl.multiple_of(block * WORDS + start, 8), 8), :]
        for k in range(3):
            product = in_place(words, k) * weight_grad[shard_row(k, start) : shard_row(k, start) + 8, :]
            first, last = (3 * start + k) // 128, (3 * (start + 7) + k) // 128
            if first == last:
                weighted[first] = weighted[first] + product
            else:
                low = start + lax.broadcasted_iota(jnp.int32, (8, 1), 0) < first_word(k, last)
                low_product = jnp.where(low, product, 0.0)
                weighted[first] = weighted[first] + low_product
                weighted[last] = weighted[last] + (product - low_product)
        yield True
    for g in range(3):
        row = pl.ds(3 * block + g, 1)
        sums[row, :] = jnp.sum(weighted[g], axis=0, keepdims=True)
        totals[row, :] = (
            weight_grad[FEATURES + g : FEATURES + g + 1, :] + weight_grad[FEATURES + 8 + g : FEATURES + 9 + g, :]
        )
    yield True


def column_groups(block, part, codes, weight_grad, raw):
    here = pl.ds(pl.multiple_of(8 * block, 8), 8)
    mine = slice(part * FEATURES, (part + 1) * FEATURES)
    totals = weight_grad[HIDDEN : HIDDEN + 4, mine] + weight_grad[HIDDEN + 8 : HIDDEN + 12, mine]
    for k in range(3):
        sums = []
        for g in range(4):
            weighted = jnp.zeros((8, WORDS), jnp.float32)
            for start in range(g * 128, g * 128 + 128, 8):
                words = codes[start : start + 8, pl.ds(pl.multiple_of(block * WORDS, WORDS), WORDS)]
                value = weight_grad[start : start + 8, part * FEATURES + k * WORDS : part * FEATURES + (k + 1) * WORDS]
                weighted = weighted + in_place(words, k) * value
            sums.append(jnp.sum(weighted, axis=0, keepdims=True))
            yield True
        columns = slice(k * WORDS, (k + 1) * WORDS)
        raw[here, columns] = jnp.concatenate([jnp.concatenate(sums, axis=0) * SHRINK[k], totals[:, columns]], axis=0)


def group_body(
    gate_hbm, up_hbm, down_hbm, tokens_hbm, grad_hbm, *small_hbm_and_rest
):
    small_hbm, rest = small_hbm_and_rest[:8], small_hbm_and_rest[8:]
    small, rest = rest[-8:], rest[:-8]
    group_work(gate_hbm, up_hbm, down_hbm, tokens_hbm, grad_hbm, small_hbm, small, *rest)


def group_work(
    gate_hbm, up_hbm, down_hbm, tokens_hbm, grad_hbm, small_hbm, small,
    own_ref, given_ref,
    gate_codes, up_codes, down_codes, gate_sems, up_sems, down_sems, tokens_ref, grad_ref, tokens_sems, grad_sems, small_sems,
    hidden_rows, gate_even, up_even, gate_odd, up_odd, down_pair, down_rows, halves, sums, totals,
):
    def copies(chunk):
        return (
            row_copy(chunk, gate_hbm, gate_codes, gate_sems),
            row_copy(chunk, up_hbm, up_codes, up_sems),
            column_copy(chunk, down_hbm, down_codes, down_sems),
        )

    def start(chunk):
        for copy in copies(chunk):
            copy.start()

    def rows_in(pair):
        return (
            pltpu.make_async_copy(tokens_hbm.at[:, pair], tokens_ref.at[:, pair], tokens_sems.at[pair]),
            pltpu.make_async_copy(grad_hbm.at[pair], grad_ref.at[pair], grad_sems.at[pair]),
        )

    gate_grad_ref, up_grad_ref, hidden_ref, gate_zeros, gate_log, up_zeros, up_log, table_ref = small
    arrivals = tables_in(small_hbm, small, small_sems)
    for copy in rows_in(0):
        copy.start()
    start(0)
    for pair in range(1, BLOCKS // 2):
        for copy in rows_in(pair):
            copy.start()
    start(1)
    for arrival in arrivals:
        arrival.wait()
    hidden_rows[...] = with_sums(hidden_ref[...], hidden_members())
    members = block_members()
    field_of_row = jnp.right_shift(lax.broadcasted_iota(jnp.int32, (OWN, 1), 0), 6)
    shrink = jnp.where(field_of_row == 0, SHRINK[0], jnp.where(field_of_row == 1, SHRINK[1], SHRINK[2]))
    shrink = jnp.broadcast_to(shrink, (OWN, LOCAL)).astype(jnp.bfloat16)

    def row_products(pair, part, gate_to, up_to):
        features = jnp.concatenate([tokens_ref[part * 2 + half, pair] * shrink for half in range(2)], axis=0)
        features = with_sums(features, members)
        for grad, to in ((gate_grad_ref, gate_to), (up_grad_ref, up_to)):
            for row in range(0, FEATURES + EXTRA, 80):
                to[row : row + 80, :] = jnp.dot(
                    features[row : row + 80, :], grad[...], preferred_element_type=jnp.float32
                )
                yield True

    def column_products(pair, down_to):
        for row in range(0, HIDDEN + EXTRA, 176):
            down_to[row : row + 176, :] = lax.dot_general(
                hidden_rows[row : row + 176, :], grad_ref[pair], CONTRACT_LAST, preferred_element_type=jnp.float32
            )
            yield True

    def groups(block, gate_from, up_from):
        yield from row_groups(block, gate_codes, gate_from, sums.at[0], totals.at[0])
        yield from row_groups(block, up_codes, up_from, sums.at[1], totals.at[1])

    def down_groups(pair):
        for part in range(2):
            yield from column_groups(pair * 2 + part, part, down_codes, down_pair, down_rows)

    for copy in rows_in(0):
        copy.wait()
    in_turn(row_products(0, 0, gate_even, up_even))

    def pair_step(pair, carry):
        for copy in copies(pair):
            copy.wait()
        following = jnp.minimum(pair + 1, BLOCKS // 2 - 1)

        @pl.when(pair < BLOCKS // 2 - 1)
        def _():
            for copy in rows_in(following):
                copy.wait()

        @pl.when(pair + 2 < CHUNKS)
        def _():
            start(pair + 2)

        in_turn(row_products(pair, 1, gate_odd, up_odd), groups(pair * 2, gate_even, up_even))
        in_turn(column_products(pair, down_pair), groups(pair * 2 + 1, gate_odd, up_odd))
        in_turn(row_products(following, 0, gate_even, up_even), down_groups(pair))
        return carry

    lax.fori_loop(0, BLOCKS // 2, pair_step, 0)

    for half, (zeros_ref, log_ref) in enumerate(((gate_zeros, gate_log), (up_zeros, up_log))):
        scale = jnp.exp(log_ref[...])
        halves[half, 0:48] = scale * (sums[half] - zeros_ref[...].astype(jnp.float32) * totals[half])
        halves[half, 48:96] = -scale * totals[half]
    found, table = down_rows[...].reshape(BLOCKS, 8, FEATURES), table_ref[...].reshape(BLOCKS, 8, FEATURES)
    found, total, zero, scale = found[:, 0:4], found[:, 4:8], table[:, 0:4], table[:, 4:8]
    finished = jnp.concatenate([scale * (found - zero * total), -scale * total], axis=1)
    down_rows[...] = finished.reshape(8 * BLOCKS, FEATURES)
    for half, begin in ((0, 0), (1, 48)):
        for j in range(3):
            halves[half, 96:144, j * 128 : (j + 1) * 128] = down_rows[begin : begin + 48, j * 128 : (j + 1) * 128]
    halves[0, 96:128, 384:] = down_rows[96:128, 0:128]
    halves[0, 128:144, 384:] = down_rows[96:112, 128:256]
    halves[1, 96:112, 384:] = down_rows[112:128, 128:256]
    halves[1, 112:144, 384:] = down_rows[96:128, 256:384]
    core = lax.axis_index("core")
    own_ref[...] = halves[core]
    given_ref[...] = halves[1 - core].astype(jnp.bfloat16)


def group_grads(tokens, grad, gate_grad, up_grad, hidden, gate_tables, up_tables, down_codes, table):
    half = struct((144, HIDDEN), jnp.float32)
    gate_codes, *gate_tables = gate_tables
    up_codes, *up_tables = up_tables
    small = (gate_grad, up_grad, hidden, *gate_tables, *up_tables, table)
    rows, columns = (FEATURES + EXTRA, HIDDEN), (HIDDEN + EXTRA, 2 * FEATURES)
    return call(
        group_body,
        (half, struct((144, HIDDEN), jnp.bfloat16)),
        [ANY] * 13,
        (VMEM, VMEM),
        [
            pltpu.VMEM((BLOCKS * WORDS, HIDDEN), jnp.int32),
            pltpu.VMEM((BLOCKS * WORDS, HIDDEN), jnp.int32),
            pltpu.VMEM((HIDDEN, BLOCKS * WORDS), jnp.int32),
        ]
        + [pltpu.SemaphoreType.DMA((CHUNKS,))] * 3
        + [
            pltpu.VMEM(TOKENS_SHAPE, jnp.bfloat16),
            pltpu.VMEM(GRAD_SHAPE, jnp.bfloat16),
            pltpu.SemaphoreType.DMA((BLOCKS // 2,)),
            pltpu.SemaphoreType.DMA((BLOCKS // 2,)),
            pltpu.SemaphoreType.DMA((8,)),
            pltpu.VMEM((HIDDEN + EXTRA, LOCAL), jnp.bfloat16),
        ]
        + [pltpu.VMEM(shape, jnp.float32) for shape in (rows,) * 4 + (columns,)]
        + [pltpu.VMEM((8 * BLOCKS, FEATURES), jnp.float32), pltpu.VMEM((2, 144, HIDDEN), jnp.float32)]
        + [pltpu.VMEM((2, 48, HIDDEN), jnp.float32)] * 2
        + [pltpu.VMEM(array.shape, array.dtype) for array in small],
        flops=3 * 2 * 128 * 6144 * 512,
        traffic=17000000,
        vmem=40,
    )(
        *from_hbm(gate_codes, up_codes, down_codes, tokens, grad, *small),
    )


def split_body(mine_ref, other_ref, gs_ref, gz_ref, us_ref, uz_ref, ds_ref, dz_ref, halves, rows):
    core = lax.axis_index("core")
    halves[core] = mine_ref[...]
    halves[1 - core] = other_ref[...]
    for half, scale_ref, zero_ref in ((0, gs_ref, gz_ref), (1, us_ref, uz_ref)):
        scale_ref[...] = halves[half, 0:48, :]
        zero_ref[...] = halves[half, 48:96, :]
        for j in range(3):
            rows[48 * half : 48 * half + 48, j * 128 : (j + 1) * 128] = halves[half, 96:144, j * 128 : (j + 1) * 128]
    rows[96:128, 0:128] = halves[0, 96:128, 384:]
    rows[96:112, 128:256] = halves[0, 128:144, 384:]
    rows[112:128, 128:256] = halves[1, 96:112, 384:]
    rows[96:128, 256:384] = halves[1, 112:144, 384:]
    natural = reorder(rows[...], True)
    for b in range(BLOCKS):
        columns = slice(b * FEATURES, (b + 1) * FEATURES)
        ds_ref[:, columns] = natural[8 * b : 8 * b + 4, :]
        dz_ref[:, columns] = natural[8 * b + 4 : 8 * b + 8, :]


def split(mine, other):
    f32 = jnp.float32
    return call(
        split_body,
        (struct((48, HIDDEN), f32),) * 4 + (struct((4, BLOCKS * FEATURES), f32),) * 2,
        [VMEM, VMEM],
        (VMEM,) * 6,
        [pltpu.VMEM((2, 144, HIDDEN), f32), pltpu.VMEM((8 * BLOCKS, FEATURES), f32)],
        traffic=1200000,
    )(mine, other)


def sum_body(parts_ref, out_ref):
    total = parts_ref[0].astype(jnp.float32)
    for part in range(1, SHARDS):
        total = total + parts_ref[part].astype(jnp.float32)
    for k in range(3):
        out_ref[pl.ds(k, THIRD, stride=3), :] = total[k * THIRD : (k + 1) * THIRD, :]


def sum_parts(parts):
    return call(sum_body, struct((OWN, LOCAL), jnp.float32), [VMEM], VMEM, traffic=1700000)(parts)


NEAR, ACROSS = ((0, 1), (2, 3)), ((0, 3), (1, 2))


def paired(block, axis, pairs):
    other = lax.ppermute(block, axis, [pair for a, b in pairs for pair in ((a, b), (b, a))])
    return jnp.concatenate([block, other])


def turned(block, axis, way):
    pairs = [(place, (place + way) % 4) for place in range(4)]
    pairs += [(4 + place, 4 + (place - way) % 4) for place in range(4)]
    return lax.ppermute(block, ("core", axis), pairs)


def swap(value, axis):
    return lax.ppermute(value, axis, [(0, 1), (1, 0)])


def shards(
    tokens,
    out_grad,
    gate_codes,
    gate_zeros,
    gate_log_scale,
    up_codes,
    up_zeros,
    up_log_scale,
    down_codes,
    down_zeros,
    down_log_scale,
):
    tokens_near, grad_near = by_field(tokens, out_grad)
    tokens_near, grad_near = paired(tokens_near, "y_lo", ((0, 1),)), paired(grad_near, "y_lo", ((0, 1),))
    tokens_near, grad_near = paired(tokens_near, "x", NEAR), paired(grad_near, "z", NEAR)
    tokens_near, gate_zeros = lax.optimization_barrier((tokens_near, gate_zeros))
    tokens_near, grad_near = paired(tokens_near, "x", ACROSS), paired(grad_near, "z", ACROSS)
    gate = unpack_rows(gate_codes, gate_zeros, gate_log_scale)
    tokens_near, gate, up_zeros = lax.optimization_barrier((tokens_near, gate, up_zeros))
    grad_near, up_log_scale = lax.optimization_barrier((grad_near, up_log_scale))
    tokens_first, grad_first = turned(tokens_near, "z", 1), turned(grad_near, "x", 1)
    tokens_second, grad_second = turned(tokens_near, "z", -1), turned(grad_near, "x", -1)
    up = unpack_rows(up_codes, up_zeros, up_log_scale)
    tokens_first, grad_first, up, down_zeros = lax.optimization_barrier((tokens_first, grad_first, up, down_zeros))
    tokens_parts = tokens_near, tokens_first, turned(tokens_first, "z", 1), tokens_second
    grad_parts = grad_near, grad_first, turned(grad_first, "x", 1), grad_second
    down, table = unpack_columns(down_codes, down_zeros, down_log_scale)
    *sums, all_tokens, all_grad = forward(tokens_parts, grad_parts, gate, up, down)
    partial, all_tokens, all_grad, gate_grad, up_grad, hidden = backward(
        tokens_parts, grad_parts, gate, up, down, sums, all_tokens, all_grad
    )
    parts = lax.all_to_all(partial.reshape(SHARDS, OWN, LOCAL), ("x", "y_lo", "z"), 0, 0, tiled=True)
    own, given = group_grads(
        all_tokens,
        all_grad,
        gate_grad,
        up_grad,
        hidden,
        (gate_codes, gate_zeros, gate_log_scale),
        (up_codes, up_zeros, up_log_scale),
        down_codes,
        table,
    )
    own = own + swap(given, "core").astype(jnp.float32)
    own = own.astype(jnp.bfloat16)
    tokens_grad = sum_parts(parts).T
    far, tokens_grad = lax.optimization_barrier((swap(own, "y_hi"), tokens_grad))
    mine = own.astype(jnp.float32) + far.astype(jnp.float32)
    theirs = swap(mine, "core")
    return (tokens_grad, *split(mine, theirs))


def solution(mesh):
    axes = jax.sharding.Mesh(mesh.devices.reshape(2, 2, N_X, N_Y, N_Z), ("y_hi", "core", "x", "y_lo", "z"))
    dp, tensor = ("y_hi", "core"), ("x", "y_lo", "z")
    columns, rows = P(None, tensor), P(tensor, None)
    return jax.shard_map(
        shards,
        mesh=axes,
        in_specs=(P(dp, tensor),) * 2 + (columns,) * 6 + (rows,) * 3,
        out_specs=(P(dp, tensor),) + (columns,) * 4 + (rows,) * 2,
        check_vma=False,
    )
```
